32 devices in a mesh: dp: 8 (over y, x, core), tensor: 4 (over z).
Axes of the slice: x: 2, y: 2, z: 4, core: 2. Of those that a mesh axis runs over, the one named last changes fastest.
Arguments:
- tokens: bfloat16 [8192, 768], P('dp'), may hold values from -6 to 6
- segments: int32 [8, 1024], P('dp'), may hold values from 0 to 3, as said below
- routes: int32 [8192, 2], P('dp'), may hold values from 0 to 3, all different within a row; in each aligned block of 1024 rows (0 to 1023, 1024 to 2047, ...) at most 704 rows name the same one
- grad_out: bfloat16 [8192, 768], P('dp'), may hold values from -6 to 6
- gain_attn: bfloat16 [768], replicated, may hold values from 0.5 to 1.5
- w_qkv: bfloat16 [3, 768, 768], P(None, None, 'tensor'), may hold values from -0.21875 to 0.21875
- w_out: bfloat16 [768, 768], P('tensor'), may hold values from -0.875 to 0.875
- rel_bias: bfloat16 [32, 12], P(None, 'tensor'), may hold values from -4 to 4
- gain_moe: bfloat16 [768], replicated, may hold values from 0.5 to 1.5
- w_router: bfloat16 [768, 4], replicated, may hold values from -0.15625 to 0.15625
- w_in: bfloat16 [4, 768, 3072], P(None, None, 'tensor'), may hold values from -0.21875 to 0.21875
- w_down: bfloat16 [4, 3072, 768], P(None, 'tensor'), may hold values from -0.15625 to 0.15625
Outputs:
- result: bfloat16 [8192, 768], P('dp')
- grad_tokens: float32 [8192, 768], P('dp')
- grad_gain_attn: float32 [768], replicated
- grad_w_qkv: float32 [3, 768, 768], P(None, None, 'tensor')
- grad_w_out: float32 [768, 768], P('tensor')
- grad_rel_bias: float32 [32, 12], P(None, 'tensor')
- grad_gain_moe: float32 [768], replicated
- grad_w_router: float32 [768, 4], replicated
- grad_w_in: float32 [4, 768, 3072], P(None, None, 'tensor')
- grad_w_down: float32 [4, 3072, 768], P(None, 'tensor')
The draws below stay inside these ranges and needn't reach their ends.
Inputs may be any that keep to these rules, and one draw needn't show every extreme that they name: `routes`: the two experts of a token differ. Among the 1024 rows of one index of dp no expert is named more than 704 times, a bound that some block reaches. `segments`: document numbers start at 0 and rise by one at each document's end; a sequence holds 2 to 4 documents, each of 204 positions or more.
All inputs are finite; a program needn't handle non-finite values.
Results may differ from the reference program's by a relative error of at most 0.017.
Values may be sent and summed in bfloat16 or wider, within the bound.
No kernel may reach another device: no remote copies, remote signals or barrier semaphores. Data moves between devices by JAX's collectives and lax.ppermute only.
A program may use at most 192 MiB of HBM per device.

```python
import math
import jax
import jax.numpy as jnp
import numpy as np
from jax import lax

D = 768
HEADS = 12
HD = 64
FF = 3072
E = 4
NB = 32
DIST = 128
LEN = 1024
SEQS_DEV = 1
DOC_MIN = 204
TOK = 1024
CAP = 704
SEQUENCES = 8
TOKENS = 8192


def draw_segments(key, part):
    key = jax.random.fold_in(key, 11)
    key_count, key_weight, key_full = jax.random.split(key, 3)
    doc_count = jax.random.randint(key_count, (SEQUENCES, 1), 2, 5)
    fullest = jax.random.randint(key_full, (), 0, SEQUENCES)
    doc_count = jnp.where(jnp.arange(SEQUENCES)[:, None] == fullest, 4, doc_count).astype(jnp.int32)
    raw_weights = jax.random.randint(key_weight, (SEQUENCES, 4), 1, 101)
    active = (jnp.arange(4)[None, :] < doc_count).astype(jnp.int32)
    weights = raw_weights * active
    spare = LEN - doc_count * DOC_MIN
    share = spare * weights // jnp.sum(weights, axis=1, keepdims=True)
    lengths = active * DOC_MIN + share
    ends = jnp.cumsum(lengths, axis=1)
    position = jnp.arange(LEN)
    passed = jnp.sum((position[None, :, None] >= ends[:, None, :]).astype(jnp.int32), axis=2)
    return jnp.minimum(passed, doc_count - 1).astype(jnp.int32)


def shard_levels(key, extent, cuts, low, high):
    gain, own = 1.0, jax.random.fold_in(key, 6)
    for dim, shards_of in cuts:
        draws = jnp.exp(jax.random.uniform(jax.random.fold_in(own, dim), (shards_of,), jnp.float32, low / len(cuts), high / len(cuts)))
        gain = gain * jnp.repeat(draws, extent[dim] // shards_of).reshape([-1 if axis == dim else 1 for axis in range(len(extent))])
    return gain


def deal_out(rng, own, number, rows, amount, top, limit, slope):
    sequence = jax.random.permutation(rng, amount)
    crowded, usual = shares(amount, rows * top, limit, slope, True), shares(amount, rows * top, limit, slope, False)
    places = jnp.arange(amount)

    def named(tallies, rotation):
        used = int((tallies > 0).sum())
        fixed = max(1, used // 4)
        moved = fixed + (places - fixed + rotation * (used - fixed)) % max(1, amount - fixed)
        return jnp.zeros((amount,), jnp.int32).at[sequence[jnp.where(places < fixed, places, moved)]].set(jnp.asarray(tallies, jnp.int32))

    tallies = jnp.where(number % 4 == 0, named(crowded, number // 4), named(usual, number - number // 4 - 1))
    mixed = jax.random.permutation(jax.random.fold_in(own, 3), amount)
    giver, sink = mixed[0:amount // 2 * 2:2], mixed[1:amount // 2 * 2:2]
    margin = jnp.minimum(tallies[giver] - 1, limit - tallies[sink]) // 2
    margin = jnp.where((giver == sequence[0]) | (sink == sequence[0]) | (tallies[sink] == 0), 0, jnp.maximum(margin, 0))
    moved = jax.random.randint(jax.random.fold_in(own, 4), (amount // 2,), 0, 1 << 20) % (margin + 1)
    tallies = tallies.at[giver].add(-moved).at[sink].add(moved)
    items = jnp.searchsorted(jnp.cumsum(tallies), jnp.arange(rows * top), side="right").astype(jnp.int32)
    table = items.reshape(top, rows).T
    table = table[jax.random.permutation(jax.random.fold_in(own, 1), rows)]
    rotation = jax.random.randint(jax.random.fold_in(own, 2), (rows, 1), 0, top)
    return jnp.take_along_axis(table, (jnp.arange(top)[None, :] + rotation) % top, axis=1)


def shares(amount, total, reach, slope, full):
    weights = [(1 << 20) // math.isqrt(rank ** slope) + 1 for rank in range(1, amount + 1)]
    largest = reach if full else min(reach, max(-(-total // amount), total * weights[0] // sum(weights)))
    least = 1 if total - largest >= amount - 1 else 0
    counts, surplus = [largest] + [least] * (amount - 1), total - largest - least * (amount - 1)
    while surplus > 0:
        candidates = [i for i in range(1, amount) if counts[i] < largest] or [i for i in range(1, amount) if counts[i] < reach]
        pool, budget = sum([weights[i] for i in candidates]), surplus
        for i in candidates:
            more = min(reach - counts[i], max(1, budget * weights[i] // pool), surplus)
            counts[i] = counts[i] + more
            surplus = surplus - more
    return np.array(counts)


def gaussian(key, dims, deviation, reach, cuts=(), dtype=jnp.bfloat16):
    array = deviation * jax.random.normal(key, dims, jnp.float32)
    if cuts:
        array = array * shard_levels(key, dims, cuts, -0.22, 0.18)
    return jnp.clip(array, -reach, reach).astype(dtype)


def setup_inputs(seed: int = 0) -> dict:
    key_list = jax.random.split(jax.random.key(seed), 13)
    tokens = gaussian(key_list[0], (TOKENS, D), 1.0, 6.0, ((0, 8),))
    segments = draw_segments(jax.random.fold_in(key_list[12], 71), 0)
    routes_keys = jax.random.split(jax.random.fold_in(key_list[2], 1), TOKENS // TOK)
    routes_turns = jax.random.permutation(jax.random.fold_in(key_list[2], 3), TOKENS // TOK)
    routes = jax.vmap(lambda own, number: deal_out(jax.random.fold_in(key_list[2], 2), own, number, TOK, E, 2, CAP, 1))(routes_keys, routes_turns).reshape((TOKENS, 2))
    grad_out = gaussian(key_list[3], (TOKENS, D), 1.0, 6.0, ((0, 8),))
    gain_attn = jnp.clip(1.0 + 0.1 * jax.random.normal(key_list[4], (D,), jnp.float32), 0.5, 1.5).astype(jnp.bfloat16)
    w_qkv = gaussian(key_list[5], (3, D, HEADS * HD), D ** -0.5, 0.21875, ((2, 4),))
    w_out = gaussian(key_list[6], (HEADS * HD, D), (HEADS * HD // 16) ** -0.5, 0.875, ((0, 4),))
    rel_bias = gaussian(key_list[7], (NB, HEADS), 1.0, 4.0, ((1, 4),))
    gain_moe = jnp.clip(1.0 + 0.1 * jax.random.normal(key_list[8], (D,), jnp.float32), 0.5, 1.5).astype(jnp.bfloat16)
    w_router = gaussian(key_list[9], (D, E), (2 * D) ** -0.5, 0.15625)
    w_in = gaussian(key_list[10], (E, D, FF), D ** -0.5, 0.21875, ((2, 4),))
    w_down = gaussian(key_list[11], (E, FF, D), (FF // 2) ** -0.5, 0.15625, ((1, 4),))
    return {"tokens": tokens, "segments": segments, "routes": routes, "grad_out": grad_out, "gain_attn": gain_attn, "w_qkv": w_qkv, "w_out": w_out, "rel_bias": rel_bias, "gain_moe": gain_moe, "w_router": w_router, "w_in": w_in, "w_down": w_down}


@jax.custom_vjp
def low(v):
    return lax.optimization_barrier(v.astype(jnp.bfloat16)).astype(jnp.float32)

@jax.custom_vjp
def low_back(v):
    return v

def low_keep(v):
    return (low(v), None)

def low_pass(kept, grad):
    return (grad,)

def back_keep(v):
    return (v, None)

def back_low(kept, grad):
    return (low(grad),)
low.defvjp(low_keep, low_pass)
low_back.defvjp(back_keep, back_low)
EPSILON = 1e-06
NEGATIVE = -1e+30
HIGHEST = lax.Precision.HIGHEST

def bucket_ids(distance):
    halfway = NB // 2
    thresholds = [int(math.ceil(halfway * (DIST / halfway) ** (step / halfway))) for step in range(halfway)]
    beyond = jnp.zeros_like(distance)
    for threshold in thresholds:
        beyond = beyond + (distance >= threshold).astype(jnp.int32)
    return jnp.where(distance < halfway, distance, halfway - 1 + beyond)

def gelu_tanh(values):
    inner_arg = 0.7978845608028654 * (values + 0.044715 * values * values * values)
    return 0.5 * values * (1.0 + jnp.tanh(inner_arg))

def slot_positions(route_rows):
    flat_routes = route_rows.reshape(-1)
    one_hot = (flat_routes[:, None] == jnp.arange(E)[None, :]).astype(jnp.int32)
    earlier = jnp.cumsum(one_hot, axis=0) - one_hot
    slot_index = lax.optimization_barrier(jnp.sum(earlier * one_hot, axis=1))
    return (flat_routes * CAP + slot_index).astype(jnp.int32)

def block_forward(inputs, gain_attn, w_qkv, w_out, rel_bias, gain_moe, w_router, w_in, w_down, seg_rows, route_rows):
    tok_rows = inputs.shape[0]
    seq_count = seg_rows.shape[0]
    scale_one = lax.rsqrt(lax.optimization_barrier(jnp.mean(inputs * inputs, axis=-1, keepdims=True)) + EPSILON)
    normed_one = low(inputs * scale_one * gain_attn)
    projected = jnp.einsum('td,cdf->ctf', normed_one, w_qkv, precision=HIGHEST)
    projected = low(low_back(projected))
    grouped = projected.reshape(3, seq_count, LEN, HEADS, HD)
    positions = jnp.arange(LEN)
    by_distance = rel_bias[bucket_ids(positions)]

    def attend(pieces):
        query_rows, key_rows, value_rows, seg_row = pieces
        raw_scores = low_back(jnp.einsum('qhe,khe->hqk', query_rows, key_rows, precision=HIGHEST))
        distance = positions[:, None] - positions[None, :]
        allowed = (distance >= 0) & (seg_row[:, None] == seg_row[None, :])
        bias_rows = jnp.transpose(by_distance[jnp.maximum(distance, 0)], (2, 0, 1))
        scores = jnp.where(allowed[None], raw_scores * HD ** (-0.5) + bias_rows, NEGATIVE)
        row_peak = lax.optimization_barrier(jnp.max(scores, axis=-1, keepdims=True))
        raised = jnp.exp(scores - row_peak)
        prob_rows = raised / lax.optimization_barrier(jnp.sum(raised, axis=-1, keepdims=True))
        return jnp.einsum('hqk,khe->qhe', low(prob_rows), value_rows, precision=HIGHEST)
    attended = lax.map(jax.checkpoint(attend), (grouped[0], grouped[1], grouped[2], seg_rows))
    attended = low(low_back(attended.reshape(tok_rows, HEADS * HD)))
    attn_sum = low_back(jnp.dot(attended, w_out, precision=HIGHEST))
    hidden_one = inputs + attn_sum
    scale_two = lax.rsqrt(lax.optimization_barrier(jnp.mean(hidden_one * hidden_one, axis=-1, keepdims=True)) + EPSILON)
    normed_two = low(hidden_one * scale_two * gain_moe)
    logits = jnp.dot(normed_two, w_router, precision=HIGHEST)
    chosen = jnp.take_along_axis(logits, route_rows, axis=1)
    row_peak = lax.optimization_barrier(jnp.max(chosen, axis=1, keepdims=True))
    raised = jnp.exp(chosen - row_peak)
    gate_values = raised / lax.optimization_barrier(jnp.sum(raised, axis=1, keepdims=True))
    position = slot_positions(route_rows)
    buffer = jnp.zeros((E * CAP, D), jnp.float32).at[position].set(jnp.repeat(normed_two, 2, axis=0))
    pre_act = low_back(jnp.einsum('ecd,edf->ecf', buffer.reshape(E, CAP, D), w_in, precision=HIGHEST))
    activated = low(gelu_tanh(pre_act))
    expert_out = low_back(jnp.einsum('ecf,efd->ecd', activated, w_down, precision=HIGHEST)).reshape(E * CAP, D)
    picked = expert_out[position].reshape(tok_rows, 2, D)
    return hidden_one + lax.optimization_barrier(jnp.sum(gate_values[:, :, None] * picked, axis=1))

def reference(tokens, segments, routes, grad_out, gain_attn, w_qkv, w_out, rel_bias, gain_moe, w_router, w_in, w_down):
    weights = tuple((weight.astype(jnp.float32) for weight in (gain_attn, w_qkv, w_out, rel_bias, gain_moe, w_router, w_in, w_down)))
    groups = TOKENS // TOK
    token_groups = tokens.astype(jnp.float32).reshape(groups, TOK, D)
    grad_groups = grad_out.astype(jnp.float32).reshape(groups, TOK, D)
    seg_groups = segments.reshape(groups, SEQS_DEV, LEN)
    route_groups = routes.reshape(groups, TOK, 2)

    def one_group(totals, pieces):
        inputs, cotangent, seg_rows, route_rows = pieces

        def forward(inputs, *params):
            return block_forward(inputs, *params, seg_rows, route_rows)
        outcome, pullback = jax.vjp(forward, inputs, *weights)
        gradients = pullback(cotangent)
        totals = tuple((running + gradient for running, gradient in zip(totals, gradients[1:])))
        return (totals, (outcome.astype(jnp.bfloat16), gradients[0]))
    initial = tuple((jnp.zeros_like(weight) for weight in weights))
    totals, (outputs, input_grads) = lax.scan(one_group, initial, (token_groups, grad_groups, seg_groups, route_groups))
    return (outputs.reshape(TOKENS, D), input_grads.reshape(TOKENS, D), totals[0], totals[1], totals[2], totals[3], totals[4], totals[5], totals[6], totals[7])
```

```python
import functools
import math

import jax
import jax.numpy as jnp
import numpy as np
from jax import lax
from jax.experimental import pallas as pl
from jax.experimental.pallas import tpu as pltpu
from jax.sharding import PartitionSpec as P

NB = 32
DIST = 128
EPSILON = 1e-06
NEGATIVE = -1e30
HIGHEST = lax.Precision.HIGHEST
F32 = jnp.float32
BF16 = jnp.bfloat16
BLK = 256
LANES = 128
VMEM_LIMIT = 56 * 1024 * 1024

NN = (((1,), (0,)), ((), ()))
NT = (((1,), (1,)), ((), ()))
TN = (((0,), (0,)), ((), ()))


def dot(a, b, dims=NN, precision=None):
    return lax.dot_general(a, b, dims, precision=precision, preferred_element_type=F32)


def bucket_of(distance):
    halfway = NB // 2
    thresholds = [
        int(math.ceil(halfway * (DIST / halfway) ** (step / halfway))) for step in range(halfway)
    ]
    beyond = sum((distance >= threshold).astype(np.int64) for threshold in thresholds)
    return np.where(distance < halfway, distance, halfway - 1 + beyond)


def near_tables():
    lanes = np.arange(2 * BLK)
    offset = np.where(lanes < BLK, lanes, lanes - 2 * BLK)
    build = np.stack([np.maximum(offset, 0), np.maximum(BLK + offset, 0)])
    gather = np.stack([lanes - (BLK - 1), lanes + 1])
    eye = np.eye(NB, dtype=np.float32)
    build_hot = eye[bucket_of(build)]
    gather_hot = eye[bucket_of(np.maximum(gather, 0))] * (gather >= 0)[..., None]
    return build_hot, gather_hot


def row_scale(values):
    return lax.rsqrt(jnp.mean(values * values, axis=-1, keepdims=True) + EPSILON)


def lane_pick(values, index):
    lanes = lax.broadcasted_iota(jnp.int32, values.shape, 1)
    return jnp.sum(jnp.where(lanes == index, values, 0.0), axis=1, keepdims=True)


def masked_scores(k_tile, qh_tile, bias, seg_k, seg_q, diagonal):
    scores = dot(k_tile, qh_tile, NT) + bias
    allowed = seg_k == seg_q
    if diagonal:
        key_at = lax.broadcasted_iota(jnp.int32, scores.shape, 0)
        query_at = lax.broadcasted_iota(jnp.int32, scores.shape, 1)
        allowed = allowed & (key_at <= query_at)
    return jnp.where(allowed, scores, NEGATIVE)


def tile_bias(bias_ref, far_ref, head, delta):
    if delta < 2:
        return bias_ref[2 * head + delta]
    return far_ref[pl.ds(head, 1), 0:1]


def attn_fwd_kernel(
    heads, head_size, tok, gain, w, seg_row, seg_col, near, far,
    normed, qh, k, v, att, ot, lse, bias, vt,
):
    rows_total = tok.shape[0]
    features = w.shape[2]
    blocks = rows_total // BLK
    gain_row = gain[...].astype(F32)
    lanes = lax.broadcasted_iota(jnp.int32, (BLK, features), 1)
    for block in range(blocks):
        rows = pl.ds(block * BLK, BLK)
        x = tok[rows, :].astype(F32)
        n = (x * row_scale(x) * gain_row).astype(BF16)
        normed[rows, :] = n
        q_rows = dot(n, w[0]).astype(BF16).astype(F32) * (head_size**-0.5)
        for head in range(heads):
            inside = (lanes >= head * head_size) & (lanes < (head + 1) * head_size)
            qh[head, rows, :] = jnp.where(inside, q_rows, 0.0).astype(BF16)
        k[rows, :] = dot(n, w[1]).astype(BF16)
        v_rows = dot(n, w[2]).astype(BF16)
        v[rows, :] = v_rows
        vt[:, rows] = v_rows.astype(F32).T.astype(BF16)
    for index in range(2 * heads):
        spread = jnp.broadcast_to(near[index : index + 1, :], (BLK, 2 * BLK))
        bias[index] = pltpu.roll(spread, 0, 1, stride=1, stride_axis=0)[:, :BLK]
    lse[...] = jnp.zeros_like(lse)

    def one_head(head, carry):
        part = pl.ds(pl.multiple_of(head * head_size, head_size), head_size)
        for qb in range(blocks):
            cols = pl.ds(qb * BLK, BLK)
            q_tile = qh[head, cols, :]
            tiles = []
            for kb in range(qb + 1):
                keys = pl.ds(kb * BLK, BLK)
                tiles.append(
                    masked_scores(
                        k[keys, :], q_tile, tile_bias(bias, far, head, qb - kb),
                        seg_col[keys, :], seg_row[:, cols], kb == qb,
                    )
                )
            peak = functools.reduce(
                jnp.maximum, [jnp.max(t, axis=0, keepdims=True) for t in tiles]
            )
            total = jnp.zeros((1, BLK), F32)
            out = jnp.zeros((head_size, BLK), F32)
            for kb in range(qb + 1):
                raised = jnp.exp(tiles[kb] - peak)
                total = total + jnp.sum(raised, axis=0, keepdims=True)
                out = out + dot(vt[part, kb * BLK : (kb + 1) * BLK], raised.astype(BF16))
            ot[part, cols] = out / total
            lse[pl.ds(head, 1), cols] = peak + jnp.log(total)
        return carry

    lax.fori_loop(0, heads, one_head, 0)
    for block in range(blocks):
        cols = pl.ds(block * BLK, BLK)
        att[cols, :] = ot[:, cols].T.astype(BF16)


def attn_bwd_kernel(heads, head_size, shares, idx, *refs):
    go_parts, refs = refs[:shares], refs[shares:]
    qh, k, v, ot, lse, bias, far, seg_row, seg_col, w = refs[:10]
    refs = refs[10:]
    gn_parts, refs = refs[:shares], refs[shares:]
    gproj, near_sum, far_sum, go, gq_t, gk, gv, kt, d_row, acc, acc_far = refs
    rows_total, features = k.shape
    blocks = rows_total // BLK
    share = rows_total // shares
    me = idx[0]
    for step in range(shares):
        start = pl.multiple_of(lax.rem(me + step, shares) * share, share)
        go[pl.ds(start, share), :] = go_parts[step][...]
    for block in range(blocks):
        cols = pl.ds(block * BLK, BLK)
        kt[:, cols] = k[cols, :].astype(F32).T.astype(BF16)
        product = go[cols, :].astype(F32).T * ot[:, cols]
        for head in range(heads):
            part = product[head * head_size : (head + 1) * head_size, :]
            d_row[head : head + 1, cols] = jnp.sum(part, axis=0, keepdims=True)
    gk[...] = jnp.zeros_like(gk)
    gv[...] = jnp.zeros_like(gv)
    near_sum[...] = jnp.zeros_like(near_sum)
    far_sum[...] = jnp.zeros_like(far_sum)
    key_at = lax.broadcasted_iota(jnp.int32, (BLK, BLK), 0)
    other_at = lax.broadcasted_iota(jnp.int32, (BLK, BLK), 1)
    flip = (key_at + other_at == BLK - 1).astype(F32)

    def one_head(head, carry):
        part = pl.ds(pl.multiple_of(head * head_size, head_size), head_size)
        lanes = lax.broadcasted_iota(jnp.int32, (BLK, features), 1)
        inside = (lanes >= head * head_size) & (lanes < (head + 1) * head_size)
        acc[...] = jnp.zeros_like(acc)
        acc_far[...] = jnp.zeros_like(acc_far)
        for qb in range(blocks):
            cols = pl.ds(qb * BLK, BLK)
            q_tile = qh[head, cols, :]
            go_tile = jnp.where(inside, go[cols, :].astype(F32), 0.0).astype(BF16)
            log_total = lse[pl.ds(head, 1), cols]
            d_tile = d_row[pl.ds(head, 1), cols]
            gq = jnp.zeros((head_size, BLK), F32)
            for kb in range(qb + 1):
                keys = pl.ds(kb * BLK, BLK)
                delta = qb - kb
                scores = masked_scores(
                    k[keys, :], q_tile, tile_bias(bias, far, head, delta),
                    seg_col[keys, :], seg_row[:, cols], delta == 0,
                )
                probs = jnp.exp(scores - log_total)
                gs = probs * (dot(v[keys, :], go_tile, NT) - d_tile)
                if delta < 2:
                    acc[delta] += gs
                else:
                    acc_far[...] += gs
                gs_low = gs.astype(BF16)
                gv[keys, :] += dot(probs.astype(BF16), go_tile)
                gk[keys, :] += dot(gs_low, q_tile)
                gq = gq + dot(kt[part, kb * BLK : (kb + 1) * BLK], gs_low)
            gq_t[part, cols] = gq * (head_size**-0.5)
        for delta in range(2):
            turned = dot(flip, acc[delta], NN, HIGHEST)
            wide = jnp.concatenate([turned, jnp.zeros_like(turned)], axis=1)
            sheared = pltpu.roll(wide, 0, 1, stride=1, stride_axis=0)
            near_sum[pl.ds(2 * head + delta, 1), :] = jnp.sum(sheared, axis=0, keepdims=True)
        far_sum[pl.ds(head, 1), :] = jnp.sum(acc_far[...], axis=0, keepdims=True)
        return carry

    lax.fori_loop(0, heads, one_head, 0)
    for block in range(blocks):
        rows = pl.ds(block * BLK, BLK)
        gproj[0, rows, :] = gq_t[:, rows].T.astype(BF16)
        gproj[1, rows, :] = gk[rows, :].astype(BF16)
        gproj[2, rows, :] = gv[rows, :].astype(BF16)
    for step in range(shares):
        start = pl.multiple_of(lax.rem(me + step, shares) * share, share)
        rows = pl.ds(start, share)
        total = dot(gproj[0, rows, :], w[0], NT)
        total = total + dot(gproj[1, rows, :], w[1], NT)
        total = total + dot(gproj[2, rows, :], w[2], NT)
        gn_parts[step][...] = total.astype(BF16)


def gelu_pair(values):
    inner = 0.7978845608028654 * (values + 0.044715 * values * values * values)
    bent = jnp.tanh(inner)
    half = 0.5 * (1.0 + bent)
    slope = 0.7978845608028654 * (1.0 + 3.0 * 0.044715 * values * values)
    return values * half, half + 0.5 * values * (1.0 - bent * bent) * slope


ROWS = 512


def moe_fwd_kernel(shares, experts, idx, *refs):
    att, refs = refs[:shares], refs[shares:]
    wo, refs = refs[:shares], refs[shares:]
    tok, gain, router, routes, cot, w_in, w_down = refs[:7]
    refs = refs[7:]
    parts, refs = refs[:shares], refs[shares:]
    normed, own, gates, ggate, act, slope, acc = refs
    rows_total = tok.shape[0]
    share = rows_total // shares
    me = idx[0]
    expert = pl.program_id(0)

    @pl.when(expert == 0)
    def _():
        gain_row = gain[...].astype(F32)
        for block in range(rows_total // BLK):
            rows = pl.ds(block * BLK, BLK)
            hidden = tok[rows, :].astype(F32)
            attn = dot(att[0][rows, :], wo[0][...])
            for step in range(1, shares):
                attn = attn + dot(att[step][rows, :], wo[step][...])
            hidden = hidden + attn
            acc[rows, :] = hidden
            n = (hidden * row_scale(hidden) * gain_row).astype(BF16)
            normed[rows, :] = n
            logits = dot(n, router[...])
            lanes = lax.broadcasted_iota(jnp.int32, logits.shape, 1)
            first = lanes == routes[rows, 0:1]
            second = lanes == routes[rows, 1:2]
            one = jnp.sum(jnp.where(first, logits, 0.0), axis=1, keepdims=True)
            two = jnp.sum(jnp.where(second, logits, 0.0), axis=1, keepdims=True)
            peak = jnp.maximum(one, two)
            one = jnp.exp(one - peak)
            two = jnp.exp(two - peak)
            both = one + two
            gates[rows, :] = jnp.where(first, one / both, jnp.where(second, two / both, 0.0))
        own[...] = acc[pl.ds(pl.multiple_of(me * share, share), share), :]
        acc[...] = jnp.zeros_like(acc)
        ggate[...] = jnp.zeros_like(ggate)

    for block in range(rows_total // ROWS):
        rows = pl.ds(block * ROWS, ROWS)
        lifted, bend = gelu_pair(dot(normed[rows, :], w_in[0]))
        lifted = lifted.astype(BF16)
        act[0, rows, :] = lifted
        slope[0, rows, :] = bend.astype(BF16)
        out = dot(lifted, w_down[0])
        gate = lane_pick(gates[rows, :], expert)
        acc[rows, :] += gate * out
        pulled = jnp.sum(cot[rows, :].astype(F32) * out, axis=1, keepdims=True)
        held = ggate[rows, :]
        lanes = lax.broadcasted_iota(jnp.int32, held.shape, 1)
        ggate[rows, :] = jnp.where(lanes == expert, pulled, held)

    @pl.when(expert == experts - 1)
    def _():
        for step in range(shares):
            start = pl.multiple_of(lax.rem(me + step, shares) * share, share)
            parts[step][...] = acc[pl.ds(start, share), :].astype(BF16)


def moe_bwd_kernel(shares, experts, idx, *refs):
    gates, ggate, cot, slope, router_t, w_in, w_down = refs[:7]
    refs = refs[7:]
    parts, refs = refs[:shares], refs[shares:]
    glog, gpre, acc = refs
    rows_total = cot.shape[0]
    share = rows_total // shares
    me = idx[0]
    expert = pl.program_id(0)

    @pl.when(expert == 0)
    def _():
        for block in range(rows_total // ROWS):
            rows = pl.ds(block * ROWS, ROWS)
            g, gg = gates[rows, :], ggate[rows, :]
            back = g * (gg - jnp.sum(g * gg, axis=1, keepdims=True))
            glog[rows, :] = back
            acc[rows, :] = dot(back, router_t[...], NN, HIGHEST)

    for block in range(rows_total // ROWS):
        rows = pl.ds(block * ROWS, ROWS)
        gate = lane_pick(gates[rows, :], expert)
        weighted = (gate * cot[rows, :].astype(F32)).astype(BF16)
        gp = (dot(weighted, w_down[0], NT) * slope[0, rows, :].astype(F32)).astype(BF16)
        gpre[0, rows, :] = gp
        acc[rows, :] += dot(gp, w_in[0], NT)

    @pl.when(expert == experts - 1)
    def _():
        for step in range(shares):
            start = pl.multiple_of(lax.rem(me + step, shares) * share, share)
            parts[step][...] = acc[pl.ds(start, share), :].astype(BF16)


def moe_weights_kernel(gates, cot, normed, act, gpre, out):
    expert = pl.program_id(0)
    gate = lane_pick(gates[...], expert)
    weighted = (gate * cot[...].astype(F32)).astype(BF16)
    out[0, 0] = dot(normed[...], gpre[0], TN).astype(BF16)
    out[0, 1] = dot(act[0], weighted, TN).astype(BF16)


def hidden_back_kernel(shares, idx, *refs):
    gx, refs = refs[:shares], refs[shares:]
    wo, refs = refs[:shares], refs[shares:]
    own, cot, gain = refs[:3]
    refs = refs[3:]
    ga, refs = refs[:shares], refs[shares:]
    gh, gh_low, ggain = refs
    share = own.shape[0]
    grad = gx[0][...].astype(F32)
    for step in range(1, shares):
        grad = grad + gx[step][...].astype(F32)
    hidden = own[...]
    scale = row_scale(hidden)
    unit = hidden * scale
    ggain[...] = jnp.sum(grad * unit, axis=0, keepdims=True)
    gained = grad * gain[...].astype(F32)
    mine = cot[pl.ds(pl.multiple_of(idx[0] * share, share), share), :].astype(F32)
    back = mine + scale * (gained - unit * jnp.mean(gained * unit, axis=-1, keepdims=True))
    gh[...] = back
    low = back.astype(BF16)
    gh_low[...] = low
    for step in range(shares):
        ga[step][...] = dot(low, wo[step][...], NT).astype(BF16)


def w_out_back_kernel(shares, idx, *refs):
    att = refs[:shares]
    gh_low, out = refs[shares:]
    share = gh_low.shape[0]
    rows = pl.ds(pl.multiple_of(idx[0] * share, share), share)
    low = gh_low[...]
    for step in range(shares):
        out[step] = dot(att[step][rows, :], low, TN).astype(BF16)


def input_back_kernel(shares, idx, *refs):
    gn, refs = refs[:shares], refs[shares:]
    tok, gh, gain, gt, ggain = refs
    share = gh.shape[0]
    grad = gn[0][...].astype(F32)
    for step in range(1, shares):
        grad = grad + gn[step][...].astype(F32)
    x = tok[pl.ds(pl.multiple_of(idx[0] * share, share), share), :].astype(F32)
    scale = row_scale(x)
    unit = x * scale
    ggain[...] = jnp.sum(grad * unit, axis=0, keepdims=True)
    gained = grad * gain[...].astype(F32)
    back = gh[...] + scale * (gained - unit * jnp.mean(gained * unit, axis=-1, keepdims=True))
    gt[...] = back.astype(BF16)


def place_kernel(shares, idx, *refs):
    blocks, out = refs[:shares], refs[shares]
    share = out.shape[0] // shares
    for step in range(shares):
        start = pl.multiple_of(lax.rem(idx[0] + shares - step, shares) * share, share)
        out[pl.ds(start, share), :] = blocks[step][...].astype(out.dtype)


SMEM = pl.BlockSpec(memory_space=pltpu.SMEM)
VMEM = pl.BlockSpec(memory_space=pltpu.VMEM)


def shaped(shape, dtype):
    return jax.ShapeDtypeStruct(shape, dtype)


def whole_call(kernel, outs, args, scratch=(), flops=0, moved=0, with_index=True):
    specs = ([SMEM] if with_index else []) + [VMEM] * (len(args) - (1 if with_index else 0))
    return pl.pallas_call(
        kernel,
        out_shape=outs,
        in_specs=specs,
        out_specs=[VMEM] * len(outs),
        scratch_shapes=list(scratch),
        compiler_params=pltpu.CompilerParams(vmem_limit_bytes=VMEM_LIMIT),
        cost_estimate=pl.CostEstimate(flops=flops, bytes_accessed=moved, transcendentals=0),
    )(*args)


def shift(value, axis, by):
    count = lax.axis_size(axis)
    return lax.ppermute(value, axis, [(i, (i + by) % count) for i in range(count)])


def swap(value, axis, bit):
    count = lax.axis_size(axis)
    return lax.ppermute(value, axis, [(i, i ^ bit) for i in range(count)])


def sum_over(value, axis):
    bit = 1
    while bit < lax.axis_size(axis):
        value = value + swap(value, axis, bit)
        bit *= 2
    return value


def body(
    tokens, segments, routes, grad_out, gain_attn, w_qkv, w_out, rel_bias,
    gain_moe, w_router, w_in, w_down,
):
    tok_rows, width = tokens.shape
    heads = rel_bias.shape[1]
    features = w_qkv.shape[2]
    head_size = features // heads
    experts, _, hidden_units = w_in.shape
    shares = lax.axis_size("tensor")
    share = tok_rows // shares
    me = lax.axis_index("tensor").astype(jnp.int32)
    idx = me.reshape(1)
    mib = 1 << 20

    half_rows = features // 2
    side = lax.axis_index("dp") % 2
    my_half = lax.dynamic_slice_in_dim(w_out, side * half_rows, half_rows, 0)
    halves = jnp.stack([shift(my_half, "tensor", by) for by in range(1, shares)])
    others = swap(halves, "dp", 1)
    low_half = jnp.where(side == 0, halves, others)
    high_half = jnp.where(side == 0, others, halves)
    fetched = jnp.concatenate([low_half, high_half], axis=1)
    wo = [w_out] + [fetched[by] for by in range(shares - 1)]

    build_hot, gather_hot = near_tables()
    near = jnp.einsum(
        "dlb,bh->hdl", jnp.asarray(build_hot, BF16), rel_bias, preferred_element_type=F32
    ).reshape(2 * heads, 2 * BLK)
    near = jnp.pad(near, ((0, 8 - 2 * heads), (0, 0)))
    far = jnp.broadcast_to(rel_bias[NB - 1].astype(F32)[:, None], (heads, LANES))
    far = jnp.pad(far, ((0, 8 - heads), (0, 0)))
    seg_row = segments.reshape(1, tok_rows)
    seg_col = segments.reshape(tok_rows, 1)
    gain_one = gain_attn.reshape(1, width)
    gain_two = gain_moe.reshape(1, width)

    normed_one, qh, k, v, att, ot, lse, bias = whole_call(
        functools.partial(attn_fwd_kernel, heads, head_size),
        [
            shaped((tok_rows, width), BF16),
            shaped((heads, tok_rows, features), BF16),
            shaped((tok_rows, features), BF16),
            shaped((tok_rows, features), BF16),
            shaped((tok_rows, features), BF16),
            shaped((features, tok_rows), F32),
            shaped((8, tok_rows), F32),
            shaped((2 * heads, BLK, BLK), F32),
        ],
        [tokens, gain_one, w_qkv, seg_row, seg_col, near, far],
        [pltpu.VMEM((features, tok_rows), BF16)],
        flops=6 * 10**9, moved=8 * mib, with_index=False,
    )
    atts = [att] + [shift(att, "tensor", by) for by in range(1, shares)]

    router_wide = jnp.pad(w_router, ((0, 0), (0, LANES - experts)))
    full = lambda shape: pl.BlockSpec(shape, lambda e: (0,) * len(shape))
    per_expert = lambda shape: pl.BlockSpec((1,) + shape, lambda e: (e, 0, 0))
    params = pltpu.CompilerParams(
        vmem_limit_bytes=VMEM_LIMIT, dimension_semantics=("arbitrary",)
    )
    moe_flops = 4 * experts * tok_rows * width * hidden_units
    fwd = pl.pallas_call(
        functools.partial(moe_fwd_kernel, shares, experts),
        grid=(experts,),
        in_specs=[SMEM]
        + [full((tok_rows, features))] * shares
        + [full((features, width))] * shares
        + [
            full((tok_rows, width)), full((1, width)), full((width, LANES)),
            full((tok_rows, 2)), full((tok_rows, width)),
            per_expert((width, hidden_units)), per_expert((hidden_units, width)),
        ],
        out_specs=[full((share, width))] * shares
        + [
            full((tok_rows, width)), full((share, width)), full((tok_rows, LANES)),
            full((tok_rows, LANES)), per_expert((tok_rows, hidden_units)),
            per_expert((tok_rows, hidden_units)),
        ],
        out_shape=[shaped((share, width), BF16)] * shares
        + [
            shaped((tok_rows, width), BF16),
            shaped((share, width), F32),
            shaped((tok_rows, LANES), F32),
            shaped((tok_rows, LANES), F32),
            shaped((experts, tok_rows, hidden_units), BF16),
            shaped((experts, tok_rows, hidden_units), BF16),
        ],
        scratch_shapes=[pltpu.VMEM((tok_rows, width), F32)],
        compiler_params=params,
        cost_estimate=pl.CostEstimate(
            flops=moe_flops, bytes_accessed=32 * mib, transcendentals=0
        ),
    )(idx, *atts, *wo, tokens, gain_two, router_wide, routes, grad_out, w_in, w_down)
    moe_parts = fwd[:shares]
    normed_two, own_hidden, gates, ggate, act, slope = fwd[shares:]

    moe_got = [moe_parts[0]] + [shift(moe_parts[by], "tensor", by) for by in range(1, shares)]

    router_t = jnp.pad(w_router.astype(F32).T, ((0, LANES - experts), (0, 0)))
    bwd = pl.pallas_call(
        functools.partial(moe_bwd_kernel, shares, experts),
        grid=(experts,),
        in_specs=[
            SMEM, full((tok_rows, LANES)), full((tok_rows, LANES)), full((tok_rows, width)),
            per_expert((tok_rows, hidden_units)), full((LANES, width)),
            per_expert((width, hidden_units)), per_expert((hidden_units, width)),
        ],
        out_specs=[full((share, width))] * shares
        + [full((tok_rows, LANES)), per_expert((tok_rows, hidden_units))],
        out_shape=[shaped((share, width), BF16)] * shares
        + [
            shaped((tok_rows, LANES), F32),
            shaped((experts, tok_rows, hidden_units), BF16),
        ],
        scratch_shapes=[pltpu.VMEM((tok_rows, width), F32)],
        compiler_params=params,
        cost_estimate=pl.CostEstimate(
            flops=moe_flops, bytes_accessed=26 * mib, transcendentals=0
        ),
    )(idx, gates, ggate, grad_out, slope, router_t, w_in, w_down)
    gx_parts = bwd[:shares]
    glog, gpre = bwd[shares:]
    gx_got = [gx_parts[0]] + [shift(gx_parts[by], "tensor", by) for by in range(1, shares)]

    expert_grads = pl.pallas_call(
        moe_weights_kernel,
        grid=(experts,),
        in_specs=[
            full((tok_rows, LANES)), full((tok_rows, width)), full((tok_rows, width)),
            per_expert((tok_rows, hidden_units)), per_expert((tok_rows, hidden_units)),
        ],
        out_specs=[pl.BlockSpec((1, 2, width, width), lambda e: (e, 0, 0, 0))],
        out_shape=[shaped((experts, 2, width, width), BF16)],
        compiler_params=params,
        cost_estimate=pl.CostEstimate(
            flops=moe_flops, bytes_accessed=26 * mib, transcendentals=0
        ),
    )(gates, grad_out, normed_two, act, gpre)[0]
    expert_rows = expert_grads.reshape(experts * 2 * width, width)
    expert_rows = lax.psum_scatter(expert_rows, "dp", scatter_dimension=0, tiled=True)
    expert_rows = lax.all_gather(expert_rows, "dp", axis=0, tiled=True)
    expert_rows = expert_rows.reshape(experts, 2, width, width)
    grad_w_in = expert_rows[:, 0].astype(F32)
    grad_w_down = expert_rows[:, 1].astype(F32)

    grad_router = jnp.dot(glog[:, :experts].T, normed_two.astype(F32), precision=HIGHEST)

    back = whole_call(
        functools.partial(hidden_back_kernel, shares),
        [shaped((share, features), BF16)] * shares
        + [shaped((share, width), F32), shaped((share, width), BF16), shaped((1, width), F32)],
        [idx, *gx_got, *wo, own_hidden, grad_out, gain_two],
        flops=3 * 10**8, moved=6 * mib,
    )
    ga_parts = back[:shares]
    grad_hidden, grad_hidden_low, ggain_two = back[shares:]
    ga_got = [ga_parts[0]] + [shift(ga_parts[by], "tensor", -by) for by in range(1, shares)]
    w_out_rows = whole_call(
        functools.partial(w_out_back_kernel, shares),
        [shaped((shares, features, width), BF16)],
        [idx, *atts, grad_hidden_low],
        flops=3 * 10**8, moved=4 * mib,
    )[0]

    result_share = own_hidden
    for piece in moe_got:
        result_share = result_share + piece.astype(F32)
    result_share = result_share.astype(BF16)
    result_got = [result_share] + [shift(result_share, "tensor", by) for by in range(1, shares)]
    result = whole_call(
        functools.partial(place_kernel, shares),
        [shaped((tok_rows, width), BF16)], [idx, *result_got], moved=3 * mib,
    )[0]

    attn_back = whole_call(
        functools.partial(attn_bwd_kernel, heads, head_size, shares),
        [shaped((share, width), BF16)] * shares
        + [
            shaped((3, tok_rows, features), BF16),
            shaped((8, 2 * BLK), F32),
            shaped((8, BLK), F32),
        ],
        [idx, *ga_got, qh, k, v, ot, lse, bias, far, seg_row, seg_col, w_qkv],
        [
            pltpu.VMEM((tok_rows, features), BF16),
            pltpu.VMEM((features, tok_rows), F32),
            pltpu.VMEM((tok_rows, features), F32),
            pltpu.VMEM((tok_rows, features), F32),
            pltpu.VMEM((features, tok_rows), BF16),
            pltpu.VMEM((8, tok_rows), F32),
            pltpu.VMEM((2, BLK, BLK), F32),
            pltpu.VMEM((BLK, BLK), F32),
        ],
        flops=14 * 10**9, moved=8 * mib,
    )
    gn_parts = attn_back[:shares]
    gproj, near_sum, far_sum = attn_back[shares:]
    gn_got = [gn_parts[0]] + [shift(gn_parts[by], "tensor", by) for by in range(1, shares)]

    qkv_rows = jnp.einsum("ctf,td->cfd", gproj, normed_one, preferred_element_type=F32)
    late_rows = jnp.concatenate(
        [
            qkv_rows.astype(BF16).reshape(3 * features, width),
            w_out_rows.reshape(shares * features, width),
        ],
        axis=0,
    )
    late_rows = lax.psum_scatter(late_rows, "dp", scatter_dimension=1, tiled=True)
    late_qkv = late_rows[: 3 * features]
    late_out = late_rows[3 * features :].reshape(shares, features, -1)
    out_sum = late_out[0].astype(F32)
    for by in range(1, shares):
        out_sum = out_sum + shift(late_out[by], "tensor", -by).astype(F32)
    late_rows = jnp.concatenate([late_qkv, out_sum.astype(BF16)], axis=0)
    late_rows = lax.all_gather(late_rows, "dp", axis=1, tiled=True)
    grad_w_qkv = late_rows[: 3 * features].reshape(3, features, width)
    grad_w_qkv = jnp.swapaxes(grad_w_qkv, 1, 2).astype(F32)
    grad_w_out = late_rows[3 * features :].astype(F32)

    gt_share, ggain_one = whole_call(
        functools.partial(input_back_kernel, shares),
        [shaped((share, width), BF16), shaped((1, width), F32)],
        [idx, *gn_got, tokens, grad_hidden, gain_one],
        moved=5 * mib,
    )
    gt_got = [gt_share] + [shift(gt_share, "tensor", by) for by in range(1, shares)]
    grad_tokens = whole_call(
        functools.partial(place_kernel, shares),
        [shaped((tok_rows, width), F32)], [idx, *gt_got], moved=5 * mib,
    )[0]

    near_part = jnp.einsum(
        "hdl,dlb->bh",
        near_sum[: 2 * heads].reshape(heads, 2, 2 * BLK),
        jnp.asarray(gather_hot, F32),
        precision=HIGHEST,
    )
    far_part = jnp.sum(far_sum[:heads], axis=1)
    grad_rel = near_part.at[NB - 1].add(far_part)
    rel_row = jnp.pad(grad_rel.reshape(1, -1), ((0, 0), (0, width - NB * heads)))
    small = jnp.concatenate([rel_row, ggain_one, ggain_two, grad_router], axis=0)
    small = sum_over(small, "dp")
    grad_rel_bias = small[0, : NB * heads].reshape(NB, heads)
    shared = sum_over(small[1:], "tensor")
    return (
        result,
        grad_tokens,
        shared[0],
        grad_w_qkv,
        grad_w_out,
        grad_rel_bias,
        shared[1],
        shared[2:].T,
        grad_w_in,
        grad_w_down,
    )


def solution(mesh):
    placed = (
        P("dp", None),
        P("dp", None),
        P("dp", None),
        P("dp", None),
        P(),
        P(None, None, "tensor"),
        P("tensor", None),
        P(None, "tensor"),
        P(),
        P(),
        P(None, None, "tensor"),
        P(None, "tensor", None),
    )
    return jax.shard_map(
        body,
        mesh=mesh,
        in_specs=placed,
        out_specs=(
            P("dp", None),
            P("dp", None),
            P(),
            P(None, None, "tensor"),
            P("tensor", None),
            P(None, "tensor"),
            P(),
            P(),
            P(None, None, "tensor"),
            P(None, "tensor", None),
        ),
        check_vma=False,
    )
```

```python
import functools
import math

import jax
import jax.numpy as jnp
import numpy as np
from jax import lax
from jax.experimental import pallas as pl
from jax.experimental.pallas import tpu as pltpu
from jax.sharding import PartitionSpec as P

NB = 32
DIST = 128
EPSILON = 1e-06
NEGATIVE = -1e30
HIGHEST = lax.Precision.HIGHEST
F32 = jnp.float32
BF16 = jnp.bfloat16
BLK = 256
LANES = 128
VMEM_LIMIT = 56 * 1024 * 1024

NN = (((1,), (0,)), ((), ()))
NT = (((1,), (1,)), ((), ()))
TN = (((0,), (0,)), ((), ()))


def dot(a, b, dims=NN, precision=None):
    return lax.dot_general(a, b, dims, precision=precision, preferred_element_type=F32)


def bucket_of(distance):
    halfway = NB // 2
    thresholds = [
        int(math.ceil(halfway * (DIST / halfway) ** (step / halfway))) for step in range(halfway)
    ]
    beyond = sum((distance >= threshold).astype(np.int64) for threshold in thresholds)
    return np.where(distance < halfway, distance, halfway - 1 + beyond)


def near_tables():
    lanes = np.arange(2 * BLK)
    offset = np.where(lanes < BLK, lanes, lanes - 2 * BLK)
    build = np.stack([np.maximum(offset, 0), np.maximum(BLK + offset, 0)])
    gather = np.stack([lanes - (BLK - 1), lanes + 1])
    eye = np.eye(NB, dtype=np.float32)
    build_hot = eye[bucket_of(build)]
    gather_hot = eye[bucket_of(np.maximum(gather, 0))] * (gather >= 0)[..., None]
    return build_hot, gather_hot


def row_scale(values):
    return lax.rsqrt(jnp.mean(values * values, axis=-1, keepdims=True) + EPSILON)


def lane_pick(values, index):
    lanes = lax.broadcasted_iota(jnp.int32, values.shape, 1)
    return jnp.sum(jnp.where(lanes == index, values, 0.0), axis=1, keepdims=True)


def masked_scores(k_tile, qh_tile, bias, seg_k, seg_q, diagonal):
    scores = dot(k_tile, qh_tile, NT) + bias
    allowed = seg_k == seg_q
    if diagonal:
        key_at = lax.broadcasted_iota(jnp.int32, scores.shape, 0)
        query_at = lax.broadcasted_iota(jnp.int32, scores.shape, 1)
        allowed = allowed & (key_at <= query_at)
    return jnp.where(allowed, scores, NEGATIVE)


def tile_bias(bias_ref, far_ref, head, delta):
    if delta < 2:
        return bias_ref[2 * head + delta]
    return far_ref[pl.ds(head, 1), 0:1]


def column_of(row):
    spread = jnp.broadcast_to(row.astype(F32), (8, row.shape[1]))
    return spread.T[:, 0:1]


def attn_fwd_kernel(piece, pieces, heads, head_size, *refs):
    tok, gain, w, seg = refs[:4]
    refs = refs[4:]
    if piece == 0:
        rel, build = refs[:2]
        refs = refs[2:]
    else:
        bias, far = refs[:2]
        refs = refs[2:]
    old_k, refs = refs[:piece], refs[piece:]
    old_vt, refs = refs[:piece], refs[piece:]
    normed, qh, k, v, vt, att, ot, lse = refs[:8]
    if piece == 0:
        bias, far = refs[8:]
    keys_of, vt_of = [*old_k, k], [*old_vt, vt]
    rows_total = tok.shape[0] // pieces
    base = piece * rows_total
    features = w.shape[1]
    blocks = rows_total // BLK
    gain_row = gain[...].astype(F32)
    lanes = lax.broadcasted_iota(jnp.int32, (BLK, features), 1)
    for block in range(blocks):
        rows = pl.ds(block * BLK, BLK)
        x = tok[pl.ds(base + block * BLK, BLK), :].astype(F32)
        n = (x * row_scale(x) * gain_row).astype(BF16)
        normed[rows, :] = n
        q_rows = dot(n, w[0], NT).astype(BF16).astype(F32) * (head_size**-0.5)
        for head in range(heads):
            inside = (lanes >= head * head_size) & (lanes < (head + 1) * head_size)
            qh[head, rows, :] = jnp.where(inside, q_rows, 0.0).astype(BF16)
        k[rows, :] = dot(n, w[1], NT).astype(BF16)
        v_rows = dot(n, w[2], NT).astype(BF16)
        v[rows, :] = v_rows
        vt[:, rows] = v_rows.astype(F32).T.astype(BF16)
    if piece == 0:
        far[...] = jnp.zeros_like(far)
        far[0:heads, :] = jnp.broadcast_to(rel[:, NB - 1 : NB].astype(F32), (heads, LANES))
        for delta in range(2):
            near = dot(rel[...], build[delta])
            for head in range(heads):
                spread = jnp.broadcast_to(near[head : head + 1, :], (BLK, 2 * BLK))
                turned = pltpu.roll(spread, 0, 1, stride=1, stride_axis=0)
                bias[2 * head + delta] = turned[:, :BLK]
    lse[...] = jnp.zeros_like(lse)
    seg_row = seg[...].astype(F32)
    seg_col = column_of(seg[...])

    def one_head(head, carry):
        part = pl.ds(pl.multiple_of(head * head_size, head_size), head_size)
        for block in range(blocks):
            qb = piece * blocks + block
            cols = pl.ds(block * BLK, BLK)
            q_tile = qh[head, cols, :]
            tiles = []
            for kb in range(qb + 1):
                keys = pl.ds(kb % blocks * BLK, BLK)
                tiles.append(
                    masked_scores(
                        keys_of[kb // blocks][keys, :], q_tile,
                        tile_bias(bias, far, head, qb - kb),
                        seg_col[kb * BLK : (kb + 1) * BLK, :],
                        seg_row[:, qb * BLK : (qb + 1) * BLK], kb == qb,
                    )
                )
            peak = functools.reduce(
                jnp.maximum, [jnp.max(t, axis=0, keepdims=True) for t in tiles]
            )
            total = jnp.zeros((1, BLK), F32)
            out = jnp.zeros((head_size, BLK), F32)
            for kb in range(qb + 1):
                raised = jnp.exp(tiles[kb] - peak)
                total = total + jnp.sum(raised, axis=0, keepdims=True)
                values = vt_of[kb // blocks][part, pl.ds(kb % blocks * BLK, BLK)]
                out = out + dot(values, raised.astype(BF16))
            ot[part, cols] = out / total
            lse[pl.ds(head, 1), cols] = peak + jnp.log(total)
        return carry

    lax.fori_loop(0, heads, one_head, 0)
    for block in range(blocks):
        cols = pl.ds(block * BLK, BLK)
        att[cols, :] = ot[:, cols].T.astype(BF16)


def attn_bwd_kernel(piece, pieces, heads, head_size, shares, idx, *refs):
    held = piece + 1
    last = held == pieces
    go_parts, refs = refs[:shares], refs[shares:]
    qh, ot, lse = refs[:3]
    refs = refs[3:]
    ks, refs = refs[:held], refs[held:]
    vs, refs = refs[:held], refs[held:]
    bias, far, seg = refs[:3]
    refs = refs[3:]
    if piece:
        gk_in, refs = refs[:piece], refs[piece:]
        gv_in, refs = refs[:piece], refs[piece:]
        gq_in, refs = refs[:piece], refs[piece:]
        acc_in, refs = refs[0], refs[1:]
    if last:
        w, hot = refs[:2]
        refs = refs[2:]
        gn_parts, refs = refs[:shares], refs[shares:]
        gproj, rel_out = refs[:2]
        refs = refs[2:]
        gk, refs = refs[:held], refs[held:]
        gv, refs = refs[:held], refs[held:]
        gq_t, acc = refs[:2]
        refs = refs[2:]
    else:
        gk, refs = refs[:held], refs[held:]
        gv, refs = refs[:held], refs[held:]
        gq_t, acc = refs[:2]
        refs = refs[2:]
    go, kt, d_row, near_sum, far_sum = refs
    rows_total, features = ks[0].shape
    blocks = rows_total // BLK
    share = rows_total // shares
    me = idx[0]
    for step in range(shares):
        start = pl.multiple_of(lax.rem(me + step, shares) * share, share)
        go[pl.ds(start, share), :] = go_parts[step][...]
    for index in range(held):
        for block in range(blocks):
            cols = pl.ds(block * BLK, BLK)
            kt[:, pl.ds((index * blocks + block) * BLK, BLK)] = (
                ks[index][cols, :].astype(F32).T.astype(BF16)
            )
        if index < piece:
            gk[index][...] = gk_in[index][...]
            gv[index][...] = gv_in[index][...]
        else:
            gk[index][...] = jnp.zeros_like(gk[index])
            gv[index][...] = jnp.zeros_like(gv[index])
    if piece:
        acc[...] = acc_in[...]
    else:
        acc[...] = jnp.zeros_like(acc)
    for block in range(blocks):
        cols = pl.ds(block * BLK, BLK)
        product = go[cols, :].astype(F32).T * ot[:, cols]
        for head in range(heads):
            part = product[head * head_size : (head + 1) * head_size, :]
            d_row[head : head + 1, cols] = jnp.sum(part, axis=0, keepdims=True)
    near_sum[...] = jnp.zeros_like(near_sum)
    far_sum[...] = jnp.zeros_like(far_sum)
    key_at = lax.broadcasted_iota(jnp.int32, (BLK, BLK), 0)
    other_at = lax.broadcasted_iota(jnp.int32, (BLK, BLK), 1)
    flip = (key_at + other_at == BLK - 1).astype(F32)
    seg_row = seg[...].astype(F32)
    seg_col = column_of(seg[...])

    def one_head(head, carry):
        part = pl.ds(pl.multiple_of(head * head_size, head_size), head_size)
        lanes = lax.broadcasted_iota(jnp.int32, (BLK, features), 1)
        inside = (lanes >= head * head_size) & (lanes < (head + 1) * head_size)
        for block in range(blocks):
            qb = piece * blocks + block
            cols = pl.ds(block * BLK, BLK)
            q_tile = qh[head, cols, :]
            go_tile = jnp.where(inside, go[cols, :].astype(F32), 0.0).astype(BF16)
            log_total = lse[pl.ds(head, 1), cols]
            d_tile = d_row[pl.ds(head, 1), cols]
            gq = jnp.zeros((head_size, BLK), F32)
            for kb in range(qb + 1):
                index = kb // blocks
                keys = pl.ds(kb % blocks * BLK, BLK)
                delta = qb - kb
                scores = masked_scores(
                    ks[index][keys, :], q_tile, tile_bias(bias, far, head, delta),
                    seg_col[kb * BLK : (kb + 1) * BLK, :],
                    seg_row[:, qb * BLK : (qb + 1) * BLK], delta == 0,
                )
                probs = jnp.exp(scores - log_total)
                gs = probs * (dot(vs[index][keys, :], go_tile, NT) - d_tile)
                if delta < 2:
                    acc[2 * head + delta] += gs
                else:
                    far_sum[pl.ds(head, 1), :] += jnp.sum(gs, axis=0, keepdims=True)
                gs_low = gs.astype(BF16)
                gv[index][keys, :] += dot(probs.astype(BF16), go_tile)
                gk[index][keys, :] += dot(gs_low, q_tile)
                gq = gq + dot(kt[part, kb * BLK : (kb + 1) * BLK], gs_low)
            gq_t[part, cols] = gq * (head_size**-0.5)
        return carry

    lax.fori_loop(0, heads, one_head, 0)
    if not last:
        return
    gqs = [*(gq_in if piece else ()), gq_t]
    for index in range(held):
        for block in range(blocks):
            rows = pl.ds(block * BLK, BLK)
            out = pl.ds((index * blocks + block) * BLK, BLK)
            gproj[0, out, :] = gqs[index][:, rows].T.astype(BF16)
            gproj[1, out, :] = gk[index][rows, :].astype(BF16)
            gproj[2, out, :] = gv[index][rows, :].astype(BF16)
    for step in range(shares):
        for index in range(pieces):
            start = index * rows_total + lax.rem(me + step, shares) * share
            rows = pl.ds(pl.multiple_of(start, share), share)
            total = dot(gproj[0, rows, :], w[0])
            total = total + dot(gproj[1, rows, :], w[1])
            total = total + dot(gproj[2, rows, :], w[2])
            gn_parts[step][pl.ds(index * share, share), :] = total.astype(BF16)
    for head in range(heads):
        for delta in range(2):
            turned = dot(flip, acc[2 * head + delta], NN, HIGHEST)
            wide = jnp.concatenate([turned, jnp.zeros_like(turned)], axis=1)
            sheared = pltpu.roll(wide, 0, 1, stride=1, stride_axis=0)
            near_sum[delta, head : head + 1, :] = jnp.sum(sheared, axis=0, keepdims=True)
    summed = dot(near_sum[0], hot[0], NN, HIGHEST) + dot(near_sum[1], hot[1], NN, HIGHEST)
    buckets = lax.broadcasted_iota(jnp.int32, summed.shape, 1)
    beyond = jnp.sum(far_sum[...], axis=1, keepdims=True)
    rel_out[...] = summed + jnp.where(buckets == NB - 1, beyond, 0.0)


def qkv_weights_kernel(pieces, *refs):
    normed = refs[:pieces]
    gproj, out = refs[pieces:]
    rows_total = normed[0].shape[0]
    for c in range(3):
        total = dot(gproj[c, pl.ds(0, rows_total), :], normed[0][...], TN)
        for index in range(1, pieces):
            rows = pl.ds(index * rows_total, rows_total)
            total = total + dot(gproj[c, rows, :], normed[index][...], TN)
        out[c] = total.astype(BF16)


def gelu_pair(values):
    squared = values * values
    bent = jnp.tanh(values * (0.7978845608028654 + 0.7978845608028654 * 0.044715 * squared))
    half = 0.5 * (1.0 + bent)
    lifted = values * half
    slope = 0.7978845608028654 + 3.0 * 0.7978845608028654 * 0.044715 * squared
    return lifted, half + lifted * (1.0 - bent) * slope


def padded_rows(values, rows):
    missing = jnp.zeros((rows - values.shape[0], values.shape[1]), values.dtype)
    return jnp.concatenate([values, missing], axis=0)


def moe_fwd_kernel(piece, pieces, shares, experts, idx, *refs):
    att, refs = refs[:shares], refs[shares:]
    wo, refs = refs[:shares], refs[shares:]
    tok, gain, router, routes, cot, w_in, w_down = refs[:7]
    refs = refs[7:]
    parts, refs = refs[:shares], refs[shares:]
    normed, own, gates, ggate, act, slope, acc = refs
    rows_total = tok.shape[0] // pieces
    base = piece * rows_total
    share = rows_total // shares
    me = idx[0]
    expert = pl.program_id(0)

    @pl.when(expert == 0)
    def _():
        gain_row = gain[...].astype(F32)
        router_wide = padded_rows(router[...].astype(F32), LANES).astype(BF16)
        for block in range(rows_total // BLK):
            rows = pl.ds(block * BLK, BLK)
            outer = pl.ds(base + block * BLK, BLK)
            attn = dot(att[0][rows, :], wo[0][...])
            for step in range(1, shares):
                attn = attn + dot(att[step][rows, :], wo[step][...])
            hidden = tok[outer, :].astype(F32) + attn
            acc[rows, :] = hidden
            n = (hidden * row_scale(hidden) * gain_row).astype(BF16)
            normed[rows, :] = n
            logits = dot(n, router_wide, NT)
            lanes = lax.broadcasted_iota(jnp.int32, logits.shape, 1)
            first = lanes == routes[outer, 0:1]
            second = lanes == routes[outer, 1:2]
            one = jnp.sum(jnp.where(first, logits, 0.0), axis=1, keepdims=True)
            two = jnp.sum(jnp.where(second, logits, 0.0), axis=1, keepdims=True)
            peak = jnp.maximum(one, two)
            one = jnp.exp(one - peak)
            two = jnp.exp(two - peak)
            both = one + two
            gates[rows, :] = jnp.where(first, one / both, jnp.where(second, two / both, 0.0))
        own[...] = acc[pl.ds(pl.multiple_of(me * share, share), share), :]
        acc[...] = jnp.zeros_like(acc)
        ggate[...] = jnp.zeros_like(ggate)

    for block in range(rows_total // ROWS):
        rows = pl.ds(block * ROWS, ROWS)
        outer = pl.ds(base + block * ROWS, ROWS)
        lifted, bend = gelu_pair(dot(normed[rows, :], w_in[0]))
        lifted = lifted.astype(BF16)
        act[0, rows, :] = lifted
        slope[0, rows, :] = bend.astype(BF16)
        out = dot(lifted, w_down[0])
        gate = lane_pick(gates[rows, :], expert)
        acc[rows, :] += gate * out
        pulled = jnp.sum(cot[outer, :].astype(F32) * out, axis=1, keepdims=True)
        held = ggate[rows, :]
        lanes = lax.broadcasted_iota(jnp.int32, held.shape, 1)
        ggate[rows, :] = jnp.where(lanes == expert, pulled, held)

    @pl.when(expert == experts - 1)
    def _():
        for step in range(shares):
            start = pl.multiple_of(lax.rem(me + step, shares) * share, share)
            parts[step][...] = acc[pl.ds(start, share), :].astype(BF16)


def moe_bwd_kernel(piece, shares, experts, idx, *refs):
    gates, ggate, cot, slope, router, w_in, w_down = refs[:7]
    refs = refs[7:]
    parts, refs = refs[:shares], refs[shares:]
    glog, gpre, acc = refs
    rows_total = gates.shape[0]
    base = piece * rows_total
    share = rows_total // shares
    me = idx[0]
    expert = pl.program_id(0)

    @pl.when(expert == 0)
    def _():
        router_wide = padded_rows(router[...].astype(F32), LANES)
        for block in range(rows_total // ROWS):
            rows = pl.ds(block * ROWS, ROWS)
            g, gg = gates[rows, :], ggate[rows, :]
            back = g * (gg - jnp.sum(g * gg, axis=1, keepdims=True))
            glog[rows, :] = back
            acc[rows, :] = dot(back, router_wide, NN, HIGHEST)

    for block in range(rows_total // ROWS):
        rows = pl.ds(block * ROWS, ROWS)
        gate = lane_pick(gates[rows, :], expert)
        weighted = cot[pl.ds(base + block * ROWS, ROWS), :].astype(F32)
        weighted = (gate * weighted).astype(BF16)
        gp = (dot(weighted, w_down[0], NT) * slope[0, rows, :].astype(F32)).astype(BF16)
        gpre[0, rows, :] = gp
        acc[rows, :] += dot(gp, w_in[0], NT)

    @pl.when(expert == experts - 1)
    def _():
        for step in range(shares):
            start = pl.multiple_of(lax.rem(me + step, shares) * share, share)
            parts[step][...] = acc[pl.ds(start, share), :].astype(BF16)


def moe_weights_kernel(pieces, cot, *refs):
    gates, refs = refs[:pieces], refs[pieces:]
    glog, refs = refs[:pieces], refs[pieces:]
    normed, refs = refs[:pieces], refs[pieces:]
    act, refs = refs[:pieces], refs[pieces:]
    gpre, refs = refs[:pieces], refs[pieces:]
    out, router = refs
    rows_total = normed[0].shape[0]
    expert = pl.program_id(0)

    @pl.when(expert == 0)
    def _():
        total = jnp.zeros((LANES, cot.shape[1]), F32)
        for index in range(pieces):
            back = glog[index][...]
            high = back.astype(BF16)
            low = (back - high.astype(F32)).astype(BF16)
            total = total + dot(high, normed[index][...], TN)
            total = total + dot(low, normed[index][...], TN)
        router[...] = total[0:8, :]

    grad_in = jnp.zeros((normed[0].shape[1], gpre[0].shape[2]), F32)
    grad_down = jnp.zeros((act[0].shape[2], cot.shape[1]), F32)
    for index in range(pieces):
        gate = lane_pick(gates[index][...], expert)
        weighted = cot[pl.ds(index * rows_total, rows_total), :].astype(F32)
        weighted = (gate * weighted).astype(BF16)
        grad_in = grad_in + dot(normed[index][...], gpre[index][0], TN)
        grad_down = grad_down + dot(act[index][0], weighted, TN)
    out[0, 0] = grad_in.astype(BF16)
    out[0, 1] = grad_down.astype(BF16)


def hidden_back_kernel(piece, pieces, shares, idx, *refs):
    gx, refs = refs[:shares], refs[shares:]
    wo, refs = refs[:shares], refs[shares:]
    own, cot, gain = refs[:3]
    refs = refs[3:]
    ga, refs = refs[:shares], refs[shares:]
    gh, gh_low, ggain = refs
    share = own.shape[0]
    grad = gx[0][...].astype(F32)
    for step in range(1, shares):
        grad = grad + gx[step][...].astype(F32)
    hidden = own[...]
    scale = row_scale(hidden)
    unit = hidden * scale
    ggain[...] = jnp.sum(grad * unit, axis=0, keepdims=True)
    gained = grad * gain[...].astype(F32)
    start = piece * (cot.shape[0] // pieces) + idx[0] * share
    mine = cot[pl.ds(pl.multiple_of(start, share), share), :].astype(F32)
    back = mine + scale * (gained - unit * jnp.mean(gained * unit, axis=-1, keepdims=True))
    gh[...] = back
    low = back.astype(BF16)
    gh_low[...] = low
    for step in range(shares):
        ga[step][...] = dot(low, wo[step][...], NT).astype(BF16)


def w_out_back_kernel(pieces, shares, idx, *refs):
    att, refs = refs[: pieces * shares], refs[pieces * shares :]
    gh_low, out = refs[:pieces], refs[pieces]
    share = gh_low[0].shape[0]
    rows = pl.ds(pl.multiple_of(idx[0] * share, share), share)
    for step in range(shares):
        total = dot(att[step][rows, :], gh_low[0][...], TN)
        for index in range(1, pieces):
            total = total + dot(att[index * shares + step][rows, :], gh_low[index][...], TN)
        out[step] = total.astype(BF16)


def join_kernel(pieces, shares, *refs):
    own, refs = refs[:pieces], refs[pieces:]
    got, out = refs[: pieces * shares], refs[pieces * shares]
    share = own[0].shape[0]
    for index in range(pieces):
        total = own[index][...]
        for step in range(shares):
            total = total + got[index * shares + step][...].astype(F32)
        out[pl.ds(index * share, share), :] = total.astype(BF16)


def input_back_kernel(pieces, shares, idx, *refs):
    gn, refs = refs[:shares], refs[shares:]
    ghs, refs = refs[:pieces], refs[pieces:]
    tok, gain, gt, ggain = refs
    share = ghs[0].shape[0]
    gain_row = gain[...].astype(F32)
    total = jnp.zeros_like(ggain)
    for index in range(pieces):
        rows = pl.ds(index * share, share)
        grad = gn[0][rows, :].astype(F32)
        for step in range(1, shares):
            grad = grad + gn[step][rows, :].astype(F32)
        start = index * (tok.shape[0] // pieces) + idx[0] * share
        x = tok[pl.ds(pl.multiple_of(start, share), share), :].astype(F32)
        scale = row_scale(x)
        unit = x * scale
        total = total + jnp.sum(grad * unit, axis=0, keepdims=True)
        gained = grad * gain_row
        back = scale * (gained - unit * jnp.mean(gained * unit, axis=-1, keepdims=True))
        gt[rows, :] = (ghs[index][...] + back).astype(BF16)
    ggain[...] = total


def place_kernel(pieces, shares, idx, *refs):
    blocks, out = refs[:shares], refs[shares]
    rows_total = out.shape[0] // pieces
    share = rows_total // shares
    for step in range(shares):
        owner = lax.rem(idx[0] + shares - step, shares)
        for index in range(pieces):
            start = pl.multiple_of(index * rows_total + owner * share, share)
            got = blocks[step][pl.ds(index * share, share), :]
            out[pl.ds(start, share), :] = got.astype(out.dtype)


ROWS = 256
PIECES = 2

SMEM = pl.BlockSpec(memory_space=pltpu.SMEM)
VMEM = pl.BlockSpec(memory_space=pltpu.VMEM)


def shaped(shape, dtype):
    return jax.ShapeDtypeStruct(shape, dtype)


def whole_call(kernel, outs, args, scratch=(), flops=0, moved=0, with_index=True):
    specs = ([SMEM] if with_index else []) + [VMEM] * (len(args) - (1 if with_index else 0))
    return pl.pallas_call(
        kernel,
        out_shape=outs,
        in_specs=specs,
        out_specs=[VMEM] * len(outs),
        scratch_shapes=list(scratch),
        compiler_params=pltpu.CompilerParams(vmem_limit_bytes=VMEM_LIMIT),
        cost_estimate=pl.CostEstimate(flops=flops, bytes_accessed=moved, transcendentals=0),
    )(*args)


def shift(value, axis, by):
    count = lax.axis_size(axis)
    return lax.ppermute(value, axis, [(i, (i + by) % count) for i in range(count)])


def swap(value, axis, bit):
    count = lax.axis_size(axis)
    return lax.ppermute(value, axis, [(i, i ^ bit) for i in range(count)])


def sum_over(value, axis):
    bit = 1
    while bit < lax.axis_size(axis):
        value = value + swap(value, axis, bit)
        bit *= 2
    return value


def halves_of(value, axis, bit, chosen):
    half = value.shape[axis] // 2
    keep = lax.dynamic_slice_in_dim(value, chosen * half, half, axis)
    send = lax.dynamic_slice_in_dim(value, (1 - chosen) * half, half, axis)
    return keep, send


def bits_of(axis):
    count = lax.axis_size(axis)
    return [1 << level for level in range(count.bit_length() - 1)]


def scatter_sum(value, mesh_axis, axis):
    me = lax.axis_index(mesh_axis)
    for bit in bits_of(mesh_axis):
        keep, send = halves_of(value, axis, bit, (me // bit) % 2)
        got = swap(send, mesh_axis, bit)
        value = (keep.astype(F32) + got.astype(F32)).astype(value.dtype)
    return value


def gather_back(value, mesh_axis, axis):
    me = lax.axis_index(mesh_axis)
    for bit in reversed(bits_of(mesh_axis)):
        got = swap(value, mesh_axis, bit)
        low = (me // bit) % 2 == 0
        value = jnp.concatenate(
            [jnp.where(low, value, got), jnp.where(low, got, value)], axis=axis
        )
    return value


def after(value, *others):
    return lax.optimization_barrier((value, *others))[0]


def body(
    tokens, segments, routes, grad_out, gain_attn, w_qkv, w_out, rel_bias,
    gain_moe, w_router, w_in, w_down,
):
    tok_rows, width = tokens.shape
    heads = rel_bias.shape[1]
    features = w_qkv.shape[2]
    head_size = features // heads
    experts, _, hidden_units = w_in.shape
    shares = lax.axis_size("tensor")
    rows = tok_rows // PIECES
    share = rows // shares
    me = lax.axis_index("tensor").astype(jnp.int32)
    idx = me.reshape(1)
    mib = 1 << 20
    others = range(1, shares)

    half_rows = features // 2
    side = lax.axis_index("dp") % 2
    my_half = lax.dynamic_slice_in_dim(w_out, side * half_rows, half_rows, 0)
    halves = [shift(my_half, "tensor", by) for by in others]

    build_hot, gather_hot = near_tables()
    build_hot = jnp.asarray(np.swapaxes(build_hot, 1, 2), BF16)
    gather_hot = jnp.asarray(gather_hot, F32)
    w_qkv_t = jnp.swapaxes(w_qkv, 1, 2)
    router_t = w_router.T
    gain_one = gain_attn.reshape(1, width)
    gain_two = gain_moe.reshape(1, width)

    def attend(piece, bias_args, old_k, old_vt):
        outs = [
            shaped((rows, width), BF16),
            shaped((heads, rows, features), BF16),
            shaped((rows, features), BF16),
            shaped((rows, features), BF16),
            shaped((features, rows), BF16),
            shaped((rows, features), BF16),
            shaped((features, rows), F32),
            shaped((8, rows), F32),
        ]
        if piece == 0:
            outs += [shaped((2 * heads, BLK, BLK), F32), shaped((8, LANES), F32)]
        return whole_call(
            functools.partial(attn_fwd_kernel, piece, PIECES, heads, head_size),
            outs,
            [tokens, gain_one, w_qkv_t, segments, *bias_args, *old_k, *old_vt],
            flops=3 * 10**9, moved=8 * mib, with_index=False,
        )

    stages = []
    bias_args = [rel_bias.T, build_hot]
    for piece in range(PIECES):
        got = attend(piece, bias_args, [s[2] for s in stages], [s[4] for s in stages])
        if piece == 0:
            bias_args = got[8:]
        stages.append(got[:8])
    bias, far = bias_args
    normed_one = [s[0] for s in stages]
    atts = [
        [stage[5]] + [shift(stage[5], "tensor", by) for by in others] for stage in stages
    ]

    fetched = after(jnp.stack(halves), stages[-1][5])
    swapped = swap(fetched, "dp", 1)
    wo = [w_out] + [
        jnp.concatenate(
            [
                jnp.where(side == 0, fetched[at], swapped[at]),
                jnp.where(side == 0, swapped[at], fetched[at]),
            ],
            axis=0,
        )
        for at in range(shares - 1)
    ]

    full = lambda shape: pl.BlockSpec(shape, lambda e: (0,) * len(shape))
    per_expert = lambda shape: pl.BlockSpec((1,) + shape, lambda e: (e, 0, 0))
    params = pltpu.CompilerParams(
        vmem_limit_bytes=VMEM_LIMIT, dimension_semantics=("arbitrary",)
    )
    moe_flops = 4 * experts * rows * width * hidden_units

    def moe_forward(piece):
        return pl.pallas_call(
            functools.partial(moe_fwd_kernel, piece, PIECES, shares, experts),
            grid=(experts,),
            in_specs=[SMEM]
            + [full((rows, features))] * shares
            + [full((features, width))] * shares
            + [
                full((tok_rows, width)), full((1, width)), full((experts, width)),
                full((tok_rows, 2)), full((tok_rows, width)),
                per_expert((width, hidden_units)), per_expert((hidden_units, width)),
            ],
            out_specs=[full((share, width))] * shares
            + [
                full((rows, width)), full((share, width)), full((rows, LANES)),
                full((rows, LANES)), per_expert((rows, hidden_units)),
                per_expert((rows, hidden_units)),
            ],
            out_shape=[shaped((share, width), BF16)] * shares
            + [
                shaped((rows, width), BF16),
                shaped((share, width), F32),
                shaped((rows, LANES), F32),
                shaped((rows, LANES), F32),
                shaped((experts, rows, hidden_units), BF16),
                shaped((experts, rows, hidden_units), BF16),
            ],
            scratch_shapes=[pltpu.VMEM((rows, width), F32)],
            compiler_params=params,
            cost_estimate=pl.CostEstimate(
                flops=moe_flops, bytes_accessed=20 * mib, transcendentals=0
            ),
        )(idx, *atts[piece], *wo, tokens, gain_two, router_t, routes, grad_out, w_in, w_down)

    def moe_backward(piece, gates, ggate, slope):
        return pl.pallas_call(
            functools.partial(moe_bwd_kernel, piece, shares, experts),
            grid=(experts,),
            in_specs=[
                SMEM, full((rows, LANES)), full((rows, LANES)), full((tok_rows, width)),
                per_expert((rows, hidden_units)), full((experts, width)),
                per_expert((width, hidden_units)), per_expert((hidden_units, width)),
            ],
            out_specs=[full((share, width))] * shares
            + [full((rows, LANES)), per_expert((rows, hidden_units))],
            out_shape=[shaped((share, width), BF16)] * shares
            + [
                shaped((rows, LANES), F32),
                shaped((experts, rows, hidden_units), BF16),
            ],
            scratch_shapes=[pltpu.VMEM((rows, width), F32)],
            compiler_params=params,
            cost_estimate=pl.CostEstimate(
                flops=moe_flops, bytes_accessed=16 * mib, transcendentals=0
            ),
        )(idx, gates, ggate, grad_out, slope, router_t, w_in, w_down)

    moe_got, gx_got, forwards, backwards = [], [], [], []
    for piece in range(PIECES):
        fwd = moe_forward(piece)
        parts, kept = fwd[:shares], fwd[shares:]
        moe_got.append([parts[0]] + [shift(parts[by], "tensor", by) for by in others])
        gates, ggate, slope = kept[2], kept[3], kept[5]
        bwd = moe_backward(piece, gates, ggate, slope)
        parts = bwd[:shares]
        gx_got.append([parts[0]] + [shift(parts[by], "tensor", by) for by in others])
        forwards.append(kept)
        backwards.append(bwd[shares:])
    normed_two = [f[0] for f in forwards]
    own_hidden = [f[1] for f in forwards]
    all_gates = [f[2] for f in forwards]
    acts = [f[4] for f in forwards]
    glogs = [b[0] for b in backwards]
    gpres = [b[1] for b in backwards]

    def hidden_back(piece, own):
        got = whole_call(
            functools.partial(hidden_back_kernel, piece, PIECES, shares),
            [shaped((share, features), BF16)] * shares
            + [
                shaped((share, width), F32), shaped((share, width), BF16),
                shaped((1, width), F32),
            ],
            [idx, *gx_got[piece], *wo, own, grad_out, gain_two],
            flops=2 * 10**8, moved=5 * mib,
        )
        parts = got[:shares]
        go = [parts[0]] + [shift(parts[by], "tensor", -by) for by in others]
        return go, got[shares:]

    def attend_back(piece, go, carried):
        held = piece + 1
        last = held == PIECES
        outs, scratch = [], []
        if last:
            outs += [shaped((PIECES * share, width), BF16)] * shares
            outs += [shaped((3, tok_rows, features), BF16), shaped((8, NB), F32)]
        sums = [((rows, features), F32)] * (2 * held)
        sums += [((features, rows), F32), ((2 * heads, BLK, BLK), F32)]
        if last:
            scratch += [pltpu.VMEM(*one) for one in sums]
        else:
            outs += [shaped(*one) for one in sums]
        scratch += [
            pltpu.VMEM((rows, features), BF16),
            pltpu.VMEM((features, tok_rows), BF16),
            pltpu.VMEM((8, rows), F32),
            pltpu.VMEM((2, 8, 2 * BLK), F32),
            pltpu.VMEM((8, BLK), F32),
        ]
        return whole_call(
            functools.partial(attn_bwd_kernel, piece, PIECES, heads, head_size, shares),
            outs,
            [
                idx, *go, stages[piece][1], stages[piece][6], stages[piece][7],
                *[s[2] for s in stages[:held]], *[s[3] for s in stages[:held]],
                bias, far, segments, *carried, *([w_qkv_t, gather_hot] if last else []),
            ],
            scratch,
            flops=7 * 10**9, moved=8 * mib,
        )

    go, back_first = hidden_back(0, own_hidden[0])
    expert_grads, router_rows = pl.pallas_call(
        functools.partial(moe_weights_kernel, PIECES),
        grid=(experts,),
        in_specs=[full((tok_rows, width))]
        + [full((rows, LANES))] * (2 * PIECES)
        + [full((rows, width))] * PIECES
        + [per_expert((rows, hidden_units))] * (2 * PIECES),
        out_specs=[
            pl.BlockSpec((1, 2, width, width), lambda e: (e, 0, 0, 0)), full((8, width))
        ],
        out_shape=[shaped((experts, 2, width, width), BF16), shaped((8, width), F32)],
        compiler_params=params,
        cost_estimate=pl.CostEstimate(
            flops=2 * moe_flops, bytes_accessed=26 * mib, transcendentals=0
        ),
    )(after(grad_out, back_first[1]), *all_gates, *glogs, *normed_two, *acts, *gpres)
    expert_rows = lax.psum(expert_grads.reshape(experts * 2 * width, width), "dp")
    expert_rows = expert_rows.reshape(experts, 2, width, width)
    grad_w_in = expert_rows[:, 0].astype(F32)
    grad_w_down = expert_rows[:, 1].astype(F32)

    go = [after(go[0], router_rows), *go[1:]]
    first = attend_back(0, go, [])
    carried = [first[0], first[1], first[2], first[3]]
    go, back_second = hidden_back(1, after(own_hidden[1], first[0]))
    grad_hidden = [back_first[0], back_second[0]]
    gh_low = [back_first[1], back_second[1]]
    ggain_two = back_first[2] + back_second[2]
    w_out_rows = whole_call(
        functools.partial(w_out_back_kernel, PIECES, shares),
        [shaped((shares, features, width), BF16)],
        [idx, *atts[0], *atts[1], *gh_low],
        flops=3 * 10**8, moved=4 * mib,
    )[0]
    result_share = whole_call(
        functools.partial(join_kernel, PIECES, shares),
        [shaped((PIECES * share, width), BF16)],
        [*own_hidden, *moe_got[0], *moe_got[1]],
        moved=4 * mib, with_index=False,
    )[0]
    result_got = [result_share] + [shift(result_share, "tensor", by) for by in others]
    result = whole_call(
        functools.partial(place_kernel, PIECES, shares),
        [shaped((tok_rows, width), BF16)], [idx, *result_got], moved=3 * mib,
    )[0]

    go = [after(go[0], w_out_rows, result_share), *go[1:]]
    second = attend_back(1, go, carried)
    gn_parts = second[:shares]
    gproj, grad_rel = second[shares:]
    gn_got = [gn_parts[0]] + [shift(gn_parts[by], "tensor", by) for by in others]

    qkv_rows = whole_call(
        functools.partial(qkv_weights_kernel, PIECES),
        [shaped((3, features, width), BF16)],
        [*normed_one, gproj],
        flops=10**9, moved=4 * mib, with_index=False,
    )[0]
    late = jnp.concatenate([qkv_rows, w_out_rows], axis=0)
    late = scatter_sum(late, "dp", 1)
    out_sum = late[3].astype(F32)
    for by in others:
        out_sum = out_sum + shift(late[3 + by], "tensor", -by).astype(F32)
    late = jnp.concatenate([late[:3], out_sum.astype(BF16)[None]], axis=0)
    late = gather_back(late, "dp", 1)
    grad_w_qkv = jnp.swapaxes(late[:3], 1, 2).astype(F32)
    grad_w_out = late[3].astype(F32)

    gt_share, ggain_one = whole_call(
        functools.partial(input_back_kernel, PIECES, shares),
        [shaped((PIECES * share, width), BF16), shaped((1, width), F32)],
        [idx, *gn_got, *grad_hidden, tokens, gain_one],
        moved=5 * mib,
    )
    gt_got = [gt_share] + [shift(gt_share, "tensor", by) for by in others]
    grad_tokens = whole_call(
        functools.partial(place_kernel, PIECES, shares),
        [shaped((tok_rows, width), F32)], [idx, *gt_got], moved=5 * mib,
    )[0]

    rel_rows = jnp.pad(grad_rel, ((0, 0), (0, width - NB)))
    small = jnp.concatenate([rel_rows, router_rows, ggain_one, ggain_two], axis=0)
    small = sum_over(small, "dp")
    grad_rel_bias = small[:heads, :NB].T
    shared = sum_over(small[8:], "tensor")
    return (
        result,
        grad_tokens,
        shared[8],
        grad_w_qkv,
        grad_w_out,
        grad_rel_bias,
        shared[9],
        shared[:experts].T,
        grad_w_in,
        grad_w_down,
    )


def solution(mesh):
    placed = (
        P("dp", None),
        P("dp", None),
        P("dp", None),
        P("dp", None),
        P(),
        P(None, None, "tensor"),
        P("tensor", None),
        P(None, "tensor"),
        P(),
        P(),
        P(None, None, "tensor"),
        P(None, "tensor", None),
    )
    return jax.shard_map(
        body,
        mesh=mesh,
        in_specs=placed,
        out_specs=(
            P("dp", None),
            P("dp", None),
            P(),
            P(None, None, "tensor"),
            P("tensor", None),
            P(None, "tensor"),
            P(),
            P(),
            P(None, None, "tensor"),
            P(None, "tensor", None),
        ),
        check_vma=False,
    )
```

```python
import functools
import math

import jax
import jax.numpy as jnp
import numpy as np
from jax import lax
from jax.experimental import pallas as pl
from jax.experimental.pallas import tpu as pltpu
from jax.sharding import PartitionSpec as P

NB = 32
DIST = 128
EPSILON = 1e-06
NEGATIVE = -1e30
HIGHEST = lax.Precision.HIGHEST
F32 = jnp.float32
BF16 = jnp.bfloat16
BLK = 256
LANES = 128
VMEM_LIMIT = 56 * 1024 * 1024

NN = (((1,), (0,)), ((), ()))
NT = (((1,), (1,)), ((), ()))
TN = (((0,), (0,)), ((), ()))


def dot(a, b, dims=NN, precision=None):
    return lax.dot_general(a, b, dims, precision=precision, preferred_element_type=F32)


def bucket_of(distance):
    halfway = NB // 2
    thresholds = [
        int(math.ceil(halfway * (DIST / halfway) ** (step / halfway))) for step in range(halfway)
    ]
    beyond = sum((distance >= threshold).astype(np.int64) for threshold in thresholds)
    return np.where(distance < halfway, distance, halfway - 1 + beyond)


def near_tables():
    lanes = np.arange(2 * BLK)
    offset = np.where(lanes < BLK, lanes, lanes - 2 * BLK)
    build = np.stack([np.maximum(offset, 0), np.maximum(BLK + offset, 0)])
    gather = np.stack([lanes - (BLK - 1), lanes + 1])
    eye = np.eye(NB, dtype=np.float32)
    build_hot = eye[bucket_of(build)]
    gather_hot = eye[bucket_of(np.maximum(gather, 0))] * (gather >= 0)[..., None]
    return build_hot, gather_hot


def row_scale(values):
    return lax.rsqrt(jnp.mean(values * values, axis=-1, keepdims=True) + EPSILON)


def lane_pick(values, index):
    lanes = lax.broadcasted_iota(jnp.int32, values.shape, 1)
    return jnp.sum(jnp.where(lanes == index, values, 0.0), axis=1, keepdims=True)


def masked_scores(k_tile, qh_tile, bias, seg_k, seg_q, diagonal):
    scores = dot(k_tile, qh_tile, NT) + bias
    allowed = seg_k == seg_q
    if diagonal:
        key_at = lax.broadcasted_iota(jnp.int32, scores.shape, 0)
        query_at = lax.broadcasted_iota(jnp.int32, scores.shape, 1)
        allowed = allowed & (key_at <= query_at)
    return jnp.where(allowed, scores, NEGATIVE)


def tile_bias(bias_ref, far_ref, head, delta):
    if delta < 2:
        return bias_ref[2 * head + delta]
    return far_ref[pl.ds(head, 1), 0:1]


def column_of(row):
    spread = jnp.broadcast_to(row.astype(F32), (8, row.shape[1]))
    return spread.T[:, 0:1]


def attn_fwd_kernel(piece, pieces, heads, head_size, *refs):
    tok, gain, w, seg = refs[:4]
    refs = refs[4:]
    if piece == 0:
        rel, build = refs[:2]
        refs = refs[2:]
    else:
        bias, far = refs[:2]
        refs = refs[2:]
    old_k, refs = refs[:piece], refs[piece:]
    old_vt, refs = refs[:piece], refs[piece:]
    normed, qh, k, v, vt, att, ot, lse = refs[:8]
    if piece == 0:
        bias, far = refs[8:]
    keys_of, vt_of = [*old_k, k], [*old_vt, vt]
    rows_total = tok.shape[0] // pieces
    base = piece * rows_total
    features = w.shape[1]
    blocks = rows_total // BLK
    gain_row = gain[...].astype(F32)
    lanes = lax.broadcasted_iota(jnp.int32, (BLK, features), 1)
    for block in range(blocks):
        rows = pl.ds(block * BLK, BLK)
        x = tok[pl.ds(base + block * BLK, BLK), :].astype(F32)
        n = (x * row_scale(x) * gain_row).astype(BF16)
        normed[rows, :] = n
        q_rows = dot(n, w[0], NT).astype(BF16).astype(F32) * (head_size**-0.5)
        for head in range(heads):
            inside = (lanes >= head * head_size) & (lanes < (head + 1) * head_size)
            qh[head, rows, :] = jnp.where(inside, q_rows, 0.0).astype(BF16)
        k[rows, :] = dot(n, w[1], NT).astype(BF16)
        v_rows = dot(n, w[2], NT).astype(BF16)
        v[rows, :] = v_rows
        vt[:, rows] = v_rows.astype(F32).T.astype(BF16)
    if piece == 0:
        far[...] = jnp.zeros_like(far)
        far[0:heads, :] = jnp.broadcast_to(rel[:, NB - 1 : NB].astype(F32), (heads, LANES))
        for delta in range(2):
            near = dot(rel[...], build[delta])
            for head in range(heads):
                spread = jnp.broadcast_to(near[head : head + 1, :], (BLK, 2 * BLK))
                turned = pltpu.roll(spread, 0, 1, stride=1, stride_axis=0)
                bias[2 * head + delta] = turned[:, :BLK]
    lse[...] = jnp.zeros_like(lse)
    seg_row = seg[...].astype(F32)
    seg_col = column_of(seg[...])

    def one_head(head, carry):
        part = pl.ds(pl.multiple_of(head * head_size, head_size), head_size)
        for block in range(blocks):
            qb = piece * blocks + block
            cols = pl.ds(block * BLK, BLK)
            q_tile = qh[head, cols, :]
            tiles = []
            for kb in range(qb + 1):
                keys = pl.ds(kb % blocks * BLK, BLK)
                tiles.append(
                    masked_scores(
                        keys_of[kb // blocks][keys, :], q_tile,
                        tile_bias(bias, far, head, qb - kb),
                        seg_col[kb * BLK : (kb + 1) * BLK, :],
                        seg_row[:, qb * BLK : (qb + 1) * BLK], kb == qb,
                    )
                )
            peak = functools.reduce(
                jnp.maximum, [jnp.max(t, axis=0, keepdims=True) for t in tiles]
            )
            total = jnp.zeros((1, BLK), F32)
            out = jnp.zeros((head_size, BLK), F32)
            for kb in range(qb + 1):
                raised = jnp.exp(tiles[kb] - peak)
                total = total + jnp.sum(raised, axis=0, keepdims=True)
                values = vt_of[kb // blocks][part, pl.ds(kb % blocks * BLK, BLK)]
                out = out + dot(values, raised.astype(BF16))
            ot[part, cols] = out / total
            lse[pl.ds(head, 1), cols] = peak + jnp.log(total)
        return carry

    lax.fori_loop(0, heads, one_head, 0)
    for block in range(blocks):
        cols = pl.ds(block * BLK, BLK)
        att[cols, :] = ot[:, cols].T.astype(BF16)


def attn_bwd_kernel(piece, pieces, heads, head_size, shares, idx, *refs):
    held = piece + 1
    last = held == pieces
    go_parts, refs = refs[:shares], refs[shares:]
    qh, ot, lse = refs[:3]
    refs = refs[3:]
    ks, refs = refs[:held], refs[held:]
    vs, refs = refs[:held], refs[held:]
    bias, far, seg = refs[:3]
    refs = refs[3:]
    if piece:
        gk_in, refs = refs[:piece], refs[piece:]
        gv_in, refs = refs[:piece], refs[piece:]
        gq_in, refs = refs[:piece], refs[piece:]
        acc_in, refs = refs[0], refs[1:]
    if last:
        w, hot = refs[:2]
        refs = refs[2:]
        gn_parts, refs = refs[:shares], refs[shares:]
        gproj, rel_out = refs[:2]
        refs = refs[2:]
        gk, refs = refs[:held], refs[held:]
        gv, refs = refs[:held], refs[held:]
        gq_t, acc = refs[:2]
        refs = refs[2:]
    else:
        gk, refs = refs[:held], refs[held:]
        gv, refs = refs[:held], refs[held:]
        gq_t, acc = refs[:2]
        refs = refs[2:]
    go, kt, d_row, near_sum, far_sum = refs
    rows_total, features = ks[0].shape
    blocks = rows_total // BLK
    share = rows_total // shares
    me = idx[0]
    for step in range(shares):
        start = pl.multiple_of((me ^ step) * share, share)
        go[pl.ds(start, share), :] = go_parts[step][...]
    for index in range(held):
        for block in range(blocks):
            cols = pl.ds(block * BLK, BLK)
            kt[:, pl.ds((index * blocks + block) * BLK, BLK)] = (
                ks[index][cols, :].astype(F32).T.astype(BF16)
            )
        if index < piece:
            gk[index][...] = gk_in[index][...]
            gv[index][...] = gv_in[index][...]
        else:
            gk[index][...] = jnp.zeros_like(gk[index])
            gv[index][...] = jnp.zeros_like(gv[index])
    if piece:
        acc[...] = acc_in[...]
    else:
        acc[...] = jnp.zeros_like(acc)
    for block in range(blocks):
        cols = pl.ds(block * BLK, BLK)
        product = go[cols, :].astype(F32).T * ot[:, cols]
        for head in range(heads):
            part = product[head * head_size : (head + 1) * head_size, :]
            d_row[head : head + 1, cols] = jnp.sum(part, axis=0, keepdims=True)
    near_sum[...] = jnp.zeros_like(near_sum)
    far_sum[...] = jnp.zeros_like(far_sum)
    key_at = lax.broadcasted_iota(jnp.int32, (BLK, BLK), 0)
    other_at = lax.broadcasted_iota(jnp.int32, (BLK, BLK), 1)
    flip = (key_at + other_at == BLK - 1).astype(F32)
    seg_row = seg[...].astype(F32)
    seg_col = column_of(seg[...])

    def one_head(head, carry):
        part = pl.ds(pl.multiple_of(head * head_size, head_size), head_size)
        lanes = lax.broadcasted_iota(jnp.int32, (BLK, features), 1)
        inside = (lanes >= head * head_size) & (lanes < (head + 1) * head_size)
        for block in range(blocks):
            qb = piece * blocks + block
            cols = pl.ds(block * BLK, BLK)
            q_tile = qh[head, cols, :]
            go_tile = jnp.where(inside, go[cols, :].astype(F32), 0.0).astype(BF16)
            log_total = lse[pl.ds(head, 1), cols]
            d_tile = d_row[pl.ds(head, 1), cols]
            gq = jnp.zeros((head_size, BLK), F32)
            for kb in range(qb + 1):
                index = kb // blocks
                keys = pl.ds(kb % blocks * BLK, BLK)
                delta = qb - kb
                scores = masked_scores(
                    ks[index][keys, :], q_tile, tile_bias(bias, far, head, delta),
                    seg_col[kb * BLK : (kb + 1) * BLK, :],
                    seg_row[:, qb * BLK : (qb + 1) * BLK], delta == 0,
                )
                probs = jnp.exp(scores - log_total)
                gs = probs * (dot(vs[index][keys, :], go_tile, NT) - d_tile)
                if delta < 2:
                    acc[2 * head + delta] += gs
                else:
                    far_sum[pl.ds(head, 1), :] += jnp.sum(gs, axis=0, keepdims=True)
                gs_low = gs.astype(BF16)
                gv[index][keys, :] += dot(probs.astype(BF16), go_tile)
                gk[index][keys, :] += dot(gs_low, q_tile)
                gq = gq + dot(kt[part, kb * BLK : (kb + 1) * BLK], gs_low)
            gq_t[part, cols] = gq * (head_size**-0.5)
        return carry

    lax.fori_loop(0, heads, one_head, 0)
    if not last:
        return
    gqs = [*(gq_in if piece else ()), gq_t]
    for index in range(held):
        for block in range(blocks):
            rows = pl.ds(block * BLK, BLK)
            out = pl.ds((index * blocks + block) * BLK, BLK)
            gproj[0, out, :] = gqs[index][:, rows].T.astype(BF16)
            gproj[1, out, :] = gk[index][rows, :].astype(BF16)
            gproj[2, out, :] = gv[index][rows, :].astype(BF16)
    for step in range(shares):
        for index in range(pieces):
            start = index * rows_total + (me ^ step) * share
            rows = pl.ds(pl.multiple_of(start, share), share)
            total = dot(gproj[0, rows, :], w[0])
            total = total + dot(gproj[1, rows, :], w[1])
            total = total + dot(gproj[2, rows, :], w[2])
            gn_parts[step][pl.ds(index * share, share), :] = total.astype(BF16)
    for head in range(heads):
        for delta in range(2):
            turned = dot(flip, acc[2 * head + delta], NN, HIGHEST)
            wide = jnp.concatenate([turned, jnp.zeros_like(turned)], axis=1)
            sheared = pltpu.roll(wide, 0, 1, stride=1, stride_axis=0)
            near_sum[delta, head : head + 1, :] = jnp.sum(sheared, axis=0, keepdims=True)
    summed = dot(near_sum[0], hot[0], NN, HIGHEST) + dot(near_sum[1], hot[1], NN, HIGHEST)
    buckets = lax.broadcasted_iota(jnp.int32, summed.shape, 1)
    beyond = jnp.sum(far_sum[...], axis=1, keepdims=True)
    rel_out[...] = summed + jnp.where(buckets == NB - 1, beyond, 0.0)


def qkv_weights_kernel(pieces, *refs):
    normed = refs[:pieces]
    gproj, out = refs[pieces:]
    rows_total = normed[0].shape[0]
    for c in range(3):
        total = dot(gproj[c, pl.ds(0, rows_total), :], normed[0][...], TN)
        for index in range(1, pieces):
            rows = pl.ds(index * rows_total, rows_total)
            total = total + dot(gproj[c, rows, :], normed[index][...], TN)
        out[c] = total.astype(BF16)


def gelu_pair(values):
    squared = values * values
    bent = jnp.tanh(values * (0.7978845608028654 + 0.7978845608028654 * 0.044715 * squared))
    half = 0.5 * (1.0 + bent)
    lifted = values * half
    slope = 0.7978845608028654 + 3.0 * 0.7978845608028654 * 0.044715 * squared
    return lifted, half + lifted * (1.0 - bent) * slope


def padded_rows(values, rows):
    missing = jnp.zeros((rows - values.shape[0], values.shape[1]), values.dtype)
    return jnp.concatenate([values, missing], axis=0)


def moe_fwd_kernel(piece, pieces, shares, experts, idx, *refs):
    att, refs = refs[:shares], refs[shares:]
    if piece == 0:
        wo_own, wo_swapped, refs = refs[0], refs[1], refs[2:]
        wo_fetched, refs = refs[: shares - 1], refs[shares - 1 :]
    else:
        wo, refs = refs[0], refs[1:]
    tok, gain, router, routes, cot, w_in, w_down = refs[:7]
    refs = refs[7:]
    parts, refs = refs[:shares], refs[shares:]
    if piece == 0:
        wo, refs = refs[0], refs[1:]
    normed, own, gates, ggate, act, slope, acc = refs
    rows_total = tok.shape[0] // pieces
    base = piece * rows_total
    share = rows_total // shares
    me = idx[0]
    expert = pl.program_id(0)

    @pl.when(expert == 0)
    def _():
        gain_row = gain[...].astype(F32)
        router_wide = padded_rows(router[...].astype(F32), LANES).astype(BF16)
        if piece == 0:
            half = wo_own.shape[0] // 2
            mine = pl.ds(pl.multiple_of(idx[1] * half, half), half)
            other = pl.ds(pl.multiple_of((1 - idx[1]) * half, half), half)
            wo[0] = wo_own[...]
            for step in range(1, shares):
                wo[step, mine, :] = wo_fetched[step - 1][...]
                wo[step, other, :] = wo_swapped[step - 1]
        for block in range(rows_total // BLK):
            rows = pl.ds(block * BLK, BLK)
            outer = pl.ds(base + block * BLK, BLK)
            attn = dot(att[0][rows, :], wo[0])
            for step in range(1, shares):
                attn = attn + dot(att[step][rows, :], wo[step])
            hidden = tok[outer, :].astype(F32) + attn
            acc[rows, :] = hidden
            n = (hidden * row_scale(hidden) * gain_row).astype(BF16)
            normed[rows, :] = n
            logits = dot(n, router_wide, NT)
            lanes = lax.broadcasted_iota(jnp.int32, logits.shape, 1)
            first = lanes == routes[outer, 0:1]
            second = lanes == routes[outer, 1:2]
            one = jnp.sum(jnp.where(first, logits, 0.0), axis=1, keepdims=True)
            two = jnp.sum(jnp.where(second, logits, 0.0), axis=1, keepdims=True)
            peak = jnp.maximum(one, two)
            one = jnp.exp(one - peak)
            two = jnp.exp(two - peak)
            both = one + two
            gates[rows, :] = jnp.where(first, one / both, jnp.where(second, two / both, 0.0))
        own[...] = acc[pl.ds(pl.multiple_of(me * share, share), share), :]
        acc[...] = jnp.zeros_like(acc)
        ggate[...] = jnp.zeros_like(ggate)

    for block in range(rows_total // ROWS):
        rows = pl.ds(block * ROWS, ROWS)
        outer = pl.ds(base + block * ROWS, ROWS)
        lifted, bend = gelu_pair(dot(normed[rows, :], w_in[0]))
        lifted = lifted.astype(BF16)
        act[0, rows, :] = lifted
        slope[0, rows, :] = bend.astype(BF16)
        out = dot(lifted, w_down[0])
        gate = lane_pick(gates[rows, :], expert)
        acc[rows, :] += gate * out
        pulled = jnp.sum(cot[outer, :].astype(F32) * out, axis=1, keepdims=True)
        held = ggate[rows, :]
        lanes = lax.broadcasted_iota(jnp.int32, held.shape, 1)
        ggate[rows, :] = jnp.where(lanes == expert, pulled, held)

    @pl.when(expert == experts - 1)
    def _():
        for step in range(shares):
            start = pl.multiple_of((me ^ step) * share, share)
            parts[step][...] = acc[pl.ds(start, share), :].astype(BF16)


def moe_bwd_kernel(piece, shares, experts, idx, *refs):
    gates, ggate, cot, slope, router, w_in, w_down = refs[:7]
    refs = refs[7:]
    parts, refs = refs[:shares], refs[shares:]
    glog, gpre, acc = refs
    rows_total = gates.shape[0]
    base = piece * rows_total
    share = rows_total // shares
    me = idx[0]
    expert = pl.program_id(0)

    @pl.when(expert == 0)
    def _():
        router_wide = padded_rows(router[...].astype(F32), LANES)
        for block in range(rows_total // ROWS):
            rows = pl.ds(block * ROWS, ROWS)
            g, gg = gates[rows, :], ggate[rows, :]
            back = g * (gg - jnp.sum(g * gg, axis=1, keepdims=True))
            glog[rows, :] = back
            acc[rows, :] = dot(back, router_wide, NN, HIGHEST)

    for block in range(rows_total // ROWS):
        rows = pl.ds(block * ROWS, ROWS)
        gate = lane_pick(gates[rows, :], expert)
        weighted = cot[pl.ds(base + block * ROWS, ROWS), :].astype(F32)
        weighted = (gate * weighted).astype(BF16)
        gp = (dot(weighted, w_down[0], NT) * slope[0, rows, :].astype(F32)).astype(BF16)
        gpre[0, rows, :] = gp
        acc[rows, :] += dot(gp, w_in[0], NT)

    @pl.when(expert == experts - 1)
    def _():
        for step in range(shares):
            start = pl.multiple_of((me ^ step) * share, share)
            parts[step][...] = acc[pl.ds(start, share), :].astype(BF16)


def moe_weights_kernel(pieces, cot, *refs):
    gates, refs = refs[:pieces], refs[pieces:]
    glog, refs = refs[:pieces], refs[pieces:]
    normed, refs = refs[:pieces], refs[pieces:]
    act, refs = refs[:pieces], refs[pieces:]
    gpre, refs = refs[:pieces], refs[pieces:]
    out, router = refs
    rows_total = normed[0].shape[0]
    expert = pl.program_id(0)

    @pl.when(expert == 0)
    def _():
        total = jnp.zeros((LANES, cot.shape[1]), F32)
        for index in range(pieces):
            back = glog[index][...]
            high = back.astype(BF16)
            low = (back - high.astype(F32)).astype(BF16)
            total = total + dot(high, normed[index][...], TN)
            total = total + dot(low, normed[index][...], TN)
        router[...] = total[0:8, :]

    grad_in = jnp.zeros((normed[0].shape[1], gpre[0].shape[2]), F32)
    grad_down = jnp.zeros((act[0].shape[2], cot.shape[1]), F32)
    for index in range(pieces):
        gate = lane_pick(gates[index][...], expert)
        weighted = cot[pl.ds(index * rows_total, rows_total), :].astype(F32)
        weighted = (gate * weighted).astype(BF16)
        grad_in = grad_in + dot(normed[index][...], gpre[index][0], TN)
        grad_down = grad_down + dot(act[index][0], weighted, TN)
    out[0, 0] = grad_in.astype(BF16)
    out[0, 1] = grad_down.astype(BF16)


def hidden_back_kernel(piece, pieces, shares, got, idx, *refs):
    gx, refs = refs[:got], refs[got:]
    wo, own, cot, gain = refs[:4]
    refs = refs[4:]
    ga, refs = refs[:shares], refs[shares:]
    gh, gh_low, ggain = refs
    share = own.shape[0]
    grad = gx[0][...].astype(F32)
    for step in range(1, got):
        grad = grad + gx[step][...].astype(F32)
    hidden = own[...]
    scale = row_scale(hidden)
    unit = hidden * scale
    ggain[...] = jnp.sum(grad * unit, axis=0, keepdims=True)
    gained = grad * gain[...].astype(F32)
    start = piece * (cot.shape[0] // pieces) + idx[0] * share
    mine = cot[pl.ds(pl.multiple_of(start, share), share), :].astype(F32)
    back = mine + scale * (gained - unit * jnp.mean(gained * unit, axis=-1, keepdims=True))
    gh[...] = back
    low = back.astype(BF16)
    gh_low[...] = low
    for step in range(shares):
        ga[step][...] = dot(low, wo[step], NT).astype(BF16)


def w_out_back_kernel(pieces, shares, idx, *refs):
    att, refs = refs[: pieces * shares], refs[pieces * shares :]
    gh_low, out = refs[:pieces], refs[pieces]
    share = gh_low[0].shape[0]
    rows = pl.ds(pl.multiple_of(idx[0] * share, share), share)
    for step in range(shares):
        total = dot(att[step][rows, :], gh_low[0][...], TN)
        for index in range(1, pieces):
            total = total + dot(att[index * shares + step][rows, :], gh_low[index][...], TN)
        out[step] = total.astype(BF16)


def join_kernel(pieces, count, *refs):
    own, refs = refs[:pieces], refs[pieces:]
    got, out = refs[: pieces * count], refs[pieces * count]
    share = own[0].shape[0]
    for index in range(pieces):
        total = own[index][...]
        for step in range(count):
            total = total + got[index * count + step][...].astype(F32)
        out[pl.ds(index * share, share), :] = total.astype(BF16)


def input_back_kernel(pieces, got, idx, *refs):
    gn, refs = refs[:got], refs[got:]
    ghs, refs = refs[:pieces], refs[pieces:]
    tok, gain, gt, ggain = refs
    share = ghs[0].shape[0]
    gain_row = gain[...].astype(F32)
    total = jnp.zeros_like(ggain)
    for index in range(pieces):
        rows = pl.ds(index * share, share)
        grad = gn[0][rows, :].astype(F32)
        for step in range(1, got):
            grad = grad + gn[step][rows, :].astype(F32)
        start = index * (tok.shape[0] // pieces) + idx[0] * share
        x = tok[pl.ds(pl.multiple_of(start, share), share), :].astype(F32)
        scale = row_scale(x)
        unit = x * scale
        total = total + jnp.sum(grad * unit, axis=0, keepdims=True)
        gained = grad * gain_row
        back = scale * (gained - unit * jnp.mean(gained * unit, axis=-1, keepdims=True))
        gt[rows, :] = (ghs[index][...] + back).astype(BF16)
    ggain[...] = total


def place_kernel(pieces, shares, idx, *refs):
    blocks, out = refs[:shares], refs[shares]
    rows_total = out.shape[0] // pieces
    share = rows_total // shares
    for step in range(shares):
        owner = idx[0] ^ step
        for index in range(pieces):
            start = pl.multiple_of(index * rows_total + owner * share, share)
            got = blocks[step][pl.ds(index * share, share), :]
            out[pl.ds(start, share), :] = got.astype(out.dtype)


ROWS = 512
PIECES = 2

SMEM = pl.BlockSpec(memory_space=pltpu.SMEM)
VMEM = pl.BlockSpec(memory_space=pltpu.VMEM)


def shaped(shape, dtype):
    return jax.ShapeDtypeStruct(shape, dtype)


def whole_call(kernel, outs, args, scratch=(), flops=0, moved=0, with_index=True):
    specs = ([SMEM] if with_index else []) + [VMEM] * (len(args) - (1 if with_index else 0))
    return pl.pallas_call(
        kernel,
        out_shape=outs,
        in_specs=specs,
        out_specs=[VMEM] * len(outs),
        scratch_shapes=list(scratch),
        compiler_params=pltpu.CompilerParams(vmem_limit_bytes=VMEM_LIMIT),
        cost_estimate=pl.CostEstimate(flops=flops, bytes_accessed=moved, transcendentals=0),
    )(*args)


def swap(value, axis, bit):
    count = lax.axis_size(axis)
    return lax.ppermute(value, axis, [(i, i ^ bit) for i in range(count)])


def sum_over(value, axis):
    bit = 1
    while bit < lax.axis_size(axis):
        value = value + swap(value, axis, bit)
        bit *= 2
    return value


def gather_parts(value, axis):
    count = lax.axis_size(axis)
    if count != 4:
        return [value] + [swap(value, axis, bit) for bit in range(1, count)]
    two = swap(value, axis, 2)
    one = swap(value, axis, 1)
    return [value, one, two, swap(two, axis, 1)]


def reduce_parts(parts, axis):
    count = lax.axis_size(axis)
    if count != 4:
        return [parts[0]] + [swap(parts[bit], axis, bit) for bit in range(1, count)]
    near = swap(parts[3], axis, 1)
    pair = (parts[2].astype(F32) + near.astype(F32)).astype(parts[2].dtype)
    return [parts[0], swap(parts[1], axis, 1), swap(pair, axis, 2)]


def halves_of(value, axis, chosen):
    half = value.shape[axis] // 2
    keep = lax.dynamic_slice_in_dim(value, chosen * half, half, axis)
    send = lax.dynamic_slice_in_dim(value, (1 - chosen) * half, half, axis)
    return keep, send


def bits_of(axis):
    count = lax.axis_size(axis)
    return [1 << level for level in range(count.bit_length() - 1)]


def scatter_sum(value, mesh_axis, axis):
    me = lax.axis_index(mesh_axis)
    for bit in bits_of(mesh_axis):
        keep, send = halves_of(value, axis, (me // bit) % 2)
        got = swap(send, mesh_axis, bit)
        value = (keep.astype(F32) + got.astype(F32)).astype(value.dtype)
    return value


def after(value, *others):
    return lax.optimization_barrier((value, *others))[0]


def body(
    tokens, segments, routes, grad_out, gain_attn, w_qkv, w_out, rel_bias,
    gain_moe, w_router, w_in, w_down,
):
    tok_rows, width = tokens.shape
    heads = rel_bias.shape[1]
    features = w_qkv.shape[2]
    head_size = features // heads
    experts, _, hidden_units = w_in.shape
    shares = lax.axis_size("tensor")
    rows = tok_rows // PIECES
    share = rows // shares
    me = lax.axis_index("tensor").astype(jnp.int32)
    side = (lax.axis_index("dp") % 2).astype(jnp.int32)
    idx = jnp.stack([me, side])
    mib = 1 << 20
    others = range(1, shares)

    build_hot, gather_hot = near_tables()
    build_hot = jnp.asarray(np.swapaxes(build_hot, 1, 2), BF16)
    gather_hot = jnp.asarray(gather_hot, F32)
    w_qkv_t = jnp.swapaxes(w_qkv, 1, 2)
    router_t = w_router.T
    gain_one = gain_attn.reshape(1, width)
    gain_two = gain_moe.reshape(1, width)

    def attend(piece, bias_args, old_k, old_vt):
        outs = [
            shaped((rows, width), BF16),
            shaped((heads, rows, features), BF16),
            shaped((rows, features), BF16),
            shaped((rows, features), BF16),
            shaped((features, rows), BF16),
            shaped((rows, features), BF16),
            shaped((features, rows), F32),
            shaped((8, rows), F32),
        ]
        if piece == 0:
            outs += [shaped((2 * heads, BLK, BLK), F32), shaped((8, LANES), F32)]
        return whole_call(
            functools.partial(attn_fwd_kernel, piece, PIECES, heads, head_size),
            outs,
            [tokens, gain_one, w_qkv_t, segments, *bias_args, *old_k, *old_vt],
            flops=3 * 10**9, moved=8 * mib, with_index=False,
        )

    stages = []
    bias_args = [rel_bias.T, build_hot]
    for piece in range(PIECES):
        got = attend(piece, bias_args, [s[2] for s in stages], [s[4] for s in stages])
        if piece == 0:
            bias_args = got[8:]
        stages.append(got[:8])
    bias, far = bias_args
    normed_one = [s[0] for s in stages]

    half_rows = features // 2
    my_half = lax.dynamic_slice_in_dim(w_out, side * half_rows, half_rows, 0)
    my_half = after(my_half, stages[0][5])
    halves = [swap(my_half, "tensor", by) for by in others]
    swapped = swap(after(jnp.stack(halves), stages[-1][5]), "dp", 1)

    atts = []
    for stage in stages:
        mine = after(stage[5], *atts[-1][1:]) if atts else stage[5]
        atts.append(gather_parts(mine, "tensor"))

    full = lambda shape: pl.BlockSpec(shape, lambda e: (0,) * len(shape))
    per_expert = lambda shape: pl.BlockSpec((1,) + shape, lambda e: (e, 0, 0))
    params = pltpu.CompilerParams(
        vmem_limit_bytes=VMEM_LIMIT, dimension_semantics=("arbitrary",)
    )
    moe_flops = 4 * experts * rows * width * hidden_units

    def moe_forward(piece, wo_args):
        wo_specs = [full(one.shape) for one in wo_args]
        wo_shape = (shares, features, width)
        return pl.pallas_call(
            functools.partial(moe_fwd_kernel, piece, PIECES, shares, experts),
            grid=(experts,),
            in_specs=[SMEM]
            + [full((rows, features))] * shares
            + wo_specs
            + [
                full((tok_rows, width)), full((1, width)), full((experts, width)),
                full((tok_rows, 2)), full((tok_rows, width)),
                per_expert((width, hidden_units)), per_expert((hidden_units, width)),
            ],
            out_specs=[full((share, width))] * shares
            + [full(wo_shape)] * (piece == 0)
            + [
                full((rows, width)), full((share, width)), full((rows, LANES)),
                full((rows, LANES)), per_expert((rows, hidden_units)),
                per_expert((rows, hidden_units)),
            ],
            out_shape=[shaped((share, width), BF16)] * shares
            + [shaped(wo_shape, BF16)] * (piece == 0)
            + [
                shaped((rows, width), BF16),
                shaped((share, width), F32),
                shaped((rows, LANES), F32),
                shaped((rows, LANES), F32),
                shaped((experts, rows, hidden_units), BF16),
                shaped((experts, rows, hidden_units), BF16),
            ],
            scratch_shapes=[pltpu.VMEM((rows, width), F32)],
            compiler_params=params,
            cost_estimate=pl.CostEstimate(
                flops=moe_flops, bytes_accessed=20 * mib, transcendentals=0
            ),
        )(
            idx, *atts[piece], *wo_args, tokens, gain_two, router_t, routes, grad_out,
            w_in, w_down,
        )

    def moe_backward(piece, gates, ggate, slope):
        return pl.pallas_call(
            functools.partial(moe_bwd_kernel, piece, shares, experts),
            grid=(experts,),
            in_specs=[
                SMEM, full((rows, LANES)), full((rows, LANES)), full((tok_rows, width)),
                per_expert((rows, hidden_units)), full((experts, width)),
                per_expert((width, hidden_units)), per_expert((hidden_units, width)),
            ],
            out_specs=[full((share, width))] * shares
            + [full((rows, LANES)), per_expert((rows, hidden_units))],
            out_shape=[shaped((share, width), BF16)] * shares
            + [
                shaped((rows, LANES), F32),
                shaped((experts, rows, hidden_units), BF16),
            ],
            scratch_shapes=[pltpu.VMEM((rows, width), F32)],
            compiler_params=params,
            cost_estimate=pl.CostEstimate(
                flops=moe_flops, bytes_accessed=16 * mib, transcendentals=0
            ),
        )(idx, gates, ggate, grad_out, slope, router_t, w_in, w_down)

    moe_got, gx_got, forwards, backwards = [], [], [], []
    wo_args = [w_out, swapped, *halves]
    for piece in range(PIECES):
        fwd = moe_forward(piece, wo_args)
        parts, kept = fwd[:shares], fwd[shares:]
        if piece == 0:
            wo, kept = kept[0], kept[1:]
            wo_args = [wo]
        moe_got.append(reduce_parts(parts, "tensor"))
        gates, ggate, slope = kept[2], kept[3], kept[5]
        bwd = moe_backward(piece, gates, ggate, slope)
        parts = bwd[:shares]
        gx_got.append(reduce_parts(parts, "tensor"))
        forwards.append(kept)
        backwards.append(bwd[shares:])
    normed_two = [f[0] for f in forwards]
    own_hidden = [f[1] for f in forwards]
    all_gates = [f[2] for f in forwards]
    acts = [f[4] for f in forwards]
    glogs = [b[0] for b in backwards]
    gpres = [b[1] for b in backwards]

    def hidden_back(piece, own):
        got = whole_call(
            functools.partial(hidden_back_kernel, piece, PIECES, shares, len(gx_got[piece])),
            [shaped((share, features), BF16)] * shares
            + [
                shaped((share, width), F32), shaped((share, width), BF16),
                shaped((1, width), F32),
            ],
            [idx, *gx_got[piece], wo, own, grad_out, gain_two],
            flops=2 * 10**8, moved=5 * mib,
        )
        parts = got[:shares]
        go = [parts[0]] + [swap(parts[by], "tensor", by) for by in others]
        return go, got[shares:]

    def attend_back(piece, go, carried):
        held = piece + 1
        last = held == PIECES
        outs, scratch = [], []
        if last:
            outs += [shaped((PIECES * share, width), BF16)] * shares
            outs += [shaped((3, tok_rows, features), BF16), shaped((8, NB), F32)]
        sums = [((rows, features), F32)] * (2 * held)
        sums += [((features, rows), F32), ((2 * heads, BLK, BLK), F32)]
        if last:
            scratch += [pltpu.VMEM(*one) for one in sums]
        else:
            outs += [shaped(*one) for one in sums]
        scratch += [
            pltpu.VMEM((rows, features), BF16),
            pltpu.VMEM((features, tok_rows), BF16),
            pltpu.VMEM((8, rows), F32),
            pltpu.VMEM((2, 8, 2 * BLK), F32),
            pltpu.VMEM((8, BLK), F32),
        ]
        return whole_call(
            functools.partial(attn_bwd_kernel, piece, PIECES, heads, head_size, shares),
            outs,
            [
                idx, *go, stages[piece][1], stages[piece][6], stages[piece][7],
                *[s[2] for s in stages[:held]], *[s[3] for s in stages[:held]],
                bias, far, segments, *carried, *([w_qkv_t, gather_hot] if last else []),
            ],
            scratch,
            flops=7 * 10**9, moved=8 * mib,
        )

    go, back_first = hidden_back(0, own_hidden[0])
    expert_grads, router_rows = pl.pallas_call(
        functools.partial(moe_weights_kernel, PIECES),
        grid=(experts,),
        in_specs=[full((tok_rows, width))]
        + [full((rows, LANES))] * (2 * PIECES)
        + [full((rows, width))] * PIECES
        + [per_expert((rows, hidden_units))] * (2 * PIECES),
        out_specs=[
            pl.BlockSpec((1, 2, width, width), lambda e: (e, 0, 0, 0)), full((8, width))
        ],
        out_shape=[shaped((experts, 2, width, width), BF16), shaped((8, width), F32)],
        compiler_params=params,
        cost_estimate=pl.CostEstimate(
            flops=2 * moe_flops, bytes_accessed=26 * mib, transcendentals=0
        ),
    )(after(grad_out, back_first[1]), *all_gates, *glogs, *normed_two, *acts, *gpres)
    expert_rows = lax.psum_scatter(
        expert_grads.reshape(experts * 2 * width, width), "dp", scatter_dimension=0, tiled=True
    )

    go_second, back_second = hidden_back(1, after(own_hidden[1], router_rows))
    result_share = whole_call(
        functools.partial(join_kernel, PIECES, len(moe_got[0])),
        [shaped((PIECES * share, width), BF16)],
        [*own_hidden, *moe_got[0], *moe_got[1]],
        moved=4 * mib, with_index=False,
    )[0]
    go = [after(go[0], back_second[1]), *go[1:]]
    first = attend_back(0, go, [])
    go_second = [after(go_second[0], first[0], result_share), *go_second[1:]]
    second = attend_back(1, go_second, first)
    grad_hidden = [back_first[0], back_second[0]]
    ggain_two = back_first[2] + back_second[2]
    gn_parts = second[:shares]
    gproj, grad_rel = second[shares:]
    gn_got = reduce_parts(gn_parts, "tensor")

    result_got = gather_parts(result_share, "tensor")
    result = whole_call(
        functools.partial(place_kernel, PIECES, shares),
        [shaped((tok_rows, width), BF16)], [idx, *result_got], moved=3 * mib,
    )[0]
    w_out_rows = whole_call(
        functools.partial(w_out_back_kernel, PIECES, shares),
        [shaped((shares, features, width), BF16)],
        [idx, *atts[0], *atts[1], back_first[1], after(back_second[1], gproj)],
        flops=3 * 10**8, moved=4 * mib,
    )[0]
    qkv_rows = whole_call(
        functools.partial(qkv_weights_kernel, PIECES),
        [shaped((3, features, width), BF16)],
        [*normed_one, gproj],
        flops=10**9, moved=4 * mib, with_index=False,
    )[0]

    gt_share, ggain_one = whole_call(
        functools.partial(input_back_kernel, PIECES, len(gn_got)),
        [shaped((PIECES * share, width), BF16), shaped((1, width), F32)],
        [idx, *gn_got, *grad_hidden, tokens, gain_one],
        moved=5 * mib,
    )
    gt_got = gather_parts(gt_share, "tensor")
    grad_tokens = whole_call(
        functools.partial(place_kernel, PIECES, shares),
        [shaped((tok_rows, width), F32)], [idx, *gt_got], moved=5 * mib,
    )[0]

    late = after(jnp.concatenate([qkv_rows, w_out_rows], axis=0), gt_share)
    late = scatter_sum(late, "dp", 1)
    out_sum = late[3].astype(F32)
    for by in others:
        out_sum = out_sum + swap(late[3 + by], "tensor", by).astype(F32)
    late_rows = late.shape[1]
    late = jnp.concatenate([late[:3], out_sum.astype(BF16)[None]], axis=0)
    shard = expert_rows.shape[0]
    both = jnp.concatenate([after(expert_rows, late), late.reshape(4 * late_rows, width)], axis=0)
    both = lax.all_gather(both, "dp", axis=0)
    expert_rows = both[:, :shard].reshape(experts, 2, width, width)
    grad_w_in = expert_rows[:, 0].astype(F32)
    grad_w_down = expert_rows[:, 1].astype(F32)
    levels = len(bits_of("dp"))
    late = both[:, shard:].reshape([2] * levels + [4, late_rows, width])
    late = jnp.transpose(late, [levels, *reversed(range(levels)), levels + 1, levels + 2])
    late = late.reshape(4, features, width)
    grad_w_qkv = jnp.swapaxes(late[:3], 1, 2).astype(F32)
    grad_w_out = late[3].astype(F32)

    rel_rows = jnp.pad(grad_rel, ((0, 0), (0, width - NB)))
    small = jnp.concatenate([rel_rows, router_rows, ggain_one, ggain_two], axis=0)
    small = sum_over(small, "dp")
    grad_rel_bias = small[:heads, :NB].T
    shared = sum_over(small[8:], "tensor")
    return (
        result,
        grad_tokens,
        shared[8],
        grad_w_qkv,
        grad_w_out,
        grad_rel_bias,
        shared[9],
        shared[:experts].T,
        grad_w_in,
        grad_w_down,
    )


def solution(mesh):
    placed = (
        P("dp", None),
        P("dp", None),
        P("dp", None),
        P("dp", None),
        P(),
        P(None, None, "tensor"),
        P("tensor", None),
        P(None, "tensor"),
        P(),
        P(),
        P(None, None, "tensor"),
        P(None, "tensor", None),
    )
    return jax.shard_map(
        body,
        mesh=mesh,
        in_specs=placed,
        out_specs=(
            P("dp", None),
            P("dp", None),
            P(),
            P(None, None, "tensor"),
            P("tensor", None),
            P(None, "tensor"),
            P(),
            P(),
            P(None, None, "tensor"),
            P(None, "tensor", None),
        ),
        check_vma=False,
    )
```

```python
import functools
import math

import jax
import jax.numpy as jnp
import numpy as np
from jax import lax
from jax.experimental import pallas as pl
from jax.experimental.pallas import tpu as pltpu
from jax.sharding import PartitionSpec as P

NB = 32
DIST = 128
EPSILON = 1e-06
NEGATIVE = -1e30
HIGHEST = lax.Precision.HIGHEST
F32 = jnp.float32
BF16 = jnp.bfloat16
BLK = 256
LANES = 128
VMEM_LIMIT = 56 * 1024 * 1024

NN = (((1,), (0,)), ((), ()))
NT = (((1,), (1,)), ((), ()))
TN = (((0,), (0,)), ((), ()))


def dot(a, b, dims=NN, precision=None):
    return lax.dot_general(a, b, dims, precision=precision, preferred_element_type=F32)


def bucket_of(distance):
    halfway = NB // 2
    thresholds = [
        int(math.ceil(halfway * (DIST / halfway) ** (step / halfway))) for step in range(halfway)
    ]
    beyond = sum((distance >= threshold).astype(np.int64) for threshold in thresholds)
    return np.where(distance < halfway, distance, halfway - 1 + beyond)


def near_tables():
    lanes = np.arange(2 * BLK)
    offset = np.where(lanes < BLK, lanes, lanes - 2 * BLK)
    build = np.stack([np.maximum(offset, 0), np.maximum(BLK + offset, 0)])
    gather = np.stack([lanes - (BLK - 1), lanes + 1])
    eye = np.eye(NB, dtype=np.float32)
    build_hot = eye[bucket_of(build)]
    gather_hot = eye[bucket_of(np.maximum(gather, 0))] * (gather >= 0)[..., None]
    return build_hot, gather_hot


def row_scale(values):
    return lax.rsqrt(jnp.mean(values * values, axis=-1, keepdims=True) + EPSILON)


def lane_pick(values, index):
    lanes = lax.broadcasted_iota(jnp.int32, values.shape, 1)
    return jnp.sum(jnp.where(lanes == index, values, 0.0), axis=1, keepdims=True)


def masked_scores(k_tile, qh_tile, bias, seg_k, seg_q, diagonal):
    scores = dot(k_tile, qh_tile, NT) + bias
    allowed = seg_k == seg_q
    if diagonal:
        key_at = lax.broadcasted_iota(jnp.int32, scores.shape, 0)
        query_at = lax.broadcasted_iota(jnp.int32, scores.shape, 1)
        allowed = allowed & (key_at <= query_at)
    return jnp.where(allowed, scores, NEGATIVE)


def tile_bias(bias_ref, far_ref, head, delta):
    if delta < 2:
        return bias_ref[2 * head + delta]
    return far_ref[pl.ds(head, 1), 0:1]


def column_of(row):
    spread = jnp.broadcast_to(row.astype(F32), (8, row.shape[1]))
    return spread.T[:, 0:1]


def attn_fwd_kernel(piece, pieces, heads, head_size, *refs):
    tok, gain, w, seg = refs[:4]
    refs = refs[4:]
    if piece == 0:
        rel, build = refs[:2]
        refs = refs[2:]
    else:
        bias, far = refs[:2]
        refs = refs[2:]
    old_k, refs = refs[:piece], refs[piece:]
    old_vt, refs = refs[:piece], refs[piece:]
    normed, qh, k, v, vt, att, ot, lse = refs[:8]
    if piece == 0:
        bias, far = refs[8:]
    keys_of, vt_of = [*old_k, k], [*old_vt, vt]
    rows_total = tok.shape[0] // pieces
    base = piece * rows_total
    features = w.shape[1]
    blocks = rows_total // BLK
    gain_row = gain[...].astype(F32)
    lanes = lax.broadcasted_iota(jnp.int32, (BLK, features), 1)
    for block in range(blocks):
        rows = pl.ds(block * BLK, BLK)
        x = tok[pl.ds(base + block * BLK, BLK), :].astype(F32)
        n = (x * row_scale(x) * gain_row).astype(BF16)
        normed[rows, :] = n
        q_rows = dot(n, w[0], NT).astype(BF16).astype(F32) * (head_size**-0.5)
        for head in range(heads):
            inside = (lanes >= head * head_size) & (lanes < (head + 1) * head_size)
            qh[head, rows, :] = jnp.where(inside, q_rows, 0.0).astype(BF16)
        k[rows, :] = dot(n, w[1], NT).astype(BF16)
        v_rows = dot(n, w[2], NT).astype(BF16)
        v[rows, :] = v_rows
        vt[:, rows] = v_rows.astype(F32).T.astype(BF16)
    if piece == 0:
        far[...] = jnp.zeros_like(far)
        far[0:heads, :] = jnp.broadcast_to(rel[:, NB - 1 : NB].astype(F32), (heads, LANES))
        for delta in range(2):
            near = dot(rel[...], build[delta])
            for head in range(heads):
                spread = jnp.broadcast_to(near[head : head + 1, :], (BLK, 2 * BLK))
                turned = pltpu.roll(spread, 0, 1, stride=1, stride_axis=0)
                bias[2 * head + delta] = turned[:, :BLK]
    lse[...] = jnp.zeros_like(lse)
    seg_row = seg[...].astype(F32)
    seg_col = column_of(seg[...])

    def one_head(head, carry):
        part = pl.ds(pl.multiple_of(head * head_size, head_size), head_size)
        for block in range(blocks):
            qb = piece * blocks + block
            cols = pl.ds(block * BLK, BLK)
            q_tile = qh[head, cols, :]
            tiles = []
            for kb in range(qb + 1):
                keys = pl.ds(kb % blocks * BLK, BLK)
                tiles.append(
                    masked_scores(
                        keys_of[kb // blocks][keys, :], q_tile,
                        tile_bias(bias, far, head, qb - kb),
                        seg_col[kb * BLK : (kb + 1) * BLK, :],
                        seg_row[:, qb * BLK : (qb + 1) * BLK], kb == qb,
                    )
                )
            peak = functools.reduce(
                jnp.maximum, [jnp.max(t, axis=0, keepdims=True) for t in tiles]
            )
            total = jnp.zeros((1, BLK), F32)
            out = jnp.zeros((head_size, BLK), F32)
            for kb in range(qb + 1):
                raised = jnp.exp(tiles[kb] - peak)
                total = total + jnp.sum(raised, axis=0, keepdims=True)
                values = vt_of[kb // blocks][part, pl.ds(kb % blocks * BLK, BLK)]
                out = out + dot(values, raised.astype(BF16))
            ot[part, cols] = out / total
            lse[pl.ds(head, 1), cols] = peak + jnp.log(total)
        return carry

    lax.fori_loop(0, heads, one_head, 0)
    for block in range(blocks):
        cols = pl.ds(block * BLK, BLK)
        att[cols, :] = ot[:, cols].T.astype(BF16)


def attn_bwd_kernel(piece, pieces, heads, head_size, shares, idx, *refs):
    held = piece + 1
    last = held == pieces
    go_parts, refs = refs[:shares], refs[shares:]
    qh, ot, lse = refs[:3]
    refs = refs[3:]
    ks, refs = refs[:held], refs[held:]
    vs, refs = refs[:held], refs[held:]
    bias, far, seg = refs[:3]
    refs = refs[3:]
    if piece:
        gk_in, refs = refs[:piece], refs[piece:]
        gv_in, refs = refs[:piece], refs[piece:]
        gq_in, refs = refs[:piece], refs[piece:]
        acc_in, refs = refs[0], refs[1:]
    if last:
        w, hot = refs[:2]
        refs = refs[2:]
        gn_parts, refs = refs[:shares], refs[shares:]
        gproj, rel_out = refs[:2]
        refs = refs[2:]
        gk, refs = refs[:held], refs[held:]
        gv, refs = refs[:held], refs[held:]
        gq_t, acc = refs[:2]
        refs = refs[2:]
    else:
        gk, refs = refs[:held], refs[held:]
        gv, refs = refs[:held], refs[held:]
        gq_t, acc = refs[:2]
        refs = refs[2:]
    go, kt, d_row, near_sum, far_sum = refs
    rows_total, features = ks[0].shape
    blocks = rows_total // BLK
    share = rows_total // shares
    me = idx[0]
    for step in range(shares):
        start = pl.multiple_of((me ^ step) * share, share)
        go[pl.ds(start, share), :] = go_parts[step][...]
    for index in range(held):
        for block in range(blocks):
            cols = pl.ds(block * BLK, BLK)
            kt[:, pl.ds((index * blocks + block) * BLK, BLK)] = (
                ks[index][cols, :].astype(F32).T.astype(BF16)
            )
        if index < piece:
            gk[index][...] = gk_in[index][...]
            gv[index][...] = gv_in[index][...]
        else:
            gk[index][...] = jnp.zeros_like(gk[index])
            gv[index][...] = jnp.zeros_like(gv[index])
    if piece:
        acc[...] = acc_in[...]
    else:
        acc[...] = jnp.zeros_like(acc)
    for block in range(blocks):
        cols = pl.ds(block * BLK, BLK)
        product = go[cols, :].astype(F32).T * ot[:, cols]
        for head in range(heads):
            part = product[head * head_size : (head + 1) * head_size, :]
            d_row[head : head + 1, cols] = jnp.sum(part, axis=0, keepdims=True)
    near_sum[...] = jnp.zeros_like(near_sum)
    far_sum[...] = jnp.zeros_like(far_sum)
    key_at = lax.broadcasted_iota(jnp.int32, (BLK, BLK), 0)
    other_at = lax.broadcasted_iota(jnp.int32, (BLK, BLK), 1)
    flip = (key_at + other_at == BLK - 1).astype(F32)
    seg_row = seg[...].astype(F32)
    seg_col = column_of(seg[...])

    def one_head(head, carry):
        part = pl.ds(pl.multiple_of(head * head_size, head_size), head_size)
        lanes = lax.broadcasted_iota(jnp.int32, (BLK, features), 1)
        inside = (lanes >= head * head_size) & (lanes < (head + 1) * head_size)
        for block in range(blocks):
            qb = piece * blocks + block
            cols = pl.ds(block * BLK, BLK)
            q_tile = qh[head, cols, :]
            go_tile = jnp.where(inside, go[cols, :].astype(F32), 0.0).astype(BF16)
            log_total = lse[pl.ds(head, 1), cols]
            d_tile = d_row[pl.ds(head, 1), cols]
            gq = jnp.zeros((head_size, BLK), F32)
            for kb in range(qb + 1):
                index = kb // blocks
                keys = pl.ds(kb % blocks * BLK, BLK)
                delta = qb - kb
                scores = masked_scores(
                    ks[index][keys, :], q_tile, tile_bias(bias, far, head, delta),
                    seg_col[kb * BLK : (kb + 1) * BLK, :],
                    seg_row[:, qb * BLK : (qb + 1) * BLK], delta == 0,
                )
                probs = jnp.exp(scores - log_total)
                gs = probs * (dot(vs[index][keys, :], go_tile, NT) - d_tile)
                if delta < 2:
                    acc[2 * head + delta] += gs
                else:
                    far_sum[pl.ds(head, 1), :] += jnp.sum(gs, axis=0, keepdims=True)
                gs_low = gs.astype(BF16)
                gv[index][keys, :] += dot(probs.astype(BF16), go_tile)
                gk[index][keys, :] += dot(gs_low, q_tile)
                gq = gq + dot(kt[part, kb * BLK : (kb + 1) * BLK], gs_low)
            gq_t[part, cols] = gq * (head_size**-0.5)
        return carry

    lax.fori_loop(0, heads, one_head, 0)
    if not last:
        return
    gqs = [*(gq_in if piece else ()), gq_t]
    for index in range(held):
        for block in range(blocks):
            rows = pl.ds(block * BLK, BLK)
            out = pl.ds((index * blocks + block) * BLK, BLK)
            gproj[0, out, :] = gqs[index][:, rows].T.astype(BF16)
            gproj[1, out, :] = gk[index][rows, :].astype(BF16)
            gproj[2, out, :] = gv[index][rows, :].astype(BF16)
    for step in range(shares):
        for index in range(pieces):
            start = index * rows_total + (me ^ step) * share
            rows = pl.ds(pl.multiple_of(start, share), share)
            total = dot(gproj[0, rows, :], w[0])
            total = total + dot(gproj[1, rows, :], w[1])
            total = total + dot(gproj[2, rows, :], w[2])
            gn_parts[step][pl.ds(index * share, share), :] = total.astype(BF16)
    for head in range(heads):
        for delta in range(2):
            turned = dot(flip, acc[2 * head + delta], NN, HIGHEST)
            wide = jnp.concatenate([turned, jnp.zeros_like(turned)], axis=1)
            sheared = pltpu.roll(wide, 0, 1, stride=1, stride_axis=0)
            near_sum[delta, head : head + 1, :] = jnp.sum(sheared, axis=0, keepdims=True)
    summed = dot(near_sum[0], hot[0], NN, HIGHEST) + dot(near_sum[1], hot[1], NN, HIGHEST)
    buckets = lax.broadcasted_iota(jnp.int32, summed.shape, 1)
    beyond = jnp.sum(far_sum[...], axis=1, keepdims=True)
    rel_out[...] = summed + jnp.where(buckets == NB - 1, beyond, 0.0)


def qkv_weights_kernel(pieces, *refs):
    normed = refs[:pieces]
    gproj, out = refs[pieces:]
    rows_total = normed[0].shape[0]
    for c in range(3):
        total = dot(gproj[c, pl.ds(0, rows_total), :], normed[0][...], TN)
        for index in range(1, pieces):
            rows = pl.ds(index * rows_total, rows_total)
            total = total + dot(gproj[c, rows, :], normed[index][...], TN)
        out[c] = total.astype(BF16)


def gelu_pair(values):
    squared = values * values
    bent = jnp.tanh(values * (0.7978845608028654 + 0.7978845608028654 * 0.044715 * squared))
    half = 0.5 * (1.0 + bent)
    lifted = values * half
    slope = 0.7978845608028654 + 3.0 * 0.7978845608028654 * 0.044715 * squared
    return lifted, half + lifted * (1.0 - bent) * slope


def padded_rows(values, rows):
    missing = jnp.zeros((rows - values.shape[0], values.shape[1]), values.dtype)
    return jnp.concatenate([values, missing], axis=0)


def block_start(index, size):
    return pl.multiple_of(index * size, size)


def moe_fwd_kernel(shares, experts, idx, *refs):
    att, refs = refs[:shares], refs[shares:]
    wo, tok, gain, router, routes, cot, w_in, w_down, parts = refs[:9]
    normed, own, gates, ggate, act, slope, acc = refs[9:]
    rows_total, features = att[0].shape
    share = rows_total // shares
    me = idx[0]
    expert = pl.program_id(0)

    @pl.when(expert == 0)
    def _():
        gain_row = gain[...].astype(F32)
        router_wide = padded_rows(router[...].astype(F32), LANES).astype(BF16)
        for block in range(rows_total // BLK):
            rows = pl.ds(block * BLK, BLK)
            attn = dot(att[0][rows, :], wo[pl.ds(block_start(me, features), features), :])
            for step in range(1, shares):
                held = wo[pl.ds(block_start(me ^ step, features), features), :]
                attn = attn + dot(att[step][rows, :], held)
            hidden = tok[rows, :].astype(F32) + attn
            acc[rows, :] = hidden
            n = (hidden * row_scale(hidden) * gain_row).astype(BF16)
            normed[rows, :] = n
            logits = dot(n, router_wide, NT)
            lanes = lax.broadcasted_iota(jnp.int32, logits.shape, 1)
            first = lanes == routes[rows, 0:1]
            second = lanes == routes[rows, 1:2]
            one = jnp.sum(jnp.where(first, logits, 0.0), axis=1, keepdims=True)
            two = jnp.sum(jnp.where(second, logits, 0.0), axis=1, keepdims=True)
            peak = jnp.maximum(one, two)
            one = jnp.exp(one - peak)
            two = jnp.exp(two - peak)
            both = one + two
            gates[rows, :] = jnp.where(first, one / both, jnp.where(second, two / both, 0.0))
        own[...] = acc[pl.ds(pl.multiple_of(me * share, share), share), :]
        acc[...] = jnp.zeros_like(acc)
        ggate[...] = jnp.zeros_like(ggate)

    for block in range(rows_total // ROWS):
        rows = pl.ds(block * ROWS, ROWS)
        lifted, bend = gelu_pair(dot(normed[rows, :], w_in[0]))
        lifted = lifted.astype(BF16)
        act[0, rows, :] = lifted
        slope[0, rows, :] = bend.astype(BF16)
        out = dot(lifted, w_down[0])
        gate = lane_pick(gates[rows, :], expert)
        acc[rows, :] += gate * out
        pulled = jnp.sum(cot[rows, :].astype(F32) * out, axis=1, keepdims=True)
        held = ggate[rows, :]
        lanes = lax.broadcasted_iota(jnp.int32, held.shape, 1)
        ggate[rows, :] = jnp.where(lanes == expert, pulled, held)

    @pl.when(expert == experts - 1)
    def _():
        parts[...] = acc[...].astype(BF16)


def moe_bwd_kernel(shares, experts, idx, *refs):
    gates, ggate, cot, slope, router, w_in, w_down = refs[:7]
    refs = refs[7:]
    parts, refs = refs[:shares], refs[shares:]
    glog, gpre, acc = refs
    rows_total = gates.shape[0]
    share = rows_total // shares
    me = idx[0]
    expert = pl.program_id(0)

    @pl.when(expert == 0)
    def _():
        router_wide = padded_rows(router[...].astype(F32), LANES)
        for block in range(rows_total // ROWS):
            rows = pl.ds(block * ROWS, ROWS)
            g, gg = gates[rows, :], ggate[rows, :]
            back = g * (gg - jnp.sum(g * gg, axis=1, keepdims=True))
            glog[rows, :] = back
            acc[rows, :] = dot(back, router_wide, NN, HIGHEST)

    for block in range(rows_total // ROWS):
        rows = pl.ds(block * ROWS, ROWS)
        gate = lane_pick(gates[rows, :], expert)
        weighted = (gate * cot[rows, :].astype(F32)).astype(BF16)
        gp = (dot(weighted, w_down[0], NT) * slope[0, rows, :].astype(F32)).astype(BF16)
        gpre[0, rows, :] = gp
        acc[rows, :] += dot(gp, w_in[0], NT)

    @pl.when(expert == experts - 1)
    def _():
        for step in range(shares):
            start = pl.multiple_of((me ^ step) * share, share)
            parts[step][...] = acc[pl.ds(start, share), :].astype(BF16)


def moe_weights_kernel(pieces, cot, *refs):
    gates, refs = refs[:pieces], refs[pieces:]
    glog, refs = refs[:pieces], refs[pieces:]
    normed, refs = refs[:pieces], refs[pieces:]
    act, refs = refs[:pieces], refs[pieces:]
    gpre, refs = refs[:pieces], refs[pieces:]
    out, router = refs
    rows_total = normed[0].shape[0]
    expert = pl.program_id(0)

    @pl.when(expert == 0)
    def _():
        total = jnp.zeros((LANES, cot.shape[1]), F32)
        for index in range(pieces):
            back = glog[index][...]
            high = back.astype(BF16)
            low = (back - high.astype(F32)).astype(BF16)
            total = total + dot(high, normed[index][...], TN)
            total = total + dot(low, normed[index][...], TN)
        router[...] = total[0:8, :]

    grad_in = jnp.zeros((normed[0].shape[1], gpre[0].shape[2]), F32)
    grad_down = jnp.zeros((act[0].shape[2], cot.shape[1]), F32)
    for index in range(pieces):
        gate = lane_pick(gates[index][...], expert)
        weighted = cot[pl.ds(index * rows_total, rows_total), :].astype(F32)
        weighted = (gate * weighted).astype(BF16)
        grad_in = grad_in + dot(normed[index][...], gpre[index][0], TN)
        grad_down = grad_down + dot(act[index][0], weighted, TN)
    out[0, 0] = grad_in.astype(BF16)
    out[0, 1] = grad_down.astype(BF16)


def hidden_back_kernel(piece, pieces, shares, got, idx, *refs):
    gx, refs = refs[:got], refs[got:]
    wo, own, cot, gain = refs[:4]
    refs = refs[4:]
    ga, refs = refs[:shares], refs[shares:]
    gh, gh_low, ggain = refs
    share = own.shape[0]
    grad = gx[0][...].astype(F32)
    for step in range(1, got):
        grad = grad + gx[step][...].astype(F32)
    hidden = own[...]
    scale = row_scale(hidden)
    unit = hidden * scale
    ggain[...] = jnp.sum(grad * unit, axis=0, keepdims=True)
    gained = grad * gain[...].astype(F32)
    start = piece * (cot.shape[0] // pieces) + idx[0] * share
    mine = cot[pl.ds(pl.multiple_of(start, share), share), :].astype(F32)
    back = mine + scale * (gained - unit * jnp.mean(gained * unit, axis=-1, keepdims=True))
    gh[...] = back
    low = back.astype(BF16)
    gh_low[...] = low
    for step in range(shares):
        features = ga[step].shape[1]
        held = wo[pl.ds(block_start(idx[0] ^ step, features), features), :]
        ga[step][...] = dot(low, held, NT).astype(BF16)


def w_out_back_kernel(pieces, shares, idx, *refs):
    att, refs = refs[: pieces * shares], refs[pieces * shares :]
    gh_low, out = refs[:pieces], refs[pieces]
    share = gh_low[0].shape[0]
    rows = pl.ds(pl.multiple_of(idx[0] * share, share), share)
    for step in range(shares):
        total = dot(att[step][rows, :], gh_low[0][...], TN)
        for index in range(1, pieces):
            total = total + dot(att[index * shares + step][rows, :], gh_low[index][...], TN)
        out[step] = total.astype(BF16)


def join_kernel(pieces, count, *refs):
    own, refs = refs[:pieces], refs[pieces:]
    got, out = refs[: pieces * count], refs[pieces * count]
    share = own[0].shape[0]
    for index in range(pieces):
        total = own[index][...]
        for step in range(count):
            total = total + got[index * count + step][...].astype(F32)
        out[pl.ds(index * share, share), :] = total.astype(BF16)


def input_back_kernel(pieces, got, idx, *refs):
    gn, refs = refs[:got], refs[got:]
    ghs, refs = refs[:pieces], refs[pieces:]
    tok, gain, gt, ggain = refs
    share = ghs[0].shape[0]
    gain_row = gain[...].astype(F32)
    total = jnp.zeros_like(ggain)
    for index in range(pieces):
        rows = pl.ds(index * share, share)
        grad = gn[0][rows, :].astype(F32)
        for step in range(1, got):
            grad = grad + gn[step][rows, :].astype(F32)
        start = index * (tok.shape[0] // pieces) + idx[0] * share
        x = tok[pl.ds(pl.multiple_of(start, share), share), :].astype(F32)
        scale = row_scale(x)
        unit = x * scale
        total = total + jnp.sum(grad * unit, axis=0, keepdims=True)
        gained = grad * gain_row
        back = scale * (gained - unit * jnp.mean(gained * unit, axis=-1, keepdims=True))
        gt[rows, :] = (ghs[index][...] + back).astype(BF16)
    ggain[...] = total


def place_kernel(pieces, shares, idx, *refs):
    blocks, out = refs[:shares], refs[shares]
    rows_total = out.shape[0] // pieces
    share = rows_total // shares
    for step in range(shares):
        owner = idx[0] ^ step
        for index in range(pieces):
            start = pl.multiple_of(index * rows_total + owner * share, share)
            got = blocks[step][pl.ds(index * share, share), :]
            out[pl.ds(start, share), :] = got.astype(out.dtype)


ROWS = 512
PIECES = 2

SMEM = pl.BlockSpec(memory_space=pltpu.SMEM)
VMEM = pl.BlockSpec(memory_space=pltpu.VMEM)


def shaped(shape, dtype):
    return jax.ShapeDtypeStruct(shape, dtype)


def whole_call(kernel, outs, args, scratch=(), flops=0, moved=0, with_index=True):
    specs = ([SMEM] if with_index else []) + [VMEM] * (len(args) - (1 if with_index else 0))
    return pl.pallas_call(
        kernel,
        out_shape=outs,
        in_specs=specs,
        out_specs=[VMEM] * len(outs),
        scratch_shapes=list(scratch),
        compiler_params=pltpu.CompilerParams(vmem_limit_bytes=VMEM_LIMIT),
        cost_estimate=pl.CostEstimate(flops=flops, bytes_accessed=moved, transcendentals=0),
    )(*args)


def swap(value, axis, bit):
    count = lax.axis_size(axis)
    return lax.ppermute(value, axis, [(i, i ^ bit) for i in range(count)])


def sum_over(value, axis):
    bit = 1
    while bit < lax.axis_size(axis):
        value = value + swap(value, axis, bit)
        bit *= 2
    return value


def exchange(parts, axis):
    return [parts[0]] + [swap(parts[bit], axis, bit) for bit in range(1, len(parts))]


def gather_parts(value, axis):
    count = lax.axis_size(axis)
    if count != 4:
        return [value] + [swap(value, axis, bit) for bit in range(1, count)]
    two = swap(value, axis, 2)
    one = swap(value, axis, 1)
    return [value, one, two, swap(two, axis, 1)]


def reduce_parts(parts, axis):
    count = lax.axis_size(axis)
    if count != 4:
        return [parts[0]] + [swap(parts[bit], axis, bit) for bit in range(1, count)]
    near = swap(parts[3], axis, 1)
    pair = (parts[2].astype(F32) + near.astype(F32)).astype(parts[2].dtype)
    return [parts[0], swap(parts[1], axis, 1), swap(pair, axis, 2)]


def halves_of(value, axis, chosen):
    half = value.shape[axis] // 2
    keep = lax.dynamic_slice_in_dim(value, chosen * half, half, axis)
    send = lax.dynamic_slice_in_dim(value, (1 - chosen) * half, half, axis)
    return keep, send


def bits_of(axis):
    count = lax.axis_size(axis)
    return [1 << level for level in range(count.bit_length() - 1)]


def scatter_sum(value, mesh_axis, axis):
    me = lax.axis_index(mesh_axis)
    for bit in bits_of(mesh_axis):
        keep, send = halves_of(value, axis, (me // bit) % 2)
        got = swap(send, mesh_axis, bit)
        value = (keep.astype(F32) + got.astype(F32)).astype(value.dtype)
    return value


def gather_back(value, mesh_axis, axis):
    me = lax.axis_index(mesh_axis)
    for bit in reversed(bits_of(mesh_axis)):
        got = swap(value, mesh_axis, bit)
        low = (me // bit) % 2 == 0
        value = jnp.concatenate(
            [jnp.where(low, value, got), jnp.where(low, got, value)], axis=axis
        )
    return value


def after(value, *others):
    return lax.optimization_barrier((value, *others))[0]


def body(
    tokens, segments, routes, grad_out, gain_attn, w_qkv, w_out, rel_bias,
    gain_moe, w_router, w_in, w_down,
):
    tok_rows, width = tokens.shape
    heads = rel_bias.shape[1]
    features = w_qkv.shape[2]
    head_size = features // heads
    experts, _, hidden_units = w_in.shape
    shares = lax.axis_size("tensor")
    rows = tok_rows // PIECES
    share = rows // shares
    me = lax.axis_index("tensor").astype(jnp.int32)
    idx = me.reshape(1)
    mib = 1 << 20
    others = range(1, shares)

    wo = lax.all_gather(w_out, "tensor", axis=0, tiled=True)
    build_hot, gather_hot = near_tables()
    build_hot = jnp.asarray(np.swapaxes(build_hot, 1, 2), BF16)
    gather_hot = jnp.asarray(gather_hot, F32)
    w_qkv_t = jnp.swapaxes(w_qkv, 1, 2)
    router_t = w_router.T
    gain_one = gain_attn.reshape(1, width)
    gain_two = gain_moe.reshape(1, width)

    def attend(piece, bias_args, old_k, old_vt):
        outs = [
            shaped((rows, width), BF16),
            shaped((heads, rows, features), BF16),
            shaped((rows, features), BF16),
            shaped((rows, features), BF16),
            shaped((features, rows), BF16),
            shaped((rows, features), BF16),
            shaped((features, rows), F32),
            shaped((8, rows), F32),
        ]
        if piece == 0:
            outs += [shaped((2 * heads, BLK, BLK), F32), shaped((8, LANES), F32)]
        return whole_call(
            functools.partial(attn_fwd_kernel, piece, PIECES, heads, head_size),
            outs,
            [tokens, gain_one, w_qkv_t, segments, *bias_args, *old_k, *old_vt],
            flops=3 * 10**9, moved=8 * mib, with_index=False,
        )

    stages = []
    bias_args = [rel_bias.T, build_hot]
    for piece in range(PIECES):
        got = attend(piece, bias_args, [s[2] for s in stages], [s[4] for s in stages])
        if piece == 0:
            bias_args = got[8:]
        stages.append(got[:8])
    bias, far = bias_args
    normed_one = [s[0] for s in stages]

    atts = []
    for stage in stages:
        mine = after(stage[5], *atts[-1][1:]) if atts else stage[5]
        atts.append(exchange([mine] * shares, "tensor"))

    full = lambda shape: pl.BlockSpec(shape, lambda e: (0,) * len(shape))
    per_expert = lambda shape: pl.BlockSpec((1,) + shape, lambda e: (e, 0, 0))
    params = pltpu.CompilerParams(
        vmem_limit_bytes=VMEM_LIMIT, dimension_semantics=("arbitrary",)
    )
    moe_flops = 4 * experts * rows * width * hidden_units

    per_piece = lambda piece, lanes: pl.BlockSpec((rows, lanes), lambda e: (piece, 0))

    def moe_forward(piece):
        return pl.pallas_call(
            functools.partial(moe_fwd_kernel, shares, experts),
            grid=(experts,),
            in_specs=[SMEM]
            + [full((rows, features))] * shares
            + [
                full((width, width)), per_piece(piece, width), full((1, width)),
                full((experts, width)), per_piece(piece, 2), per_piece(piece, width),
                per_expert((width, hidden_units)), per_expert((hidden_units, width)),
            ],
            out_specs=[
                full((rows, width)),
                full((rows, width)), full((share, width)), full((rows, LANES)),
                full((rows, LANES)), per_expert((rows, hidden_units)),
                per_expert((rows, hidden_units)),
            ],
            out_shape=[
                shaped((rows, width), BF16),
                shaped((rows, width), BF16),
                shaped((share, width), F32),
                shaped((rows, LANES), F32),
                shaped((rows, LANES), F32),
                shaped((experts, rows, hidden_units), BF16),
                shaped((experts, rows, hidden_units), BF16),
            ],
            scratch_shapes=[pltpu.VMEM((rows, width), F32)],
            compiler_params=params,
            cost_estimate=pl.CostEstimate(
                flops=moe_flops, bytes_accessed=20 * mib, transcendentals=0
            ),
        )(
            idx, *atts[piece], wo, tokens, gain_two, router_t, routes, grad_out, w_in, w_down
        )

    def moe_backward(piece, gates, ggate, slope):
        return pl.pallas_call(
            functools.partial(moe_bwd_kernel, shares, experts),
            grid=(experts,),
            in_specs=[
                SMEM, full((rows, LANES)), full((rows, LANES)), per_piece(piece, width),
                per_expert((rows, hidden_units)), full((experts, width)),
                per_expert((width, hidden_units)), per_expert((hidden_units, width)),
            ],
            out_specs=[full((share, width))] * shares
            + [full((rows, LANES)), per_expert((rows, hidden_units))],
            out_shape=[shaped((share, width), BF16)] * shares
            + [
                shaped((rows, LANES), F32),
                shaped((experts, rows, hidden_units), BF16),
            ],
            scratch_shapes=[pltpu.VMEM((rows, width), F32)],
            compiler_params=params,
            cost_estimate=pl.CostEstimate(
                flops=moe_flops, bytes_accessed=16 * mib, transcendentals=0
            ),
        )(idx, gates, ggate, grad_out, slope, router_t, w_in, w_down)

    moe_got, gx_got, forwards, backwards = [], [], [], []
    for piece in range(PIECES):
        fwd = moe_forward(piece)
        moe_sum, kept = fwd[0], fwd[1:]
        moe_got.append(
            [lax.psum_scatter(moe_sum, "tensor", scatter_dimension=0, tiled=True)]
        )
        gates, ggate, slope = kept[2], kept[3], kept[5]
        bwd = moe_backward(piece, gates, ggate, slope)
        parts = bwd[:shares]
        gx_got.append(exchange(parts, "tensor"))
        forwards.append(kept)
        backwards.append(bwd[shares:])
    normed_two = [f[0] for f in forwards]
    own_hidden = [f[1] for f in forwards]
    all_gates = [f[2] for f in forwards]
    acts = [f[4] for f in forwards]
    glogs = [b[0] for b in backwards]
    gpres = [b[1] for b in backwards]

    def hidden_back(piece, own):
        got = whole_call(
            functools.partial(hidden_back_kernel, piece, PIECES, shares, len(gx_got[piece])),
            [shaped((share, features), BF16)] * shares
            + [
                shaped((share, width), F32), shaped((share, width), BF16),
                shaped((1, width), F32),
            ],
            [idx, *gx_got[piece], wo, own, grad_out, gain_two],
            flops=2 * 10**8, moved=5 * mib,
        )
        parts = got[:shares]
        go = exchange(parts, "tensor")
        return go, got[shares:]

    def attend_back(piece, go, carried):
        held = piece + 1
        last = held == PIECES
        outs, scratch = [], []
        if last:
            outs += [shaped((PIECES * share, width), BF16)] * shares
            outs += [shaped((3, tok_rows, features), BF16), shaped((8, NB), F32)]
        sums = [((rows, features), F32)] * (2 * held)
        sums += [((features, rows), F32), ((2 * heads, BLK, BLK), F32)]
        if last:
            scratch += [pltpu.VMEM(*one) for one in sums]
        else:
            outs += [shaped(*one) for one in sums]
        scratch += [
            pltpu.VMEM((rows, features), BF16),
            pltpu.VMEM((features, tok_rows), BF16),
            pltpu.VMEM((8, rows), F32),
            pltpu.VMEM((2, 8, 2 * BLK), F32),
            pltpu.VMEM((8, BLK), F32),
        ]
        return whole_call(
            functools.partial(attn_bwd_kernel, piece, PIECES, heads, head_size, shares),
            outs,
            [
                idx, *go, stages[piece][1], stages[piece][6], stages[piece][7],
                *[s[2] for s in stages[:held]], *[s[3] for s in stages[:held]],
                bias, far, segments, *carried, *([w_qkv_t, gather_hot] if last else []),
            ],
            scratch,
            flops=7 * 10**9, moved=8 * mib,
        )

    go, back_first = hidden_back(0, own_hidden[0])
    expert_grads, router_rows = pl.pallas_call(
        functools.partial(moe_weights_kernel, PIECES),
        grid=(experts,),
        in_specs=[full((tok_rows, width))]
        + [full((rows, LANES))] * (2 * PIECES)
        + [full((rows, width))] * PIECES
        + [per_expert((rows, hidden_units))] * (2 * PIECES),
        out_specs=[
            pl.BlockSpec((1, 2, width, width), lambda e: (e, 0, 0, 0)), full((8, width))
        ],
        out_shape=[shaped((experts, 2, width, width), BF16), shaped((8, width), F32)],
        compiler_params=params,
        cost_estimate=pl.CostEstimate(
            flops=2 * moe_flops, bytes_accessed=26 * mib, transcendentals=0
        ),
    )(after(grad_out, back_first[1]), *all_gates, *glogs, *normed_two, *acts, *gpres)
    expert_rows = lax.psum_scatter(
        expert_grads.reshape(experts * 2 * width, width), "dp", scatter_dimension=0, tiled=True
    )

    go_second, back_second = hidden_back(1, after(own_hidden[1], router_rows))
    result_share = whole_call(
        functools.partial(join_kernel, PIECES, len(moe_got[0])),
        [shaped((PIECES * share, width), BF16)],
        [*own_hidden, *moe_got[0], *moe_got[1]],
        moved=4 * mib, with_index=False,
    )[0]
    go = [after(go[0], back_second[1]), *go[1:]]
    first = attend_back(0, go, [])
    go_second = [after(go_second[0], first[0], result_share), *go_second[1:]]
    second = attend_back(1, go_second, first)
    grad_hidden = [back_first[0], back_second[0]]
    ggain_two = back_first[2] + back_second[2]
    gn_parts = second[:shares]
    gproj, grad_rel = second[shares:]
    gn_got = reduce_parts(gn_parts, "tensor")

    result_got = gather_parts(result_share, "tensor")
    result = whole_call(
        functools.partial(place_kernel, PIECES, shares),
        [shaped((tok_rows, width), BF16)], [idx, *result_got], moved=3 * mib,
    )[0]
    w_out_rows = whole_call(
        functools.partial(w_out_back_kernel, PIECES, shares),
        [shaped((shares, features, width), BF16)],
        [idx, *atts[0], *atts[1], back_first[1], after(back_second[1], gproj)],
        flops=3 * 10**8, moved=4 * mib,
    )[0]
    qkv_rows = whole_call(
        functools.partial(qkv_weights_kernel, PIECES),
        [shaped((3, features, width), BF16)],
        [*normed_one, gproj],
        flops=10**9, moved=4 * mib, with_index=False,
    )[0]

    gt_share, ggain_one = whole_call(
        functools.partial(input_back_kernel, PIECES, len(gn_got)),
        [shaped((PIECES * share, width), BF16), shaped((1, width), F32)],
        [idx, *gn_got, *grad_hidden, tokens, gain_one],
        moved=5 * mib,
    )
    gt_got = gather_parts(gt_share, "tensor")
    grad_tokens = whole_call(
        functools.partial(place_kernel, PIECES, shares),
        [shaped((tok_rows, width), F32)], [idx, *gt_got], moved=5 * mib,
    )[0]

    late = after(jnp.concatenate([qkv_rows, w_out_rows], axis=0), gt_got[2])
    late = scatter_sum(late, "dp", 1)
    out_sum = late[3].astype(F32)
    for by in others:
        out_sum = out_sum + swap(late[3 + by], "tensor", by).astype(F32)
    late = jnp.concatenate([late[:3], out_sum.astype(BF16)[None]], axis=0)
    late = gather_back(late, "dp", 1)
    expert_rows = lax.all_gather(after(expert_rows, gt_got[2]), "dp", axis=0, tiled=True)
    expert_rows = expert_rows.reshape(experts, 2, width, width)
    grad_w_in = expert_rows[:, 0].astype(F32)
    grad_w_down = expert_rows[:, 1].astype(F32)
    grad_w_qkv = jnp.swapaxes(late[:3], 1, 2).astype(F32)
    grad_w_out = late[3].astype(F32)

    rel_rows = jnp.pad(grad_rel, ((0, 0), (0, width - NB)))
    small = jnp.concatenate([rel_rows, router_rows, ggain_one, ggain_two], axis=0)
    small = sum_over(small, "dp")
    grad_rel_bias = small[:heads, :NB].T
    shared = sum_over(small[8:], "tensor")
    return (
        result,
        grad_tokens,
        shared[8],
        grad_w_qkv,
        grad_w_out,
        grad_rel_bias,
        shared[9],
        shared[:experts].T,
        grad_w_in,
        grad_w_down,
    )


def solution(mesh):
    placed = (
        P("dp", None),
        P("dp", None),
        P("dp", None),
        P("dp", None),
        P(),
        P(None, None, "tensor"),
        P("tensor", None),
        P(None, "tensor"),
        P(),
        P(),
        P(None, None, "tensor"),
        P(None, "tensor", None),
    )
    return jax.shard_map(
        body,
        mesh=mesh,
        in_specs=placed,
        out_specs=(
            P("dp", None),
            P("dp", None),
            P(),
            P(None, None, "tensor"),
            P("tensor", None),
            P(None, "tensor"),
            P(),
            P(),
            P(None, None, "tensor"),
            P(None, "tensor", None),
        ),
        check_vma=False,
    )
```

```python
import functools
import math

import jax
import jax.numpy as jnp
import numpy as np
from jax import lax
from jax.experimental import pallas as pl
from jax.experimental.pallas import tpu as pltpu
from jax.sharding import PartitionSpec as P

NB = 32
DIST = 128
EPSILON = 1e-06
NEGATIVE = -1e30
HIGHEST = lax.Precision.HIGHEST
F32 = jnp.float32
BF16 = jnp.bfloat16
BLK = 256
LANES = 128
VMEM_LIMIT = 56 * 1024 * 1024

NN = (((1,), (0,)), ((), ()))
NT = (((1,), (1,)), ((), ()))
TN = (((0,), (0,)), ((), ()))


def dot(a, b, dims=NN, precision=None):
    return lax.dot_general(a, b, dims, precision=precision, preferred_element_type=F32)


def bucket_of(distance):
    halfway = NB // 2
    thresholds = [
        int(math.ceil(halfway * (DIST / halfway) ** (step / halfway))) for step in range(halfway)
    ]
    beyond = sum((distance >= threshold).astype(np.int64) for threshold in thresholds)
    return np.where(distance < halfway, distance, halfway - 1 + beyond)


def near_tables():
    lanes = np.arange(2 * BLK)
    offset = np.where(lanes < BLK, lanes, lanes - 2 * BLK)
    build = np.stack([np.maximum(offset, 0), np.maximum(BLK + offset, 0)])
    gather = np.stack([lanes - (BLK - 1), lanes + 1])
    eye = np.eye(NB, dtype=np.float32)
    build_hot = eye[bucket_of(build)]
    gather_hot = eye[bucket_of(np.maximum(gather, 0))] * (gather >= 0)[..., None]
    return build_hot, gather_hot


def row_scale(values):
    return lax.rsqrt(jnp.mean(values * values, axis=-1, keepdims=True) + EPSILON)


def lane_pick(values, index):
    lanes = lax.broadcasted_iota(jnp.int32, values.shape, 1)
    return jnp.sum(jnp.where(lanes == index, values, 0.0), axis=1, keepdims=True)


def masked_scores(k_tile, qh_tile, bias, seg_k, seg_q, diagonal):
    scores = dot(k_tile, qh_tile, NT) + bias
    allowed = seg_k == seg_q
    if diagonal:
        key_at = lax.broadcasted_iota(jnp.int32, scores.shape, 0)
        query_at = lax.broadcasted_iota(jnp.int32, scores.shape, 1)
        allowed = allowed & (key_at <= query_at)
    return jnp.where(allowed, scores, NEGATIVE)


def tile_bias(bias_ref, far_ref, head, delta):
    if delta < 2:
        return bias_ref[2 * head + delta]
    return far_ref[pl.ds(head, 1), 0:1]


def column_of(row):
    spread = jnp.broadcast_to(row.astype(F32), (8, row.shape[1]))
    return spread.T[:, 0:1]


def attn_fwd_kernel(piece, pieces, heads, head_size, *refs):
    tok, gain, w, seg = refs[:4]
    refs = refs[4:]
    if piece == 0:
        rel, build = refs[:2]
        refs = refs[2:]
    else:
        bias, far = refs[:2]
        refs = refs[2:]
    old_k, refs = refs[:piece], refs[piece:]
    old_vt, refs = refs[:piece], refs[piece:]
    normed, qh, k, v, vt, att, ot, lse = refs[:8]
    if piece == 0:
        bias, far = refs[8:]
    keys_of, vt_of = [*old_k, k], [*old_vt, vt]
    rows_total = tok.shape[0] // pieces
    base = piece * rows_total
    features = w.shape[1]
    blocks = rows_total // BLK
    gain_row = gain[...].astype(F32).reshape(1, -1)
    lanes = lax.broadcasted_iota(jnp.int32, (BLK, features), 1)
    for block in range(blocks):
        rows = pl.ds(block * BLK, BLK)
        x = tok[pl.ds(base + block * BLK, BLK), :].astype(F32)
        n = (x * row_scale(x) * gain_row).astype(BF16)
        normed[rows, :] = n
        q_rows = dot(n, w[0], NT).astype(BF16).astype(F32) * (head_size**-0.5)
        for head in range(heads):
            inside = (lanes >= head * head_size) & (lanes < (head + 1) * head_size)
            qh[head, rows, :] = jnp.where(inside, q_rows, 0.0).astype(BF16)
        k[rows, :] = dot(n, w[1], NT).astype(BF16)
        v_rows = dot(n, w[2], NT).astype(BF16)
        v[rows, :] = v_rows
        vt[:, rows] = v_rows.astype(F32).T.astype(BF16)
    if piece == 0:
        far[...] = jnp.zeros_like(far)
        far[0:heads, :] = jnp.broadcast_to(rel[:, NB - 1 : NB].astype(F32), (heads, LANES))
        for delta in range(2):
            near = dot(rel[...], build[delta])
            for head in range(heads):
                spread = jnp.broadcast_to(near[head : head + 1, :], (BLK, 2 * BLK))
                turned = pltpu.roll(spread, 0, 1, stride=1, stride_axis=0)
                bias[2 * head + delta] = turned[:, :BLK]
    lse[...] = jnp.zeros_like(lse)
    seg_row = seg[...].astype(F32)
    seg_col = column_of(seg[...])

    def one_head(head, carry):
        part = pl.ds(pl.multiple_of(head * head_size, head_size), head_size)
        for block in range(blocks):
            qb = piece * blocks + block
            cols = pl.ds(block * BLK, BLK)
            q_tile = qh[head, cols, :]
            tiles = []
            for kb in range(qb + 1):
                keys = pl.ds(kb % blocks * BLK, BLK)
                tiles.append(
                    masked_scores(
                        keys_of[kb // blocks][keys, :], q_tile,
                        tile_bias(bias, far, head, qb - kb),
                        seg_col[kb * BLK : (kb + 1) * BLK, :],
                        seg_row[:, qb * BLK : (qb + 1) * BLK], kb == qb,
                    )
                )
            peak = functools.reduce(
                jnp.maximum, [jnp.max(t, axis=0, keepdims=True) for t in tiles]
            )
            total = jnp.zeros((1, BLK), F32)
            out = jnp.zeros((head_size, BLK), F32)
            for kb in range(qb + 1):
                raised = jnp.exp(tiles[kb] - peak)
                total = total + jnp.sum(raised, axis=0, keepdims=True)
                values = vt_of[kb // blocks][part, pl.ds(kb % blocks * BLK, BLK)]
                out = out + dot(values, raised.astype(BF16))
            ot[part, cols] = out / total
            lse[pl.ds(head, 1), cols] = peak + jnp.log(total)
        return carry

    lax.fori_loop(0, heads, one_head, 0)
    for block in range(blocks):
        cols = pl.ds(block * BLK, BLK)
        att[cols, :] = ot[:, cols].T.astype(BF16)


def attn_bwd_kernel(piece, pieces, heads, head_size, shares, idx, *refs):
    held = piece + 1
    last = held == pieces
    go, qh, ot, lse = refs[:4]
    refs = refs[4:]
    ks, refs = refs[:held], refs[held:]
    vs, refs = refs[:held], refs[held:]
    bias, far, seg = refs[:3]
    refs = refs[3:]
    if piece:
        gk_in, refs = refs[:piece], refs[piece:]
        gv_in, refs = refs[:piece], refs[piece:]
        gq_in, refs = refs[:piece], refs[piece:]
        acc_in, refs = refs[0], refs[1:]
    if last:
        w, hot = refs[:2]
        refs = refs[2:]
        gn_parts, refs = refs[:shares], refs[shares:]
        gproj, rel_out = refs[:2]
        refs = refs[2:]
        gk, refs = refs[:held], refs[held:]
        gv, refs = refs[:held], refs[held:]
        gq_t, acc = refs[:2]
        refs = refs[2:]
    else:
        gk, refs = refs[:held], refs[held:]
        gv, refs = refs[:held], refs[held:]
        gq_t, acc = refs[:2]
        refs = refs[2:]
    kt, d_row, near_sum, far_sum = refs
    rows_total, features = ks[0].shape
    blocks = rows_total // BLK
    share = rows_total // shares
    me = idx[0]
    for index in range(held):
        for block in range(blocks):
            cols = pl.ds(block * BLK, BLK)
            kt[:, pl.ds((index * blocks + block) * BLK, BLK)] = (
                ks[index][cols, :].astype(F32).T.astype(BF16)
            )
        if index < piece:
            gk[index][...] = gk_in[index][...]
            gv[index][...] = gv_in[index][...]
        else:
            gk[index][...] = jnp.zeros_like(gk[index])
            gv[index][...] = jnp.zeros_like(gv[index])
    if piece:
        acc[...] = acc_in[...]
    else:
        acc[...] = jnp.zeros_like(acc)
    for block in range(blocks):
        cols = pl.ds(block * BLK, BLK)
        product = go[cols, :].astype(F32).T * ot[:, cols]
        for head in range(heads):
            part = product[head * head_size : (head + 1) * head_size, :]
            d_row[head : head + 1, cols] = jnp.sum(part, axis=0, keepdims=True)
    near_sum[...] = jnp.zeros_like(near_sum)
    far_sum[...] = jnp.zeros_like(far_sum)
    key_at = lax.broadcasted_iota(jnp.int32, (BLK, BLK), 0)
    other_at = lax.broadcasted_iota(jnp.int32, (BLK, BLK), 1)
    flip = (key_at + other_at == BLK - 1).astype(F32)
    seg_row = seg[...].astype(F32)
    seg_col = column_of(seg[...])

    def one_head(head, carry):
        part = pl.ds(pl.multiple_of(head * head_size, head_size), head_size)
        lanes = lax.broadcasted_iota(jnp.int32, (BLK, features), 1)
        inside = (lanes >= head * head_size) & (lanes < (head + 1) * head_size)
        for block in range(blocks):
            qb = piece * blocks + block
            cols = pl.ds(block * BLK, BLK)
            q_tile = qh[head, cols, :]
            go_tile = jnp.where(inside, go[cols, :].astype(F32), 0.0).astype(BF16)
            log_total = lse[pl.ds(head, 1), cols]
            d_tile = d_row[pl.ds(head, 1), cols]
            gq = jnp.zeros((head_size, BLK), F32)
            for kb in range(qb + 1):
                index = kb // blocks
                keys = pl.ds(kb % blocks * BLK, BLK)
                delta = qb - kb
                scores = masked_scores(
                    ks[index][keys, :], q_tile, tile_bias(bias, far, head, delta),
                    seg_col[kb * BLK : (kb + 1) * BLK, :],
                    seg_row[:, qb * BLK : (qb + 1) * BLK], delta == 0,
                )
                probs = jnp.exp(scores - log_total)
                gs = probs * (dot(vs[index][keys, :], go_tile, NT) - d_tile)
                if delta < 2:
                    acc[2 * head + delta] += gs
                else:
                    far_sum[pl.ds(head, 1), :] += jnp.sum(gs, axis=0, keepdims=True)
                gs_low = gs.astype(BF16)
                gv[index][keys, :] += dot(probs.astype(BF16), go_tile)
                gk[index][keys, :] += dot(gs_low, q_tile)
                gq = gq + dot(kt[part, kb * BLK : (kb + 1) * BLK], gs_low)
            gq_t[part, cols] = gq * (head_size**-0.5)
        return carry

    lax.fori_loop(0, heads, one_head, 0)
    if not last:
        return
    gqs = [*(gq_in if piece else ()), gq_t]
    for index in range(held):
        for block in range(blocks):
            rows = pl.ds(block * BLK, BLK)
            out = pl.ds((index * blocks + block) * BLK, BLK)
            gproj[0, out, :] = gqs[index][:, rows].T.astype(BF16)
            gproj[1, out, :] = gk[index][rows, :].astype(BF16)
            gproj[2, out, :] = gv[index][rows, :].astype(BF16)
    for step in range(shares):
        for index in range(pieces):
            start = index * rows_total + (me ^ step) * share
            rows = pl.ds(pl.multiple_of(start, share), share)
            total = dot(gproj[0, rows, :], w[0])
            total = total + dot(gproj[1, rows, :], w[1])
            total = total + dot(gproj[2, rows, :], w[2])
            gn_parts[step][pl.ds(index * share, share), :] = total.astype(BF16)
    for head in range(heads):
        for delta in range(2):
            turned = dot(flip, acc[2 * head + delta], NN, HIGHEST)
            wide = jnp.concatenate([turned, jnp.zeros_like(turned)], axis=1)
            sheared = pltpu.roll(wide, 0, 1, stride=1, stride_axis=0)
            near_sum[delta, head : head + 1, :] = jnp.sum(sheared, axis=0, keepdims=True)
    summed = dot(near_sum[0], hot[0], NN, HIGHEST) + dot(near_sum[1], hot[1], NN, HIGHEST)
    buckets = lax.broadcasted_iota(jnp.int32, summed.shape, 1)
    beyond = jnp.sum(far_sum[...], axis=1, keepdims=True)
    rel_out[...] = summed + jnp.where(buckets == NB - 1, beyond, 0.0)


def qkv_weights_kernel(pieces, *refs):
    normed = refs[:pieces]
    gproj, out = refs[pieces:]
    rows_total = normed[0].shape[0]
    for c in range(3):
        total = dot(gproj[c, pl.ds(0, rows_total), :], normed[0][...], TN)
        for index in range(1, pieces):
            rows = pl.ds(index * rows_total, rows_total)
            total = total + dot(gproj[c, rows, :], normed[index][...], TN)
        out[c] = total.astype(BF16)


def gelu_pair(values):
    squared = values * values
    bent = jnp.tanh(values * (0.7978845608028654 + 0.7978845608028654 * 0.044715 * squared))
    half = 0.5 * (1.0 + bent)
    lifted = values * half
    slope = 0.7978845608028654 + 3.0 * 0.7978845608028654 * 0.044715 * squared
    return lifted, half + lifted * (1.0 - bent) * slope


def padded_rows(values, rows):
    missing = jnp.zeros((rows - values.shape[0], values.shape[1]), values.dtype)
    return jnp.concatenate([values, missing], axis=0)


def moe_fwd_kernel(piece, pieces, shares, experts, idx, *refs):
    att, refs = refs[:shares], refs[shares:]
    if piece == 0:
        wo_fetched, wo_swapped, refs = refs[0], refs[1], refs[2:]
    else:
        wo, refs = refs[0], refs[1:]
    tok, gain, router, routes, cot, w_in, w_down = refs[:7]
    refs = refs[7:]
    parts, refs = refs[0], refs[1:]
    if piece == 0:
        wo, refs = refs[0], refs[1:]
    normed, own, gates, ggate, act, slope, acc = refs
    rows_total = tok.shape[0] // pieces
    base = piece * rows_total
    share = rows_total // shares
    me = idx[0]
    expert = pl.program_id(0)

    @pl.when(expert == 0)
    def _():
        gain_row = gain[...].astype(F32).reshape(1, -1)
        router_wide = padded_rows(router[...].astype(F32), LANES).astype(BF16)
        if piece == 0:
            half = wo_fetched.shape[1]
            mine = pl.ds(pl.multiple_of(idx[1] * half, half), half)
            other = pl.ds(pl.multiple_of((1 - idx[1]) * half, half), half)
            for step in range(shares):
                wo[step, mine, :] = wo_fetched[me ^ step]
                wo[step, other, :] = wo_swapped[me ^ step]
        for block in range(rows_total // BLK):
            rows = pl.ds(block * BLK, BLK)
            outer = pl.ds(base + block * BLK, BLK)
            attn = dot(att[0][rows, :], wo[0])
            for step in range(1, shares):
                attn = attn + dot(att[step][rows, :], wo[step])
            hidden = tok[outer, :].astype(F32) + attn
            acc[rows, :] = hidden
            n = (hidden * row_scale(hidden) * gain_row).astype(BF16)
            normed[rows, :] = n
            logits = dot(n, router_wide, NT)
            lanes = lax.broadcasted_iota(jnp.int32, logits.shape, 1)
            first = lanes == routes[outer, 0:1]
            second = lanes == routes[outer, 1:2]
            one = jnp.sum(jnp.where(first, logits, 0.0), axis=1, keepdims=True)
            two = jnp.sum(jnp.where(second, logits, 0.0), axis=1, keepdims=True)
            peak = jnp.maximum(one, two)
            one = jnp.exp(one - peak)
            two = jnp.exp(two - peak)
            both = one + two
            gates[rows, :] = jnp.where(first, one / both, jnp.where(second, two / both, 0.0))
        own[...] = acc[pl.ds(pl.multiple_of(me * share, share), share), :]
        acc[...] = jnp.zeros_like(acc)
        ggate[...] = jnp.zeros_like(ggate)

    for block in range(rows_total // ROWS):
        rows = pl.ds(block * ROWS, ROWS)
        outer = pl.ds(base + block * ROWS, ROWS)
        lifted, bend = gelu_pair(dot(normed[rows, :], w_in[0]))
        lifted = lifted.astype(BF16)
        act[0, rows, :] = lifted
        slope[0, rows, :] = bend.astype(BF16)
        out = dot(lifted, w_down[0])
        gate = lane_pick(gates[rows, :], expert)
        acc[rows, :] += gate * out
        pulled = jnp.sum(cot[outer, :].astype(F32) * out, axis=1, keepdims=True)
        held = ggate[rows, :]
        lanes = lax.broadcasted_iota(jnp.int32, held.shape, 1)
        ggate[rows, :] = jnp.where(lanes == expert, pulled, held)

    @pl.when(expert == experts - 1)
    def _():
        parts[...] = acc[...].astype(BF16)


def moe_bwd_kernel(piece, shares, experts, idx, *refs):
    gates, ggate, cot, slope, router, w_in, w_down = refs[:7]
    refs = refs[7:]
    parts, refs = refs[:shares], refs[shares:]
    glog, gpre, acc = refs
    rows_total = gates.shape[0]
    base = piece * rows_total
    share = rows_total // shares
    me = idx[0]
    expert = pl.program_id(0)

    @pl.when(expert == 0)
    def _():
        router_wide = padded_rows(router[...].astype(F32), LANES)
        for block in range(rows_total // ROWS):
            rows = pl.ds(block * ROWS, ROWS)
            g, gg = gates[rows, :], ggate[rows, :]
            back = g * (gg - jnp.sum(g * gg, axis=1, keepdims=True))
            glog[rows, :] = back
            acc[rows, :] = dot(back, router_wide, NN, HIGHEST)

    for block in range(rows_total // ROWS):
        rows = pl.ds(block * ROWS, ROWS)
        gate = lane_pick(gates[rows, :], expert)
        weighted = cot[pl.ds(base + block * ROWS, ROWS), :].astype(F32)
        weighted = (gate * weighted).astype(BF16)
        gp = (dot(weighted, w_down[0], NT) * slope[0, rows, :].astype(F32)).astype(BF16)
        gpre[0, rows, :] = gp
        acc[rows, :] += dot(gp, w_in[0], NT)

    @pl.when(expert == experts - 1)
    def _():
        for step in range(shares):
            start = pl.multiple_of((me ^ step) * share, share)
            parts[step][...] = acc[pl.ds(start, share), :].astype(BF16)


def moe_weights_kernel(pieces, cot, *refs):
    gates, refs = refs[:pieces], refs[pieces:]
    glog, refs = refs[:pieces], refs[pieces:]
    normed, refs = refs[:pieces], refs[pieces:]
    act, refs = refs[:pieces], refs[pieces:]
    gpre, refs = refs[:pieces], refs[pieces:]
    out, router = refs
    rows_total = normed[0].shape[0]
    expert = pl.program_id(0)

    @pl.when(expert == 0)
    def _():
        total = jnp.zeros((LANES, cot.shape[1]), F32)
        for index in range(pieces):
            back = glog[index][...]
            high = back.astype(BF16)
            low = (back - high.astype(F32)).astype(BF16)
            total = total + dot(high, normed[index][...], TN)
            total = total + dot(low, normed[index][...], TN)
        router[...] = total[0:8, :]

    grad_in = jnp.zeros((normed[0].shape[1], gpre[0].shape[2]), F32)
    grad_down = jnp.zeros((act[0].shape[2], cot.shape[1]), F32)
    for index in range(pieces):
        gate = lane_pick(gates[index][...], expert)
        weighted = cot[pl.ds(index * rows_total, rows_total), :].astype(F32)
        weighted = (gate * weighted).astype(BF16)
        grad_in = grad_in + dot(normed[index][...], gpre[index][0], TN)
        grad_down = grad_down + dot(act[index][0], weighted, TN)
    out[0, 0] = grad_in.astype(BF16)
    out[0, 1] = grad_down.astype(BF16)


def hidden_back_kernel(piece, pieces, shares, got, idx, *refs):
    gx, refs = refs[:got], refs[got:]
    wo, own, cot, gain = refs[:4]
    refs = refs[4:]
    ga, gh, gh_low, ggain = refs
    share = own.shape[0]
    grad = gx[0][...].astype(F32)
    for step in range(1, got):
        grad = grad + gx[step][...].astype(F32)
    hidden = own[...]
    scale = row_scale(hidden)
    unit = hidden * scale
    ggain[...] = jnp.sum(grad * unit, axis=0, keepdims=True)
    gained = grad * gain[...].astype(F32).reshape(1, -1)
    start = piece * (cot.shape[0] // pieces) + idx[0] * share
    mine = cot[pl.ds(pl.multiple_of(start, share), share), :].astype(F32)
    back = mine + scale * (gained - unit * jnp.mean(gained * unit, axis=-1, keepdims=True))
    gh[...] = back
    low = back.astype(BF16)
    gh_low[...] = low
    for step in range(shares):
        ga[idx[0] ^ step] = dot(low, wo[step], NT).astype(BF16)


def w_out_back_kernel(pieces, shares, idx, *refs):
    att, refs = refs[: pieces * shares], refs[pieces * shares :]
    gh_low, out = refs[:pieces], refs[pieces]
    share = gh_low[0].shape[0]
    rows = pl.ds(pl.multiple_of(idx[0] * share, share), share)
    for step in range(shares):
        total = dot(att[step][rows, :], gh_low[0][...], TN)
        for index in range(1, pieces):
            total = total + dot(att[index * shares + step][rows, :], gh_low[index][...], TN)
        out[step] = total.astype(BF16)


def join_kernel(pieces, count, *refs):
    own, refs = refs[:pieces], refs[pieces:]
    got, out = refs[: pieces * count], refs[pieces * count]
    share = own[0].shape[0]
    for index in range(pieces):
        total = own[index][...]
        for step in range(count):
            total = total + got[index * count + step][...].astype(F32)
        out[pl.ds(index * share, share), :] = total.astype(BF16)


def input_back_kernel(pieces, got, idx, *refs):
    gn, refs = refs[:got], refs[got:]
    ghs, refs = refs[:pieces], refs[pieces:]
    tok, gain, gt, ggain = refs
    share = ghs[0].shape[0]
    gain_row = gain[...].astype(F32).reshape(1, -1)
    total = jnp.zeros_like(ggain)
    for index in range(pieces):
        rows = pl.ds(index * share, share)
        grad = gn[0][rows, :].astype(F32)
        for step in range(1, got):
            grad = grad + gn[step][rows, :].astype(F32)
        start = index * (tok.shape[0] // pieces) + idx[0] * share
        x = tok[pl.ds(pl.multiple_of(start, share), share), :].astype(F32)
        scale = row_scale(x)
        unit = x * scale
        total = total + jnp.sum(grad * unit, axis=0, keepdims=True)
        gained = grad * gain_row
        back = scale * (gained - unit * jnp.mean(gained * unit, axis=-1, keepdims=True))
        gt[rows, :] = (ghs[index][...] + back).astype(BF16)
    ggain[...] = total


def place_kernel(pieces, shares, idx, *refs):
    blocks, out = refs[:shares], refs[shares]
    rows_total = out.shape[0] // pieces
    share = rows_total // shares
    for step in range(shares):
        owner = idx[0] ^ step
        for index in range(pieces):
            start = pl.multiple_of(index * rows_total + owner * share, share)
            got = blocks[step][pl.ds(index * share, share), :]
            out[pl.ds(start, share), :] = got.astype(out.dtype)


ROWS = 512
PIECES = 1

SMEM = pl.BlockSpec(memory_space=pltpu.SMEM)
VMEM = pl.BlockSpec(memory_space=pltpu.VMEM)


def shaped(shape, dtype):
    return jax.ShapeDtypeStruct(shape, dtype)


def whole_call(kernel, outs, args, scratch=(), flops=0, moved=0, with_index=True):
    specs = ([SMEM] if with_index else []) + [VMEM] * (len(args) - (1 if with_index else 0))
    return pl.pallas_call(
        kernel,
        out_shape=outs,
        in_specs=specs,
        out_specs=[VMEM] * len(outs),
        scratch_shapes=list(scratch),
        compiler_params=pltpu.CompilerParams(vmem_limit_bytes=VMEM_LIMIT),
        cost_estimate=pl.CostEstimate(flops=flops, bytes_accessed=moved, transcendentals=0),
    )(*args)


def swap(value, axis, bit):
    count = lax.axis_size(axis)
    return lax.ppermute(value, axis, [(i, i ^ bit) for i in range(count)])


def sum_over(value, axis):
    bit = 1
    while bit < lax.axis_size(axis):
        value = value + swap(value, axis, bit)
        bit *= 2
    return value


def gather_parts(value, axis):
    count = lax.axis_size(axis)
    if count != 4:
        return [value] + [swap(value, axis, bit) for bit in range(1, count)]
    two = swap(value, axis, 2)
    one = swap(value, axis, 1)
    return [value, one, two, swap(two, axis, 1)]


def reduce_near(parts, axis):
    return swap(parts[3], axis, 1), swap(parts[1], axis, 1)


def reduce_far(parts, near, axis):
    pair = (parts[2].astype(F32) + near[0].astype(F32)).astype(parts[2].dtype)
    return [parts[0], near[1], swap(pair, axis, 2)], pair


def exchange(parts, axis):
    return [parts[0]] + [swap(parts[bit], axis, bit) for bit in range(1, len(parts))]


def halves_of(value, axis, chosen):
    half = value.shape[axis] // 2
    keep = lax.dynamic_slice_in_dim(value, chosen * half, half, axis)
    send = lax.dynamic_slice_in_dim(value, (1 - chosen) * half, half, axis)
    return keep, send


def bits_of(axis):
    count = lax.axis_size(axis)
    return [1 << level for level in range(count.bit_length() - 1)]


def gather_back(value, mesh_axis, axis):
    me = lax.axis_index(mesh_axis)
    for bit in reversed(bits_of(mesh_axis)):
        got = swap(value, mesh_axis, bit)
        low = (me // bit) % 2 == 0
        value = jnp.concatenate(
            [jnp.where(low, value, got), jnp.where(low, got, value)], axis=axis
        )
    return value


def after(value, *others):
    return lax.optimization_barrier((value, *others))[0]


def body(
    tokens, segments, routes, grad_out, gain_attn, w_qkv, w_out, rel_bias,
    gain_moe, w_router, w_in, w_down,
):
    tok_rows, width = tokens.shape
    heads = rel_bias.shape[1]
    features = w_qkv.shape[2]
    head_size = features // heads
    experts, _, hidden_units = w_in.shape
    shares = lax.axis_size("tensor")
    rows = tok_rows // PIECES
    share = rows // shares
    me = lax.axis_index("tensor").astype(jnp.int32)
    side = (lax.axis_index("dp") % 2).astype(jnp.int32)
    idx = jnp.stack([me, side])
    mib = 1 << 20
    others = range(1, shares)
    four = shares == 4

    half_rows = features // 2
    my_half = lax.dynamic_slice_in_dim(w_out, side * half_rows, half_rows, 0)
    halves = lax.all_gather(my_half, "tensor", axis=0)

    build_hot, gather_hot = near_tables()
    build_hot = jnp.asarray(np.swapaxes(build_hot, 1, 2), BF16)
    gather_hot = jnp.asarray(gather_hot, F32)
    w_qkv_t = jnp.swapaxes(w_qkv, 1, 2)
    router_t = w_router.T

    normed_one, qh, k, v, _, att, ot, lse, bias, far = whole_call(
        functools.partial(attn_fwd_kernel, 0, PIECES, heads, head_size),
        [
            shaped((rows, width), BF16),
            shaped((heads, rows, features), BF16),
            shaped((rows, features), BF16),
            shaped((rows, features), BF16),
            shaped((features, rows), BF16),
            shaped((rows, features), BF16),
            shaped((features, rows), F32),
            shaped((8, rows), F32),
            shaped((2 * heads, BLK, BLK), F32),
            shaped((8, LANES), F32),
        ],
        [tokens, gain_attn, w_qkv_t, segments, rel_bias.T, build_hot],
        flops=6 * 10**9, moved=8 * mib, with_index=False,
    )
    atts = gather_parts(att, "tensor")
    swapped = swap(after(halves, att), "dp", 1)

    full = lambda shape: pl.BlockSpec(shape, lambda e: (0,) * len(shape))
    per_expert = lambda shape: pl.BlockSpec((1,) + shape, lambda e: (e, 0, 0))
    params = pltpu.CompilerParams(
        vmem_limit_bytes=VMEM_LIMIT, dimension_semantics=("arbitrary",)
    )
    moe_flops = 4 * experts * rows * width * hidden_units

    fwd = pl.pallas_call(
        functools.partial(moe_fwd_kernel, 0, PIECES, shares, experts),
        grid=(experts,),
        in_specs=[SMEM]
        + [full((rows, features))] * shares
        + [full((shares, half_rows, width))] * 2
        + [
            full((rows, width)), full((width,)), full((experts, width)),
            full((rows, 2)), full((rows, width)),
            per_expert((width, hidden_units)), per_expert((hidden_units, width)),
        ],
        out_specs=[
            full((rows, width)), full((shares, features, width)), full((rows, width)),
            full((share, width)), full((rows, LANES)), full((rows, LANES)),
            per_expert((rows, hidden_units)), per_expert((rows, hidden_units)),
        ],
        out_shape=[
            shaped((rows, width), BF16),
            shaped((shares, features, width), BF16),
            shaped((rows, width), BF16),
            shaped((share, width), F32),
            shaped((rows, LANES), F32),
            shaped((rows, LANES), F32),
            shaped((experts, rows, hidden_units), BF16),
            shaped((experts, rows, hidden_units), BF16),
        ],
        scratch_shapes=[pltpu.VMEM((rows, width), F32)],
        compiler_params=params,
        cost_estimate=pl.CostEstimate(
            flops=moe_flops, bytes_accessed=32 * mib, transcendentals=0
        ),
    )(
        idx, *atts, halves, swapped, tokens, gain_moe, router_t, routes, grad_out,
        w_in, w_down,
    )
    moe_sum, wo, normed_two, own_hidden, gates, ggate, act, slope = fwd
    moe_rows = lax.psum_scatter(moe_sum, "tensor", scatter_dimension=0, tiled=True)

    bwd = pl.pallas_call(
        functools.partial(moe_bwd_kernel, 0, shares, experts),
        grid=(experts,),
        in_specs=[
            SMEM, full((rows, LANES)), full((rows, LANES)), full((rows, width)),
            per_expert((rows, hidden_units)), full((experts, width)),
            per_expert((width, hidden_units)), per_expert((hidden_units, width)),
        ],
        out_specs=[full((share, width))] * shares
        + [full((rows, LANES)), per_expert((rows, hidden_units))],
        out_shape=[shaped((share, width), BF16)] * shares
        + [
            shaped((rows, LANES), F32),
            shaped((experts, rows, hidden_units), BF16),
        ],
        scratch_shapes=[pltpu.VMEM((rows, width), F32)],
        compiler_params=params,
        cost_estimate=pl.CostEstimate(
            flops=moe_flops, bytes_accessed=26 * mib, transcendentals=0
        ),
    )(idx, gates, ggate, grad_out, slope, router_t, w_in, w_down)
    gx_parts = bwd[:shares]
    glog, gpre = bwd[shares:]
    gx_near = reduce_near(gx_parts, "tensor") if four else exchange(gx_parts, "tensor")[1:]

    expert_grads, router_rows = pl.pallas_call(
        functools.partial(moe_weights_kernel, PIECES),
        grid=(experts,),
        in_specs=[
            full((rows, width)), full((rows, LANES)), full((rows, LANES)), full((rows, width)),
            per_expert((rows, hidden_units)), per_expert((rows, hidden_units)),
        ],
        out_specs=[
            pl.BlockSpec((1, 2, width, width), lambda e: (e, 0, 0, 0)), full((8, width))
        ],
        out_shape=[shaped((experts, 2, width, width), BF16), shaped((8, width), F32)],
        compiler_params=params,
        cost_estimate=pl.CostEstimate(
            flops=moe_flops, bytes_accessed=26 * mib, transcendentals=0
        ),
    )(grad_out, gates, glog, normed_two, act, gpre)
    expert_rows = after(expert_grads.reshape(experts * 2 * width, width), *gx_near)
    expert_rows = lax.psum_scatter(expert_rows, "dp", scatter_dimension=0, tiled=True)

    if four:
        gx_near = after(gx_near[0], router_rows), gx_near[1]
        gx_got, _ = reduce_far(gx_parts, gx_near, "tensor")
    else:
        gx_got = [gx_parts[0], *gx_near]
    ga, grad_hidden, gh_low, ggain_two = whole_call(
        functools.partial(hidden_back_kernel, 0, PIECES, shares, len(gx_got)),
        [
            shaped((shares, share, features), BF16), shaped((share, width), F32),
            shaped((share, width), BF16), shaped((1, width), F32),
        ],
        [idx, *gx_got, wo, own_hidden, grad_out, gain_moe],
        flops=3 * 10**8, moved=5 * mib,
    )
    go = lax.all_to_all(ga, "tensor", split_axis=0, concat_axis=0, tiled=True)
    go = go.reshape(rows, features)

    result_share = whole_call(
        functools.partial(join_kernel, PIECES, 1),
        [shaped((share, width), BF16)],
        [own_hidden, moe_rows],
        moved=2 * mib, with_index=False,
    )[0]
    result_got = gather_parts(result_share, "tensor")
    result = whole_call(
        functools.partial(place_kernel, PIECES, shares),
        [shaped((rows, width), BF16)], [idx, *result_got], moved=3 * mib,
    )[0]

    attn_back = whole_call(
        functools.partial(attn_bwd_kernel, 0, PIECES, heads, head_size, shares),
        [shaped((share, width), BF16)] * shares
        + [shaped((3, rows, features), BF16), shaped((8, NB), F32)],
        [
            idx, after(go, result_share), qh, ot, lse, k, v, bias, far, segments,
            w_qkv_t, gather_hot,
        ],
        [pltpu.VMEM((rows, features), F32)] * 2
        + [
            pltpu.VMEM((features, rows), F32),
            pltpu.VMEM((2 * heads, BLK, BLK), F32),
            pltpu.VMEM((features, rows), BF16),
            pltpu.VMEM((8, rows), F32),
            pltpu.VMEM((2, 8, 2 * BLK), F32),
            pltpu.VMEM((8, BLK), F32),
        ],
        flops=14 * 10**9, moved=8 * mib,
    )
    gn_parts = attn_back[:shares]
    gproj, grad_rel = attn_back[shares:]

    qkv_rows = whole_call(
        functools.partial(qkv_weights_kernel, PIECES),
        [shaped((3, features, width), BF16)],
        [normed_one, gproj],
        flops=10**9, moved=4 * mib, with_index=False,
    )[0]
    w_out_rows = whole_call(
        functools.partial(w_out_back_kernel, PIECES, shares),
        [shaped((shares, features, width), BF16)],
        [idx, *atts, after(gh_low, gproj)],
        flops=3 * 10**8, moved=4 * mib,
    )[0]
    late = jnp.concatenate([qkv_rows, w_out_rows], axis=0)
    if four:
        near = reduce_near(gn_parts, "tensor")
        gn_got, mark = reduce_far(gn_parts, (after(near[0], late), near[1]), "tensor")
    else:
        gn_got = exchange(gn_parts, "tensor")
        mark = gn_got[-1]

    place = lax.axis_index("dp")

    def halve(value, bit, *ready):
        keep, send = halves_of(value, 1, (place // bit) % 2)
        got = swap(after(send, *ready), "dp", bit)
        return (keep.astype(F32) + got.astype(F32)).astype(BF16)

    late = after(late, mark)
    for bit in bits_of("dp")[:2]:
        late = halve(late, bit)
    grad_hidden = after(grad_hidden, late)

    gt_share, ggain_one = whole_call(
        functools.partial(input_back_kernel, PIECES, len(gn_got)),
        [shaped((share, width), BF16), shaped((1, width), F32)],
        [idx, *gn_got, grad_hidden, tokens, gain_attn],
        moved=5 * mib,
    )
    gt_got = gather_parts(gt_share, "tensor")
    grad_tokens = whole_call(
        functools.partial(place_kernel, PIECES, shares),
        [shaped((rows, width), F32)], [idx, *gt_got], moved=5 * mib,
    )[0]

    for bit in bits_of("dp")[2:]:
        late = halve(late, bit, gt_got[2])
    out_sum = late[3].astype(F32)
    for by in others:
        out_sum = out_sum + swap(late[3 + by], "tensor", by).astype(F32)
    late = jnp.concatenate([late[:3], out_sum.astype(BF16)[None]], axis=0)
    late = gather_back(late, "dp", 1)
    expert_rows = lax.all_gather(after(expert_rows, gt_share), "dp", axis=0, tiled=True)
    expert_rows = expert_rows.reshape(experts, 2, width, width)
    grad_w_in = expert_rows[:, 0].astype(F32)
    grad_w_down = expert_rows[:, 1].astype(F32)
    grad_w_qkv = jnp.swapaxes(late[:3], 1, 2).astype(F32)
    grad_w_out = late[3].astype(F32)

    rel_rows = jnp.pad(grad_rel, ((0, 0), (0, width - NB)))
    small = jnp.concatenate([rel_rows, router_rows, ggain_one, ggain_two], axis=0)
    small = sum_over(small, "dp")
    grad_rel_bias = small[:heads, :NB].T
    shared = sum_over(small[8:], "tensor")
    return (
        result,
        grad_tokens,
        shared[8],
        grad_w_qkv,
        grad_w_out,
        grad_rel_bias,
        shared[9],
        shared[:experts].T,
        grad_w_in,
        grad_w_down,
    )


def solution(mesh):
    placed = (
        P("dp", None),
        P("dp", None),
        P("dp", None),
        P("dp", None),
        P(),
        P(None, None, "tensor"),
        P("tensor", None),
        P(None, "tensor"),
        P(),
        P(),
        P(None, None, "tensor"),
        P(None, "tensor", None),
    )
    return jax.shard_map(
        body,
        mesh=mesh,
        in_specs=placed,
        out_specs=(
            P("dp", None),
            P("dp", None),
            P(),
            P(None, None, "tensor"),
            P("tensor", None),
            P(None, "tensor"),
            P(),
            P(),
            P(None, None, "tensor"),
            P(None, "tensor", None),
        ),
        check_vma=False,
    )
```

```python
import functools
import math

import jax
import jax.numpy as jnp
import numpy as np
from jax import lax
from jax.experimental import pallas as pl
from jax.experimental.pallas import tpu as pltpu
from jax.sharding import PartitionSpec as P

NB = 32
DIST = 128
EPSILON = 1e-06
NEGATIVE = -1e30
HIGHEST = lax.Precision.HIGHEST
F32 = jnp.float32
BF16 = jnp.bfloat16
BLK = 256
LANES = 128
VMEM_LIMIT = 56 * 1024 * 1024

NN = (((1,), (0,)), ((), ()))
NT = (((1,), (1,)), ((), ()))
TN = (((0,), (0,)), ((), ()))


def dot(a, b, dims=NN, precision=None):
    return lax.dot_general(a, b, dims, precision=precision, preferred_element_type=F32)


def bucket_of(distance):
    halfway = NB // 2
    thresholds = [
        int(math.ceil(halfway * (DIST / halfway) ** (step / halfway))) for step in range(halfway)
    ]
    beyond = sum((distance >= threshold).astype(np.int64) for threshold in thresholds)
    return np.where(distance < halfway, distance, halfway - 1 + beyond)


def near_tables():
    lanes = np.arange(2 * BLK)
    offset = np.where(lanes < BLK, lanes, lanes - 2 * BLK)
    build = np.stack([np.maximum(offset, 0), np.maximum(BLK + offset, 0)])
    gather = np.stack([lanes - (BLK - 1), lanes + 1])
    eye = np.eye(NB, dtype=np.float32)
    build_hot = eye[bucket_of(build)]
    gather_hot = eye[bucket_of(np.maximum(gather, 0))] * (gather >= 0)[..., None]
    return build_hot, gather_hot


def row_scale(values):
    return lax.rsqrt(jnp.mean(values * values, axis=-1, keepdims=True) + EPSILON)


def lane_pick(values, index):
    lanes = lax.broadcasted_iota(jnp.int32, values.shape, 1)
    return jnp.sum(jnp.where(lanes == index, values, 0.0), axis=1, keepdims=True)


def masked_scores(k_tile, qh_tile, bias, seg_k, seg_q, diagonal):
    scores = dot(k_tile, qh_tile, NT) + bias
    allowed = seg_k == seg_q
    if diagonal:
        key_at = lax.broadcasted_iota(jnp.int32, scores.shape, 0)
        query_at = lax.broadcasted_iota(jnp.int32, scores.shape, 1)
        allowed = allowed & (key_at <= query_at)
    return jnp.where(allowed, scores, NEGATIVE)


def tile_bias(bias_ref, far_ref, head, delta):
    if delta < 2:
        return bias_ref[2 * head + delta]
    return far_ref[pl.ds(head, 1), 0:1]


def column_of(row):
    spread = jnp.broadcast_to(row.astype(F32), (8, row.shape[1]))
    return spread.T[:, 0:1]


def attn_fwd_kernel(piece, pieces, heads, head_size, *refs):
    tok, gain, w, seg = refs[:4]
    refs = refs[4:]
    if piece == 0:
        rel, build = refs[:2]
        refs = refs[2:]
    else:
        bias, far = refs[:2]
        refs = refs[2:]
    old_k, refs = refs[:piece], refs[piece:]
    old_vt, refs = refs[:piece], refs[piece:]
    normed, qh, k, v, vt, att, ot, lse = refs[:8]
    if piece == 0:
        bias, far = refs[8:]
    keys_of, vt_of = [*old_k, k], [*old_vt, vt]
    rows_total = tok.shape[0] // pieces
    base = piece * rows_total
    features = w.shape[1]
    blocks = rows_total // BLK
    gain_row = gain[...].astype(F32).reshape(1, -1)
    lanes = lax.broadcasted_iota(jnp.int32, (BLK, features), 1)
    for block in range(blocks):
        rows = pl.ds(block * BLK, BLK)
        x = tok[pl.ds(base + block * BLK, BLK), :].astype(F32)
        n = (x * row_scale(x) * gain_row).astype(BF16)
        normed[rows, :] = n
        q_rows = dot(n, w[0], NT).astype(BF16).astype(F32) * (head_size**-0.5)
        for head in range(heads):
            inside = (lanes >= head * head_size) & (lanes < (head + 1) * head_size)
            qh[head, rows, :] = jnp.where(inside, q_rows, 0.0).astype(BF16)
        k[rows, :] = dot(n, w[1], NT).astype(BF16)
        v_rows = dot(n, w[2], NT).astype(BF16)
        v[rows, :] = v_rows
        vt[:, rows] = v_rows.astype(F32).T.astype(BF16)
    if piece == 0:
        far[...] = jnp.zeros_like(far)
        far[0:heads, :] = jnp.broadcast_to(rel[:, NB - 1 : NB].astype(F32), (heads, LANES))
        for delta in range(2):
            near = dot(rel[...], build[delta])
            for head in range(heads):
                spread = jnp.broadcast_to(near[head : head + 1, :], (BLK, 2 * BLK))
                turned = pltpu.roll(spread, 0, 1, stride=1, stride_axis=0)
                bias[2 * head + delta] = turned[:, :BLK]
    lse[...] = jnp.zeros_like(lse)
    seg_row = seg[...].astype(F32)
    seg_col = column_of(seg[...])

    def one_head(head, carry):
        part = pl.ds(pl.multiple_of(head * head_size, head_size), head_size)
        for block in range(blocks):
            qb = piece * blocks + block
            cols = pl.ds(block * BLK, BLK)
            q_tile = qh[head, cols, :]
            tiles = []
            for kb in range(qb + 1):
                keys = pl.ds(kb % blocks * BLK, BLK)
                tiles.append(
                    masked_scores(
                        keys_of[kb // blocks][keys, :], q_tile,
                        tile_bias(bias, far, head, qb - kb),
                        seg_col[kb * BLK : (kb + 1) * BLK, :],
                        seg_row[:, qb * BLK : (qb + 1) * BLK], kb == qb,
                    )
                )
            peak = functools.reduce(
                jnp.maximum, [jnp.max(t, axis=0, keepdims=True) for t in tiles]
            )
            total = jnp.zeros((1, BLK), F32)
            out = jnp.zeros((head_size, BLK), F32)
            for kb in range(qb + 1):
                raised = jnp.exp(tiles[kb] - peak)
                total = total + jnp.sum(raised, axis=0, keepdims=True)
                values = vt_of[kb // blocks][part, pl.ds(kb % blocks * BLK, BLK)]
                out = out + dot(values, raised.astype(BF16))
            ot[part, cols] = out / total
            lse[pl.ds(head, 1), cols] = peak + jnp.log(total)
        return carry

    lax.fori_loop(0, heads, one_head, 0)
    for block in range(blocks):
        cols = pl.ds(block * BLK, BLK)
        att[cols, :] = ot[:, cols].T.astype(BF16)


def attn_bwd_kernel(piece, pieces, heads, head_size, shares, idx, *refs):
    held = piece + 1
    last = held == pieces
    go_parts, refs = refs[:shares], refs[shares:]
    tok, router, gain_two, qh, ot, lse = refs[:6]
    refs = refs[6:]
    ks, refs = refs[:held], refs[held:]
    vs, refs = refs[:held], refs[held:]
    bias, far, seg = refs[:3]
    refs = refs[3:]
    if piece:
        gk_in, refs = refs[:piece], refs[piece:]
        gv_in, refs = refs[:piece], refs[piece:]
        gq_in, refs = refs[:piece], refs[piece:]
        acc_in, refs = refs[0], refs[1:]
    if last:
        w, hot = refs[:2]
        refs = refs[2:]
        gn_parts, refs = refs[:shares], refs[shares:]
        gproj, misc = refs[:2]
        refs = refs[2:]
        gk, refs = refs[:held], refs[held:]
        gv, refs = refs[:held], refs[held:]
        gq_t, acc = refs[:2]
        refs = refs[2:]
    else:
        gk, refs = refs[:held], refs[held:]
        gv, refs = refs[:held], refs[held:]
        gq_t, acc = refs[:2]
        refs = refs[2:]
    go, misc_sum, kt, d_row, near_sum, far_sum = refs
    rows_total, features = ks[0].shape
    blocks = rows_total // BLK
    share = rows_total // shares
    me = idx[0]
    for step in range(shares):
        start = pl.multiple_of((me ^ step) * share, share)
        go[pl.ds(start, share), :] = go_parts[step][...]
    for index in range(held):
        for block in range(blocks):
            cols = pl.ds(block * BLK, BLK)
            kt[:, pl.ds((index * blocks + block) * BLK, BLK)] = (
                ks[index][cols, :].astype(F32).T.astype(BF16)
            )
        if index < piece:
            gk[index][...] = gk_in[index][...]
            gv[index][...] = gv_in[index][...]
        else:
            gk[index][...] = jnp.zeros_like(gk[index])
            gv[index][...] = jnp.zeros_like(gv[index])
    if piece:
        acc[...] = acc_in[...]
    else:
        acc[...] = jnp.zeros_like(acc)
    for block in range(blocks):
        cols = pl.ds(block * BLK, BLK)
        product = go[cols, :].astype(F32).T * ot[:, cols]
        for head in range(heads):
            part = product[head * head_size : (head + 1) * head_size, :]
            d_row[head : head + 1, cols] = jnp.sum(part, axis=0, keepdims=True)
    near_sum[...] = jnp.zeros_like(near_sum)
    far_sum[...] = jnp.zeros_like(far_sum)
    key_at = lax.broadcasted_iota(jnp.int32, (BLK, BLK), 0)
    other_at = lax.broadcasted_iota(jnp.int32, (BLK, BLK), 1)
    flip = (key_at + other_at == BLK - 1).astype(F32)
    seg_row = seg[...].astype(F32)
    seg_col = column_of(seg[...])

    def one_head(head, carry):
        part = pl.ds(pl.multiple_of(head * head_size, head_size), head_size)
        lanes = lax.broadcasted_iota(jnp.int32, (BLK, features), 1)
        inside = (lanes >= head * head_size) & (lanes < (head + 1) * head_size)
        for block in range(blocks):
            qb = piece * blocks + block
            cols = pl.ds(block * BLK, BLK)
            q_tile = qh[head, cols, :]
            go_tile = jnp.where(inside, go[cols, :].astype(F32), 0.0).astype(BF16)
            log_total = lse[pl.ds(head, 1), cols]
            d_tile = d_row[pl.ds(head, 1), cols]
            gq = jnp.zeros((head_size, BLK), F32)
            for kb in range(qb + 1):
                index = kb // blocks
                keys = pl.ds(kb % blocks * BLK, BLK)
                delta = qb - kb
                scores = masked_scores(
                    ks[index][keys, :], q_tile, tile_bias(bias, far, head, delta),
                    seg_col[kb * BLK : (kb + 1) * BLK, :],
                    seg_row[:, qb * BLK : (qb + 1) * BLK], delta == 0,
                )
                probs = jnp.exp(scores - log_total)
                gs = probs * (dot(vs[index][keys, :], go_tile, NT) - d_tile)
                if delta < 2:
                    acc[2 * head + delta] += gs
                else:
                    far_sum[pl.ds(head, 1), :] += jnp.sum(gs, axis=0, keepdims=True)
                gs_low = gs.astype(BF16)
                gv[index][keys, :] += dot(probs.astype(BF16), go_tile)
                gk[index][keys, :] += dot(gs_low, q_tile)
                gq = gq + dot(kt[part, kb * BLK : (kb + 1) * BLK], gs_low)
            gq_t[part, cols] = gq * (head_size**-0.5)
        return carry

    lax.fori_loop(0, heads, one_head, 0)
    if not last:
        return
    gqs = [*(gq_in if piece else ()), gq_t]
    for index in range(held):
        for block in range(blocks):
            rows = pl.ds(block * BLK, BLK)
            out = pl.ds((index * blocks + block) * BLK, BLK)
            gproj[0, out, :] = gqs[index][:, rows].T.astype(BF16)
            gproj[1, out, :] = gk[index][rows, :].astype(BF16)
            gproj[2, out, :] = gv[index][rows, :].astype(BF16)
    gain_one = jnp.zeros_like(gain_two)
    for step in range(shares):
        for index in range(pieces):
            start = index * rows_total + (me ^ step) * share
            rows = pl.ds(pl.multiple_of(start, share), share)
            total = dot(gproj[0, rows, :], w[0])
            total = total + dot(gproj[1, rows, :], w[1])
            total = total + dot(gproj[2, rows, :], w[2])
            gn_parts[step][pl.ds(index * share, share), :] = total.astype(BF16)
            x = tok[rows, :].astype(F32)
            gain_one = gain_one + jnp.sum(total * (x * row_scale(x)), axis=0, keepdims=True)
    for head in range(heads):
        for delta in range(2):
            turned = dot(flip, acc[2 * head + delta], NN, HIGHEST)
            wide = jnp.concatenate([turned, jnp.zeros_like(turned)], axis=1)
            sheared = pltpu.roll(wide, 0, 1, stride=1, stride_axis=0)
            near_sum[delta, head : head + 1, :] = jnp.sum(sheared, axis=0, keepdims=True)
    summed = dot(near_sum[0], hot[0], NN, HIGHEST) + dot(near_sum[1], hot[1], NN, HIGHEST)
    buckets = lax.broadcasted_iota(jnp.int32, summed.shape, 1)
    beyond = jnp.sum(far_sum[...], axis=1, keepdims=True)
    summed = summed + jnp.where(buckets == NB - 1, beyond, 0.0)
    misc_sum[...] = jnp.zeros_like(misc_sum)
    misc_sum[pl.ds(pl.multiple_of(me * 8, 8), 8), 0:NB] = summed
    misc_sum[8 * shares : 8 * shares + 8, :] = router[...]
    misc_sum[8 * shares + 8 : 8 * shares + 9, :] = gain_one
    misc_sum[8 * shares + 9 : 8 * shares + 10, :] = gain_two[...]
    misc[...] = misc_sum[...].astype(BF16)


def qkv_weights_kernel(pieces, *refs):
    normed = refs[:pieces]
    gproj, out = refs[pieces:]
    rows_total = normed[0].shape[0]
    for c in range(3):
        total = dot(gproj[c, pl.ds(0, rows_total), :], normed[0][...], TN)
        for index in range(1, pieces):
            rows = pl.ds(index * rows_total, rows_total)
            total = total + dot(gproj[c, rows, :], normed[index][...], TN)
        out[c] = total.astype(BF16)


def gelu_pair(values):
    squared = values * values
    bent = jnp.tanh(values * (0.7978845608028654 + 0.7978845608028654 * 0.044715 * squared))
    half = 0.5 * (1.0 + bent)
    lifted = values * half
    slope = 0.7978845608028654 + 3.0 * 0.7978845608028654 * 0.044715 * squared
    return lifted, half + lifted * (1.0 - bent) * slope


def padded_rows(values, rows):
    missing = jnp.zeros((rows - values.shape[0], values.shape[1]), values.dtype)
    return jnp.concatenate([values, missing], axis=0)


def moe_fwd_kernel(piece, pieces, shares, experts, idx, *refs):
    att, refs = refs[:shares], refs[shares:]
    if piece == 0:
        wo_own, wo_swapped, refs = refs[0], refs[1], refs[2:]
        wo_fetched, refs = refs[: shares - 1], refs[shares - 1 :]
    else:
        wo, refs = refs[0], refs[1:]
    tok, gain, router, routes, cot, w_in, w_down = refs[:7]
    refs = refs[7:]
    parts, refs = refs[:shares], refs[shares:]
    if piece == 0:
        wo, refs = refs[0], refs[1:]
    normed, own, gates, ggate, act, slope, acc = refs
    rows_total = tok.shape[0] // pieces
    base = piece * rows_total
    share = rows_total // shares
    me = idx[0]
    expert = pl.program_id(0)

    @pl.when(expert == 0)
    def _():
        gain_row = gain[...].astype(F32).reshape(1, -1)
        router_wide = padded_rows(router[...].astype(F32), LANES).astype(BF16)
        if piece == 0:
            half = wo_own.shape[0] // 2
            mine = pl.ds(pl.multiple_of(idx[1] * half, half), half)
            other = pl.ds(pl.multiple_of((1 - idx[1]) * half, half), half)
            wo[0] = wo_own[...]
            for step in range(1, shares):
                wo[step, mine, :] = wo_fetched[step - 1][...]
                wo[step, other, :] = wo_swapped[step - 1]
        for block in range(rows_total // BLK):
            rows = pl.ds(block * BLK, BLK)
            outer = pl.ds(base + block * BLK, BLK)
            attn = dot(att[0][rows, :], wo[0])
            for step in range(1, shares):
                attn = attn + dot(att[step][rows, :], wo[step])
            hidden = tok[outer, :].astype(F32) + attn
            acc[rows, :] = hidden
            n = (hidden * row_scale(hidden) * gain_row).astype(BF16)
            normed[rows, :] = n
            logits = dot(n, router_wide, NT)
            lanes = lax.broadcasted_iota(jnp.int32, logits.shape, 1)
            first = lanes == routes[outer, 0:1]
            second = lanes == routes[outer, 1:2]
            one = jnp.sum(jnp.where(first, logits, 0.0), axis=1, keepdims=True)
            two = jnp.sum(jnp.where(second, logits, 0.0), axis=1, keepdims=True)
            peak = jnp.maximum(one, two)
            one = jnp.exp(one - peak)
            two = jnp.exp(two - peak)
            both = one + two
            gates[rows, :] = jnp.where(first, one / both, jnp.where(second, two / both, 0.0))
        own[...] = acc[pl.ds(pl.multiple_of(me * share, share), share), :]
        acc[...] = jnp.zeros_like(acc)
        ggate[...] = jnp.zeros_like(ggate)

    for block in range(rows_total // ROWS):
        rows = pl.ds(block * ROWS, ROWS)
        outer = pl.ds(base + block * ROWS, ROWS)
        lifted, bend = gelu_pair(dot(normed[rows, :], w_in[0]))
        lifted = lifted.astype(BF16)
        act[0, rows, :] = lifted
        slope[0, rows, :] = bend.astype(BF16)
        out = dot(lifted, w_down[0])
        gate = lane_pick(gates[rows, :], expert)
        acc[rows, :] += gate * out
        pulled = jnp.sum(cot[outer, :].astype(F32) * out, axis=1, keepdims=True)
        held = ggate[rows, :]
        lanes = lax.broadcasted_iota(jnp.int32, held.shape, 1)
        ggate[rows, :] = jnp.where(lanes == expert, pulled, held)

    @pl.when(expert == experts - 1)
    def _():
        for step in range(shares):
            start = pl.multiple_of((me ^ step) * share, share)
            parts[step][...] = acc[pl.ds(start, share), :].astype(BF16)


def moe_bwd_kernel(piece, shares, experts, idx, *refs):
    gates, ggate, cot, slope, router, w_in, w_down = refs[:7]
    refs = refs[7:]
    parts, refs = refs[:shares], refs[shares:]
    glog, gpre, acc = refs
    rows_total = gates.shape[0]
    base = piece * rows_total
    share = rows_total // shares
    me = idx[0]
    expert = pl.program_id(0)

    @pl.when(expert == 0)
    def _():
        router_wide = padded_rows(router[...].astype(F32), LANES)
        for block in range(rows_total // ROWS):
            rows = pl.ds(block * ROWS, ROWS)
            g, gg = gates[rows, :], ggate[rows, :]
            back = g * (gg - jnp.sum(g * gg, axis=1, keepdims=True))
            glog[rows, :] = back
            acc[rows, :] = dot(back, router_wide, NN, HIGHEST)

    for block in range(rows_total // ROWS):
        rows = pl.ds(block * ROWS, ROWS)
        gate = lane_pick(gates[rows, :], expert)
        weighted = cot[pl.ds(base + block * ROWS, ROWS), :].astype(F32)
        weighted = (gate * weighted).astype(BF16)
        gp = (dot(weighted, w_down[0], NT) * slope[0, rows, :].astype(F32)).astype(BF16)
        gpre[0, rows, :] = gp
        acc[rows, :] += dot(gp, w_in[0], NT)

    @pl.when(expert == experts - 1)
    def _():
        for step in range(shares):
            start = pl.multiple_of((me ^ step) * share, share)
            parts[step][...] = acc[pl.ds(start, share), :].astype(BF16)


def moe_weights_kernel(pieces, cot, *refs):
    gates, refs = refs[:pieces], refs[pieces:]
    glog, refs = refs[:pieces], refs[pieces:]
    normed, refs = refs[:pieces], refs[pieces:]
    act, refs = refs[:pieces], refs[pieces:]
    gpre, refs = refs[:pieces], refs[pieces:]
    out, router = refs
    rows_total = normed[0].shape[0]
    expert = pl.program_id(0)

    @pl.when(expert == 0)
    def _():
        total = jnp.zeros((LANES, cot.shape[1]), F32)
        for index in range(pieces):
            back = glog[index][...]
            high = back.astype(BF16)
            low = (back - high.astype(F32)).astype(BF16)
            total = total + dot(high, normed[index][...], TN)
            total = total + dot(low, normed[index][...], TN)
        router[...] = total[0:8, :]

    grad_in = jnp.zeros((normed[0].shape[1], gpre[0].shape[2]), F32)
    grad_down = jnp.zeros((act[0].shape[2], cot.shape[1]), F32)
    for index in range(pieces):
        gate = lane_pick(gates[index][...], expert)
        weighted = cot[pl.ds(index * rows_total, rows_total), :].astype(F32)
        weighted = (gate * weighted).astype(BF16)
        grad_in = grad_in + dot(normed[index][...], gpre[index][0], TN)
        grad_down = grad_down + dot(act[index][0], weighted, TN)
    out[0, 0] = grad_in.astype(BF16)
    out[0, 1] = grad_down.astype(BF16)


def hidden_back_kernel(piece, pieces, shares, got, idx, *refs):
    gx, refs = refs[:got], refs[got:]
    wo, own, cot, gain = refs[:4]
    refs = refs[4:]
    ga, refs = refs[:shares], refs[shares:]
    gh, gh_low, ggain = refs
    share = own.shape[0]
    grad = gx[0][...].astype(F32)
    for step in range(1, got):
        grad = grad + gx[step][...].astype(F32)
    hidden = own[...]
    scale = row_scale(hidden)
    unit = hidden * scale
    ggain[...] = jnp.sum(grad * unit, axis=0, keepdims=True)
    gained = grad * gain[...].astype(F32).reshape(1, -1)
    start = piece * (cot.shape[0] // pieces) + idx[0] * share
    mine = cot[pl.ds(pl.multiple_of(start, share), share), :].astype(F32)
    back = mine + scale * (gained - unit * jnp.mean(gained * unit, axis=-1, keepdims=True))
    gh[...] = back
    low = back.astype(BF16)
    gh_low[...] = low
    for step in range(shares):
        ga[step][...] = dot(low, wo[step], NT).astype(BF16)


def w_out_back_kernel(pieces, shares, idx, *refs):
    att, refs = refs[: pieces * shares], refs[pieces * shares :]
    gh_low, out = refs[:pieces], refs[pieces]
    share = gh_low[0].shape[0]
    rows = pl.ds(pl.multiple_of(idx[0] * share, share), share)
    for step in range(shares):
        total = dot(att[step][rows, :], gh_low[0][...], TN)
        for index in range(1, pieces):
            total = total + dot(att[index * shares + step][rows, :], gh_low[index][...], TN)
        out[step] = total.astype(BF16)


def join_kernel(pieces, count, *refs):
    own, refs = refs[:pieces], refs[pieces:]
    got, out = refs[: pieces * count], refs[pieces * count]
    share = own[0].shape[0]
    for index in range(pieces):
        total = own[index][...]
        for step in range(count):
            total = total + got[index * count + step][...].astype(F32)
        out[pl.ds(index * share, share), :] = total.astype(BF16)


def input_back_kernel(pieces, got, idx, *refs):
    gn, refs = refs[:got], refs[got:]
    ghs, refs = refs[:pieces], refs[pieces:]
    tok, gain, gt = refs
    share = ghs[0].shape[0]
    gain_row = gain[...].astype(F32).reshape(1, -1)
    for index in range(pieces):
        rows = pl.ds(index * share, share)
        grad = gn[0][rows, :].astype(F32)
        for step in range(1, got):
            grad = grad + gn[step][rows, :].astype(F32)
        start = index * (tok.shape[0] // pieces) + idx[0] * share
        x = tok[pl.ds(pl.multiple_of(start, share), share), :].astype(F32)
        scale = row_scale(x)
        unit = x * scale
        gained = grad * gain_row
        back = scale * (gained - unit * jnp.mean(gained * unit, axis=-1, keepdims=True))
        gt[rows, :] = (ghs[index][...] + back).astype(BF16)


def place_kernel(pieces, shares, idx, *refs):
    blocks, out = refs[:shares], refs[shares]
    rows_total = out.shape[0] // pieces
    share = rows_total // shares
    for step in range(shares):
        owner = idx[0] ^ step
        for index in range(pieces):
            start = pl.multiple_of(index * rows_total + owner * share, share)
            got = blocks[step][pl.ds(index * share, share), :]
            out[pl.ds(start, share), :] = got.astype(out.dtype)


ROWS = 512
PIECES = 1

SMEM = pl.BlockSpec(memory_space=pltpu.SMEM)
VMEM = pl.BlockSpec(memory_space=pltpu.VMEM)


def shaped(shape, dtype):
    return jax.ShapeDtypeStruct(shape, dtype)


def whole_call(kernel, outs, args, scratch=(), flops=0, moved=0, with_index=True):
    specs = ([SMEM] if with_index else []) + [VMEM] * (len(args) - (1 if with_index else 0))
    return pl.pallas_call(
        kernel,
        out_shape=outs,
        in_specs=specs,
        out_specs=[VMEM] * len(outs),
        scratch_shapes=list(scratch),
        compiler_params=pltpu.CompilerParams(vmem_limit_bytes=VMEM_LIMIT),
        cost_estimate=pl.CostEstimate(flops=flops, bytes_accessed=moved, transcendentals=0),
    )(*args)


def swap(value, axis, bit):
    count = lax.axis_size(axis)
    return lax.ppermute(value, axis, [(i, i ^ bit) for i in range(count)])


def sum_over(value, axis):
    bit = 1
    while bit < lax.axis_size(axis):
        value = value + swap(value, axis, bit)
        bit *= 2
    return value


def gather_parts(value, axis):
    count = lax.axis_size(axis)
    if count != 4:
        return [value] + [swap(value, axis, bit) for bit in range(1, count)]
    two = swap(value, axis, 2)
    one = swap(value, axis, 1)
    return [value, one, two, swap(two, axis, 1)]


def reduce_near(parts, axis):
    return swap(parts[3], axis, 1), swap(parts[1], axis, 1)


def reduce_far(parts, near, axis):
    pair = (parts[2].astype(F32) + near[0].astype(F32)).astype(parts[2].dtype)
    return [parts[0], near[1], swap(pair, axis, 2)], pair


def exchange(parts, axis):
    return [parts[0]] + [swap(parts[bit], axis, bit) for bit in range(1, len(parts))]


def halves_of(value, axis, chosen):
    half = value.shape[axis] // 2
    keep = lax.dynamic_slice_in_dim(value, chosen * half, half, axis)
    send = lax.dynamic_slice_in_dim(value, (1 - chosen) * half, half, axis)
    return keep, send


def bits_of(axis):
    count = lax.axis_size(axis)
    return [1 << level for level in range(count.bit_length() - 1)]


def gather_back(value, mesh_axis, axis):
    me = lax.axis_index(mesh_axis)
    for bit in reversed(bits_of(mesh_axis)):
        got = swap(value, mesh_axis, bit)
        low = (me // bit) % 2 == 0
        value = jnp.concatenate(
            [jnp.where(low, value, got), jnp.where(low, got, value)], axis=axis
        )
    return value


def after(value, *others):
    return lax.optimization_barrier((value, *others))[0]


def body(
    tokens, segments, routes, grad_out, gain_attn, w_qkv, w_out, rel_bias,
    gain_moe, w_router, w_in, w_down,
):
    tok_rows, width = tokens.shape
    heads = rel_bias.shape[1]
    features = w_qkv.shape[2]
    head_size = features // heads
    experts, _, hidden_units = w_in.shape
    shares = lax.axis_size("tensor")
    rows = tok_rows // PIECES
    share = rows // shares
    me = lax.axis_index("tensor").astype(jnp.int32)
    side = (lax.axis_index("dp") % 2).astype(jnp.int32)
    idx = jnp.stack([me, side])
    mib = 1 << 20
    others = range(1, shares)
    four = shares == 4

    half_rows = features // 2
    my_half = lax.dynamic_slice_in_dim(w_out, side * half_rows, half_rows, 0)
    halves = [swap(my_half, "tensor", by) for by in others]

    build_hot, gather_hot = near_tables()
    build_hot = jnp.asarray(np.swapaxes(build_hot, 1, 2), BF16)
    gather_hot = jnp.asarray(gather_hot, F32)
    w_qkv_t = jnp.swapaxes(w_qkv, 1, 2)
    router_t = w_router.T

    normed_one, qh, k, v, _, att, ot, lse, bias, far = whole_call(
        functools.partial(attn_fwd_kernel, 0, PIECES, heads, head_size),
        [
            shaped((rows, width), BF16),
            shaped((heads, rows, features), BF16),
            shaped((rows, features), BF16),
            shaped((rows, features), BF16),
            shaped((features, rows), BF16),
            shaped((rows, features), BF16),
            shaped((features, rows), F32),
            shaped((8, rows), F32),
            shaped((2 * heads, BLK, BLK), F32),
            shaped((8, LANES), F32),
        ],
        [tokens, gain_attn, w_qkv_t, segments, rel_bias.T, build_hot],
        flops=6 * 10**9, moved=8 * mib, with_index=False,
    )
    atts = gather_parts(att, "tensor")
    swapped = swap(jnp.stack(halves), "dp", 1)

    full = lambda shape: pl.BlockSpec(shape, lambda e: (0,) * len(shape))
    per_expert = lambda shape: pl.BlockSpec((1,) + shape, lambda e: (e, 0, 0))
    params = pltpu.CompilerParams(
        vmem_limit_bytes=VMEM_LIMIT, dimension_semantics=("arbitrary",)
    )
    moe_flops = 4 * experts * rows * width * hidden_units

    fwd = pl.pallas_call(
        functools.partial(moe_fwd_kernel, 0, PIECES, shares, experts),
        grid=(experts,),
        in_specs=[SMEM]
        + [full((rows, features))] * shares
        + [full((features, width)), full((shares - 1, half_rows, width))]
        + [full((half_rows, width))] * (shares - 1)
        + [
            full((rows, width)), full((width,)), full((experts, width)),
            full((rows, 2)), full((rows, width)),
            per_expert((width, hidden_units)), per_expert((hidden_units, width)),
        ],
        out_specs=[full((share, width))] * shares
        + [
            full((shares, features, width)), full((rows, width)),
            full((share, width)), full((rows, LANES)), full((rows, LANES)),
            per_expert((rows, hidden_units)), per_expert((rows, hidden_units)),
        ],
        out_shape=[shaped((share, width), BF16)] * shares
        + [
            shaped((shares, features, width), BF16),
            shaped((rows, width), BF16),
            shaped((share, width), F32),
            shaped((rows, LANES), F32),
            shaped((rows, LANES), F32),
            shaped((experts, rows, hidden_units), BF16),
            shaped((experts, rows, hidden_units), BF16),
        ],
        scratch_shapes=[pltpu.VMEM((rows, width), F32)],
        compiler_params=params,
        cost_estimate=pl.CostEstimate(
            flops=moe_flops, bytes_accessed=32 * mib, transcendentals=0
        ),
    )(
        idx, *atts, w_out, swapped, *halves, tokens, gain_moe, router_t, routes, grad_out,
        w_in, w_down,
    )
    moe_parts = fwd[:shares]
    wo, normed_two, own_hidden, gates, ggate, act, slope = fwd[shares:]
    if four:
        moe_near = reduce_near(moe_parts, "tensor")
    else:
        moe_near = exchange(moe_parts, "tensor")[1:]

    bwd = pl.pallas_call(
        functools.partial(moe_bwd_kernel, 0, shares, experts),
        grid=(experts,),
        in_specs=[
            SMEM, full((rows, LANES)), full((rows, LANES)), full((rows, width)),
            per_expert((rows, hidden_units)), full((experts, width)),
            per_expert((width, hidden_units)), per_expert((hidden_units, width)),
        ],
        out_specs=[full((share, width))] * shares
        + [full((rows, LANES)), per_expert((rows, hidden_units))],
        out_shape=[shaped((share, width), BF16)] * shares
        + [
            shaped((rows, LANES), F32),
            shaped((experts, rows, hidden_units), BF16),
        ],
        scratch_shapes=[pltpu.VMEM((rows, width), F32)],
        compiler_params=params,
        cost_estimate=pl.CostEstimate(
            flops=moe_flops, bytes_accessed=26 * mib, transcendentals=0
        ),
    )(idx, gates, ggate, grad_out, slope, router_t, w_in, w_down)
    gx_parts = [after(part, *moe_near) for part in bwd[:shares]]
    glog, gpre = bwd[shares:]
    gx_near = reduce_near(gx_parts, "tensor") if four else exchange(gx_parts, "tensor")[1:]

    expert_grads, router_rows = pl.pallas_call(
        functools.partial(moe_weights_kernel, PIECES),
        grid=(experts,),
        in_specs=[
            full((rows, width)), full((rows, LANES)), full((rows, LANES)), full((rows, width)),
            per_expert((rows, hidden_units)), per_expert((rows, hidden_units)),
        ],
        out_specs=[
            pl.BlockSpec((1, 2, width, width), lambda e: (e, 0, 0, 0)), full((8, width))
        ],
        out_shape=[shaped((experts, 2, width, width), BF16), shaped((8, width), F32)],
        compiler_params=params,
        cost_estimate=pl.CostEstimate(
            flops=moe_flops, bytes_accessed=26 * mib, transcendentals=0
        ),
    )(grad_out, gates, glog, normed_two, act, gpre)
    expert_rows = after(expert_grads.reshape(experts * 2 * width, width), *gx_near)
    expert_rows = lax.psum_scatter(expert_rows, "dp", scatter_dimension=0, tiled=True)

    if four:
        gx_near = after(gx_near[0], router_rows), gx_near[1]
        gx_got, _ = reduce_far(gx_parts, gx_near, "tensor")
    else:
        gx_got = [gx_parts[0], *gx_near]
    back = whole_call(
        functools.partial(hidden_back_kernel, 0, PIECES, shares, len(gx_got)),
        [shaped((share, features), BF16)] * shares
        + [shaped((share, width), F32), shaped((share, width), BF16), shaped((1, width), F32)],
        [idx, *gx_got, wo, own_hidden, grad_out, gain_moe],
        flops=3 * 10**8, moved=5 * mib,
    )
    go = exchange(back[:shares], "tensor")
    grad_hidden, gh_low, ggain_two = back[shares:]

    if four:
        moe_near = after(moe_near[0], gh_low), moe_near[1]
        moe_got, _ = reduce_far(moe_parts, moe_near, "tensor")
    else:
        moe_got = [moe_parts[0], *moe_near]
    result_share = whole_call(
        functools.partial(join_kernel, PIECES, len(moe_got)),
        [shaped((share, width), BF16)],
        [own_hidden, *moe_got],
        moved=3 * mib, with_index=False,
    )[0]
    attn_back = whole_call(
        functools.partial(attn_bwd_kernel, 0, PIECES, heads, head_size, shares),
        [shaped((share, width), BF16)] * shares
        + [shaped((3, rows, features), BF16), shaped((features, width), BF16)],
        [
            idx, *go, tokens, router_rows, ggain_two, qh, ot, lse, k, v, bias, far, segments,
            w_qkv_t, gather_hot,
        ],
        [pltpu.VMEM((rows, features), F32)] * 2
        + [
            pltpu.VMEM((features, rows), F32),
            pltpu.VMEM((2 * heads, BLK, BLK), F32),
            pltpu.VMEM((rows, features), BF16),
            pltpu.VMEM((features, width), F32),
            pltpu.VMEM((features, rows), BF16),
            pltpu.VMEM((8, rows), F32),
            pltpu.VMEM((2, 8, 2 * BLK), F32),
            pltpu.VMEM((8, BLK), F32),
        ],
        flops=14 * 10**9, moved=8 * mib,
    )
    gn_parts = [after(part, moe_got[-1]) for part in attn_back[:shares]]
    gproj, misc = attn_back[shares:]

    qkv_rows = whole_call(
        functools.partial(qkv_weights_kernel, PIECES),
        [shaped((3, features, width), BF16)],
        [normed_one, gproj],
        flops=10**9, moved=4 * mib, with_index=False,
    )[0]
    w_out_rows = whole_call(
        functools.partial(w_out_back_kernel, PIECES, shares),
        [shaped((shares, features, width), BF16)],
        [idx, *atts, after(gh_low, gproj)],
        flops=3 * 10**8, moved=4 * mib,
    )[0]
    late = jnp.concatenate([qkv_rows, misc[None], w_out_rows], axis=0)
    if four:
        near = reduce_near(gn_parts, "tensor")
        near = after(near[0], late, near[1]), near[1]
        gn_got, mark = reduce_far(gn_parts, near, "tensor")
    else:
        gn_got = exchange(gn_parts, "tensor")
        mark = gn_got[-1]

    place = lax.axis_index("dp")

    def halve(value, bit, *ready):
        keep, send = halves_of(value, 1, (place // bit) % 2)
        got = swap(after(send, *ready), "dp", bit)
        return (keep.astype(F32) + got.astype(F32)).astype(BF16)

    late = after(late, mark)
    late = halve(late, 1)
    grad_hidden = after(grad_hidden, late)

    expert_rows = after(expert_rows, mark)
    gt_share = whole_call(
        functools.partial(input_back_kernel, PIECES, len(gn_got)),
        [shaped((share, width), BF16)],
        [idx, *gn_got, grad_hidden, tokens, gain_attn],
        moved=5 * mib,
    )[0]
    gt_got = gather_parts(gt_share, "tensor")
    grad_tokens = whole_call(
        functools.partial(place_kernel, PIECES, shares),
        [shaped((rows, width), F32)], [idx, *gt_got], moved=5 * mib,
    )[0]

    result_got = gather_parts(after(result_share, gt_got[2]), "tensor")
    result = whole_call(
        functools.partial(place_kernel, PIECES, shares),
        [shaped((rows, width), BF16)], [idx, *result_got], moved=3 * mib,
    )[0]

    for level, bit in enumerate(bits_of("dp")[1:]):
        late = halve(late, bit, gt_got[2] if level else gt_share)

    out_sum, small = late[4].astype(F32), [late[3]]
    for by in others:
        got = swap(jnp.stack([late[4 + by], late[3]]), "tensor", by)
        out_sum = out_sum + got[0].astype(F32)
        small.append(got[1])
    small = [one.astype(F32) for one in small]
    while len(small) > 1:
        small = [small[at] + small[at + 1] for at in range(0, len(small), 2)]
    late = jnp.concatenate(
        [late[:3], jnp.stack([small[0].astype(BF16), out_sum.astype(BF16)])], axis=0
    )
    late = gather_back(after(late, *gt_got[1:], result_got[2]), "dp", 1)
    expert_rows = lax.all_gather(expert_rows, "dp", axis=0, tiled=True)
    expert_rows = expert_rows.reshape(experts, 2, width, width)
    grad_w_in = expert_rows[:, 0].astype(F32)
    grad_w_down = expert_rows[:, 1].astype(F32)
    grad_w_qkv = jnp.swapaxes(late[:3], 1, 2).astype(F32)
    grad_w_out = late[4].astype(F32)
    small = late[3].astype(F32)
    grad_rel = lax.dynamic_slice_in_dim(small, me * 8, 8, 0)
    first = 8 * shares
    return (
        result,
        grad_tokens,
        small[first + 8],
        grad_w_qkv,
        grad_w_out,
        grad_rel[:heads, :NB].T,
        small[first + 9],
        small[first : first + experts].T,
        grad_w_in,
        grad_w_down,
    )


def solution(mesh):
    placed = (
        P("dp", None),
        P("dp", None),
        P("dp", None),
        P("dp", None),
        P(),
        P(None, None, "tensor"),
        P("tensor", None),
        P(None, "tensor"),
        P(),
        P(),
        P(None, None, "tensor"),
        P(None, "tensor", None),
    )
    return jax.shard_map(
        body,
        mesh=mesh,
        in_specs=placed,
        out_specs=(
            P("dp", None),
            P("dp", None),
            P(),
            P(None, None, "tensor"),
            P("tensor", None),
            P(None, "tensor"),
            P(),
            P(),
            P(None, None, "tensor"),
            P(None, "tensor", None),
        ),
        check_vma=False,
    )
```

```python
import functools
import math

import jax
import jax.numpy as jnp
import numpy as np
from jax import lax
from jax.experimental import pallas as pl
from jax.experimental.pallas import tpu as pltpu
from jax.sharding import PartitionSpec as P

NB = 32
DIST = 128
EPSILON = 1e-06
NEGATIVE = -1e30
HIGHEST = lax.Precision.HIGHEST
F32 = jnp.float32
BF16 = jnp.bfloat16
BLK = 256
LANES = 128
VMEM_LIMIT = 56 * 1024 * 1024

NN = (((1,), (0,)), ((), ()))
NT = (((1,), (1,)), ((), ()))
TN = (((0,), (0,)), ((), ()))


def dot(a, b, dims=NN, precision=None):
    return lax.dot_general(a, b, dims, precision=precision, preferred_element_type=F32)


def bucket_of(distance):
    halfway = NB // 2
    thresholds = [
        int(math.ceil(halfway * (DIST / halfway) ** (step / halfway))) for step in range(halfway)
    ]
    beyond = sum((distance >= threshold).astype(np.int64) for threshold in thresholds)
    return np.where(distance < halfway, distance, halfway - 1 + beyond)


def near_tables():
    lanes = np.arange(2 * BLK)
    offset = np.where(lanes < BLK, lanes, lanes - 2 * BLK)
    build = np.stack([np.maximum(offset, 0), np.maximum(BLK + offset, 0)])
    gather = np.stack([lanes - (BLK - 1), lanes + 1])
    eye = np.eye(NB, dtype=np.float32)
    build_hot = eye[bucket_of(build)]
    gather_hot = eye[bucket_of(np.maximum(gather, 0))] * (gather >= 0)[..., None]
    return build_hot, gather_hot


def row_scale(values):
    return lax.rsqrt(jnp.mean(values * values, axis=-1, keepdims=True) + EPSILON)


def lane_pick(values, index):
    lanes = lax.broadcasted_iota(jnp.int32, values.shape, 1)
    return jnp.sum(jnp.where(lanes == index, values, 0.0), axis=1, keepdims=True)


def masked_scores(k_tile, qh_tile, bias, seg_k, seg_q, diagonal):
    scores = dot(k_tile, qh_tile, NT) + bias
    allowed = seg_k == seg_q
    if diagonal:
        key_at = lax.broadcasted_iota(jnp.int32, scores.shape, 0)
        query_at = lax.broadcasted_iota(jnp.int32, scores.shape, 1)
        allowed = allowed & (key_at <= query_at)
    return jnp.where(allowed, scores, NEGATIVE)


def tile_bias(bias_ref, far_ref, head, delta):
    if delta < 2:
        return bias_ref[2 * head + delta]
    return far_ref[pl.ds(head, 1), 0:1]


def column_of(row):
    spread = jnp.broadcast_to(row.astype(F32), (8, row.shape[1]))
    return spread.T[:, 0:1]


def attn_fwd_kernel(piece, pieces, heads, head_size, *refs):
    tok, gain, w, seg = refs[:4]
    refs = refs[4:]
    if piece == 0:
        rel, build = refs[:2]
        refs = refs[2:]
    else:
        bias, far = refs[:2]
        refs = refs[2:]
    old_k, refs = refs[:piece], refs[piece:]
    old_vt, refs = refs[:piece], refs[piece:]
    normed, qh, k, v, vt, att, ot, lse = refs[:8]
    if piece == 0:
        bias, far = refs[8:]
    keys_of, vt_of = [*old_k, k], [*old_vt, vt]
    rows_total = tok.shape[0] // pieces
    base = piece * rows_total
    features = w.shape[1]
    blocks = rows_total // BLK
    gain_row = gain[...].astype(F32).reshape(1, -1)
    lanes = lax.broadcasted_iota(jnp.int32, (BLK, features), 1)
    for block in range(blocks):
        rows = pl.ds(block * BLK, BLK)
        x = tok[pl.ds(base + block * BLK, BLK), :].astype(F32)
        n = (x * row_scale(x) * gain_row).astype(BF16)
        normed[rows, :] = n
        q_rows = dot(n, w[0], NT).astype(BF16).astype(F32) * (head_size**-0.5)
        for head in range(heads):
            inside = (lanes >= head * head_size) & (lanes < (head + 1) * head_size)
            qh[head, rows, :] = jnp.where(inside, q_rows, 0.0).astype(BF16)
        k[rows, :] = dot(n, w[1], NT).astype(BF16)
        v_rows = dot(n, w[2], NT).astype(BF16)
        v[rows, :] = v_rows
        vt[:, rows] = v_rows.astype(F32).T.astype(BF16)
    if piece == 0:
        far[...] = jnp.zeros_like(far)
        far[0:heads, :] = jnp.broadcast_to(rel[:, NB - 1 : NB].astype(F32), (heads, LANES))
        for delta in range(2):
            near = dot(rel[...], build[delta])
            for head in range(heads):
                spread = jnp.broadcast_to(near[head : head + 1, :], (BLK, 2 * BLK))
                turned = pltpu.roll(spread, 0, 1, stride=1, stride_axis=0)
                bias[2 * head + delta] = turned[:, :BLK]
    lse[...] = jnp.zeros_like(lse)
    seg_row = seg[...].astype(F32)
    seg_col = column_of(seg[...])

    def one_head(head, carry):
        part = pl.ds(pl.multiple_of(head * head_size, head_size), head_size)
        for block in range(blocks):
            qb = piece * blocks + block
            cols = pl.ds(block * BLK, BLK)
            q_tile = qh[head, cols, :]
            tiles = []
            for kb in range(qb + 1):
                keys = pl.ds(kb % blocks * BLK, BLK)
                tiles.append(
                    masked_scores(
                        keys_of[kb // blocks][keys, :], q_tile,
                        tile_bias(bias, far, head, qb - kb),
                        seg_col[kb * BLK : (kb + 1) * BLK, :],
                        seg_row[:, qb * BLK : (qb + 1) * BLK], kb == qb,
                    )
                )
            peak = functools.reduce(
                jnp.maximum, [jnp.max(t, axis=0, keepdims=True) for t in tiles]
            )
            total = jnp.zeros((1, BLK), F32)
            out = jnp.zeros((head_size, BLK), F32)
            for kb in range(qb + 1):
                raised = jnp.exp(tiles[kb] - peak)
                total = total + jnp.sum(raised, axis=0, keepdims=True)
                values = vt_of[kb // blocks][part, pl.ds(kb % blocks * BLK, BLK)]
                out = out + dot(values, raised.astype(BF16))
            ot[part, cols] = out / total
            lse[pl.ds(head, 1), cols] = peak + jnp.log(total)
        return carry

    lax.fori_loop(0, heads, one_head, 0)
    for block in range(blocks):
        cols = pl.ds(block * BLK, BLK)
        att[cols, :] = ot[:, cols].T.astype(BF16)


def attn_bwd_kernel(piece, pieces, heads, head_size, shares, idx, *refs):
    held = piece + 1
    last = held == pieces
    go_parts, refs = refs[:shares], refs[shares:]
    tok, router, gain_two, qh, ot, lse = refs[:6]
    refs = refs[6:]
    ks, refs = refs[:held], refs[held:]
    vs, refs = refs[:held], refs[held:]
    bias, far, seg = refs[:3]
    refs = refs[3:]
    if piece:
        gk_in, refs = refs[:piece], refs[piece:]
        gv_in, refs = refs[:piece], refs[piece:]
        gq_in, refs = refs[:piece], refs[piece:]
        acc_in, refs = refs[0], refs[1:]
    if last:
        w, hot = refs[:2]
        refs = refs[2:]
        gn_parts, refs = refs[:shares], refs[shares:]
        gproj, misc = refs[:2]
        refs = refs[2:]
        gk, refs = refs[:held], refs[held:]
        gv, refs = refs[:held], refs[held:]
        gq_t, acc = refs[:2]
        refs = refs[2:]
    else:
        gk, refs = refs[:held], refs[held:]
        gv, refs = refs[:held], refs[held:]
        gq_t, acc = refs[:2]
        refs = refs[2:]
    go, misc_sum, kt, d_row, near_sum, far_sum = refs
    rows_total, features = ks[0].shape
    blocks = rows_total // BLK
    share = rows_total // shares
    me = idx[0]
    for step in range(shares):
        start = pl.multiple_of((me ^ step) * share, share)
        go[pl.ds(start, share), :] = go_parts[step][...]
    for index in range(held):
        for block in range(blocks):
            cols = pl.ds(block * BLK, BLK)
            kt[:, pl.ds((index * blocks + block) * BLK, BLK)] = (
                ks[index][cols, :].astype(F32).T.astype(BF16)
            )
        if index < piece:
            gk[index][...] = gk_in[index][...]
            gv[index][...] = gv_in[index][...]
        else:
            gk[index][...] = jnp.zeros_like(gk[index])
            gv[index][...] = jnp.zeros_like(gv[index])
    if piece:
        acc[...] = acc_in[...]
    else:
        acc[...] = jnp.zeros_like(acc)
    for block in range(blocks):
        cols = pl.ds(block * BLK, BLK)
        product = go[cols, :].astype(F32).T * ot[:, cols]
        for head in range(heads):
            part = product[head * head_size : (head + 1) * head_size, :]
            d_row[head : head + 1, cols] = jnp.sum(part, axis=0, keepdims=True)
    near_sum[...] = jnp.zeros_like(near_sum)
    far_sum[...] = jnp.zeros_like(far_sum)
    key_at = lax.broadcasted_iota(jnp.int32, (BLK, BLK), 0)
    other_at = lax.broadcasted_iota(jnp.int32, (BLK, BLK), 1)
    flip = (key_at + other_at == BLK - 1).astype(F32)
    seg_row = seg[...].astype(F32)
    seg_col = column_of(seg[...])

    def one_head(head, carry):
        part = pl.ds(pl.multiple_of(head * head_size, head_size), head_size)
        lanes = lax.broadcasted_iota(jnp.int32, (BLK, features), 1)
        inside = (lanes >= head * head_size) & (lanes < (head + 1) * head_size)
        for block in range(blocks):
            qb = piece * blocks + block
            cols = pl.ds(block * BLK, BLK)
            q_tile = qh[head, cols, :]
            go_tile = jnp.where(inside, go[cols, :].astype(F32), 0.0).astype(BF16)
            log_total = lse[pl.ds(head, 1), cols]
            d_tile = d_row[pl.ds(head, 1), cols]
            gq = jnp.zeros((head_size, BLK), F32)
            for kb in range(qb + 1):
                index = kb // blocks
                keys = pl.ds(kb % blocks * BLK, BLK)
                delta = qb - kb
                scores = masked_scores(
                    ks[index][keys, :], q_tile, tile_bias(bias, far, head, delta),
                    seg_col[kb * BLK : (kb + 1) * BLK, :],
                    seg_row[:, qb * BLK : (qb + 1) * BLK], delta == 0,
                )
                probs = jnp.exp(scores - log_total)
                gs = probs * (dot(vs[index][keys, :], go_tile, NT) - d_tile)
                if delta < 2:
                    acc[2 * head + delta] += gs
                else:
                    far_sum[pl.ds(head, 1), :] += jnp.sum(gs, axis=0, keepdims=True)
                gs_low = gs.astype(BF16)
                gv[index][keys, :] += dot(probs.astype(BF16), go_tile)
                gk[index][keys, :] += dot(gs_low, q_tile)
                gq = gq + dot(kt[part, kb * BLK : (kb + 1) * BLK], gs_low)
            gq_t[part, cols] = gq * (head_size**-0.5)
        return carry

    lax.fori_loop(0, heads, one_head, 0)
    if not last:
        return
    gqs = [*(gq_in if piece else ()), gq_t]
    for index in range(held):
        for block in range(blocks):
            rows = pl.ds(block * BLK, BLK)
            out = pl.ds((index * blocks + block) * BLK, BLK)
            gproj[0, out, :] = gqs[index][:, rows].T.astype(BF16)
            gproj[1, out, :] = gk[index][rows, :].astype(BF16)
            gproj[2, out, :] = gv[index][rows, :].astype(BF16)
    gain_one = jnp.zeros_like(gain_two)
    for step in range(shares):
        for index in range(pieces):
            start = index * rows_total + (me ^ step) * share
            rows = pl.ds(pl.multiple_of(start, share), share)
            total = dot(gproj[0, rows, :], w[0])
            total = total + dot(gproj[1, rows, :], w[1])
            total = total + dot(gproj[2, rows, :], w[2])
            gn_parts[step][pl.ds(index * share, share), :] = total.astype(BF16)
            x = tok[rows, :].astype(F32)
            gain_one = gain_one + jnp.sum(total * (x * row_scale(x)), axis=0, keepdims=True)
    for head in range(heads):
        for delta in range(2):
            turned = dot(flip, acc[2 * head + delta], NN, HIGHEST)
            wide = jnp.concatenate([turned, jnp.zeros_like(turned)], axis=1)
            sheared = pltpu.roll(wide, 0, 1, stride=1, stride_axis=0)
            near_sum[delta, head : head + 1, :] = jnp.sum(sheared, axis=0, keepdims=True)
    summed = dot(near_sum[0], hot[0], NN, HIGHEST) + dot(near_sum[1], hot[1], NN, HIGHEST)
    buckets = lax.broadcasted_iota(jnp.int32, summed.shape, 1)
    beyond = jnp.sum(far_sum[...], axis=1, keepdims=True)
    summed = summed + jnp.where(buckets == NB - 1, beyond, 0.0)
    misc_sum[...] = jnp.zeros_like(misc_sum)
    misc_sum[pl.ds(pl.multiple_of(me * 8, 8), 8), 0:NB] = summed
    misc_sum[8 * shares : 8 * shares + 8, :] = router[...]
    misc_sum[8 * shares + 8 : 8 * shares + 9, :] = gain_one
    misc_sum[8 * shares + 9 : 8 * shares + 10, :] = gain_two[...]
    misc[...] = misc_sum[...].astype(BF16)


def qkv_weights_kernel(pieces, *refs):
    normed = refs[:pieces]
    gproj, out = refs[pieces:]
    rows_total = normed[0].shape[0]
    for c in range(3):
        total = dot(gproj[c, pl.ds(0, rows_total), :], normed[0][...], TN)
        for index in range(1, pieces):
            rows = pl.ds(index * rows_total, rows_total)
            total = total + dot(gproj[c, rows, :], normed[index][...], TN)
        out[c] = total.astype(BF16)


def gelu_pair(values):
    squared = values * values
    bent = jnp.tanh(values * (0.7978845608028654 + 0.7978845608028654 * 0.044715 * squared))
    half = 0.5 * (1.0 + bent)
    lifted = values * half
    slope = 0.7978845608028654 + 3.0 * 0.7978845608028654 * 0.044715 * squared
    return lifted, half + lifted * (1.0 - bent) * slope


def padded_rows(values, rows):
    missing = jnp.zeros((rows - values.shape[0], values.shape[1]), values.dtype)
    return jnp.concatenate([values, missing], axis=0)


def moe_fwd_kernel(piece, pieces, shares, experts, idx, *refs):
    att, refs = refs[:shares], refs[shares:]
    if piece == 0:
        wo_own, wo_swapped, refs = refs[0], refs[1], refs[2:]
        wo_fetched, refs = refs[: shares - 1], refs[shares - 1 :]
    else:
        wo, refs = refs[0], refs[1:]
    tok, gain, router, routes, cot, w_in, w_down = refs[:7]
    refs = refs[7:]
    parts, refs = refs[:shares], refs[shares:]
    if piece == 0:
        wo, refs = refs[0], refs[1:]
    normed, own, gates, ggate, act, slope, acc = refs
    rows_total = tok.shape[0] // pieces
    base = piece * rows_total
    share = rows_total // shares
    me = idx[0]
    expert = pl.program_id(0)

    @pl.when(expert == 0)
    def _():
        gain_row = gain[...].astype(F32).reshape(1, -1)
        router_wide = padded_rows(router[...].astype(F32), LANES).astype(BF16)
        if piece == 0:
            half = wo_own.shape[0] // 2
            mine = pl.ds(pl.multiple_of(idx[1] * half, half), half)
            other = pl.ds(pl.multiple_of((1 - idx[1]) * half, half), half)
            wo[0] = wo_own[...]
            for step in range(1, shares):
                wo[step, mine, :] = wo_fetched[step - 1][...]
                wo[step, other, :] = wo_swapped[step - 1]
        for block in range(rows_total // BLK):
            rows = pl.ds(block * BLK, BLK)
            outer = pl.ds(base + block * BLK, BLK)
            attn = dot(att[0][rows, :], wo[0])
            for step in range(1, shares):
                attn = attn + dot(att[step][rows, :], wo[step])
            hidden = tok[outer, :].astype(F32) + attn
            acc[rows, :] = hidden
            n = (hidden * row_scale(hidden) * gain_row).astype(BF16)
            normed[rows, :] = n
            logits = dot(n, router_wide, NT)
            lanes = lax.broadcasted_iota(jnp.int32, logits.shape, 1)
            first = lanes == routes[outer, 0:1]
            second = lanes == routes[outer, 1:2]
            one = jnp.sum(jnp.where(first, logits, 0.0), axis=1, keepdims=True)
            two = jnp.sum(jnp.where(second, logits, 0.0), axis=1, keepdims=True)
            peak = jnp.maximum(one, two)
            one = jnp.exp(one - peak)
            two = jnp.exp(two - peak)
            both = one + two
            gates[rows, :] = jnp.where(first, one / both, jnp.where(second, two / both, 0.0))
        own[...] = acc[pl.ds(pl.multiple_of(me * share, share), share), :]
        acc[...] = jnp.zeros_like(acc)
        ggate[...] = jnp.zeros_like(ggate)

    for block in range(rows_total // ROWS):
        rows = pl.ds(block * ROWS, ROWS)
        outer = pl.ds(base + block * ROWS, ROWS)
        lifted, bend = gelu_pair(dot(normed[rows, :], w_in[0]))
        lifted = lifted.astype(BF16)
        act[0, rows, :] = lifted
        slope[0, rows, :] = bend.astype(BF16)
        out = dot(lifted, w_down[0])
        gate = lane_pick(gates[rows, :], expert)
        acc[rows, :] += gate * out
        pulled = jnp.sum(cot[outer, :].astype(F32) * out, axis=1, keepdims=True)
        held = ggate[rows, :]
        lanes = lax.broadcasted_iota(jnp.int32, held.shape, 1)
        ggate[rows, :] = jnp.where(lanes == expert, pulled, held)

    @pl.when(expert == experts - 1)
    def _():
        for step in range(shares):
            start = pl.multiple_of((me ^ step) * share, share)
            parts[step][...] = acc[pl.ds(start, share), :].astype(BF16)


def moe_bwd_kernel(piece, shares, experts, idx, *refs):
    gates, ggate, cot, slope, router, w_in, w_down = refs[:7]
    refs = refs[7:]
    parts, refs = refs[:shares], refs[shares:]
    glog, gpre, acc = refs
    rows_total = gates.shape[0]
    base = piece * rows_total
    share = rows_total // shares
    me = idx[0]
    expert = pl.program_id(0)

    @pl.when(expert == 0)
    def _():
        router_wide = padded_rows(router[...].astype(F32), LANES)
        for block in range(rows_total // ROWS):
            rows = pl.ds(block * ROWS, ROWS)
            g, gg = gates[rows, :], ggate[rows, :]
            back = g * (gg - jnp.sum(g * gg, axis=1, keepdims=True))
            glog[rows, :] = back
            acc[rows, :] = dot(back, router_wide, NN, HIGHEST)

    for block in range(rows_total // ROWS):
        rows = pl.ds(block * ROWS, ROWS)
        gate = lane_pick(gates[rows, :], expert)
        weighted = cot[pl.ds(base + block * ROWS, ROWS), :].astype(F32)
        weighted = (gate * weighted).astype(BF16)
        gp = (dot(weighted, w_down[0], NT) * slope[0, rows, :].astype(F32)).astype(BF16)
        gpre[0, rows, :] = gp
        acc[rows, :] += dot(gp, w_in[0], NT)

    @pl.when(expert == experts - 1)
    def _():
        for step in range(shares):
            start = pl.multiple_of((me ^ step) * share, share)
            parts[step][...] = acc[pl.ds(start, share), :].astype(BF16)


def moe_weights_kernel(pieces, cot, *refs):
    gates, refs = refs[:pieces], refs[pieces:]
    glog, refs = refs[:pieces], refs[pieces:]
    normed, refs = refs[:pieces], refs[pieces:]
    act, refs = refs[:pieces], refs[pieces:]
    gpre, refs = refs[:pieces], refs[pieces:]
    out, router = refs
    rows_total = normed[0].shape[0]
    expert = pl.program_id(0)

    @pl.when(expert == 0)
    def _():
        total = jnp.zeros((LANES, cot.shape[1]), F32)
        for index in range(pieces):
            back = glog[index][...]
            high = back.astype(BF16)
            low = (back - high.astype(F32)).astype(BF16)
            total = total + dot(high, normed[index][...], TN)
            total = total + dot(low, normed[index][...], TN)
        router[...] = total[0:8, :]

    grad_in = jnp.zeros((normed[0].shape[1], gpre[0].shape[2]), F32)
    grad_down = jnp.zeros((act[0].shape[2], cot.shape[1]), F32)
    for index in range(pieces):
        gate = lane_pick(gates[index][...], expert)
        weighted = cot[pl.ds(index * rows_total, rows_total), :].astype(F32)
        weighted = (gate * weighted).astype(BF16)
        grad_in = grad_in + dot(normed[index][...], gpre[index][0], TN)
        grad_down = grad_down + dot(act[index][0], weighted, TN)
    out[0, 0] = grad_in.astype(BF16)
    out[0, 1] = grad_down.astype(BF16)


def hidden_back_kernel(piece, pieces, shares, got, idx, *refs):
    gx, refs = refs[:got], refs[got:]
    wo, own, cot, gain = refs[:4]
    refs = refs[4:]
    ga, refs = refs[:shares], refs[shares:]
    gh, gh_low, ggain = refs
    share = own.shape[0]
    grad = gx[0][...].astype(F32)
    for step in range(1, got):
        grad = grad + gx[step][...].astype(F32)
    hidden = own[...]
    scale = row_scale(hidden)
    unit = hidden * scale
    ggain[...] = jnp.sum(grad * unit, axis=0, keepdims=True)
    gained = grad * gain[...].astype(F32).reshape(1, -1)
    start = piece * (cot.shape[0] // pieces) + idx[0] * share
    mine = cot[pl.ds(pl.multiple_of(start, share), share), :].astype(F32)
    back = mine + scale * (gained - unit * jnp.mean(gained * unit, axis=-1, keepdims=True))
    gh[...] = back
    low = back.astype(BF16)
    gh_low[...] = low
    for step in range(shares):
        ga[step][...] = dot(low, wo[step], NT).astype(BF16)


def w_out_back_kernel(pieces, shares, idx, *refs):
    att, refs = refs[: pieces * shares], refs[pieces * shares :]
    gh_low, out = refs[:pieces], refs[pieces]
    share = gh_low[0].shape[0]
    rows = pl.ds(pl.multiple_of(idx[0] * share, share), share)
    for step in range(shares):
        total = dot(att[step][rows, :], gh_low[0][...], TN)
        for index in range(1, pieces):
            total = total + dot(att[index * shares + step][rows, :], gh_low[index][...], TN)
        out[step] = total.astype(BF16)


def join_kernel(pieces, count, *refs):
    own, refs = refs[:pieces], refs[pieces:]
    got, out = refs[: pieces * count], refs[pieces * count]
    share = own[0].shape[0]
    for index in range(pieces):
        total = own[index][...]
        for step in range(count):
            total = total + got[index * count + step][...].astype(F32)
        out[pl.ds(index * share, share), :] = total.astype(BF16)


def input_back_kernel(pieces, got, idx, *refs):
    gn, refs = refs[:got], refs[got:]
    ghs, refs = refs[:pieces], refs[pieces:]
    tok, gain, gt = refs
    share = ghs[0].shape[0]
    gain_row = gain[...].astype(F32).reshape(1, -1)
    for index in range(pieces):
        rows = pl.ds(index * share, share)
        grad = gn[0][rows, :].astype(F32)
        for step in range(1, got):
            grad = grad + gn[step][rows, :].astype(F32)
        start = index * (tok.shape[0] // pieces) + idx[0] * share
        x = tok[pl.ds(pl.multiple_of(start, share), share), :].astype(F32)
        scale = row_scale(x)
        unit = x * scale
        gained = grad * gain_row
        back = scale * (gained - unit * jnp.mean(gained * unit, axis=-1, keepdims=True))
        gt[rows, :] = (ghs[index][...] + back).astype(BF16)


def place_kernel(pieces, shares, idx, *refs):
    blocks, out = refs[:shares], refs[shares]
    rows_total = out.shape[0] // pieces
    share = rows_total // shares
    for step in range(shares):
        owner = idx[0] ^ step
        for index in range(pieces):
            start = pl.multiple_of(index * rows_total + owner * share, share)
            got = blocks[step][pl.ds(index * share, share), :]
            out[pl.ds(start, share), :] = got.astype(out.dtype)


ROWS = 512
PIECES = 1

SMEM = pl.BlockSpec(memory_space=pltpu.SMEM)
VMEM = pl.BlockSpec(memory_space=pltpu.VMEM)


def shaped(shape, dtype):
    return jax.ShapeDtypeStruct(shape, dtype)


def whole_call(kernel, outs, args, scratch=(), flops=0, moved=0, with_index=True):
    specs = ([SMEM] if with_index else []) + [VMEM] * (len(args) - (1 if with_index else 0))
    return pl.pallas_call(
        kernel,
        out_shape=outs,
        in_specs=specs,
        out_specs=[VMEM] * len(outs),
        scratch_shapes=list(scratch),
        compiler_params=pltpu.CompilerParams(vmem_limit_bytes=VMEM_LIMIT),
        cost_estimate=pl.CostEstimate(flops=flops, bytes_accessed=moved, transcendentals=0),
    )(*args)


def swap(value, axis, bit):
    count = lax.axis_size(axis)
    return lax.ppermute(value, axis, [(i, i ^ bit) for i in range(count)])


def sum_over(value, axis):
    bit = 1
    while bit < lax.axis_size(axis):
        value = value + swap(value, axis, bit)
        bit *= 2
    return value


def gather_parts(value, axis):
    count = lax.axis_size(axis)
    if count != 4:
        return [value] + [swap(value, axis, bit) for bit in range(1, count)]
    two = swap(value, axis, 2)
    one = swap(value, axis, 1)
    return [value, one, two, swap(after(two, one), axis, 1)]


def reduce_near(parts, axis):
    return swap(parts[3], axis, 1), swap(parts[1], axis, 1)


def reduce_far(parts, near, axis):
    pair = (parts[2].astype(F32) + near[0].astype(F32)).astype(parts[2].dtype)
    return [parts[0], near[1], swap(pair, axis, 2)], pair


def exchange(parts, axis):
    return [parts[0]] + [swap(parts[bit], axis, bit) for bit in range(1, len(parts))]


def halves_of(value, axis, chosen):
    half = value.shape[axis] // 2
    keep = lax.dynamic_slice_in_dim(value, chosen * half, half, axis)
    send = lax.dynamic_slice_in_dim(value, (1 - chosen) * half, half, axis)
    return keep, send


def bits_of(axis):
    count = lax.axis_size(axis)
    return [1 << level for level in range(count.bit_length() - 1)]


def gather_back(value, mesh_axis, axis):
    me = lax.axis_index(mesh_axis)
    for bit in reversed(bits_of(mesh_axis)):
        got = swap(value, mesh_axis, bit)
        low = (me // bit) % 2 == 0
        value = jnp.concatenate(
            [jnp.where(low, value, got), jnp.where(low, got, value)], axis=axis
        )
    return value


def together(*values):
    return lax.optimization_barrier(values)


def after(value, *others):
    return lax.optimization_barrier((value, *others))[0]


def body(
    tokens, segments, routes, grad_out, gain_attn, w_qkv, w_out, rel_bias,
    gain_moe, w_router, w_in, w_down,
):
    tok_rows, width = tokens.shape
    heads = rel_bias.shape[1]
    features = w_qkv.shape[2]
    head_size = features // heads
    experts, _, hidden_units = w_in.shape
    shares = lax.axis_size("tensor")
    rows = tok_rows // PIECES
    share = rows // shares
    me = lax.axis_index("tensor").astype(jnp.int32)
    side = (lax.axis_index("dp") % 2).astype(jnp.int32)
    idx = jnp.stack([me, side])
    mib = 1 << 20
    others = range(1, shares)
    four = shares == 4

    half_rows = features // 2
    my_half = lax.dynamic_slice_in_dim(w_out, side * half_rows, half_rows, 0)
    halves = [swap(my_half, "tensor", by) for by in others]

    build_hot, gather_hot = near_tables()
    build_hot = jnp.asarray(np.swapaxes(build_hot, 1, 2), BF16)
    gather_hot = jnp.asarray(gather_hot, F32)
    w_qkv_t = jnp.swapaxes(w_qkv, 1, 2)
    router_t = w_router.T

    normed_one, qh, k, v, _, att, ot, lse, bias, far = whole_call(
        functools.partial(attn_fwd_kernel, 0, PIECES, heads, head_size),
        [
            shaped((rows, width), BF16),
            shaped((heads, rows, features), BF16),
            shaped((rows, features), BF16),
            shaped((rows, features), BF16),
            shaped((features, rows), BF16),
            shaped((rows, features), BF16),
            shaped((features, rows), F32),
            shaped((8, rows), F32),
            shaped((2 * heads, BLK, BLK), F32),
            shaped((8, LANES), F32),
        ],
        [tokens, gain_attn, w_qkv_t, segments, rel_bias.T, build_hot],
        flops=6 * 10**9, moved=8 * mib, with_index=False,
    )
    att = after(att, *halves)
    atts = gather_parts(att, "tensor")
    swapped = swap(after(jnp.stack(halves), att), "dp", 1)

    full = lambda shape: pl.BlockSpec(shape, lambda e: (0,) * len(shape))
    per_expert = lambda shape: pl.BlockSpec((1,) + shape, lambda e: (e, 0, 0))
    params = pltpu.CompilerParams(
        vmem_limit_bytes=VMEM_LIMIT, dimension_semantics=("arbitrary",)
    )
    moe_flops = 4 * experts * rows * width * hidden_units

    fwd = pl.pallas_call(
        functools.partial(moe_fwd_kernel, 0, PIECES, shares, experts),
        grid=(experts,),
        in_specs=[SMEM]
        + [full((rows, features))] * shares
        + [full((features, width)), full((shares - 1, half_rows, width))]
        + [full((half_rows, width))] * (shares - 1)
        + [
            full((rows, width)), full((width,)), full((experts, width)),
            full((rows, 2)), full((rows, width)),
            per_expert((width, hidden_units)), per_expert((hidden_units, width)),
        ],
        out_specs=[full((share, width))] * shares
        + [
            full((shares, features, width)), full((rows, width)),
            full((share, width)), full((rows, LANES)), full((rows, LANES)),
            per_expert((rows, hidden_units)), per_expert((rows, hidden_units)),
        ],
        out_shape=[shaped((share, width), BF16)] * shares
        + [
            shaped((shares, features, width), BF16),
            shaped((rows, width), BF16),
            shaped((share, width), F32),
            shaped((rows, LANES), F32),
            shaped((rows, LANES), F32),
            shaped((experts, rows, hidden_units), BF16),
            shaped((experts, rows, hidden_units), BF16),
        ],
        scratch_shapes=[pltpu.VMEM((rows, width), F32)],
        compiler_params=params,
        cost_estimate=pl.CostEstimate(
            flops=moe_flops, bytes_accessed=32 * mib, transcendentals=0
        ),
    )(
        idx, *atts, w_out, swapped, *halves, tokens, gain_moe, router_t, routes, grad_out,
        w_in, w_down,
    )
    moe_parts = fwd[:shares]
    wo, normed_two, own_hidden, gates, ggate, act, slope = fwd[shares:]
    if four:
        moe_near = reduce_near(moe_parts, "tensor")
    else:
        moe_near = exchange(moe_parts, "tensor")[1:]

    bwd = pl.pallas_call(
        functools.partial(moe_bwd_kernel, 0, shares, experts),
        grid=(experts,),
        in_specs=[
            SMEM, full((rows, LANES)), full((rows, LANES)), full((rows, width)),
            per_expert((rows, hidden_units)), full((experts, width)),
            per_expert((width, hidden_units)), per_expert((hidden_units, width)),
        ],
        out_specs=[full((share, width))] * shares
        + [full((rows, LANES)), per_expert((rows, hidden_units))],
        out_shape=[shaped((share, width), BF16)] * shares
        + [
            shaped((rows, LANES), F32),
            shaped((experts, rows, hidden_units), BF16),
        ],
        scratch_shapes=[pltpu.VMEM((rows, width), F32)],
        compiler_params=params,
        cost_estimate=pl.CostEstimate(
            flops=moe_flops, bytes_accessed=26 * mib, transcendentals=0
        ),
    )(idx, gates, ggate, grad_out, slope, router_t, w_in, w_down)
    gx_parts = [after(part, *moe_near) for part in bwd[:shares]]
    glog, gpre = bwd[shares:]
    gx_near = reduce_near(gx_parts, "tensor") if four else exchange(gx_parts, "tensor")[1:]

    expert_grads, router_rows = pl.pallas_call(
        functools.partial(moe_weights_kernel, PIECES),
        grid=(experts,),
        in_specs=[
            full((rows, width)), full((rows, LANES)), full((rows, LANES)), full((rows, width)),
            per_expert((rows, hidden_units)), per_expert((rows, hidden_units)),
        ],
        out_specs=[
            pl.BlockSpec((1, 2, width, width), lambda e: (e, 0, 0, 0)), full((8, width))
        ],
        out_shape=[shaped((experts, 2, width, width), BF16), shaped((8, width), F32)],
        compiler_params=params,
        cost_estimate=pl.CostEstimate(
            flops=moe_flops, bytes_accessed=26 * mib, transcendentals=0
        ),
    )(grad_out, gates, glog, normed_two, act, gpre)
    expert_rows = after(expert_grads.reshape(experts * 2 * width, width), *gx_near)
    expert_rows = lax.psum_scatter(expert_rows, "dp", scatter_dimension=0, tiled=True)

    if four:
        gx_near = after(gx_near[0], router_rows), gx_near[1]
        gx_got, _ = reduce_far(gx_parts, gx_near, "tensor")
    else:
        gx_got = [gx_parts[0], *gx_near]
    back = whole_call(
        functools.partial(hidden_back_kernel, 0, PIECES, shares, len(gx_got)),
        [shaped((share, features), BF16)] * shares
        + [shaped((share, width), F32), shaped((share, width), BF16), shaped((1, width), F32)],
        [idx, *gx_got, wo, own_hidden, grad_out, gain_moe],
        flops=3 * 10**8, moved=5 * mib,
    )
    go = exchange(back[:shares], "tensor")
    grad_hidden, gh_low, ggain_two = back[shares:]

    if four:
        moe_near = after(moe_near[0], *go[1:]), moe_near[1]
        moe_got, _ = reduce_far(moe_parts, moe_near, "tensor")
    else:
        moe_got = [moe_parts[0], *moe_near]
    result_share = whole_call(
        functools.partial(join_kernel, PIECES, len(moe_got)),
        [shaped((share, width), BF16)],
        [own_hidden, *moe_got],
        moved=3 * mib, with_index=False,
    )[0]
    attn_back = whole_call(
        functools.partial(attn_bwd_kernel, 0, PIECES, heads, head_size, shares),
        [shaped((share, width), BF16)] * shares
        + [shaped((3, rows, features), BF16), shaped((features, width), BF16)],
        [
            idx, *go, tokens, router_rows, ggain_two, qh, ot, lse, k, v, bias, far, segments,
            w_qkv_t, gather_hot,
        ],
        [pltpu.VMEM((rows, features), F32)] * 2
        + [
            pltpu.VMEM((features, rows), F32),
            pltpu.VMEM((2 * heads, BLK, BLK), F32),
            pltpu.VMEM((rows, features), BF16),
            pltpu.VMEM((features, width), F32),
            pltpu.VMEM((features, rows), BF16),
            pltpu.VMEM((8, rows), F32),
            pltpu.VMEM((2, 8, 2 * BLK), F32),
            pltpu.VMEM((8, BLK), F32),
        ],
        flops=14 * 10**9, moved=8 * mib,
    )
    gn_parts = [after(part, moe_got[-1]) for part in attn_back[:shares]]
    gproj, misc = attn_back[shares:]

    qkv_rows = whole_call(
        functools.partial(qkv_weights_kernel, PIECES),
        [shaped((3, features, width), BF16)],
        [normed_one, gproj],
        flops=10**9, moved=4 * mib, with_index=False,
    )[0]
    w_out_rows = whole_call(
        functools.partial(w_out_back_kernel, PIECES, shares),
        [shaped((shares, features, width), BF16)],
        [idx, *atts, after(gh_low, gproj)],
        flops=3 * 10**8, moved=4 * mib,
    )[0]
    late = jnp.concatenate([qkv_rows, misc[None], w_out_rows], axis=0)
    if four:
        near = reduce_near(gn_parts, "tensor")
        near = after(near[0], late, near[1]), near[1]
        gn_got, mark = reduce_far(gn_parts, near, "tensor")
    else:
        gn_got = exchange(gn_parts, "tensor")
        mark = gn_got[-1]

    place = lax.axis_index("dp")

    def halve(value, bit, *ready):
        keep, send = halves_of(value, 1, (place // bit) % 2)
        got = swap(after(send, *ready), "dp", bit)
        return (keep.astype(F32) + got.astype(F32)).astype(BF16)

    late = after(late, mark)
    late = halve(late, 1)
    grad_hidden = after(grad_hidden, late)

    expert_rows = after(expert_rows, mark)
    gt_share = whole_call(
        functools.partial(input_back_kernel, PIECES, len(gn_got)),
        [shaped((share, width), BF16)],
        [idx, *gn_got, grad_hidden, tokens, gain_attn],
        moved=5 * mib,
    )[0]
    bits = bits_of("dp")
    if four:
        keep, send = halves_of(late, 1, (place // bits[1]) % 2)
        got = together(
            swap(gt_share, "tensor", 2), swap(gt_share, "tensor", 1),
            swap(after(send, gt_share), "dp", bits[1]),
        )
        gt_got = [gt_share, got[1], got[0]]
        late = (keep.astype(F32) + got[2].astype(F32)).astype(BF16)
        share_now = after(result_share, got[0])
        keep, send = halves_of(late, 1, (place // bits[2]) % 2)
        got = together(
            swap(gt_got[2], "tensor", 1), swap(share_now, "tensor", 2),
            swap(share_now, "tensor", 1), swap(send, "dp", bits[2]),
        )
        gt_got.append(got[0])
        result_got = [result_share, got[2], got[1]]
        late = (keep.astype(F32) + got[3].astype(F32)).astype(BF16)
        for bit in bits[3:]:
            late = halve(late, bit)
    else:
        gt_got = gather_parts(gt_share, "tensor")
        result_got = gather_parts(result_share, "tensor")
        for bit in bits[1:]:
            late = halve(late, bit)
    grad_tokens = whole_call(
        functools.partial(place_kernel, PIECES, shares),
        [shaped((rows, width), F32)], [idx, *gt_got], moved=5 * mib,
    )[0]

    sent = [swap(jnp.stack([late[4 + by], late[3]]), "tensor", by) for by in others]
    if four:
        *sent, last = together(*sent, swap(result_got[2], "tensor", 1))
        result_got.append(last)
    result = whole_call(
        functools.partial(place_kernel, PIECES, shares),
        [shaped((rows, width), BF16)], [idx, *result_got], moved=3 * mib,
    )[0]
    out_sum, small = late[4].astype(F32), [late[3]]
    for got in sent:
        out_sum = out_sum + got[0].astype(F32)
        small.append(got[1])
    small = [one.astype(F32) for one in small]
    while len(small) > 1:
        small = [small[at] + small[at + 1] for at in range(0, len(small), 2)]
    late = jnp.concatenate(
        [late[:3], jnp.stack([small[0].astype(BF16), out_sum.astype(BF16)])], axis=0
    )

    expert_rows = lax.all_gather(expert_rows, "dp", axis=0, tiled=True)
    expert_rows = expert_rows.reshape(experts, 2, width, width)
    grad_w_in = expert_rows[:, 0].astype(F32)
    grad_w_down = expert_rows[:, 1].astype(F32)
    late = gather_back(after(late, grad_w_in, grad_w_down, grad_tokens), "dp", 1)
    grad_w_qkv = jnp.swapaxes(late[:3], 1, 2).astype(F32)
    grad_w_out = late[4].astype(F32)
    small = late[3].astype(F32)
    grad_rel = lax.dynamic_slice_in_dim(small, me * 8, 8, 0)
    first = 8 * shares
    return (
        result,
        grad_tokens,
        small[first + 8],
        grad_w_qkv,
        grad_w_out,
        grad_rel[:heads, :NB].T,
        small[first + 9],
        small[first : first + experts].T,
        grad_w_in,
        grad_w_down,
    )


def solution(mesh):
    placed = (
        P("dp", None),
        P("dp", None),
        P("dp", None),
        P("dp", None),
        P(),
        P(None, None, "tensor"),
        P("tensor", None),
        P(None, "tensor"),
        P(),
        P(),
        P(None, None, "tensor"),
        P(None, "tensor", None),
    )
    return jax.shard_map(
        body,
        mesh=mesh,
        in_specs=placed,
        out_specs=(
            P("dp", None),
            P("dp", None),
            P(),
            P(None, None, "tensor"),
            P("tensor", None),
            P(None, "tensor"),
            P(),
            P(),
            P(None, None, "tensor"),
            P(None, "tensor", None),
        ),
        check_vma=False,
    )
```

```python
import functools
import math

import jax
import jax.numpy as jnp
import numpy as np
from jax import lax
from jax.experimental import pallas as pl
from jax.experimental.pallas import tpu as pltpu
from jax.sharding import PartitionSpec as P

NB = 32
DIST = 128
EPSILON = 1e-06
NEGATIVE = -1e30
HIGHEST = lax.Precision.HIGHEST
F32 = jnp.float32
BF16 = jnp.bfloat16
BLK = 256
LANES = 128
VMEM_LIMIT = 56 * 1024 * 1024

NN = (((1,), (0,)), ((), ()))
NT = (((1,), (1,)), ((), ()))
TN = (((0,), (0,)), ((), ()))


def dot(a, b, dims=NN, precision=None):
    return lax.dot_general(a, b, dims, precision=precision, preferred_element_type=F32)


def bucket_of(distance):
    halfway = NB // 2
    thresholds = [
        int(math.ceil(halfway * (DIST / halfway) ** (step / halfway))) for step in range(halfway)
    ]
    beyond = sum((distance >= threshold).astype(np.int64) for threshold in thresholds)
    return np.where(distance < halfway, distance, halfway - 1 + beyond)


def near_tables():
    lanes = np.arange(2 * BLK)
    offset = np.where(lanes < BLK, lanes, lanes - 2 * BLK)
    build = np.stack([np.maximum(offset, 0), np.maximum(BLK + offset, 0)])
    gather = np.stack([lanes - (BLK - 1), lanes + 1])
    eye = np.eye(NB, dtype=np.float32)
    build_hot = eye[bucket_of(build)]
    gather_hot = eye[bucket_of(np.maximum(gather, 0))] * (gather >= 0)[..., None]
    return build_hot, gather_hot


def row_scale(values):
    return lax.rsqrt(jnp.mean(values * values, axis=-1, keepdims=True) + EPSILON)


def lane_pick(values, index):
    lanes = lax.broadcasted_iota(jnp.int32, values.shape, 1)
    return jnp.sum(jnp.where(lanes == index, values, 0.0), axis=1, keepdims=True)


def masked_scores(k_tile, qh_tile, bias, seg_k, seg_q, diagonal):
    scores = dot(k_tile, qh_tile, NT) + bias
    allowed = seg_k == seg_q
    if diagonal:
        key_at = lax.broadcasted_iota(jnp.int32, scores.shape, 0)
        query_at = lax.broadcasted_iota(jnp.int32, scores.shape, 1)
        allowed = allowed & (key_at <= query_at)
    return jnp.where(allowed, scores, NEGATIVE)


def tile_bias(bias_ref, far_ref, head, delta):
    if delta < 2:
        return bias_ref[2 * head + delta]
    return far_ref[pl.ds(head, 1), 0:1]


def column_of(row):
    spread = jnp.broadcast_to(row.astype(F32), (8, row.shape[1]))
    return spread.T[:, 0:1]


def attn_fwd_kernel(piece, pieces, heads, head_size, *refs):
    tok, gain, w, seg = refs[:4]
    refs = refs[4:]
    if piece == 0:
        rel, build = refs[:2]
        refs = refs[2:]
    else:
        bias, far = refs[:2]
        refs = refs[2:]
    old_k, refs = refs[:piece], refs[piece:]
    old_vt, refs = refs[:piece], refs[piece:]
    normed, qh, k, v, vt, att, ot, lse = refs[:8]
    if piece == 0:
        bias, far = refs[8:]
    keys_of, vt_of = [*old_k, k], [*old_vt, vt]
    rows_total = tok.shape[0] // pieces
    base = piece * rows_total
    features = w.shape[1]
    blocks = rows_total // BLK
    gain_row = gain[...].astype(F32).reshape(1, -1)
    lanes = lax.broadcasted_iota(jnp.int32, (BLK, features), 1)
    for block in range(blocks):
        rows = pl.ds(block * BLK, BLK)
        x = tok[pl.ds(base + block * BLK, BLK), :].astype(F32)
        n = (x * row_scale(x) * gain_row).astype(BF16)
        normed[rows, :] = n
        q_rows = dot(n, w[0], NT).astype(BF16).astype(F32) * (head_size**-0.5)
        for head in range(heads):
            inside = (lanes >= head * head_size) & (lanes < (head + 1) * head_size)
            qh[head, rows, :] = jnp.where(inside, q_rows, 0.0).astype(BF16)
        k[rows, :] = dot(n, w[1], NT).astype(BF16)
        v_rows = dot(n, w[2], NT).astype(BF16)
        v[rows, :] = v_rows
        vt[:, rows] = v_rows.astype(F32).T.astype(BF16)
    if piece == 0:
        far[...] = jnp.zeros_like(far)
        far[0:heads, :] = jnp.broadcast_to(rel[:, NB - 1 : NB].astype(F32), (heads, LANES))
        for delta in range(2):
            near = dot(rel[...], build[delta])
            for head in range(heads):
                spread = jnp.broadcast_to(near[head : head + 1, :], (BLK, 2 * BLK))
                turned = pltpu.roll(spread, 0, 1, stride=1, stride_axis=0)
                bias[2 * head + delta] = turned[:, :BLK]
    lse[...] = jnp.zeros_like(lse)
    seg_row = seg[...].astype(F32)
    seg_col = column_of(seg[...])

    def one_head(head, carry):
        part = pl.ds(pl.multiple_of(head * head_size, head_size), head_size)
        for block in range(blocks):
            qb = piece * blocks + block
            cols = pl.ds(block * BLK, BLK)
            q_tile = qh[head, cols, :]
            tiles = []
            for kb in range(qb + 1):
                keys = pl.ds(kb % blocks * BLK, BLK)
                tiles.append(
                    masked_scores(
                        keys_of[kb // blocks][keys, :], q_tile,
                        tile_bias(bias, far, head, qb - kb),
                        seg_col[kb * BLK : (kb + 1) * BLK, :],
                        seg_row[:, qb * BLK : (qb + 1) * BLK], kb == qb,
                    )
                )
            peak = functools.reduce(
                jnp.maximum, [jnp.max(t, axis=0, keepdims=True) for t in tiles]
            )
            total = jnp.zeros((1, BLK), F32)
            out = jnp.zeros((head_size, BLK), F32)
            for kb in range(qb + 1):
                raised = jnp.exp(tiles[kb] - peak)
                total = total + jnp.sum(raised, axis=0, keepdims=True)
                values = vt_of[kb // blocks][part, pl.ds(kb % blocks * BLK, BLK)]
                out = out + dot(values, raised.astype(BF16))
            ot[part, cols] = out / total
            lse[pl.ds(head, 1), cols] = peak + jnp.log(total)
        return carry

    lax.fori_loop(0, heads, one_head, 0)
    for block in range(blocks):
        cols = pl.ds(block * BLK, BLK)
        att[cols, :] = ot[:, cols].T.astype(BF16)


def attn_bwd_kernel(piece, pieces, heads, head_size, shares, idx, *refs):
    held = piece + 1
    last = held == pieces
    go_parts, refs = refs[:shares], refs[shares:]
    tok, router, gain_two, qh, ot, lse = refs[:6]
    refs = refs[6:]
    ks, refs = refs[:held], refs[held:]
    vs, refs = refs[:held], refs[held:]
    bias, far, seg = refs[:3]
    refs = refs[3:]
    if piece:
        gk_in, refs = refs[:piece], refs[piece:]
        gv_in, refs = refs[:piece], refs[piece:]
        gq_in, refs = refs[:piece], refs[piece:]
        acc_in, refs = refs[0], refs[1:]
    if last:
        w, hot = refs[:2]
        refs = refs[2:]
        gn_parts, refs = refs[:shares], refs[shares:]
        gproj, misc = refs[:2]
        refs = refs[2:]
        gk, refs = refs[:held], refs[held:]
        gv, refs = refs[:held], refs[held:]
        gq_t, acc = refs[:2]
        refs = refs[2:]
    else:
        gk, refs = refs[:held], refs[held:]
        gv, refs = refs[:held], refs[held:]
        gq_t, acc = refs[:2]
        refs = refs[2:]
    go, misc_sum, kt, d_row, near_sum, far_sum = refs
    rows_total, features = ks[0].shape
    blocks = rows_total // BLK
    share = rows_total // shares
    me = idx[0]
    for step in range(shares):
        start = pl.multiple_of((me ^ step) * share, share)
        go[pl.ds(start, share), :] = go_parts[step][...]
    for index in range(held):
        for block in range(blocks):
            cols = pl.ds(block * BLK, BLK)
            kt[:, pl.ds((index * blocks + block) * BLK, BLK)] = (
                ks[index][cols, :].astype(F32).T.astype(BF16)
            )
        if index < piece:
            gk[index][...] = gk_in[index][...]
            gv[index][...] = gv_in[index][...]
        else:
            gk[index][...] = jnp.zeros_like(gk[index])
            gv[index][...] = jnp.zeros_like(gv[index])
    if piece:
        acc[...] = acc_in[...]
    else:
        acc[...] = jnp.zeros_like(acc)
    for block in range(blocks):
        cols = pl.ds(block * BLK, BLK)
        product = go[cols, :].astype(F32).T * ot[:, cols]
        for head in range(heads):
            part = product[head * head_size : (head + 1) * head_size, :]
            d_row[head : head + 1, cols] = jnp.sum(part, axis=0, keepdims=True)
    near_sum[...] = jnp.zeros_like(near_sum)
    far_sum[...] = jnp.zeros_like(far_sum)
    key_at = lax.broadcasted_iota(jnp.int32, (BLK, BLK), 0)
    other_at = lax.broadcasted_iota(jnp.int32, (BLK, BLK), 1)
    flip = (key_at + other_at == BLK - 1).astype(F32)
    seg_row = seg[...].astype(F32)
    seg_col = column_of(seg[...])

    def one_head(head, carry):
        part = pl.ds(pl.multiple_of(head * head_size, head_size), head_size)
        lanes = lax.broadcasted_iota(jnp.int32, (BLK, features), 1)
        inside = (lanes >= head * head_size) & (lanes < (head + 1) * head_size)
        for block in range(blocks):
            qb = piece * blocks + block
            cols = pl.ds(block * BLK, BLK)
            q_tile = qh[head, cols, :]
            go_tile = jnp.where(inside, go[cols, :].astype(F32), 0.0).astype(BF16)
            log_total = lse[pl.ds(head, 1), cols]
            d_tile = d_row[pl.ds(head, 1), cols]
            gq = jnp.zeros((head_size, BLK), F32)
            for kb in range(qb + 1):
                index = kb // blocks
                keys = pl.ds(kb % blocks * BLK, BLK)
                delta = qb - kb
                scores = masked_scores(
                    ks[index][keys, :], q_tile, tile_bias(bias, far, head, delta),
                    seg_col[kb * BLK : (kb + 1) * BLK, :],
                    seg_row[:, qb * BLK : (qb + 1) * BLK], delta == 0,
                )
                probs = jnp.exp(scores - log_total)
                gs = probs * (dot(vs[index][keys, :], go_tile, NT) - d_tile)
                if delta < 2:
                    acc[2 * head + delta] += gs
                else:
                    far_sum[pl.ds(head, 1), :] += jnp.sum(gs, axis=0, keepdims=True)
                gs_low = gs.astype(BF16)
                gv[index][keys, :] += dot(probs.astype(BF16), go_tile)
                gk[index][keys, :] += dot(gs_low, q_tile)
                gq = gq + dot(kt[part, kb * BLK : (kb + 1) * BLK], gs_low)
            gq_t[part, cols] = gq * (head_size**-0.5)
        return carry

    lax.fori_loop(0, heads, one_head, 0)
    if not last:
        return
    gqs = [*(gq_in if piece else ()), gq_t]
    for index in range(held):
        for block in range(blocks):
            rows = pl.ds(block * BLK, BLK)
            out = pl.ds((index * blocks + block) * BLK, BLK)
            gproj[0, out, :] = gqs[index][:, rows].T.astype(BF16)
            gproj[1, out, :] = gk[index][rows, :].astype(BF16)
            gproj[2, out, :] = gv[index][rows, :].astype(BF16)
    gain_one = jnp.zeros_like(gain_two)
    for step in range(shares):
        for index in range(pieces):
            start = index * rows_total + (me ^ step) * share
            rows = pl.ds(pl.multiple_of(start, share), share)
            total = dot(gproj[0, rows, :], w[0])
            total = total + dot(gproj[1, rows, :], w[1])
            total = total + dot(gproj[2, rows, :], w[2])
            gn_parts[step][pl.ds(index * share, share), :] = total.astype(BF16)
            x = tok[rows, :].astype(F32)
            gain_one = gain_one + jnp.sum(total * (x * row_scale(x)), axis=0, keepdims=True)
    for head in range(heads):
        for delta in range(2):
            turned = dot(flip, acc[2 * head + delta], NN, HIGHEST)
            wide = jnp.concatenate([turned, jnp.zeros_like(turned)], axis=1)
            sheared = pltpu.roll(wide, 0, 1, stride=1, stride_axis=0)
            near_sum[delta, head : head + 1, :] = jnp.sum(sheared, axis=0, keepdims=True)
    summed = dot(near_sum[0], hot[0], NN, HIGHEST) + dot(near_sum[1], hot[1], NN, HIGHEST)
    buckets = lax.broadcasted_iota(jnp.int32, summed.shape, 1)
    beyond = jnp.sum(far_sum[...], axis=1, keepdims=True)
    summed = summed + jnp.where(buckets == NB - 1, beyond, 0.0)
    misc_sum[...] = jnp.zeros_like(misc_sum)
    misc_sum[pl.ds(pl.multiple_of(me * 8, 8), 8), 0:NB] = summed
    misc_sum[8 * shares : 8 * shares + 8, :] = router[...]
    misc_sum[8 * shares + 8 : 8 * shares + 9, :] = gain_one
    misc_sum[8 * shares + 9 : 8 * shares + 10, :] = gain_two[...]
    misc[...] = misc_sum[...].astype(BF16)


def qkv_weights_kernel(pieces, *refs):
    normed = refs[:pieces]
    gproj, out = refs[pieces:]
    rows_total = normed[0].shape[0]
    for c in range(3):
        total = dot(gproj[c, pl.ds(0, rows_total), :], normed[0][...], TN)
        for index in range(1, pieces):
            rows = pl.ds(index * rows_total, rows_total)
            total = total + dot(gproj[c, rows, :], normed[index][...], TN)
        out[c] = total.astype(BF16)


def gelu_pair(values):
    squared = values * values
    bent = jnp.tanh(values * (0.7978845608028654 + 0.7978845608028654 * 0.044715 * squared))
    half = 0.5 * (1.0 + bent)
    lifted = values * half
    slope = 0.7978845608028654 + 3.0 * 0.7978845608028654 * 0.044715 * squared
    return lifted, half + lifted * (1.0 - bent) * slope


def padded_rows(values, rows):
    missing = jnp.zeros((rows - values.shape[0], values.shape[1]), values.dtype)
    return jnp.concatenate([values, missing], axis=0)


def moe_fwd_kernel(piece, pieces, shares, experts, idx, *refs):
    att, refs = refs[:shares], refs[shares:]
    if piece == 0:
        wo_own, wo_swapped, refs = refs[0], refs[1], refs[2:]
        wo_fetched, refs = refs[: shares - 1], refs[shares - 1 :]
    else:
        wo, refs = refs[0], refs[1:]
    tok, gain, router, routes, cot, w_in, w_down = refs[:7]
    refs = refs[7:]
    parts, refs = refs[:shares], refs[shares:]
    if piece == 0:
        wo, refs = refs[0], refs[1:]
    normed, own, gates, ggate, act, slope, acc = refs
    rows_total = tok.shape[0] // pieces
    base = piece * rows_total
    share = rows_total // shares
    me = idx[0]
    expert = pl.program_id(0)

    @pl.when(expert == 0)
    def _():
        gain_row = gain[...].astype(F32).reshape(1, -1)
        router_wide = padded_rows(router[...].astype(F32), LANES).astype(BF16)
        if piece == 0:
            half = wo_own.shape[0] // 2
            mine = pl.ds(pl.multiple_of(idx[1] * half, half), half)
            other = pl.ds(pl.multiple_of((1 - idx[1]) * half, half), half)
            wo[0] = wo_own[...]
            for step in range(1, shares):
                wo[step, mine, :] = wo_fetched[step - 1][...]
                wo[step, other, :] = wo_swapped[step - 1]
        for block in range(rows_total // BLK):
            rows = pl.ds(block * BLK, BLK)
            outer = pl.ds(base + block * BLK, BLK)
            attn = dot(att[0][rows, :], wo[0])
            for step in range(1, shares):
                attn = attn + dot(att[step][rows, :], wo[step])
            hidden = tok[outer, :].astype(F32) + attn
            acc[rows, :] = hidden
            n = (hidden * row_scale(hidden) * gain_row).astype(BF16)
            normed[rows, :] = n
            logits = dot(n, router_wide, NT)
            lanes = lax.broadcasted_iota(jnp.int32, logits.shape, 1)
            first = lanes == routes[outer, 0:1]
            second = lanes == routes[outer, 1:2]
            one = jnp.sum(jnp.where(first, logits, 0.0), axis=1, keepdims=True)
            two = jnp.sum(jnp.where(second, logits, 0.0), axis=1, keepdims=True)
            peak = jnp.maximum(one, two)
            one = jnp.exp(one - peak)
            two = jnp.exp(two - peak)
            both = one + two
            gates[rows, :] = jnp.where(first, one / both, jnp.where(second, two / both, 0.0))
        own[...] = acc[pl.ds(pl.multiple_of(me * share, share), share), :]
        acc[...] = jnp.zeros_like(acc)
        ggate[...] = jnp.zeros_like(ggate)

    for block in range(rows_total // ROWS):
        rows = pl.ds(block * ROWS, ROWS)
        outer = pl.ds(base + block * ROWS, ROWS)
        lifted, bend = gelu_pair(dot(normed[rows, :], w_in[0]))
        lifted = lifted.astype(BF16)
        act[0, rows, :] = lifted
        slope[0, rows, :] = bend.astype(BF16)
        out = dot(lifted, w_down[0])
        gate = lane_pick(gates[rows, :], expert)
        acc[rows, :] += gate * out
        pulled = jnp.sum(cot[outer, :].astype(F32) * out, axis=1, keepdims=True)
        held = ggate[rows, :]
        lanes = lax.broadcasted_iota(jnp.int32, held.shape, 1)
        ggate[rows, :] = jnp.where(lanes == expert, pulled, held)

    @pl.when(expert == experts - 1)
    def _():
        for step in range(shares):
            start = pl.multiple_of((me ^ step) * share, share)
            parts[step][...] = acc[pl.ds(start, share), :].astype(BF16)


def moe_bwd_kernel(piece, shares, experts, idx, *refs):
    gates, ggate, cot, slope, router, w_in, w_down = refs[:7]
    refs = refs[7:]
    parts, refs = refs[:shares], refs[shares:]
    glog, gpre, acc = refs
    rows_total = gates.shape[0]
    base = piece * rows_total
    share = rows_total // shares
    me = idx[0]
    expert = pl.program_id(0)

    @pl.when(expert == 0)
    def _():
        router_wide = padded_rows(router[...].astype(F32), LANES)
        for block in range(rows_total // ROWS):
            rows = pl.ds(block * ROWS, ROWS)
            g, gg = gates[rows, :], ggate[rows, :]
            back = g * (gg - jnp.sum(g * gg, axis=1, keepdims=True))
            glog[rows, :] = back
            acc[rows, :] = dot(back, router_wide, NN, HIGHEST)

    for block in range(rows_total // ROWS):
        rows = pl.ds(block * ROWS, ROWS)
        gate = lane_pick(gates[rows, :], expert)
        weighted = cot[pl.ds(base + block * ROWS, ROWS), :].astype(F32)
        weighted = (gate * weighted).astype(BF16)
        gp = (dot(weighted, w_down[0], NT) * slope[0, rows, :].astype(F32)).astype(BF16)
        gpre[0, rows, :] = gp
        acc[rows, :] += dot(gp, w_in[0], NT)

    @pl.when(expert == experts - 1)
    def _():
        for step in range(shares):
            start = pl.multiple_of((me ^ step) * share, share)
            parts[step][...] = acc[pl.ds(start, share), :].astype(BF16)


def moe_weights_kernel(pieces, cot, *refs):
    gates, refs = refs[:pieces], refs[pieces:]
    glog, refs = refs[:pieces], refs[pieces:]
    normed, refs = refs[:pieces], refs[pieces:]
    act, refs = refs[:pieces], refs[pieces:]
    gpre, refs = refs[:pieces], refs[pieces:]
    out, router = refs
    rows_total = normed[0].shape[0]
    expert = pl.program_id(0)

    @pl.when(expert == 0)
    def _():
        total = jnp.zeros((LANES, cot.shape[1]), F32)
        for index in range(pieces):
            back = glog[index][...]
            high = back.astype(BF16)
            low = (back - high.astype(F32)).astype(BF16)
            total = total + dot(high, normed[index][...], TN)
            total = total + dot(low, normed[index][...], TN)
        router[...] = total[0:8, :]

    grad_in = jnp.zeros((normed[0].shape[1], gpre[0].shape[2]), F32)
    grad_down = jnp.zeros((act[0].shape[2], cot.shape[1]), F32)
    for index in range(pieces):
        gate = lane_pick(gates[index][...], expert)
        weighted = cot[pl.ds(index * rows_total, rows_total), :].astype(F32)
        weighted = (gate * weighted).astype(BF16)
        grad_in = grad_in + dot(normed[index][...], gpre[index][0], TN)
        grad_down = grad_down + dot(act[index][0], weighted, TN)
    out[0, 0] = grad_in.astype(BF16)
    out[0, 1] = grad_down.astype(BF16)


def hidden_back_kernel(piece, pieces, shares, got, idx, *refs):
    gx, refs = refs[:got], refs[got:]
    wo, own, cot, gain = refs[:4]
    refs = refs[4:]
    ga, refs = refs[:shares], refs[shares:]
    gh, gh_low, ggain = refs
    share = own.shape[0]
    grad = gx[0][...].astype(F32)
    for step in range(1, got):
        grad = grad + gx[step][...].astype(F32)
    hidden = own[...]
    scale = row_scale(hidden)
    unit = hidden * scale
    ggain[...] = jnp.sum(grad * unit, axis=0, keepdims=True)
    gained = grad * gain[...].astype(F32).reshape(1, -1)
    start = piece * (cot.shape[0] // pieces) + idx[0] * share
    mine = cot[pl.ds(pl.multiple_of(start, share), share), :].astype(F32)
    back = mine + scale * (gained - unit * jnp.mean(gained * unit, axis=-1, keepdims=True))
    gh[...] = back
    low = back.astype(BF16)
    gh_low[...] = low
    for step in range(shares):
        ga[step][...] = dot(low, wo[step], NT).astype(BF16)


def w_out_back_kernel(pieces, shares, idx, *refs):
    att, refs = refs[: pieces * shares], refs[pieces * shares :]
    gh_low, out = refs[:pieces], refs[pieces]
    share = gh_low[0].shape[0]
    rows = pl.ds(pl.multiple_of(idx[0] * share, share), share)
    for step in range(shares):
        total = dot(att[step][rows, :], gh_low[0][...], TN)
        for index in range(1, pieces):
            total = total + dot(att[index * shares + step][rows, :], gh_low[index][...], TN)
        out[step] = total.astype(BF16)


def join_kernel(pieces, count, *refs):
    own, refs = refs[:pieces], refs[pieces:]
    got, out = refs[: pieces * count], refs[pieces * count]
    share = own[0].shape[0]
    for index in range(pieces):
        total = own[index][...]
        for step in range(count):
            total = total + got[index * count + step][...].astype(F32)
        out[pl.ds(index * share, share), :] = total.astype(BF16)


def input_back_kernel(pieces, got, idx, *refs):
    gn, refs = refs[:got], refs[got:]
    ghs, refs = refs[:pieces], refs[pieces:]
    tok, gain, gt = refs
    share = ghs[0].shape[0]
    gain_row = gain[...].astype(F32).reshape(1, -1)
    for index in range(pieces):
        rows = pl.ds(index * share, share)
        grad = gn[0][rows, :].astype(F32)
        for step in range(1, got):
            grad = grad + gn[step][rows, :].astype(F32)
        start = index * (tok.shape[0] // pieces) + idx[0] * share
        x = tok[pl.ds(pl.multiple_of(start, share), share), :].astype(F32)
        scale = row_scale(x)
        unit = x * scale
        gained = grad * gain_row
        back = scale * (gained - unit * jnp.mean(gained * unit, axis=-1, keepdims=True))
        gt[rows, :] = (ghs[index][...] + back).astype(BF16)


def place_kernel(pieces, shares, idx, *refs):
    blocks, out = refs[:shares], refs[shares]
    rows_total = out.shape[0] // pieces
    share = rows_total // shares
    for step in range(shares):
        owner = idx[0] ^ step
        for index in range(pieces):
            start = pl.multiple_of(index * rows_total + owner * share, share)
            got = blocks[step][pl.ds(index * share, share), :]
            out[pl.ds(start, share), :] = got.astype(out.dtype)


ROWS = 1024
PIECES = 1

SMEM = pl.BlockSpec(memory_space=pltpu.SMEM)
VMEM = pl.BlockSpec(memory_space=pltpu.VMEM)


def shaped(shape, dtype):
    return jax.ShapeDtypeStruct(shape, dtype)


def whole_call(kernel, outs, args, scratch=(), flops=0, moved=0, with_index=True):
    specs = ([SMEM] if with_index else []) + [VMEM] * (len(args) - (1 if with_index else 0))
    return pl.pallas_call(
        kernel,
        out_shape=outs,
        in_specs=specs,
        out_specs=[VMEM] * len(outs),
        scratch_shapes=list(scratch),
        compiler_params=pltpu.CompilerParams(vmem_limit_bytes=VMEM_LIMIT),
        cost_estimate=pl.CostEstimate(flops=flops, bytes_accessed=moved, transcendentals=0),
    )(*args)


def swap(value, axis, bit):
    count = lax.axis_size(axis)
    return lax.ppermute(value, axis, [(i, i ^ bit) for i in range(count)])


def sum_over(value, axis):
    bit = 1
    while bit < lax.axis_size(axis):
        value = value + swap(value, axis, bit)
        bit *= 2
    return value


def gather_parts(value, axis):
    count = lax.axis_size(axis)
    if count != 4:
        return [value] + [swap(value, axis, bit) for bit in range(1, count)]
    two = swap(value, axis, 2)
    one = swap(value, axis, 1)
    return [value, one, two, swap(after(two, one), axis, 1)]


def reduce_near(parts, axis):
    return swap(parts[3], axis, 1), swap(parts[1], axis, 1)


def reduce_far(parts, near, axis):
    pair = (parts[2].astype(F32) + near[0].astype(F32)).astype(parts[2].dtype)
    return [parts[0], near[1], swap(pair, axis, 2)], pair


def exchange(parts, axis):
    return [parts[0]] + [swap(parts[bit], axis, bit) for bit in range(1, len(parts))]


def halves_of(value, axis, chosen):
    half = value.shape[axis] // 2
    keep = lax.dynamic_slice_in_dim(value, chosen * half, half, axis)
    send = lax.dynamic_slice_in_dim(value, (1 - chosen) * half, half, axis)
    return keep, send


def bits_of(axis):
    count = lax.axis_size(axis)
    return [1 << level for level in range(count.bit_length() - 1)]


def gather_back(value, mesh_axis, axis):
    me = lax.axis_index(mesh_axis)
    for bit in reversed(bits_of(mesh_axis)):
        got = swap(value, mesh_axis, bit)
        low = (me // bit) % 2 == 0
        value = jnp.concatenate(
            [jnp.where(low, value, got), jnp.where(low, got, value)], axis=axis
        )
    return value


def together(*values):
    return lax.optimization_barrier(values)


def after(value, *others):
    return lax.optimization_barrier((value, *others))[0]


def body(
    tokens, segments, routes, grad_out, gain_attn, w_qkv, w_out, rel_bias,
    gain_moe, w_router, w_in, w_down,
):
    tok_rows, width = tokens.shape
    heads = rel_bias.shape[1]
    features = w_qkv.shape[2]
    head_size = features // heads
    experts, _, hidden_units = w_in.shape
    shares = lax.axis_size("tensor")
    rows = tok_rows // PIECES
    share = rows // shares
    me = lax.axis_index("tensor").astype(jnp.int32)
    side = (lax.axis_index("dp") % 2).astype(jnp.int32)
    idx = jnp.stack([me, side])
    mib = 1 << 20
    others = range(1, shares)
    four = shares == 4

    half_rows = features // 2
    my_half = lax.dynamic_slice_in_dim(w_out, side * half_rows, half_rows, 0)
    halves = [swap(my_half, "tensor", by) for by in others]

    build_hot, gather_hot = near_tables()
    build_hot = jnp.asarray(np.swapaxes(build_hot, 1, 2), BF16)
    gather_hot = jnp.asarray(gather_hot, F32)
    w_qkv_t = jnp.swapaxes(w_qkv, 1, 2)
    router_t = w_router.T

    normed_one, qh, k, v, _, att, ot, lse, bias, far = whole_call(
        functools.partial(attn_fwd_kernel, 0, PIECES, heads, head_size),
        [
            shaped((rows, width), BF16),
            shaped((heads, rows, features), BF16),
            shaped((rows, features), BF16),
            shaped((rows, features), BF16),
            shaped((features, rows), BF16),
            shaped((rows, features), BF16),
            shaped((features, rows), F32),
            shaped((8, rows), F32),
            shaped((2 * heads, BLK, BLK), F32),
            shaped((8, LANES), F32),
        ],
        [tokens, gain_attn, w_qkv_t, segments, rel_bias.T, build_hot],
        flops=6 * 10**9, moved=8 * mib, with_index=False,
    )
    att = after(att, *halves)
    atts = gather_parts(att, "tensor")
    swapped = swap(after(jnp.stack(halves), att), "dp", 1)

    full = lambda shape: pl.BlockSpec(shape, lambda e: (0,) * len(shape))
    per_expert = lambda shape: pl.BlockSpec((1,) + shape, lambda e: (e, 0, 0))
    params = pltpu.CompilerParams(
        vmem_limit_bytes=VMEM_LIMIT, dimension_semantics=("arbitrary",)
    )
    moe_flops = 4 * experts * rows * width * hidden_units

    fwd = pl.pallas_call(
        functools.partial(moe_fwd_kernel, 0, PIECES, shares, experts),
        grid=(experts,),
        in_specs=[SMEM]
        + [full((rows, features))] * shares
        + [full((features, width)), full((shares - 1, half_rows, width))]
        + [full((half_rows, width))] * (shares - 1)
        + [
            full((rows, width)), full((width,)), full((experts, width)),
            full((rows, 2)), full((rows, width)),
            per_expert((width, hidden_units)), per_expert((hidden_units, width)),
        ],
        out_specs=[full((share, width))] * shares
        + [
            full((shares, features, width)), full((rows, width)),
            full((share, width)), full((rows, LANES)), full((rows, LANES)),
            per_expert((rows, hidden_units)), per_expert((rows, hidden_units)),
        ],
        out_shape=[shaped((share, width), BF16)] * shares
        + [
            shaped((shares, features, width), BF16),
            shaped((rows, width), BF16),
            shaped((share, width), F32),
            shaped((rows, LANES), F32),
            shaped((rows, LANES), F32),
            shaped((experts, rows, hidden_units), BF16),
            shaped((experts, rows, hidden_units), BF16),
        ],
        scratch_shapes=[pltpu.VMEM((rows, width), F32)],
        compiler_params=params,
        cost_estimate=pl.CostEstimate(
            flops=moe_flops, bytes_accessed=32 * mib, transcendentals=0
        ),
    )(
        idx, *atts, w_out, swapped, *halves, tokens, gain_moe, router_t, routes, grad_out,
        w_in, w_down,
    )
    moe_parts = fwd[:shares]
    wo, normed_two, own_hidden, gates, ggate, act, slope = fwd[shares:]
    if four:
        moe_near = reduce_near(moe_parts, "tensor")
    else:
        moe_near = exchange(moe_parts, "tensor")[1:]

    bwd = pl.pallas_call(
        functools.partial(moe_bwd_kernel, 0, shares, experts),
        grid=(experts,),
        in_specs=[
            SMEM, full((rows, LANES)), full((rows, LANES)), full((rows, width)),
            per_expert((rows, hidden_units)), full((experts, width)),
            per_expert((width, hidden_units)), per_expert((hidden_units, width)),
        ],
        out_specs=[full((share, width))] * shares
        + [full((rows, LANES)), per_expert((rows, hidden_units))],
        out_shape=[shaped((share, width), BF16)] * shares
        + [
            shaped((rows, LANES), F32),
            shaped((experts, rows, hidden_units), BF16),
        ],
        scratch_shapes=[pltpu.VMEM((rows, width), F32)],
        compiler_params=params,
        cost_estimate=pl.CostEstimate(
            flops=moe_flops, bytes_accessed=26 * mib, transcendentals=0
        ),
    )(idx, gates, ggate, grad_out, slope, router_t, w_in, w_down)
    gx_parts = [after(part, *moe_near) for part in bwd[:shares]]
    glog, gpre = bwd[shares:]
    gx_near = reduce_near(gx_parts, "tensor") if four else exchange(gx_parts, "tensor")[1:]

    expert_grads, router_rows = pl.pallas_call(
        functools.partial(moe_weights_kernel, PIECES),
        grid=(experts,),
        in_specs=[
            full((rows, width)), full((rows, LANES)), full((rows, LANES)), full((rows, width)),
            per_expert((rows, hidden_units)), per_expert((rows, hidden_units)),
        ],
        out_specs=[
            pl.BlockSpec((1, 2, width, width), lambda e: (e, 0, 0, 0)), full((8, width))
        ],
        out_shape=[shaped((experts, 2, width, width), BF16), shaped((8, width), F32)],
        compiler_params=params,
        cost_estimate=pl.CostEstimate(
            flops=moe_flops, bytes_accessed=26 * mib, transcendentals=0
        ),
    )(grad_out, gates, glog, normed_two, act, gpre)
    expert_rows = after(expert_grads.reshape(experts * 2 * width, width), *gx_near)
    expert_rows = lax.psum_scatter(expert_rows, "dp", scatter_dimension=0, tiled=True)

    if four:
        gx_near = after(gx_near[0], router_rows), gx_near[1]
        gx_got, _ = reduce_far(gx_parts, gx_near, "tensor")
    else:
        gx_got = [gx_parts[0], *gx_near]
    back = whole_call(
        functools.partial(hidden_back_kernel, 0, PIECES, shares, len(gx_got)),
        [shaped((share, features), BF16)] * shares
        + [shaped((share, width), F32), shaped((share, width), BF16), shaped((1, width), F32)],
        [idx, *gx_got, wo, own_hidden, grad_out, gain_moe],
        flops=3 * 10**8, moved=5 * mib,
    )
    go = exchange(back[:shares], "tensor")
    grad_hidden, gh_low, ggain_two = back[shares:]

    if four:
        moe_near = after(moe_near[0], *go[1:]), moe_near[1]
        moe_got, _ = reduce_far(moe_parts, moe_near, "tensor")
    else:
        moe_got = [moe_parts[0], *moe_near]
    result_share = whole_call(
        functools.partial(join_kernel, PIECES, len(moe_got)),
        [shaped((share, width), BF16)],
        [own_hidden, *moe_got],
        moved=3 * mib, with_index=False,
    )[0]
    attn_back = whole_call(
        functools.partial(attn_bwd_kernel, 0, PIECES, heads, head_size, shares),
        [shaped((share, width), BF16)] * shares
        + [shaped((3, rows, features), BF16), shaped((features, width), BF16)],
        [
            idx, *go, tokens, router_rows, ggain_two, qh, ot, lse, k, v, bias, far, segments,
            w_qkv_t, gather_hot,
        ],
        [pltpu.VMEM((rows, features), F32)] * 2
        + [
            pltpu.VMEM((features, rows), F32),
            pltpu.VMEM((2 * heads, BLK, BLK), F32),
            pltpu.VMEM((rows, features), BF16),
            pltpu.VMEM((features, width), F32),
            pltpu.VMEM((features, rows), BF16),
            pltpu.VMEM((8, rows), F32),
            pltpu.VMEM((2, 8, 2 * BLK), F32),
            pltpu.VMEM((8, BLK), F32),
        ],
        flops=14 * 10**9, moved=8 * mib,
    )
    gn_parts = [after(part, moe_got[-1]) for part in attn_back[:shares]]
    gproj, misc = attn_back[shares:]

    qkv_rows = whole_call(
        functools.partial(qkv_weights_kernel, PIECES),
        [shaped((3, features, width), BF16)],
        [normed_one, gproj],
        flops=10**9, moved=4 * mib, with_index=False,
    )[0]
    w_out_rows = whole_call(
        functools.partial(w_out_back_kernel, PIECES, shares),
        [shaped((shares, features, width), BF16)],
        [idx, *atts, after(gh_low, gproj)],
        flops=3 * 10**8, moved=4 * mib,
    )[0]
    late = jnp.concatenate([qkv_rows, misc[None], w_out_rows], axis=0)
    if four:
        near = reduce_near(gn_parts, "tensor")
        near = after(near[0], late, near[1]), near[1]
        gn_got, mark = reduce_far(gn_parts, near, "tensor")
    else:
        gn_got = exchange(gn_parts, "tensor")
        mark = gn_got[-1]

    place = lax.axis_index("dp")

    def halve(value, bit, *ready):
        keep, send = halves_of(value, 1, (place // bit) % 2)
        got = swap(after(send, *ready), "dp", bit)
        return (keep.astype(F32) + got.astype(F32)).astype(BF16)

    late = after(late, mark)
    bits = bits_of("dp")
    late = halve(late, 1)
    grad_hidden = after(grad_hidden, late)

    expert_rows = after(expert_rows, mark)
    gt_share = whole_call(
        functools.partial(input_back_kernel, PIECES, len(gn_got)),
        [shaped((share, width), BF16)],
        [idx, *gn_got, grad_hidden, tokens, gain_attn],
        moved=5 * mib,
    )[0]
    keep, send = halves_of(late, 1, (place // bits[1]) % 2)
    two, one, got = together(
        swap(gt_share, "tensor", 2), swap(gt_share, "tensor", 1),
        swap(after(send, gt_share), "dp", bits[1]),
    )
    late = (keep.astype(F32) + got.astype(F32)).astype(BF16)
    keep, send = halves_of(late, 1, (place // bits[2]) % 2)
    share_now = after(result_share, two)
    three, result_two, result_one, got = together(
        swap(two, "tensor", 1), swap(share_now, "tensor", 2), swap(share_now, "tensor", 1),
        swap(send, "dp", bits[2]),
    )
    late = (keep.astype(F32) + got.astype(F32)).astype(BF16)
    for bit in bits[3:]:
        late = halve(late, bit)
    grad_tokens = whole_call(
        functools.partial(place_kernel, PIECES, shares),
        [shaped((rows, width), F32)], [idx, gt_share, one, two, three], moved=5 * mib,
    )[0]

    *sent, _ = together(
        *[swap(jnp.stack([late[4 + by], late[3]]), "tensor", by) for by in others], grad_tokens
    )
    out_sum, small = late[4].astype(F32), [late[3]]
    for got in sent:
        out_sum = out_sum + got[0].astype(F32)
        small.append(got[1])
    small = [part.astype(F32) for part in small]
    while len(small) > 1:
        small = [small[at] + small[at + 1] for at in range(0, len(small), 2)]
    late = jnp.concatenate(
        [late[:3], jnp.stack([small[0].astype(BF16), out_sum.astype(BF16)])], axis=0
    )

    expert_rows = lax.all_gather(expert_rows, "dp", axis=0, tiled=True)

    def joined(value, got, bit):
        low = (place // bit) % 2 == 0
        return jnp.concatenate([jnp.where(low, value, got), jnp.where(low, got, value)], axis=1)

    for bit in reversed(bits[3:]):
        late = joined(late, swap(late, "dp", bit), bit)
    got, result_three = together(
        swap(late, "dp", bits[2]), swap(result_two, "tensor", 1)
    )
    late = joined(late, got, bits[2])
    grad_w_in = expert_rows.reshape(experts, 2, width, width)[:, 0].astype(F32)
    got = after(swap(late, "dp", bits[1]), grad_w_in)
    late = joined(late, got, bits[1])
    expert_rows = after(expert_rows, got)
    grad_w_down = expert_rows.reshape(experts, 2, width, width)[:, 1].astype(F32)
    result = whole_call(
        functools.partial(place_kernel, PIECES, shares),
        [shaped((rows, width), BF16)],
        [idx, result_share, result_one, result_two, result_three],
        moved=3 * mib,
    )[0]
    got = after(swap(late, "dp", bits[0]), grad_w_down, result)
    late = joined(late, got, bits[0])
    grad_w_qkv = jnp.swapaxes(late[:3], 1, 2).astype(F32)
    grad_w_out = late[4].astype(F32)
    small = late[3].astype(F32)
    grad_rel = lax.dynamic_slice_in_dim(small, me * 8, 8, 0)
    first = 8 * shares
    return (
        result,
        grad_tokens,
        small[first + 8],
        grad_w_qkv,
        grad_w_out,
        grad_rel[:heads, :NB].T,
        small[first + 9],
        small[first : first + experts].T,
        grad_w_in,
        grad_w_down,
    )


def solution(mesh):
    placed = (
        P("dp", None),
        P("dp", None),
        P("dp", None),
        P("dp", None),
        P(),
        P(None, None, "tensor"),
        P("tensor", None),
        P(None, "tensor"),
        P(),
        P(),
        P(None, None, "tensor"),
        P(None, "tensor", None),
    )
    return jax.shard_map(
        body,
        mesh=mesh,
        in_specs=placed,
        out_specs=(
            P("dp", None),
            P("dp", None),
            P(),
            P(None, None, "tensor"),
            P("tensor", None),
            P(None, "tensor"),
            P(),
            P(),
            P(None, None, "tensor"),
            P(None, "tensor", None),
        ),
        check_vma=False,
    )
```

```python
import functools
import math

import jax
import jax.numpy as jnp
import numpy as np
from jax import lax
from jax.experimental import pallas as pl
from jax.experimental.pallas import tpu as pltpu
from jax.sharding import PartitionSpec as P

NB = 32
DIST = 128
EPSILON = 1e-06
NEGATIVE = -1e30
HIGHEST = lax.Precision.HIGHEST
F32 = jnp.float32
BF16 = jnp.bfloat16
BLK = 256
LANES = 128
VMEM_LIMIT = 56 * 1024 * 1024

NN = (((1,), (0,)), ((), ()))
NT = (((1,), (1,)), ((), ()))
TN = (((0,), (0,)), ((), ()))


def dot(a, b, dims=NN, precision=None):
    return lax.dot_general(a, b, dims, precision=precision, preferred_element_type=F32)


def bucket_of(distance):
    halfway = NB // 2
    thresholds = [
        int(math.ceil(halfway * (DIST / halfway) ** (step / halfway))) for step in range(halfway)
    ]
    beyond = sum((distance >= threshold).astype(np.int64) for threshold in thresholds)
    return np.where(distance < halfway, distance, halfway - 1 + beyond)


def near_tables():
    lanes = np.arange(2 * BLK)
    offset = np.where(lanes < BLK, lanes, lanes - 2 * BLK)
    build = np.stack([np.maximum(offset, 0), np.maximum(BLK + offset, 0)])
    gather = np.stack([lanes - (BLK - 1), lanes + 1])
    eye = np.eye(NB, dtype=np.float32)
    build_hot = eye[bucket_of(build)]
    gather_hot = eye[bucket_of(np.maximum(gather, 0))] * (gather >= 0)[..., None]
    return build_hot, gather_hot


def row_scale(values):
    return lax.rsqrt(jnp.mean(values * values, axis=-1, keepdims=True) + EPSILON)


def lane_pick(values, index):
    lanes = lax.broadcasted_iota(jnp.int32, values.shape, 1)
    return jnp.sum(jnp.where(lanes == index, values, 0.0), axis=1, keepdims=True)


def masked_scores(k_tile, qh_tile, bias, seg_k, seg_q, diagonal):
    scores = dot(k_tile, qh_tile, NT) + bias
    allowed = seg_k == seg_q
    if diagonal:
        key_at = lax.broadcasted_iota(jnp.int32, scores.shape, 0)
        query_at = lax.broadcasted_iota(jnp.int32, scores.shape, 1)
        allowed = allowed & (key_at <= query_at)
    return jnp.where(allowed, scores, NEGATIVE)


def tile_bias(bias_ref, far_ref, head, delta):
    if delta < 2:
        return bias_ref[2 * head + delta]
    return far_ref[pl.ds(head, 1), 0:1]


def column_of(row):
    spread = jnp.broadcast_to(row.astype(F32), (8, row.shape[1]))
    return spread.T[:, 0:1]


def attn_fwd_kernel(piece, pieces, heads, head_size, *refs):
    tok, gain, w, seg = refs[:4]
    refs = refs[4:]
    if piece == 0:
        rel, build = refs[:2]
        refs = refs[2:]
    else:
        bias, far = refs[:2]
        refs = refs[2:]
    old_k, refs = refs[:piece], refs[piece:]
    old_vt, refs = refs[:piece], refs[piece:]
    normed, qh, k, v, vt, att, ot, lse = refs[:8]
    if piece == 0:
        bias, far = refs[8:]
    keys_of, vt_of = [*old_k, k], [*old_vt, vt]
    rows_total = tok.shape[0] // pieces
    base = piece * rows_total
    features = w.shape[1]
    blocks = rows_total // BLK
    gain_row = gain[...].astype(F32).reshape(1, -1)
    lanes = lax.broadcasted_iota(jnp.int32, (BLK, features), 1)
    for block in range(blocks):
        rows = pl.ds(block * BLK, BLK)
        x = tok[pl.ds(base + block * BLK, BLK), :].astype(F32)
        n = (x * row_scale(x) * gain_row).astype(BF16)
        normed[rows, :] = n
        q_rows = dot(n, w[0], NT).astype(BF16).astype(F32) * (head_size**-0.5)
        for head in range(heads):
            inside = (lanes >= head * head_size) & (lanes < (head + 1) * head_size)
            qh[head, rows, :] = jnp.where(inside, q_rows, 0.0).astype(BF16)
        k[rows, :] = dot(n, w[1], NT).astype(BF16)
        v_rows = dot(n, w[2], NT).astype(BF16)
        v[rows, :] = v_rows
        vt[:, rows] = v_rows.astype(F32).T.astype(BF16)
    if piece == 0:
        far[...] = jnp.zeros_like(far)
        far[0:heads, :] = jnp.broadcast_to(rel[:, NB - 1 : NB].astype(F32), (heads, LANES))
        for delta in range(2):
            near = dot(rel[...], build[delta])
            for head in range(heads):
                spread = jnp.broadcast_to(near[head : head + 1, :], (BLK, 2 * BLK))
                turned = pltpu.roll(spread, 0, 1, stride=1, stride_axis=0)
                bias[2 * head + delta] = turned[:, :BLK]
    lse[...] = jnp.zeros_like(lse)
    seg_row = seg[...].astype(F32)
    seg_col = column_of(seg[...])

    def one_head(head, carry):
        part = pl.ds(pl.multiple_of(head * head_size, head_size), head_size)
        for block in range(blocks):
            qb = piece * blocks + block
            cols = pl.ds(block * BLK, BLK)
            q_tile = qh[head, cols, :]
            tiles = []
            for kb in range(qb + 1):
                keys = pl.ds(kb % blocks * BLK, BLK)
                tiles.append(
                    masked_scores(
                        keys_of[kb // blocks][keys, :], q_tile,
                        tile_bias(bias, far, head, qb - kb),
                        seg_col[kb * BLK : (kb + 1) * BLK, :],
                        seg_row[:, qb * BLK : (qb + 1) * BLK], kb == qb,
                    )
                )
            peak = functools.reduce(
                jnp.maximum, [jnp.max(t, axis=0, keepdims=True) for t in tiles]
            )
            total = jnp.zeros((1, BLK), F32)
            out = jnp.zeros((head_size, BLK), F32)
            for kb in range(qb + 1):
                raised = jnp.exp(tiles[kb] - peak)
                total = total + jnp.sum(raised, axis=0, keepdims=True)
                values = vt_of[kb // blocks][part, pl.ds(kb % blocks * BLK, BLK)]
                out = out + dot(values, raised.astype(BF16))
            ot[part, cols] = out / total
            lse[pl.ds(head, 1), cols] = peak + jnp.log(total)
        return carry

    lax.fori_loop(0, heads, one_head, 0)
    for block in range(blocks):
        cols = pl.ds(block * BLK, BLK)
        att[cols, :] = ot[:, cols].T.astype(BF16)


def attn_bwd_kernel(piece, pieces, heads, head_size, shares, idx, *refs):
    held = piece + 1
    last = held == pieces
    go_parts, refs = refs[:shares], refs[shares:]
    tok, router, gain_two, qh, ot, lse = refs[:6]
    refs = refs[6:]
    ks, refs = refs[:held], refs[held:]
    vs, refs = refs[:held], refs[held:]
    bias, far, seg = refs[:3]
    refs = refs[3:]
    if piece:
        gk_in, refs = refs[:piece], refs[piece:]
        gv_in, refs = refs[:piece], refs[piece:]
        gq_in, refs = refs[:piece], refs[piece:]
        acc_in, refs = refs[0], refs[1:]
    if last:
        w, hot = refs[:2]
        refs = refs[2:]
        gn_parts, refs = refs[:shares], refs[shares:]
        gproj, misc = refs[:2]
        refs = refs[2:]
        gk, refs = refs[:held], refs[held:]
        gv, refs = refs[:held], refs[held:]
        gq_t, acc = refs[:2]
        refs = refs[2:]
    else:
        gk, refs = refs[:held], refs[held:]
        gv, refs = refs[:held], refs[held:]
        gq_t, acc = refs[:2]
        refs = refs[2:]
    go, misc_sum, kt, d_row, near_sum, far_sum = refs
    rows_total, features = ks[0].shape
    blocks = rows_total // BLK
    share = rows_total // shares
    me = idx[0]
    for step in range(shares):
        start = pl.multiple_of((me ^ step) * share, share)
        go[pl.ds(start, share), :] = go_parts[step][...]
    for index in range(held):
        for block in range(blocks):
            cols = pl.ds(block * BLK, BLK)
            kt[:, pl.ds((index * blocks + block) * BLK, BLK)] = (
                ks[index][cols, :].astype(F32).T.astype(BF16)
            )
        if index < piece:
            gk[index][...] = gk_in[index][...]
            gv[index][...] = gv_in[index][...]
        else:
            gk[index][...] = jnp.zeros_like(gk[index])
            gv[index][...] = jnp.zeros_like(gv[index])
    if piece:
        acc[...] = acc_in[...]
    else:
        acc[...] = jnp.zeros_like(acc)
    for block in range(blocks):
        cols = pl.ds(block * BLK, BLK)
        product = go[cols, :].astype(F32).T * ot[:, cols]
        for head in range(heads):
            part = product[head * head_size : (head + 1) * head_size, :]
            d_row[head : head + 1, cols] = jnp.sum(part, axis=0, keepdims=True)
    near_sum[...] = jnp.zeros_like(near_sum)
    far_sum[...] = jnp.zeros_like(far_sum)
    key_at = lax.broadcasted_iota(jnp.int32, (BLK, BLK), 0)
    other_at = lax.broadcasted_iota(jnp.int32, (BLK, BLK), 1)
    flip = (key_at + other_at == BLK - 1).astype(F32)
    seg_row = seg[...].astype(F32)
    seg_col = column_of(seg[...])

    def one_head(head, carry):
        part = pl.ds(pl.multiple_of(head * head_size, head_size), head_size)
        lanes = lax.broadcasted_iota(jnp.int32, (BLK, features), 1)
        inside = (lanes >= head * head_size) & (lanes < (head + 1) * head_size)
        for block in range(blocks):
            qb = piece * blocks + block
            cols = pl.ds(block * BLK, BLK)
            q_tile = qh[head, cols, :]
            go_tile = jnp.where(inside, go[cols, :].astype(F32), 0.0).astype(BF16)
            log_total = lse[pl.ds(head, 1), cols]
            d_tile = d_row[pl.ds(head, 1), cols]
            gq = jnp.zeros((head_size, BLK), F32)
            for kb in range(qb + 1):
                index = kb // blocks
                keys = pl.ds(kb % blocks * BLK, BLK)
                delta = qb - kb
                scores = masked_scores(
                    ks[index][keys, :], q_tile, tile_bias(bias, far, head, delta),
                    seg_col[kb * BLK : (kb + 1) * BLK, :],
                    seg_row[:, qb * BLK : (qb + 1) * BLK], delta == 0,
                )
                probs = jnp.exp(scores - log_total)
                gs = probs * (dot(vs[index][keys, :], go_tile, NT) - d_tile)
                if delta < 2:
                    acc[2 * head + delta] += gs
                else:
                    far_sum[pl.ds(head, 1), :] += jnp.sum(gs, axis=0, keepdims=True)
                gs_low = gs.astype(BF16)
                gv[index][keys, :] += dot(probs.astype(BF16), go_tile)
                gk[index][keys, :] += dot(gs_low, q_tile)
                gq = gq + dot(kt[part, kb * BLK : (kb + 1) * BLK], gs_low)
            gq_t[part, cols] = gq * (head_size**-0.5)
        return carry

    lax.fori_loop(0, heads, one_head, 0)
    if not last:
        return
    gqs = [*(gq_in if piece else ()), gq_t]
    for index in range(held):
        for block in range(blocks):
            rows = pl.ds(block * BLK, BLK)
            out = pl.ds((index * blocks + block) * BLK, BLK)
            gproj[0, out, :] = gqs[index][:, rows].T.astype(BF16)
            gproj[1, out, :] = gk[index][rows, :].astype(BF16)
            gproj[2, out, :] = gv[index][rows, :].astype(BF16)
    gain_one = jnp.zeros_like(gain_two)
    for step in range(shares):
        for index in range(pieces):
            start = index * rows_total + (me ^ step) * share
            rows = pl.ds(pl.multiple_of(start, share), share)
            total = dot(gproj[0, rows, :], w[0])
            total = total + dot(gproj[1, rows, :], w[1])
            total = total + dot(gproj[2, rows, :], w[2])
            gn_parts[step][pl.ds(index * share, share), :] = total.astype(BF16)
            x = tok[rows, :].astype(F32)
            gain_one = gain_one + jnp.sum(total * (x * row_scale(x)), axis=0, keepdims=True)
    for head in range(heads):
        for delta in range(2):
            turned = dot(flip, acc[2 * head + delta], NN, HIGHEST)
            wide = jnp.concatenate([turned, jnp.zeros_like(turned)], axis=1)
            sheared = pltpu.roll(wide, 0, 1, stride=1, stride_axis=0)
            near_sum[delta, head : head + 1, :] = jnp.sum(sheared, axis=0, keepdims=True)
    summed = dot(near_sum[0], hot[0], NN, HIGHEST) + dot(near_sum[1], hot[1], NN, HIGHEST)
    buckets = lax.broadcasted_iota(jnp.int32, summed.shape, 1)
    beyond = jnp.sum(far_sum[...], axis=1, keepdims=True)
    summed = summed + jnp.where(buckets == NB - 1, beyond, 0.0)
    misc_sum[...] = jnp.zeros_like(misc_sum)
    misc_sum[pl.ds(pl.multiple_of(me * 8, 8), 8), 0:NB] = summed
    misc_sum[8 * shares : 8 * shares + 8, :] = router[...]
    misc_sum[8 * shares + 8 : 8 * shares + 9, :] = gain_one
    misc_sum[8 * shares + 9 : 8 * shares + 10, :] = gain_two[...]
    misc[...] = misc_sum[...].astype(BF16)


def qkv_weights_kernel(pieces, *refs):
    normed = refs[:pieces]
    gproj, out = refs[pieces:]
    rows_total = normed[0].shape[0]
    for c in range(3):
        total = dot(gproj[c, pl.ds(0, rows_total), :], normed[0][...], TN)
        for index in range(1, pieces):
            rows = pl.ds(index * rows_total, rows_total)
            total = total + dot(gproj[c, rows, :], normed[index][...], TN)
        out[c] = total.astype(BF16)


def gelu_pair(values):
    squared = values * values
    bent = jnp.tanh(values * (0.7978845608028654 + 0.7978845608028654 * 0.044715 * squared))
    half = 0.5 * (1.0 + bent)
    lifted = values * half
    slope = 0.7978845608028654 + 3.0 * 0.7978845608028654 * 0.044715 * squared
    return lifted, half + lifted * (1.0 - bent) * slope


def padded_rows(values, rows):
    missing = jnp.zeros((rows - values.shape[0], values.shape[1]), values.dtype)
    return jnp.concatenate([values, missing], axis=0)


def moe_fwd_kernel(piece, pieces, shares, experts, idx, *refs):
    att, refs = refs[:shares], refs[shares:]
    if piece == 0:
        wo_own, wo_swapped, refs = refs[0], refs[1], refs[2:]
        wo_fetched, refs = refs[: shares - 1], refs[shares - 1 :]
    else:
        wo, refs = refs[0], refs[1:]
    tok, gain, router, routes, cot, w_in, w_down = refs[:7]
    refs = refs[7:]
    parts, refs = refs[:shares], refs[shares:]
    if piece == 0:
        wo, refs = refs[0], refs[1:]
    normed, own, gates, ggate, act, slope, acc = refs
    rows_total = tok.shape[0] // pieces
    base = piece * rows_total
    share = rows_total // shares
    me = idx[0]
    expert = pl.program_id(0)

    @pl.when(expert == 0)
    def _():
        gain_row = gain[...].astype(F32).reshape(1, -1)
        router_wide = padded_rows(router[...].astype(F32), LANES).astype(BF16)
        if piece == 0:
            half = wo_own.shape[0] // 2
            mine = pl.ds(pl.multiple_of(idx[1] * half, half), half)
            other = pl.ds(pl.multiple_of((1 - idx[1]) * half, half), half)
            wo[0] = wo_own[...]
            for step in range(1, shares):
                wo[step, mine, :] = wo_fetched[step - 1][...]
                wo[step, other, :] = wo_swapped[step - 1]
        for block in range(rows_total // BLK):
            rows = pl.ds(block * BLK, BLK)
            outer = pl.ds(base + block * BLK, BLK)
            attn = dot(att[0][rows, :], wo[0])
            for step in range(1, shares):
                attn = attn + dot(att[step][rows, :], wo[step])
            hidden = tok[outer, :].astype(F32) + attn
            acc[rows, :] = hidden
            n = (hidden * row_scale(hidden) * gain_row).astype(BF16)
            normed[rows, :] = n
            logits = dot(n, router_wide, NT)
            lanes = lax.broadcasted_iota(jnp.int32, logits.shape, 1)
            first = lanes == routes[outer, 0:1]
            second = lanes == routes[outer, 1:2]
            one = jnp.sum(jnp.where(first, logits, 0.0), axis=1, keepdims=True)
            two = jnp.sum(jnp.where(second, logits, 0.0), axis=1, keepdims=True)
            peak = jnp.maximum(one, two)
            one = jnp.exp(one - peak)
            two = jnp.exp(two - peak)
            both = one + two
            gates[rows, :] = jnp.where(first, one / both, jnp.where(second, two / both, 0.0))
        own[...] = acc[pl.ds(pl.multiple_of(me * share, share), share), :]
        acc[...] = jnp.zeros_like(acc)
        ggate[...] = jnp.zeros_like(ggate)

    for block in range(rows_total // ROWS):
        rows = pl.ds(block * ROWS, ROWS)
        outer = pl.ds(base + block * ROWS, ROWS)
        lifted, bend = gelu_pair(dot(normed[rows, :], w_in[0]))
        lifted = lifted.astype(BF16)
        act[0, rows, :] = lifted
        slope[0, rows, :] = bend.astype(BF16)
        out = dot(lifted, w_down[0])
        gate = lane_pick(gates[rows, :], expert)
        acc[rows, :] += gate * out
        pulled = jnp.sum(cot[outer, :].astype(F32) * out, axis=1, keepdims=True)
        held = ggate[rows, :]
        lanes = lax.broadcasted_iota(jnp.int32, held.shape, 1)
        ggate[rows, :] = jnp.where(lanes == expert, pulled, held)

    @pl.when(expert == experts - 1)
    def _():
        for step in range(shares):
            start = pl.multiple_of((me ^ step) * share, share)
            parts[step][...] = acc[pl.ds(start, share), :].astype(BF16)


def moe_bwd_kernel(piece, shares, experts, idx, *refs):
    gates, ggate, cot, slope, router, w_in, w_down = refs[:7]
    refs = refs[7:]
    parts, refs = refs[:shares], refs[shares:]
    glog, gpre, acc = refs
    rows_total = gates.shape[0]
    base = piece * rows_total
    share = rows_total // shares
    me = idx[0]
    expert = pl.program_id(0)

    @pl.when(expert == 0)
    def _():
        router_wide = padded_rows(router[...].astype(F32), LANES)
        for block in range(rows_total // ROWS):
            rows = pl.ds(block * ROWS, ROWS)
            g, gg = gates[rows, :], ggate[rows, :]
            back = g * (gg - jnp.sum(g * gg, axis=1, keepdims=True))
            glog[rows, :] = back
            acc[rows, :] = dot(back, router_wide, NN, HIGHEST)

    for block in range(rows_total // ROWS):
        rows = pl.ds(block * ROWS, ROWS)
        gate = lane_pick(gates[rows, :], expert)
        weighted = cot[pl.ds(base + block * ROWS, ROWS), :].astype(F32)
        weighted = (gate * weighted).astype(BF16)
        gp = (dot(weighted, w_down[0], NT) * slope[0, rows, :].astype(F32)).astype(BF16)
        gpre[0, rows, :] = gp
        acc[rows, :] += dot(gp, w_in[0], NT)

    @pl.when(expert == experts - 1)
    def _():
        for step in range(shares):
            start = pl.multiple_of((me ^ step) * share, share)
            parts[step][...] = acc[pl.ds(start, share), :].astype(BF16)


def moe_weights_kernel(pieces, cot, *refs):
    gates, refs = refs[:pieces], refs[pieces:]
    glog, refs = refs[:pieces], refs[pieces:]
    normed, refs = refs[:pieces], refs[pieces:]
    act, refs = refs[:pieces], refs[pieces:]
    gpre, refs = refs[:pieces], refs[pieces:]
    out, router = refs
    rows_total = normed[0].shape[0]
    expert = pl.program_id(0)

    @pl.when(expert == 0)
    def _():
        total = jnp.zeros((LANES, cot.shape[1]), F32)
        for index in range(pieces):
            back = glog[index][...]
            high = back.astype(BF16)
            low = (back - high.astype(F32)).astype(BF16)
            total = total + dot(high, normed[index][...], TN)
            total = total + dot(low, normed[index][...], TN)
        router[...] = total[0:8, :]

    grad_in = jnp.zeros((normed[0].shape[1], gpre[0].shape[2]), F32)
    grad_down = jnp.zeros((act[0].shape[2], cot.shape[1]), F32)
    for index in range(pieces):
        gate = lane_pick(gates[index][...], expert)
        weighted = cot[pl.ds(index * rows_total, rows_total), :].astype(F32)
        weighted = (gate * weighted).astype(BF16)
        grad_in = grad_in + dot(normed[index][...], gpre[index][0], TN)
        grad_down = grad_down + dot(act[index][0], weighted, TN)
    out[0, 0] = grad_in.astype(BF16)
    out[0, 1] = grad_down.astype(BF16)


def hidden_back_kernel(piece, pieces, shares, got, idx, *refs):
    gx, refs = refs[:got], refs[got:]
    wo, own, cot, gain = refs[:4]
    refs = refs[4:]
    ga, refs = refs[:shares], refs[shares:]
    gh, gh_low, ggain = refs
    share = own.shape[0]
    grad = gx[0][...].astype(F32)
    for step in range(1, got):
        grad = grad + gx[step][...].astype(F32)
    hidden = own[...]
    scale = row_scale(hidden)
    unit = hidden * scale
    ggain[...] = jnp.sum(grad * unit, axis=0, keepdims=True)
    gained = grad * gain[...].astype(F32).reshape(1, -1)
    start = piece * (cot.shape[0] // pieces) + idx[0] * share
    mine = cot[pl.ds(pl.multiple_of(start, share), share), :].astype(F32)
    back = mine + scale * (gained - unit * jnp.mean(gained * unit, axis=-1, keepdims=True))
    gh[...] = back
    low = back.astype(BF16)
    gh_low[...] = low
    for step in range(shares):
        ga[step][...] = dot(low, wo[step], NT).astype(BF16)


def w_out_back_kernel(pieces, shares, idx, *refs):
    att, refs = refs[: pieces * shares], refs[pieces * shares :]
    gh_low, out = refs[:pieces], refs[pieces]
    share = gh_low[0].shape[0]
    rows = pl.ds(pl.multiple_of(idx[0] * share, share), share)
    for step in range(shares):
        total = dot(att[step][rows, :], gh_low[0][...], TN)
        for index in range(1, pieces):
            total = total + dot(att[index * shares + step][rows, :], gh_low[index][...], TN)
        out[step] = total.astype(BF16)


def join_kernel(pieces, count, *refs):
    own, refs = refs[:pieces], refs[pieces:]
    got, out = refs[: pieces * count], refs[pieces * count]
    share = own[0].shape[0]
    for index in range(pieces):
        total = own[index][...]
        for step in range(count):
            total = total + got[index * count + step][...].astype(F32)
        out[pl.ds(index * share, share), :] = total.astype(BF16)


def input_back_kernel(pieces, got, idx, *refs):
    gn, refs = refs[:got], refs[got:]
    ghs, refs = refs[:pieces], refs[pieces:]
    tok, gain, gt = refs
    share = ghs[0].shape[0]
    gain_row = gain[...].astype(F32).reshape(1, -1)
    for index in range(pieces):
        rows = pl.ds(index * share, share)
        grad = gn[0][rows, :].astype(F32)
        for step in range(1, got):
            grad = grad + gn[step][rows, :].astype(F32)
        start = index * (tok.shape[0] // pieces) + idx[0] * share
        x = tok[pl.ds(pl.multiple_of(start, share), share), :].astype(F32)
        scale = row_scale(x)
        unit = x * scale
        gained = grad * gain_row
        back = scale * (gained - unit * jnp.mean(gained * unit, axis=-1, keepdims=True))
        gt[rows, :] = (ghs[index][...] + back).astype(BF16)


def place_kernel(pieces, shares, idx, *refs):
    blocks, out = refs[:shares], refs[shares]
    rows_total = out.shape[0] // pieces
    share = rows_total // shares
    for step in range(shares):
        owner = idx[0] ^ step
        for index in range(pieces):
            start = pl.multiple_of(index * rows_total + owner * share, share)
            got = blocks[step][pl.ds(index * share, share), :]
            out[pl.ds(start, share), :] = got.astype(out.dtype)


ROWS = 512
PIECES = 1

SMEM = pl.BlockSpec(memory_space=pltpu.SMEM)
VMEM = pl.BlockSpec(memory_space=pltpu.VMEM)


def shaped(shape, dtype):
    return jax.ShapeDtypeStruct(shape, dtype)


def whole_call(kernel, outs, args, scratch=(), flops=0, moved=0, with_index=True):
    specs = ([SMEM] if with_index else []) + [VMEM] * (len(args) - (1 if with_index else 0))
    return pl.pallas_call(
        kernel,
        out_shape=outs,
        in_specs=specs,
        out_specs=[VMEM] * len(outs),
        scratch_shapes=list(scratch),
        compiler_params=pltpu.CompilerParams(vmem_limit_bytes=VMEM_LIMIT),
        cost_estimate=pl.CostEstimate(flops=flops, bytes_accessed=moved, transcendentals=0),
    )(*args)


def swap(value, axis, bit):
    count = lax.axis_size(axis)
    return lax.ppermute(value, axis, [(i, i ^ bit) for i in range(count)])


def sum_over(value, axis):
    bit = 1
    while bit < lax.axis_size(axis):
        value = value + swap(value, axis, bit)
        bit *= 2
    return value


def gather_parts(value, axis):
    count = lax.axis_size(axis)
    if count != 4:
        return [value] + [swap(value, axis, bit) for bit in range(1, count)]
    two = swap(value, axis, 2)
    one = swap(value, axis, 1)
    return [value, one, two, swap(after(two, one), axis, 1)]


def reduce_near(parts, axis):
    return swap(parts[3], axis, 1), swap(parts[1], axis, 1)


def reduce_far(parts, near, axis):
    pair = (parts[2].astype(F32) + near[0].astype(F32)).astype(parts[2].dtype)
    return [parts[0], near[1], swap(pair, axis, 2)], pair


def exchange(parts, axis):
    return [parts[0]] + [swap(parts[bit], axis, bit) for bit in range(1, len(parts))]


def halves_of(value, axis, chosen):
    half = value.shape[axis] // 2
    keep = lax.dynamic_slice_in_dim(value, chosen * half, half, axis)
    send = lax.dynamic_slice_in_dim(value, (1 - chosen) * half, half, axis)
    return keep, send


def bits_of(axis):
    count = lax.axis_size(axis)
    return [1 << level for level in range(count.bit_length() - 1)]


def gather_back(value, mesh_axis, axis):
    me = lax.axis_index(mesh_axis)
    for bit in reversed(bits_of(mesh_axis)):
        got = swap(value, mesh_axis, bit)
        low = (me // bit) % 2 == 0
        value = jnp.concatenate(
            [jnp.where(low, value, got), jnp.where(low, got, value)], axis=axis
        )
    return value


def together(*values):
    return lax.optimization_barrier(values)


def after(value, *others):
    return lax.optimization_barrier((value, *others))[0]


def body(
    tokens, segments, routes, grad_out, gain_attn, w_qkv, w_out, rel_bias,
    gain_moe, w_router, w_in, w_down,
):
    tok_rows, width = tokens.shape
    heads = rel_bias.shape[1]
    features = w_qkv.shape[2]
    head_size = features // heads
    experts, _, hidden_units = w_in.shape
    shares = lax.axis_size("tensor")
    rows = tok_rows // PIECES
    share = rows // shares
    me = lax.axis_index("tensor").astype(jnp.int32)
    side = (lax.axis_index("dp") % 2).astype(jnp.int32)
    idx = jnp.stack([me, side])
    mib = 1 << 20
    others = range(1, shares)
    four = shares == 4

    half_rows = features // 2
    my_half = lax.dynamic_slice_in_dim(w_out, side * half_rows, half_rows, 0)
    halves = [swap(my_half, "tensor", by) for by in others]

    build_hot, gather_hot = near_tables()
    build_hot = jnp.asarray(np.swapaxes(build_hot, 1, 2), BF16)
    gather_hot = jnp.asarray(gather_hot, F32)
    w_qkv_t = jnp.swapaxes(w_qkv, 1, 2)
    router_t = w_router.T

    normed_one, qh, k, v, _, att, ot, lse, bias, far = whole_call(
        functools.partial(attn_fwd_kernel, 0, PIECES, heads, head_size),
        [
            shaped((rows, width), BF16),
            shaped((heads, rows, features), BF16),
            shaped((rows, features), BF16),
            shaped((rows, features), BF16),
            shaped((features, rows), BF16),
            shaped((rows, features), BF16),
            shaped((features, rows), F32),
            shaped((8, rows), F32),
            shaped((2 * heads, BLK, BLK), F32),
            shaped((8, LANES), F32),
        ],
        [tokens, gain_attn, w_qkv_t, segments, rel_bias.T, build_hot],
        flops=6 * 10**9, moved=8 * mib, with_index=False,
    )
    att = after(att, *halves)
    atts = gather_parts(att, "tensor")
    swapped = swap(after(jnp.stack(halves), att), "dp", 1)

    full = lambda shape: pl.BlockSpec(shape, lambda e: (0,) * len(shape))
    per_expert = lambda shape: pl.BlockSpec((1,) + shape, lambda e: (e, 0, 0))
    params = pltpu.CompilerParams(
        vmem_limit_bytes=VMEM_LIMIT, dimension_semantics=("arbitrary",)
    )
    moe_flops = 4 * experts * rows * width * hidden_units

    fwd = pl.pallas_call(
        functools.partial(moe_fwd_kernel, 0, PIECES, shares, experts),
        grid=(experts,),
        in_specs=[SMEM]
        + [full((rows, features))] * shares
        + [full((features, width)), full((shares - 1, half_rows, width))]
        + [full((half_rows, width))] * (shares - 1)
        + [
            full((rows, width)), full((width,)), full((experts, width)),
            full((rows, 2)), full((rows, width)),
            per_expert((width, hidden_units)), per_expert((hidden_units, width)),
        ],
        out_specs=[full((share, width))] * shares
        + [
            full((shares, features, width)), full((rows, width)),
            full((share, width)), full((rows, LANES)), full((rows, LANES)),
            per_expert((rows, hidden_units)), per_expert((rows, hidden_units)),
        ],
        out_shape=[shaped((share, width), BF16)] * shares
        + [
            shaped((shares, features, width), BF16),
            shaped((rows, width), BF16),
            shaped((share, width), F32),
            shaped((rows, LANES), F32),
            shaped((rows, LANES), F32),
            shaped((experts, rows, hidden_units), BF16),
            shaped((experts, rows, hidden_units), BF16),
        ],
        scratch_shapes=[pltpu.VMEM((rows, width), F32)],
        compiler_params=params,
        cost_estimate=pl.CostEstimate(
            flops=moe_flops, bytes_accessed=32 * mib, transcendentals=0
        ),
    )(
        idx, *atts, w_out, swapped, *halves, tokens, gain_moe, router_t, routes, grad_out,
        w_in, w_down,
    )
    moe_parts = fwd[:shares]
    wo, normed_two, own_hidden, gates, ggate, act, slope = fwd[shares:]
    if four:
        moe_near = reduce_near(moe_parts, "tensor")
    else:
        moe_near = exchange(moe_parts, "tensor")[1:]

    bwd = pl.pallas_call(
        functools.partial(moe_bwd_kernel, 0, shares, experts),
        grid=(experts,),
        in_specs=[
            SMEM, full((rows, LANES)), full((rows, LANES)), full((rows, width)),
            per_expert((rows, hidden_units)), full((experts, width)),
            per_expert((width, hidden_units)), per_expert((hidden_units, width)),
        ],
        out_specs=[full((share, width))] * shares
        + [full((rows, LANES)), per_expert((rows, hidden_units))],
        out_shape=[shaped((share, width), BF16)] * shares
        + [
            shaped((rows, LANES), F32),
            shaped((experts, rows, hidden_units), BF16),
        ],
        scratch_shapes=[pltpu.VMEM((rows, width), F32)],
        compiler_params=params,
        cost_estimate=pl.CostEstimate(
            flops=moe_flops, bytes_accessed=26 * mib, transcendentals=0
        ),
    )(idx, gates, ggate, grad_out, slope, router_t, w_in, w_down)
    gx_parts = [after(part, *moe_near) for part in bwd[:shares]]
    glog, gpre = bwd[shares:]
    gx_near = reduce_near(gx_parts, "tensor") if four else exchange(gx_parts, "tensor")[1:]

    expert_grads, router_rows = pl.pallas_call(
        functools.partial(moe_weights_kernel, PIECES),
        grid=(experts,),
        in_specs=[
            full((rows, width)), full((rows, LANES)), full((rows, LANES)), full((rows, width)),
            per_expert((rows, hidden_units)), per_expert((rows, hidden_units)),
        ],
        out_specs=[
            pl.BlockSpec((1, 2, width, width), lambda e: (e, 0, 0, 0)), full((8, width))
        ],
        out_shape=[shaped((experts, 2, width, width), BF16), shaped((8, width), F32)],
        compiler_params=params,
        cost_estimate=pl.CostEstimate(
            flops=moe_flops, bytes_accessed=26 * mib, transcendentals=0
        ),
    )(grad_out, gates, glog, normed_two, act, gpre)
    expert_rows = after(expert_grads.reshape(experts * 2 * width, width), *gx_near)
    expert_rows = lax.psum_scatter(expert_rows, "dp", scatter_dimension=0, tiled=True)

    if four:
        gx_near = after(gx_near[0], router_rows), gx_near[1]
        gx_got, _ = reduce_far(gx_parts, gx_near, "tensor")
    else:
        gx_got = [gx_parts[0], *gx_near]
    back = whole_call(
        functools.partial(hidden_back_kernel, 0, PIECES, shares, len(gx_got)),
        [shaped((share, features), BF16)] * shares
        + [shaped((share, width), F32), shaped((share, width), BF16), shaped((1, width), F32)],
        [idx, *gx_got, wo, own_hidden, grad_out, gain_moe],
        flops=3 * 10**8, moved=5 * mib,
    )
    go = exchange(back[:shares], "tensor")
    grad_hidden, gh_low, ggain_two = back[shares:]
    w_out_rows = whole_call(
        functools.partial(w_out_back_kernel, PIECES, shares),
        [shaped((shares, features, width), BF16)],
        [idx, *atts, gh_low],
        flops=3 * 10**8, moved=4 * mib,
    )[0]
    go[1:] = after(go[1], w_out_rows), *go[2:]

    if four:
        moe_near = after(moe_near[0], *go[1:]), moe_near[1]
        moe_got, _ = reduce_far(moe_parts, moe_near, "tensor")
    else:
        moe_got = [moe_parts[0], *moe_near]
    result_share = whole_call(
        functools.partial(join_kernel, PIECES, len(moe_got)),
        [shaped((share, width), BF16)],
        [own_hidden, *moe_got],
        moved=3 * mib, with_index=False,
    )[0]
    attn_back = whole_call(
        functools.partial(attn_bwd_kernel, 0, PIECES, heads, head_size, shares),
        [shaped((share, width), BF16)] * shares
        + [shaped((3, rows, features), BF16), shaped((features, width), BF16)],
        [
            idx, *go, tokens, router_rows, ggain_two, qh, ot, lse, k, v, bias, far, segments,
            w_qkv_t, gather_hot,
        ],
        [pltpu.VMEM((rows, features), F32)] * 2
        + [
            pltpu.VMEM((features, rows), F32),
            pltpu.VMEM((2 * heads, BLK, BLK), F32),
            pltpu.VMEM((rows, features), BF16),
            pltpu.VMEM((features, width), F32),
            pltpu.VMEM((features, rows), BF16),
            pltpu.VMEM((8, rows), F32),
            pltpu.VMEM((2, 8, 2 * BLK), F32),
            pltpu.VMEM((8, BLK), F32),
        ],
        flops=14 * 10**9, moved=8 * mib,
    )
    gn_parts = [after(part, moe_got[-1]) for part in attn_back[:shares]]
    gproj, misc = attn_back[shares:]

    qkv_rows = whole_call(
        functools.partial(qkv_weights_kernel, PIECES),
        [shaped((3, features, width), BF16)],
        [normed_one, gproj],
        flops=10**9, moved=4 * mib, with_index=False,
    )[0]
    late = jnp.concatenate([qkv_rows, misc[None], w_out_rows], axis=0)
    if four:
        near = reduce_near(gn_parts, "tensor")
        near = after(near[0], late, near[1]), near[1]
        gn_got, mark = reduce_far(gn_parts, near, "tensor")
    else:
        gn_got = exchange(gn_parts, "tensor")
        mark = gn_got[-1]

    place = lax.axis_index("dp")

    def halve(value, bit, *ready):
        keep, send = halves_of(value, 1, (place // bit) % 2)
        got = swap(after(send, *ready), "dp", bit)
        return (keep.astype(F32) + got.astype(F32)).astype(BF16)

    bits = bits_of("dp")
    late = halve(late, 1)
    keep, send = halves_of(late, 1, (place // bits[1]) % 2)
    got = swap(send[:4], "dp", bits[1]), swap(send[4:], "dp", bits[1])

    expert_rows = after(expert_rows, mark)
    gt_share = whole_call(
        functools.partial(input_back_kernel, PIECES, len(gn_got)),
        [shaped((share, width), BF16)],
        [idx, *gn_got, grad_hidden, tokens, gain_attn],
        moved=5 * mib,
    )[0]
    gt_now, result_share, *got = together(gt_share, result_share, *got)
    got = jnp.concatenate(got, axis=0)
    late = (keep.astype(F32) + got.astype(F32)).astype(BF16)
    keep, send = halves_of(late, 1, (place // bits[2]) % 2)
    two, one, got = together(
        swap(gt_now, "tensor", 2), swap(gt_now, "tensor", 1), swap(send, "dp", bits[2])
    )
    late = (keep.astype(F32) + got.astype(F32)).astype(BF16)
    for bit in bits[3:]:
        late = halve(late, bit)

    sent = together(*[swap(jnp.stack([late[4 + by], late[3]]), "tensor", by) for by in others])
    share_now = after(result_share, two)
    three, result_two, result_one = (
        swap(two, "tensor", 1), swap(share_now, "tensor", 2), swap(share_now, "tensor", 1)
    )
    out_sum, small = late[4].astype(F32), [late[3]]
    for got in sent:
        out_sum = out_sum + got[0].astype(F32)
        small.append(got[1])
    small = [part.astype(F32) for part in small]
    while len(small) > 1:
        small = [small[at] + small[at + 1] for at in range(0, len(small), 2)]
    late = jnp.concatenate(
        [late[:3], jnp.stack([small[0].astype(BF16), out_sum.astype(BF16)])], axis=0
    )

    expert_rows = lax.all_gather(expert_rows, "dp", axis=0, tiled=True)

    def joined(value, got, bit):
        low = (place // bit) % 2 == 0
        return jnp.concatenate([jnp.where(low, value, got), jnp.where(low, got, value)], axis=1)

    for bit in reversed(bits[3:]):
        late = joined(late, swap(late, "dp", bit), bit)
    got, three, result_two, result_one = together(
        swap(late, "dp", bits[2]), three, result_two, result_one
    )
    late = joined(late, got, bits[2])
    grad_tokens = whole_call(
        functools.partial(place_kernel, PIECES, shares),
        [shaped((rows, width), F32)], [idx, gt_share, one, two, three], moved=5 * mib,
    )[0]
    grad_w_in = expert_rows.reshape(experts, 2, width, width)[:, 0].astype(F32)
    got, result_three, _, _ = together(
        swap(late, "dp", bits[1]), swap(result_two, "tensor", 1), grad_w_in, grad_tokens
    )
    late = joined(late, got, bits[1])
    expert_rows = after(expert_rows, got)
    grad_w_down = expert_rows.reshape(experts, 2, width, width)[:, 1].astype(F32)
    result = whole_call(
        functools.partial(place_kernel, PIECES, shares),
        [shaped((rows, width), BF16)],
        [idx, result_share, result_one, result_two, result_three],
        moved=3 * mib,
    )[0]
    got = after(swap(late, "dp", bits[0]), grad_w_down, result)
    late = joined(late, got, bits[0])
    grad_w_qkv = jnp.swapaxes(late[:3], 1, 2).astype(F32)
    grad_w_out = late[4].astype(F32)
    small = late[3].astype(F32)
    grad_rel = lax.dynamic_slice_in_dim(small, me * 8, 8, 0)
    first = 8 * shares
    return (
        result,
        grad_tokens,
        small[first + 8],
        grad_w_qkv,
        grad_w_out,
        grad_rel[:heads, :NB].T,
        small[first + 9],
        small[first : first + experts].T,
        grad_w_in,
        grad_w_down,
    )


def solution(mesh):
    placed = (
        P("dp", None),
        P("dp", None),
        P("dp", None),
        P("dp", None),
        P(),
        P(None, None, "tensor"),
        P("tensor", None),
        P(None, "tensor"),
        P(),
        P(),
        P(None, None, "tensor"),
        P(None, "tensor", None),
    )
    return jax.shard_map(
        body,
        mesh=mesh,
        in_specs=placed,
        out_specs=(
            P("dp", None),
            P("dp", None),
            P(),
            P(None, None, "tensor"),
            P("tensor", None),
            P(None, "tensor"),
            P(),
            P(),
            P(None, None, "tensor"),
            P(None, "tensor", None),
        ),
        check_vma=False,
    )
```

```python
import functools
import math

import jax
import jax.numpy as jnp
import numpy as np
from jax import lax
from jax.experimental import pallas as pl
from jax.experimental.pallas import tpu as pltpu
from jax.sharding import PartitionSpec as P

NB = 32
DIST = 128
EPSILON = 1e-06
NEGATIVE = -1e30
HIGHEST = lax.Precision.HIGHEST
F32 = jnp.float32
BF16 = jnp.bfloat16
BLK = 256
LANES = 128
VMEM_LIMIT = 56 * 1024 * 1024

NN = (((1,), (0,)), ((), ()))
NT = (((1,), (1,)), ((), ()))
TN = (((0,), (0,)), ((), ()))


def dot(a, b, dims=NN, precision=None):
    return lax.dot_general(a, b, dims, precision=precision, preferred_element_type=F32)


def bucket_of(distance):
    halfway = NB // 2
    thresholds = [
        int(math.ceil(halfway * (DIST / halfway) ** (step / halfway))) for step in range(halfway)
    ]
    beyond = sum((distance >= threshold).astype(np.int64) for threshold in thresholds)
    return np.where(distance < halfway, distance, halfway - 1 + beyond)


def near_tables():
    lanes = np.arange(2 * BLK)
    offset = np.where(lanes < BLK, lanes, lanes - 2 * BLK)
    build = np.stack([np.maximum(offset, 0), np.maximum(BLK + offset, 0)])
    gather = np.stack([lanes - (BLK - 1), lanes + 1])
    eye = np.eye(NB, dtype=np.float32)
    build_hot = eye[bucket_of(build)]
    gather_hot = eye[bucket_of(np.maximum(gather, 0))] * (gather >= 0)[..., None]
    return build_hot, gather_hot


def row_scale(values):
    return lax.rsqrt(jnp.mean(values * values, axis=-1, keepdims=True) + EPSILON)


def lane_pick(values, index):
    lanes = lax.broadcasted_iota(jnp.int32, values.shape, 1)
    return jnp.sum(jnp.where(lanes == index, values, 0.0), axis=1, keepdims=True)


def masked_scores(k_tile, qh_tile, bias, seg_k, seg_q, diagonal):
    scores = dot(k_tile, qh_tile, NT) + bias
    allowed = seg_k == seg_q
    if diagonal:
        key_at = lax.broadcasted_iota(jnp.int32, scores.shape, 0)
        query_at = lax.broadcasted_iota(jnp.int32, scores.shape, 1)
        allowed = allowed & (key_at <= query_at)
    return jnp.where(allowed, scores, NEGATIVE)


def tile_bias(bias_ref, far_ref, head, delta):
    if delta < 2:
        return bias_ref[2 * head + delta]
    return far_ref[pl.ds(head, 1), 0:1]


def column_of(row):
    spread = jnp.broadcast_to(row.astype(F32), (8, row.shape[1]))
    return spread.T[:, 0:1]


def attn_fwd_kernel(piece, pieces, heads, head_size, *refs):
    tok, gain, w, seg = refs[:4]
    refs = refs[4:]
    if piece == 0:
        rel, build = refs[:2]
        refs = refs[2:]
    else:
        bias, far = refs[:2]
        refs = refs[2:]
    old_k, refs = refs[:piece], refs[piece:]
    old_vt, refs = refs[:piece], refs[piece:]
    normed, qh, k, v, vt, att, ot, lse = refs[:8]
    if piece == 0:
        bias, far = refs[8:]
    keys_of, vt_of = [*old_k, k], [*old_vt, vt]
    rows_total = tok.shape[0] // pieces
    base = piece * rows_total
    features = w.shape[1]
    blocks = rows_total // BLK
    gain_row = gain[...].astype(F32).reshape(1, -1)
    lanes = lax.broadcasted_iota(jnp.int32, (BLK, features), 1)
    for block in range(blocks):
        rows = pl.ds(block * BLK, BLK)
        x = tok[pl.ds(base + block * BLK, BLK), :].astype(F32)
        n = (x * row_scale(x) * gain_row).astype(BF16)
        normed[rows, :] = n
        q_rows = dot(n, w[0], NT).astype(BF16).astype(F32) * (head_size**-0.5)
        for head in range(heads):
            inside = (lanes >= head * head_size) & (lanes < (head + 1) * head_size)
            qh[head, rows, :] = jnp.where(inside, q_rows, 0.0).astype(BF16)
        k[rows, :] = dot(n, w[1], NT).astype(BF16)
        v_rows = dot(n, w[2], NT).astype(BF16)
        v[rows, :] = v_rows
        vt[:, rows] = v_rows.astype(F32).T.astype(BF16)
    if piece == 0:
        far[...] = jnp.zeros_like(far)
        far[0:heads, :] = jnp.broadcast_to(rel[:, NB - 1 : NB].astype(F32), (heads, LANES))
        for delta in range(2):
            near = dot(rel[...], build[delta])
            for head in range(heads):
                spread = jnp.broadcast_to(near[head : head + 1, :], (BLK, 2 * BLK))
                turned = pltpu.roll(spread, 0, 1, stride=1, stride_axis=0)
                bias[2 * head + delta] = turned[:, :BLK]
    lse[...] = jnp.zeros_like(lse)
    seg_row = seg[...].astype(F32)
    seg_col = column_of(seg[...])

    def one_head(head, carry):
        part = pl.ds(pl.multiple_of(head * head_size, head_size), head_size)
        for block in range(blocks):
            qb = piece * blocks + block
            cols = pl.ds(block * BLK, BLK)
            q_tile = qh[head, cols, :]
            tiles = []
            for kb in range(qb + 1):
                keys = pl.ds(kb % blocks * BLK, BLK)
                tiles.append(
                    masked_scores(
                        keys_of[kb // blocks][keys, :], q_tile,
                        tile_bias(bias, far, head, qb - kb),
                        seg_col[kb * BLK : (kb + 1) * BLK, :],
                        seg_row[:, qb * BLK : (qb + 1) * BLK], kb == qb,
                    )
                )
            peak = functools.reduce(
                jnp.maximum, [jnp.max(t, axis=0, keepdims=True) for t in tiles]
            )
            total = jnp.zeros((1, BLK), F32)
            out = jnp.zeros((head_size, BLK), F32)
            for kb in range(qb + 1):
                raised = jnp.exp(tiles[kb] - peak)
                total = total + jnp.sum(raised, axis=0, keepdims=True)
                values = vt_of[kb // blocks][part, pl.ds(kb % blocks * BLK, BLK)]
                out = out + dot(values, raised.astype(BF16))
            ot[part, cols] = out / total
            lse[pl.ds(head, 1), cols] = peak + jnp.log(total)
        return carry

    lax.fori_loop(0, heads, one_head, 0)
    for block in range(blocks):
        cols = pl.ds(block * BLK, BLK)
        att[cols, :] = ot[:, cols].T.astype(BF16)


def attn_bwd_kernel(piece, pieces, heads, head_size, shares, idx, *refs):
    held = piece + 1
    last = held == pieces
    go_parts, refs = refs[:shares], refs[shares:]
    tok, router, gain_two, qh, ot, lse = refs[:6]
    refs = refs[6:]
    ks, refs = refs[:held], refs[held:]
    vs, refs = refs[:held], refs[held:]
    bias, far, seg = refs[:3]
    refs = refs[3:]
    if piece:
        gk_in, refs = refs[:piece], refs[piece:]
        gv_in, refs = refs[:piece], refs[piece:]
        gq_in, refs = refs[:piece], refs[piece:]
        acc_in, refs = refs[0], refs[1:]
    if last:
        w, hot = refs[:2]
        refs = refs[2:]
        gn_parts, refs = refs[:shares], refs[shares:]
        gproj, misc = refs[:2]
        refs = refs[2:]
        gk, refs = refs[:held], refs[held:]
        gv, refs = refs[:held], refs[held:]
        gq_t, acc = refs[:2]
        refs = refs[2:]
    else:
        gk, refs = refs[:held], refs[held:]
        gv, refs = refs[:held], refs[held:]
        gq_t, acc = refs[:2]
        refs = refs[2:]
    go, misc_sum, kt, d_row, near_sum, far_sum = refs
    rows_total, features = ks[0].shape
    blocks = rows_total // BLK
    share = rows_total // shares
    me = idx[0]
    for step in range(shares):
        start = pl.multiple_of((me ^ step) * share, share)
        go[pl.ds(start, share), :] = go_parts[step][...]
    for index in range(held):
        for block in range(blocks):
            cols = pl.ds(block * BLK, BLK)
            kt[:, pl.ds((index * blocks + block) * BLK, BLK)] = (
                ks[index][cols, :].astype(F32).T.astype(BF16)
            )
        if index < piece:
            gk[index][...] = gk_in[index][...]
            gv[index][...] = gv_in[index][...]
        else:
            gk[index][...] = jnp.zeros_like(gk[index])
            gv[index][...] = jnp.zeros_like(gv[index])
    if piece:
        acc[...] = acc_in[...]
    else:
        acc[...] = jnp.zeros_like(acc)
    for block in range(blocks):
        cols = pl.ds(block * BLK, BLK)
        product = go[cols, :].astype(F32).T * ot[:, cols]
        for head in range(heads):
            part = product[head * head_size : (head + 1) * head_size, :]
            d_row[head : head + 1, cols] = jnp.sum(part, axis=0, keepdims=True)
    near_sum[...] = jnp.zeros_like(near_sum)
    far_sum[...] = jnp.zeros_like(far_sum)
    key_at = lax.broadcasted_iota(jnp.int32, (BLK, BLK), 0)
    other_at = lax.broadcasted_iota(jnp.int32, (BLK, BLK), 1)
    flip = (key_at + other_at == BLK - 1).astype(F32)
    seg_row = seg[...].astype(F32)
    seg_col = column_of(seg[...])

    def one_head(head, carry):
        part = pl.ds(pl.multiple_of(head * head_size, head_size), head_size)
        lanes = lax.broadcasted_iota(jnp.int32, (BLK, features), 1)
        inside = (lanes >= head * head_size) & (lanes < (head + 1) * head_size)
        for block in range(blocks):
            qb = piece * blocks + block
            cols = pl.ds(block * BLK, BLK)
            q_tile = qh[head, cols, :]
            go_tile = jnp.where(inside, go[cols, :].astype(F32), 0.0).astype(BF16)
            log_total = lse[pl.ds(head, 1), cols]
            d_tile = d_row[pl.ds(head, 1), cols]
            gq = jnp.zeros((head_size, BLK), F32)
            for kb in range(qb + 1):
                index = kb // blocks
                keys = pl.ds(kb % blocks * BLK, BLK)
                delta = qb - kb
                scores = masked_scores(
                    ks[index][keys, :], q_tile, tile_bias(bias, far, head, delta),
                    seg_col[kb * BLK : (kb + 1) * BLK, :],
                    seg_row[:, qb * BLK : (qb + 1) * BLK], delta == 0,
                )
                probs = jnp.exp(scores - log_total)
                gs = probs * (dot(vs[index][keys, :], go_tile, NT) - d_tile)
                if delta < 2:
                    acc[2 * head + delta] += gs
                else:
                    far_sum[pl.ds(head, 1), :] += jnp.sum(gs, axis=0, keepdims=True)
                gs_low = gs.astype(BF16)
                gv[index][keys, :] += dot(probs.astype(BF16), go_tile)
                gk[index][keys, :] += dot(gs_low, q_tile)
                gq = gq + dot(kt[part, kb * BLK : (kb + 1) * BLK], gs_low)
            gq_t[part, cols] = gq * (head_size**-0.5)
        return carry

    lax.fori_loop(0, heads, one_head, 0)
    if not last:
        return
    gqs = [*(gq_in if piece else ()), gq_t]
    for index in range(held):
        for block in range(blocks):
            rows = pl.ds(block * BLK, BLK)
            out = pl.ds((index * blocks + block) * BLK, BLK)
            gproj[0, out, :] = gqs[index][:, rows].T.astype(BF16)
            gproj[1, out, :] = gk[index][rows, :].astype(BF16)
            gproj[2, out, :] = gv[index][rows, :].astype(BF16)
    gain_one = jnp.zeros_like(gain_two)
    for step in range(shares):
        for index in range(pieces):
            start = index * rows_total + (me ^ step) * share
            rows = pl.ds(pl.multiple_of(start, share), share)
            total = dot(gproj[0, rows, :], w[0])
            total = total + dot(gproj[1, rows, :], w[1])
            total = total + dot(gproj[2, rows, :], w[2])
            gn_parts[step][pl.ds(index * share, share), :] = total.astype(BF16)
            x = tok[rows, :].astype(F32)
            gain_one = gain_one + jnp.sum(total * (x * row_scale(x)), axis=0, keepdims=True)
    for head in range(heads):
        for delta in range(2):
            turned = dot(flip, acc[2 * head + delta], NN, HIGHEST)
            wide = jnp.concatenate([turned, jnp.zeros_like(turned)], axis=1)
            sheared = pltpu.roll(wide, 0, 1, stride=1, stride_axis=0)
            near_sum[delta, head : head + 1, :] = jnp.sum(sheared, axis=0, keepdims=True)
    summed = dot(near_sum[0], hot[0], NN, HIGHEST) + dot(near_sum[1], hot[1], NN, HIGHEST)
    buckets = lax.broadcasted_iota(jnp.int32, summed.shape, 1)
    beyond = jnp.sum(far_sum[...], axis=1, keepdims=True)
    summed = summed + jnp.where(buckets == NB - 1, beyond, 0.0)
    misc_sum[...] = jnp.zeros_like(misc_sum)
    misc_sum[pl.ds(pl.multiple_of(me * 8, 8), 8), 0:NB] = summed
    misc_sum[8 * shares : 8 * shares + 8, :] = router[...]
    misc_sum[8 * shares + 8 : 8 * shares + 9, :] = gain_one
    misc_sum[8 * shares + 9 : 8 * shares + 10, :] = gain_two[...]
    misc[...] = misc_sum[...].astype(BF16)


def qkv_weights_kernel(pieces, *refs):
    normed = refs[:pieces]
    gproj, out = refs[pieces:]
    rows_total = normed[0].shape[0]
    for c in range(3):
        total = dot(gproj[c, pl.ds(0, rows_total), :], normed[0][...], TN)
        for index in range(1, pieces):
            rows = pl.ds(index * rows_total, rows_total)
            total = total + dot(gproj[c, rows, :], normed[index][...], TN)
        out[c] = total.astype(BF16)


def gelu_pair(values):
    squared = values * values
    bent = jnp.tanh(values * (0.7978845608028654 + 0.7978845608028654 * 0.044715 * squared))
    half = 0.5 * (1.0 + bent)
    lifted = values * half
    slope = 0.7978845608028654 + 3.0 * 0.7978845608028654 * 0.044715 * squared
    return lifted, half + lifted * (1.0 - bent) * slope


def padded_rows(values, rows):
    missing = jnp.zeros((rows - values.shape[0], values.shape[1]), values.dtype)
    return jnp.concatenate([values, missing], axis=0)


def moe_fwd_kernel(piece, pieces, shares, experts, idx, *refs):
    att, refs = refs[:shares], refs[shares:]
    if piece == 0:
        wo_own, wo_swapped, refs = refs[0], refs[1], refs[2:]
        wo_fetched, refs = refs[: shares - 1], refs[shares - 1 :]
    else:
        wo, refs = refs[0], refs[1:]
    tok, gain, router, routes, cot, w_in, w_down = refs[:7]
    refs = refs[7:]
    parts, refs = refs[:shares], refs[shares:]
    if piece == 0:
        wo, refs = refs[0], refs[1:]
    normed, own, gates, ggate, act, slope, acc = refs
    rows_total = tok.shape[0] // pieces
    base = piece * rows_total
    share = rows_total // shares
    me = idx[0]
    expert = pl.program_id(0)

    @pl.when(expert == 0)
    def _():
        gain_row = gain[...].astype(F32).reshape(1, -1)
        router_wide = padded_rows(router[...].astype(F32), LANES).astype(BF16)
        if piece == 0:
            half = wo_own.shape[0] // 2
            mine = pl.ds(pl.multiple_of(idx[1] * half, half), half)
            other = pl.ds(pl.multiple_of((1 - idx[1]) * half, half), half)
            wo[0] = wo_own[...]
            for step in range(1, shares):
                wo[step, mine, :] = wo_fetched[step - 1][...]
                wo[step, other, :] = wo_swapped[step - 1]
        for block in range(rows_total // BLK):
            rows = pl.ds(block * BLK, BLK)
            outer = pl.ds(base + block * BLK, BLK)
            attn = dot(att[0][rows, :], wo[0])
            for step in range(1, shares):
                attn = attn + dot(att[step][rows, :], wo[step])
            hidden = tok[outer, :].astype(F32) + attn
            acc[rows, :] = hidden
            n = (hidden * row_scale(hidden) * gain_row).astype(BF16)
            normed[rows, :] = n
            logits = dot(n, router_wide, NT)
            lanes = lax.broadcasted_iota(jnp.int32, logits.shape, 1)
            first = lanes == routes[outer, 0:1]
            second = lanes == routes[outer, 1:2]
            one = jnp.sum(jnp.where(first, logits, 0.0), axis=1, keepdims=True)
            two = jnp.sum(jnp.where(second, logits, 0.0), axis=1, keepdims=True)
            peak = jnp.maximum(one, two)
            one = jnp.exp(one - peak)
            two = jnp.exp(two - peak)
            both = one + two
            gates[rows, :] = jnp.where(first, one / both, jnp.where(second, two / both, 0.0))
        own[...] = acc[pl.ds(pl.multiple_of(me * share, share), share), :]
        acc[...] = jnp.zeros_like(acc)
        ggate[...] = jnp.zeros_like(ggate)

    for block in range(rows_total // ROWS):
        rows = pl.ds(block * ROWS, ROWS)
        outer = pl.ds(base + block * ROWS, ROWS)
        lifted, bend = gelu_pair(dot(normed[rows, :], w_in[0]))
        lifted = lifted.astype(BF16)
        act[0, rows, :] = lifted
        slope[0, rows, :] = bend.astype(BF16)
        out = dot(lifted, w_down[0])
        gate = lane_pick(gates[rows, :], expert)
        acc[rows, :] += gate * out
        pulled = jnp.sum(cot[outer, :].astype(F32) * out, axis=1, keepdims=True)
        held = ggate[rows, :]
        lanes = lax.broadcasted_iota(jnp.int32, held.shape, 1)
        ggate[rows, :] = jnp.where(lanes == expert, pulled, held)

    @pl.when(expert == experts - 1)
    def _():
        for step in range(shares):
            start = pl.multiple_of((me ^ step) * share, share)
            parts[step][...] = acc[pl.ds(start, share), :].astype(BF16)


def moe_bwd_kernel(piece, shares, experts, idx, *refs):
    gates, ggate, cot, slope, router, w_in, w_down = refs[:7]
    refs = refs[7:]
    parts, refs = refs[:shares], refs[shares:]
    glog, gpre, acc = refs
    rows_total = gates.shape[0]
    base = piece * rows_total
    share = rows_total // shares
    me = idx[0]
    expert = pl.program_id(0)

    @pl.when(expert == 0)
    def _():
        router_wide = padded_rows(router[...].astype(F32), LANES)
        for block in range(rows_total // ROWS):
            rows = pl.ds(block * ROWS, ROWS)
            g, gg = gates[rows, :], ggate[rows, :]
            back = g * (gg - jnp.sum(g * gg, axis=1, keepdims=True))
            glog[rows, :] = back
            acc[rows, :] = dot(back, router_wide, NN, HIGHEST)

    for block in range(rows_total // ROWS):
        rows = pl.ds(block * ROWS, ROWS)
        gate = lane_pick(gates[rows, :], expert)
        weighted = cot[pl.ds(base + block * ROWS, ROWS), :].astype(F32)
        weighted = (gate * weighted).astype(BF16)
        gp = (dot(weighted, w_down[0], NT) * slope[0, rows, :].astype(F32)).astype(BF16)
        gpre[0, rows, :] = gp
        acc[rows, :] += dot(gp, w_in[0], NT)

    @pl.when(expert == experts - 1)
    def _():
        for step in range(shares):
            start = pl.multiple_of((me ^ step) * share, share)
            parts[step][...] = acc[pl.ds(start, share), :].astype(BF16)


def moe_weights_kernel(pieces, cot, *refs):
    gates, refs = refs[:pieces], refs[pieces:]
    glog, refs = refs[:pieces], refs[pieces:]
    normed, refs = refs[:pieces], refs[pieces:]
    act, refs = refs[:pieces], refs[pieces:]
    gpre, refs = refs[:pieces], refs[pieces:]
    out, router = refs
    rows_total = normed[0].shape[0]
    expert = pl.program_id(0)

    @pl.when(expert == 0)
    def _():
        total = jnp.zeros((LANES, cot.shape[1]), F32)
        for index in range(pieces):
            back = glog[index][...]
            high = back.astype(BF16)
            low = (back - high.astype(F32)).astype(BF16)
            total = total + dot(high, normed[index][...], TN)
            total = total + dot(low, normed[index][...], TN)
        router[...] = total[0:8, :]

    grad_in = jnp.zeros((normed[0].shape[1], gpre[0].shape[2]), F32)
    grad_down = jnp.zeros((act[0].shape[2], cot.shape[1]), F32)
    for index in range(pieces):
        gate = lane_pick(gates[index][...], expert)
        weighted = cot[pl.ds(index * rows_total, rows_total), :].astype(F32)
        weighted = (gate * weighted).astype(BF16)
        grad_in = grad_in + dot(normed[index][...], gpre[index][0], TN)
        grad_down = grad_down + dot(act[index][0], weighted, TN)
    out[0, 0] = grad_in.astype(BF16)
    out[0, 1] = grad_down.astype(BF16)


def hidden_back_kernel(piece, pieces, shares, got, idx, *refs):
    gx, refs = refs[:got], refs[got:]
    wo, own, cot, gain = refs[:4]
    refs = refs[4:]
    ga, refs = refs[:shares], refs[shares:]
    gh, gh_low, ggain = refs
    share = own.shape[0]
    grad = gx[0][...].astype(F32)
    for step in range(1, got):
        grad = grad + gx[step][...].astype(F32)
    hidden = own[...]
    scale = row_scale(hidden)
    unit = hidden * scale
    ggain[...] = jnp.sum(grad * unit, axis=0, keepdims=True)
    gained = grad * gain[...].astype(F32).reshape(1, -1)
    start = piece * (cot.shape[0] // pieces) + idx[0] * share
    mine = cot[pl.ds(pl.multiple_of(start, share), share), :].astype(F32)
    back = mine + scale * (gained - unit * jnp.mean(gained * unit, axis=-1, keepdims=True))
    gh[...] = back
    low = back.astype(BF16)
    gh_low[...] = low
    for step in range(shares):
        ga[step][...] = dot(low, wo[step], NT).astype(BF16)


def w_out_back_kernel(pieces, shares, idx, *refs):
    att, refs = refs[: pieces * shares], refs[pieces * shares :]
    gh_low, out = refs[:pieces], refs[pieces]
    share = gh_low[0].shape[0]
    rows = pl.ds(pl.multiple_of(idx[0] * share, share), share)
    for step in range(shares):
        total = dot(att[step][rows, :], gh_low[0][...], TN)
        for index in range(1, pieces):
            total = total + dot(att[index * shares + step][rows, :], gh_low[index][...], TN)
        out[step] = total.astype(BF16)


def join_kernel(pieces, count, *refs):
    own, refs = refs[:pieces], refs[pieces:]
    got, out = refs[: pieces * count], refs[pieces * count]
    share = own[0].shape[0]
    for index in range(pieces):
        total = own[index][...]
        for step in range(count):
            total = total + got[index * count + step][...].astype(F32)
        out[pl.ds(index * share, share), :] = total.astype(BF16)


def input_back_kernel(pieces, got, idx, *refs):
    gn, refs = refs[:got], refs[got:]
    ghs, refs = refs[:pieces], refs[pieces:]
    tok, gain, gt = refs
    share = ghs[0].shape[0]
    gain_row = gain[...].astype(F32).reshape(1, -1)
    for index in range(pieces):
        rows = pl.ds(index * share, share)
        grad = gn[0][rows, :].astype(F32)
        for step in range(1, got):
            grad = grad + gn[step][rows, :].astype(F32)
        start = index * (tok.shape[0] // pieces) + idx[0] * share
        x = tok[pl.ds(pl.multiple_of(start, share), share), :].astype(F32)
        scale = row_scale(x)
        unit = x * scale
        gained = grad * gain_row
        back = scale * (gained - unit * jnp.mean(gained * unit, axis=-1, keepdims=True))
        gt[rows, :] = (ghs[index][...] + back).astype(BF16)


def place_kernel(pieces, shares, idx, *refs):
    blocks, out = refs[:shares], refs[shares]
    rows_total = out.shape[0] // pieces
    share = rows_total // shares
    for step in range(shares):
        owner = idx[0] ^ step
        for index in range(pieces):
            start = pl.multiple_of(index * rows_total + owner * share, share)
            got = blocks[step][pl.ds(index * share, share), :]
            out[pl.ds(start, share), :] = got.astype(out.dtype)


ROWS = 512
PIECES = 1

SMEM = pl.BlockSpec(memory_space=pltpu.SMEM)
VMEM = pl.BlockSpec(memory_space=pltpu.VMEM)


def shaped(shape, dtype):
    return jax.ShapeDtypeStruct(shape, dtype)


def whole_call(kernel, outs, args, scratch=(), flops=0, moved=0, with_index=True):
    specs = ([SMEM] if with_index else []) + [VMEM] * (len(args) - (1 if with_index else 0))
    return pl.pallas_call(
        kernel,
        out_shape=outs,
        in_specs=specs,
        out_specs=[VMEM] * len(outs),
        scratch_shapes=list(scratch),
        compiler_params=pltpu.CompilerParams(vmem_limit_bytes=VMEM_LIMIT),
        cost_estimate=pl.CostEstimate(flops=flops, bytes_accessed=moved, transcendentals=0),
    )(*args)


def swap(value, axis, bit):
    count = lax.axis_size(axis)
    return lax.ppermute(value, axis, [(i, i ^ bit) for i in range(count)])


def sum_over(value, axis):
    bit = 1
    while bit < lax.axis_size(axis):
        value = value + swap(value, axis, bit)
        bit *= 2
    return value


def gather_parts(value, axis):
    count = lax.axis_size(axis)
    if count != 4:
        return [value] + [swap(value, axis, bit) for bit in range(1, count)]
    two = swap(value, axis, 2)
    one = swap(value, axis, 1)
    return [value, one, two, swap(after(two, one), axis, 1)]


def reduce_near(parts, axis):
    return swap(parts[3], axis, 1), swap(parts[1], axis, 1)


def reduce_far(parts, near, axis):
    pair = (parts[2].astype(F32) + near[0].astype(F32)).astype(parts[2].dtype)
    return [parts[0], near[1], swap(pair, axis, 2)], pair


def exchange(parts, axis):
    return [parts[0]] + [swap(parts[bit], axis, bit) for bit in range(1, len(parts))]


def halves_of(value, axis, chosen):
    half = value.shape[axis] // 2
    keep = lax.dynamic_slice_in_dim(value, chosen * half, half, axis)
    send = lax.dynamic_slice_in_dim(value, (1 - chosen) * half, half, axis)
    return keep, send


def bits_of(axis):
    count = lax.axis_size(axis)
    return [1 << level for level in range(count.bit_length() - 1)]


def gather_back(value, mesh_axis, axis):
    me = lax.axis_index(mesh_axis)
    for bit in reversed(bits_of(mesh_axis)):
        got = swap(value, mesh_axis, bit)
        low = (me // bit) % 2 == 0
        value = jnp.concatenate(
            [jnp.where(low, value, got), jnp.where(low, got, value)], axis=axis
        )
    return value


def together(*values):
    return lax.optimization_barrier(values)


def after(value, *others):
    return lax.optimization_barrier((value, *others))[0]


def body(
    tokens, segments, routes, grad_out, gain_attn, w_qkv, w_out, rel_bias,
    gain_moe, w_router, w_in, w_down,
):
    tok_rows, width = tokens.shape
    heads = rel_bias.shape[1]
    features = w_qkv.shape[2]
    head_size = features // heads
    experts, _, hidden_units = w_in.shape
    shares = lax.axis_size("tensor")
    rows = tok_rows // PIECES
    share = rows // shares
    me = lax.axis_index("tensor").astype(jnp.int32)
    side = (lax.axis_index("dp") % 2).astype(jnp.int32)
    idx = jnp.stack([me, side])
    mib = 1 << 20
    others = range(1, shares)
    four = shares == 4

    half_rows = features // 2
    my_half = lax.dynamic_slice_in_dim(w_out, side * half_rows, half_rows, 0)
    halves = [swap(my_half, "tensor", by) for by in others]

    build_hot, gather_hot = near_tables()
    build_hot = jnp.asarray(np.swapaxes(build_hot, 1, 2), BF16)
    gather_hot = jnp.asarray(gather_hot, F32)
    w_qkv_t = jnp.swapaxes(w_qkv, 1, 2)
    router_t = w_router.T

    normed_one, qh, k, v, _, att, ot, lse, bias, far = whole_call(
        functools.partial(attn_fwd_kernel, 0, PIECES, heads, head_size),
        [
            shaped((rows, width), BF16),
            shaped((heads, rows, features), BF16),
            shaped((rows, features), BF16),
            shaped((rows, features), BF16),
            shaped((features, rows), BF16),
            shaped((rows, features), BF16),
            shaped((features, rows), F32),
            shaped((8, rows), F32),
            shaped((2 * heads, BLK, BLK), F32),
            shaped((8, LANES), F32),
        ],
        [tokens, gain_attn, w_qkv_t, segments, rel_bias.T, build_hot],
        flops=6 * 10**9, moved=8 * mib, with_index=False,
    )
    att = after(att, *halves)
    atts = gather_parts(att, "tensor")
    swapped = swap(after(jnp.stack(halves), att), "dp", 1)

    full = lambda shape: pl.BlockSpec(shape, lambda e: (0,) * len(shape))
    per_expert = lambda shape: pl.BlockSpec((1,) + shape, lambda e: (e, 0, 0))
    params = pltpu.CompilerParams(
        vmem_limit_bytes=VMEM_LIMIT, dimension_semantics=("arbitrary",)
    )
    moe_flops = 4 * experts * rows * width * hidden_units

    fwd = pl.pallas_call(
        functools.partial(moe_fwd_kernel, 0, PIECES, shares, experts),
        grid=(experts,),
        in_specs=[SMEM]
        + [full((rows, features))] * shares
        + [full((features, width)), full((shares - 1, half_rows, width))]
        + [full((half_rows, width))] * (shares - 1)
        + [
            full((rows, width)), full((width,)), full((experts, width)),
            full((rows, 2)), full((rows, width)),
            per_expert((width, hidden_units)), per_expert((hidden_units, width)),
        ],
        out_specs=[full((share, width))] * shares
        + [
            full((shares, features, width)), full((rows, width)),
            full((share, width)), full((rows, LANES)), full((rows, LANES)),
            per_expert((rows, hidden_units)), per_expert((rows, hidden_units)),
        ],
        out_shape=[shaped((share, width), BF16)] * shares
        + [
            shaped((shares, features, width), BF16),
            shaped((rows, width), BF16),
            shaped((share, width), F32),
            shaped((rows, LANES), F32),
            shaped((rows, LANES), F32),
            shaped((experts, rows, hidden_units), BF16),
            shaped((experts, rows, hidden_units), BF16),
        ],
        scratch_shapes=[pltpu.VMEM((rows, width), F32)],
        compiler_params=params,
        cost_estimate=pl.CostEstimate(
            flops=moe_flops, bytes_accessed=32 * mib, transcendentals=0
        ),
    )(
        idx, *atts, w_out, swapped, *halves, tokens, gain_moe, router_t, routes, grad_out,
        w_in, w_down,
    )
    moe_parts = fwd[:shares]
    wo, normed_two, own_hidden, gates, ggate, act, slope = fwd[shares:]
    if four:
        moe_near = reduce_near(moe_parts, "tensor")
    else:
        moe_near = exchange(moe_parts, "tensor")[1:]

    bwd = pl.pallas_call(
        functools.partial(moe_bwd_kernel, 0, shares, experts),
        grid=(experts,),
        in_specs=[
            SMEM, full((rows, LANES)), full((rows, LANES)), full((rows, width)),
            per_expert((rows, hidden_units)), full((experts, width)),
            per_expert((width, hidden_units)), per_expert((hidden_units, width)),
        ],
        out_specs=[full((share, width))] * shares
        + [full((rows, LANES)), per_expert((rows, hidden_units))],
        out_shape=[shaped((share, width), BF16)] * shares
        + [
            shaped((rows, LANES), F32),
            shaped((experts, rows, hidden_units), BF16),
        ],
        scratch_shapes=[pltpu.VMEM((rows, width), F32)],
        compiler_params=params,
        cost_estimate=pl.CostEstimate(
            flops=moe_flops, bytes_accessed=26 * mib, transcendentals=0
        ),
    )(idx, gates, ggate, grad_out, slope, router_t, w_in, w_down)
    gx_parts = [after(part, *moe_near) for part in bwd[:shares]]
    glog, gpre = bwd[shares:]
    gx_near = reduce_near(gx_parts, "tensor") if four else exchange(gx_parts, "tensor")[1:]

    expert_grads, router_rows = pl.pallas_call(
        functools.partial(moe_weights_kernel, PIECES),
        grid=(experts,),
        in_specs=[
            full((rows, width)), full((rows, LANES)), full((rows, LANES)), full((rows, width)),
            per_expert((rows, hidden_units)), per_expert((rows, hidden_units)),
        ],
        out_specs=[
            pl.BlockSpec((1, 2, width, width), lambda e: (e, 0, 0, 0)), full((8, width))
        ],
        out_shape=[shaped((experts, 2, width, width), BF16), shaped((8, width), F32)],
        compiler_params=params,
        cost_estimate=pl.CostEstimate(
            flops=moe_flops, bytes_accessed=26 * mib, transcendentals=0
        ),
    )(grad_out, gates, glog, normed_two, act, gpre)
    expert_rows = after(expert_grads.reshape(experts * 2 * width, width), *gx_near)
    expert_rows = lax.psum_scatter(expert_rows, "dp", scatter_dimension=0, tiled=True)

    if four:
        gx_near = after(gx_near[0], router_rows), gx_near[1]
        gx_got, _ = reduce_far(gx_parts, gx_near, "tensor")
    else:
        gx_got = [gx_parts[0], *gx_near]
    back = whole_call(
        functools.partial(hidden_back_kernel, 0, PIECES, shares, len(gx_got)),
        [shaped((share, features), BF16)] * shares
        + [shaped((share, width), F32), shaped((share, width), BF16), shaped((1, width), F32)],
        [idx, *gx_got, wo, own_hidden, grad_out, gain_moe],
        flops=3 * 10**8, moved=5 * mib,
    )
    go = exchange(back[:shares], "tensor")
    grad_hidden, gh_low, ggain_two = back[shares:]
    w_out_rows = whole_call(
        functools.partial(w_out_back_kernel, PIECES, shares),
        [shaped((shares, features, width), BF16)],
        [idx, *atts, gh_low],
        flops=3 * 10**8, moved=4 * mib,
    )[0]
    go[1:] = after(go[1], w_out_rows), *go[2:]

    if four:
        moe_near = after(moe_near[0], *go[1:]), moe_near[1]
        moe_got, _ = reduce_far(moe_parts, moe_near, "tensor")
    else:
        moe_got = [moe_parts[0], *moe_near]
    result_share = whole_call(
        functools.partial(join_kernel, PIECES, len(moe_got)),
        [shaped((share, width), BF16)],
        [own_hidden, *moe_got],
        moved=3 * mib, with_index=False,
    )[0]
    attn_back = whole_call(
        functools.partial(attn_bwd_kernel, 0, PIECES, heads, head_size, shares),
        [shaped((share, width), BF16)] * shares
        + [shaped((3, rows, features), BF16), shaped((features, width), BF16)],
        [
            idx, *go, tokens, router_rows, ggain_two, qh, ot, lse, k, v, bias, far, segments,
            w_qkv_t, gather_hot,
        ],
        [pltpu.VMEM((rows, features), F32)] * 2
        + [
            pltpu.VMEM((features, rows), F32),
            pltpu.VMEM((2 * heads, BLK, BLK), F32),
            pltpu.VMEM((rows, features), BF16),
            pltpu.VMEM((features, width), F32),
            pltpu.VMEM((features, rows), BF16),
            pltpu.VMEM((8, rows), F32),
            pltpu.VMEM((2, 8, 2 * BLK), F32),
            pltpu.VMEM((8, BLK), F32),
        ],
        flops=14 * 10**9, moved=8 * mib,
    )
    gn_parts = [after(part, moe_got[-1]) for part in attn_back[:shares]]
    gproj, misc = attn_back[shares:]

    qkv_rows = whole_call(
        functools.partial(qkv_weights_kernel, PIECES),
        [shaped((3, features, width), BF16)],
        [normed_one, gproj],
        flops=10**9, moved=4 * mib, with_index=False,
    )[0]
    late = jnp.concatenate([qkv_rows, misc[None], w_out_rows], axis=0)
    if four:
        near = reduce_near(gn_parts, "tensor")
        near = after(near[0], late, near[1]), near[1]
        gn_got, mark = reduce_far(gn_parts, near, "tensor")
    else:
        gn_got = exchange(gn_parts, "tensor")
        mark = gn_got[-1]

    place = lax.axis_index("dp")

    def halve(value, bit, *ready):
        keep, send = halves_of(value, 1, (place // bit) % 2)
        got = swap(after(send, *ready), "dp", bit)
        return (keep.astype(F32) + got.astype(F32)).astype(BF16)

    bits = bits_of("dp")
    late = halve(late, 1)
    keep, send = halves_of(late, 1, (place // bits[1]) % 2)
    got = swap(send[:4], "dp", bits[1]), swap(send[4:], "dp", bits[1])

    expert_rows = after(expert_rows, mark)
    gt_share = whole_call(
        functools.partial(input_back_kernel, PIECES, len(gn_got)),
        [shaped((share, width), BF16)],
        [idx, *gn_got, grad_hidden, tokens, gain_attn],
        moved=5 * mib,
    )[0]
    result_one = swap(after(result_share, mark), "tensor", 1)
    gt_now, result_one, *got = together(gt_share, result_one, *got)
    got = jnp.concatenate(got, axis=0)
    late = (keep.astype(F32) + got.astype(F32)).astype(BF16)
    keep, send = halves_of(late, 1, (place // bits[2]) % 2)
    two, one, got = together(
        swap(gt_now, "tensor", 2), swap(gt_now, "tensor", 1), swap(send, "dp", bits[2])
    )
    late = (keep.astype(F32) + got.astype(F32)).astype(BF16)
    for bit in bits[3:]:
        late = halve(late, bit)

    sent = together(*[swap(jnp.stack([late[4 + by], late[3]]), "tensor", by) for by in others])
    three = swap(two, "tensor", 1)
    result_two = swap(after(result_share, two), "tensor", 2)
    out_sum, small = late[4].astype(F32), [late[3]]
    for got in sent:
        out_sum = out_sum + got[0].astype(F32)
        small.append(got[1])
    small = [part.astype(F32) for part in small]
    while len(small) > 1:
        small = [small[at] + small[at + 1] for at in range(0, len(small), 2)]
    late = jnp.concatenate(
        [late[:3], jnp.stack([small[0].astype(BF16), out_sum.astype(BF16)])], axis=0
    )

    expert_rows = lax.all_gather(expert_rows, "dp", axis=0, tiled=True)

    def joined(value, got, bit):
        low = (place // bit) % 2 == 0
        return jnp.concatenate([jnp.where(low, value, got), jnp.where(low, got, value)], axis=1)

    for bit in reversed(bits[3:]):
        late = joined(late, swap(late, "dp", bit), bit)
    grad_tokens = whole_call(
        functools.partial(place_kernel, PIECES, shares),
        [shaped((rows, width), F32)], [idx, gt_share, one, two, three], moved=5 * mib,
    )[0]
    got, _, result_two = together(swap(late, "dp", bits[2]), grad_tokens, result_two)
    late = joined(late, got, bits[2])
    grad_w_in = expert_rows.reshape(experts, 2, width, width)[:, 0].astype(F32)
    got, _, result_three = together(
        swap(late, "dp", bits[1]), grad_w_in, swap(result_two, "tensor", 1)
    )
    late = joined(late, got, bits[1])
    expert_rows = after(expert_rows, got)
    grad_w_down = expert_rows.reshape(experts, 2, width, width)[:, 1].astype(F32)
    result = whole_call(
        functools.partial(place_kernel, PIECES, shares),
        [shaped((rows, width), BF16)],
        [idx, result_share, result_one, result_two, result_three],
        moved=3 * mib,
    )[0]
    got = after(swap(late, "dp", bits[0]), grad_w_down, result)
    late = joined(late, got, bits[0])
    grad_w_qkv = jnp.swapaxes(late[:3], 1, 2).astype(F32)
    grad_w_out = late[4].astype(F32)
    small = late[3].astype(F32)
    grad_rel = lax.dynamic_slice_in_dim(small, me * 8, 8, 0)
    first = 8 * shares
    return (
        result,
        grad_tokens,
        small[first + 8],
        grad_w_qkv,
        grad_w_out,
        grad_rel[:heads, :NB].T,
        small[first + 9],
        small[first : first + experts].T,
        grad_w_in,
        grad_w_down,
    )


def solution(mesh):
    placed = (
        P("dp", None),
        P("dp", None),
        P("dp", None),
        P("dp", None),
        P(),
        P(None, None, "tensor"),
        P("tensor", None),
        P(None, "tensor"),
        P(),
        P(),
        P(None, None, "tensor"),
        P(None, "tensor", None),
    )
    return jax.shard_map(
        body,
        mesh=mesh,
        in_specs=placed,
        out_specs=(
            P("dp", None),
            P("dp", None),
            P(),
            P(None, None, "tensor"),
            P("tensor", None),
            P(None, "tensor"),
            P(),
            P(),
            P(None, None, "tensor"),
            P(None, "tensor", None),
        ),
        check_vma=False,
    )
```

```python
import functools
import math

import jax
import jax.numpy as jnp
import numpy as np
from jax import lax
from jax.experimental import pallas as pl
from jax.experimental.pallas import tpu as pltpu
from jax.sharding import PartitionSpec as P

NB = 32
DIST = 128
EPSILON = 1e-06
NEGATIVE = -1e30
HIGHEST = lax.Precision.HIGHEST
F32 = jnp.float32
BF16 = jnp.bfloat16
BLK = 256
LANES = 128
VMEM_LIMIT = 56 * 1024 * 1024

NN = (((1,), (0,)), ((), ()))
NT = (((1,), (1,)), ((), ()))
TN = (((0,), (0,)), ((), ()))


def dot(a, b, dims=NN, precision=None):
    return lax.dot_general(a, b, dims, precision=precision, preferred_element_type=F32)


def bucket_of(distance):
    halfway = NB // 2
    thresholds = [
        int(math.ceil(halfway * (DIST / halfway) ** (step / halfway))) for step in range(halfway)
    ]
    beyond = sum((distance >= threshold).astype(np.int64) for threshold in thresholds)
    return np.where(distance < halfway, distance, halfway - 1 + beyond)


def near_tables():
    lanes = np.arange(2 * BLK)
    offset = np.where(lanes < BLK, lanes, lanes - 2 * BLK)
    build = np.stack([np.maximum(offset, 0), np.maximum(BLK + offset, 0)])
    gather = np.stack([lanes - (BLK - 1), lanes + 1])
    eye = np.eye(NB, dtype=np.float32)
    build_hot = eye[bucket_of(build)]
    gather_hot = eye[bucket_of(np.maximum(gather, 0))] * (gather >= 0)[..., None]
    return build_hot, gather_hot


def row_scale(values):
    return lax.rsqrt(jnp.mean(values * values, axis=-1, keepdims=True) + EPSILON)


def lane_pick(values, index):
    lanes = lax.broadcasted_iota(jnp.int32, values.shape, 1)
    return jnp.sum(jnp.where(lanes == index, values, 0.0), axis=1, keepdims=True)


def masked_scores(k_tile, qh_tile, bias, seg_k, seg_q, diagonal):
    scores = dot(k_tile, qh_tile, NT) + bias
    allowed = seg_k == seg_q
    if diagonal:
        key_at = lax.broadcasted_iota(jnp.int32, scores.shape, 0)
        query_at = lax.broadcasted_iota(jnp.int32, scores.shape, 1)
        allowed = allowed & (key_at <= query_at)
    return jnp.where(allowed, scores, NEGATIVE)


def tile_bias(bias_ref, far_ref, head, delta):
    if delta < 2:
        return bias_ref[2 * head + delta]
    return far_ref[pl.ds(head, 1), 0:1]


def column_of(row):
    spread = jnp.broadcast_to(row.astype(F32), (8, row.shape[1]))
    return spread.T[:, 0:1]


def attn_fwd_kernel(piece, pieces, heads, head_size, *refs):
    tok, gain, w, seg = refs[:4]
    refs = refs[4:]
    if piece == 0:
        rel, build = refs[:2]
        refs = refs[2:]
    else:
        bias, far = refs[:2]
        refs = refs[2:]
    old_k, refs = refs[:piece], refs[piece:]
    old_vt, refs = refs[:piece], refs[piece:]
    normed, qh, k, v, vt, att, ot, lse = refs[:8]
    if piece == 0:
        bias, far = refs[8:]
    keys_of, vt_of = [*old_k, k], [*old_vt, vt]
    rows_total = tok.shape[0] // pieces
    base = piece * rows_total
    features = w.shape[1]
    blocks = rows_total // BLK
    gain_row = gain[...].astype(F32).reshape(1, -1)
    lanes = lax.broadcasted_iota(jnp.int32, (BLK, features), 1)
    for block in range(blocks):
        rows = pl.ds(block * BLK, BLK)
        x = tok[pl.ds(base + block * BLK, BLK), :].astype(F32)
        n = (x * row_scale(x) * gain_row).astype(BF16)
        normed[rows, :] = n
        q_rows = dot(n, w[0], NT).astype(BF16).astype(F32) * (head_size**-0.5)
        for head in range(heads):
            inside = (lanes >= head * head_size) & (lanes < (head + 1) * head_size)
            qh[head, rows, :] = jnp.where(inside, q_rows, 0.0).astype(BF16)
        k[rows, :] = dot(n, w[1], NT).astype(BF16)
        v_rows = dot(n, w[2], NT).astype(BF16)
        v[rows, :] = v_rows
        vt[:, rows] = v_rows.astype(F32).T.astype(BF16)
    if piece == 0:
        far[...] = jnp.zeros_like(far)
        far[0:heads, :] = jnp.broadcast_to(rel[:, NB - 1 : NB].astype(F32), (heads, LANES))
        for delta in range(2):
            near = dot(rel[...], build[delta])
            for head in range(heads):
                spread = jnp.broadcast_to(near[head : head + 1, :], (BLK, 2 * BLK))
                turned = pltpu.roll(spread, 0, 1, stride=1, stride_axis=0)
                bias[2 * head + delta] = turned[:, :BLK]
    lse[...] = jnp.zeros_like(lse)
    seg_row = seg[...].astype(F32)
    seg_col = column_of(seg[...])

    def one_head(head, carry):
        part = pl.ds(pl.multiple_of(head * head_size, head_size), head_size)
        for block in range(blocks):
            qb = piece * blocks + block
            cols = pl.ds(block * BLK, BLK)
            q_tile = qh[head, cols, :]
            tiles = []
            for kb in range(qb + 1):
                keys = pl.ds(kb % blocks * BLK, BLK)
                tiles.append(
                    masked_scores(
                        keys_of[kb // blocks][keys, :], q_tile,
                        tile_bias(bias, far, head, qb - kb),
                        seg_col[kb * BLK : (kb + 1) * BLK, :],
                        seg_row[:, qb * BLK : (qb + 1) * BLK], kb == qb,
                    )
                )
            peak = functools.reduce(
                jnp.maximum, [jnp.max(t, axis=0, keepdims=True) for t in tiles]
            )
            total = jnp.zeros((1, BLK), F32)
            out = jnp.zeros((head_size, BLK), F32)
            for kb in range(qb + 1):
                raised = jnp.exp(tiles[kb] - peak)
                total = total + jnp.sum(raised, axis=0, keepdims=True)
                values = vt_of[kb // blocks][part, pl.ds(kb % blocks * BLK, BLK)]
                out = out + dot(values, raised.astype(BF16))
            ot[part, cols] = out / total
            lse[pl.ds(head, 1), cols] = peak + jnp.log(total)
        return carry

    lax.fori_loop(0, heads, one_head, 0)
    for block in range(blocks):
        cols = pl.ds(block * BLK, BLK)
        att[cols, :] = ot[:, cols].T.astype(BF16)


def attn_bwd_kernel(piece, pieces, heads, head_size, shares, idx, *refs):
    held = piece + 1
    last = held == pieces
    go_parts, refs = refs[:shares], refs[shares:]
    tok, router, gain_two, qh, ot, lse = refs[:6]
    refs = refs[6:]
    ks, refs = refs[:held], refs[held:]
    vs, refs = refs[:held], refs[held:]
    bias, far, seg = refs[:3]
    refs = refs[3:]
    if piece:
        gk_in, refs = refs[:piece], refs[piece:]
        gv_in, refs = refs[:piece], refs[piece:]
        gq_in, refs = refs[:piece], refs[piece:]
        acc_in, refs = refs[0], refs[1:]
    if last:
        w, hot = refs[:2]
        refs = refs[2:]
        gn_parts, refs = refs[:shares], refs[shares:]
        gproj, misc = refs[:2]
        refs = refs[2:]
        gk, refs = refs[:held], refs[held:]
        gv, refs = refs[:held], refs[held:]
        gq_t, acc = refs[:2]
        refs = refs[2:]
    else:
        gk, refs = refs[:held], refs[held:]
        gv, refs = refs[:held], refs[held:]
        gq_t, acc = refs[:2]
        refs = refs[2:]
    go, misc_sum, kt, d_row, near_sum, far_sum = refs
    rows_total, features = ks[0].shape
    blocks = rows_total // BLK
    share = rows_total // shares
    me = idx[0]
    for step in range(shares):
        start = pl.multiple_of((me ^ step) * share, share)
        go[pl.ds(start, share), :] = go_parts[step][...]
    for index in range(held):
        for block in range(blocks):
            cols = pl.ds(block * BLK, BLK)
            kt[:, pl.ds((index * blocks + block) * BLK, BLK)] = (
                ks[index][cols, :].astype(F32).T.astype(BF16)
            )
        if index < piece:
            gk[index][...] = gk_in[index][...]
            gv[index][...] = gv_in[index][...]
        else:
            gk[index][...] = jnp.zeros_like(gk[index])
            gv[index][...] = jnp.zeros_like(gv[index])
    if piece:
        acc[...] = acc_in[...]
    else:
        acc[...] = jnp.zeros_like(acc)
    for block in range(blocks):
        cols = pl.ds(block * BLK, BLK)
        product = go[cols, :].astype(F32).T * ot[:, cols]
        for head in range(heads):
            part = product[head * head_size : (head + 1) * head_size, :]
            d_row[head : head + 1, cols] = jnp.sum(part, axis=0, keepdims=True)
    near_sum[...] = jnp.zeros_like(near_sum)
    far_sum[...] = jnp.zeros_like(far_sum)
    key_at = lax.broadcasted_iota(jnp.int32, (BLK, BLK), 0)
    other_at = lax.broadcasted_iota(jnp.int32, (BLK, BLK), 1)
    flip = (key_at + other_at == BLK - 1).astype(F32)
    seg_row = seg[...].astype(F32)
    seg_col = column_of(seg[...])

    def one_head(head, carry):
        part = pl.ds(pl.multiple_of(head * head_size, head_size), head_size)
        lanes = lax.broadcasted_iota(jnp.int32, (BLK, features), 1)
        inside = (lanes >= head * head_size) & (lanes < (head + 1) * head_size)
        for block in range(blocks):
            qb = piece * blocks + block
            cols = pl.ds(block * BLK, BLK)
            q_tile = qh[head, cols, :]
            go_tile = jnp.where(inside, go[cols, :].astype(F32), 0.0).astype(BF16)
            log_total = lse[pl.ds(head, 1), cols]
            d_tile = d_row[pl.ds(head, 1), cols]
            gq = jnp.zeros((head_size, BLK), F32)
            for kb in range(qb + 1):
                index = kb // blocks
                keys = pl.ds(kb % blocks * BLK, BLK)
                delta = qb - kb
                scores = masked_scores(
                    ks[index][keys, :], q_tile, tile_bias(bias, far, head, delta),
                    seg_col[kb * BLK : (kb + 1) * BLK, :],
                    seg_row[:, qb * BLK : (qb + 1) * BLK], delta == 0,
                )
                probs = jnp.exp(scores - log_total)
                gs = probs * (dot(vs[index][keys, :], go_tile, NT) - d_tile)
                if delta < 2:
                    acc[2 * head + delta] += gs
                else:
                    far_sum[pl.ds(head, 1), :] += jnp.sum(gs, axis=0, keepdims=True)
                gs_low = gs.astype(BF16)
                gv[index][keys, :] += dot(probs.astype(BF16), go_tile)
                gk[index][keys, :] += dot(gs_low, q_tile)
                gq = gq + dot(kt[part, kb * BLK : (kb + 1) * BLK], gs_low)
            gq_t[part, cols] = gq * (head_size**-0.5)
        return carry

    lax.fori_loop(0, heads, one_head, 0)
    if not last:
        return
    gqs = [*(gq_in if piece else ()), gq_t]
    for index in range(held):
        for block in range(blocks):
            rows = pl.ds(block * BLK, BLK)
            out = pl.ds((index * blocks + block) * BLK, BLK)
            gproj[0, out, :] = gqs[index][:, rows].T.astype(BF16)
            gproj[1, out, :] = gk[index][rows, :].astype(BF16)
            gproj[2, out, :] = gv[index][rows, :].astype(BF16)
    gain_one = jnp.zeros_like(gain_two)
    for step in range(shares):
        for index in range(pieces):
            start = index * rows_total + (me ^ step) * share
            rows = pl.ds(pl.multiple_of(start, share), share)
            total = dot(gproj[0, rows, :], w[0])
            total = total + dot(gproj[1, rows, :], w[1])
            total = total + dot(gproj[2, rows, :], w[2])
            gn_parts[step][pl.ds(index * share, share), :] = total.astype(BF16)
            x = tok[rows, :].astype(F32)
            gain_one = gain_one + jnp.sum(total * (x * row_scale(x)), axis=0, keepdims=True)
    for head in range(heads):
        for delta in range(2):
            turned = dot(flip, acc[2 * head + delta], NN, HIGHEST)
            wide = jnp.concatenate([turned, jnp.zeros_like(turned)], axis=1)
            sheared = pltpu.roll(wide, 0, 1, stride=1, stride_axis=0)
            near_sum[delta, head : head + 1, :] = jnp.sum(sheared, axis=0, keepdims=True)
    summed = dot(near_sum[0], hot[0], NN, HIGHEST) + dot(near_sum[1], hot[1], NN, HIGHEST)
    buckets = lax.broadcasted_iota(jnp.int32, summed.shape, 1)
    beyond = jnp.sum(far_sum[...], axis=1, keepdims=True)
    summed = summed + jnp.where(buckets == NB - 1, beyond, 0.0)
    misc_sum[...] = jnp.zeros_like(misc_sum)
    misc_sum[pl.ds(pl.multiple_of(me * 8, 8), 8), 0:NB] = summed
    misc_sum[8 * shares : 8 * shares + 8, :] = router[...]
    misc_sum[8 * shares + 8 : 8 * shares + 9, :] = gain_one
    misc_sum[8 * shares + 9 : 8 * shares + 10, :] = gain_two[...]
    misc[...] = misc_sum[...].astype(BF16)


def qkv_weights_kernel(pieces, *refs):
    normed = refs[:pieces]
    gproj, out = refs[pieces:]
    rows_total = normed[0].shape[0]
    for c in range(3):
        total = dot(gproj[c, pl.ds(0, rows_total), :], normed[0][...], TN)
        for index in range(1, pieces):
            rows = pl.ds(index * rows_total, rows_total)
            total = total + dot(gproj[c, rows, :], normed[index][...], TN)
        out[c] = total.astype(BF16)


def gelu_pair(values):
    squared = values * values
    bent = jnp.tanh(values * (0.7978845608028654 + 0.7978845608028654 * 0.044715 * squared))
    half = 0.5 * (1.0 + bent)
    lifted = values * half
    slope = 0.7978845608028654 + 3.0 * 0.7978845608028654 * 0.044715 * squared
    return lifted, half + lifted * (1.0 - bent) * slope


def padded_rows(values, rows):
    missing = jnp.zeros((rows - values.shape[0], values.shape[1]), values.dtype)
    return jnp.concatenate([values, missing], axis=0)


def moe_fwd_kernel(piece, pieces, shares, experts, idx, *refs):
    att, refs = refs[:shares], refs[shares:]
    if piece == 0:
        wo_own, wo_swapped, refs = refs[0], refs[1], refs[2:]
        wo_fetched, refs = refs[: shares - 1], refs[shares - 1 :]
    else:
        wo, refs = refs[0], refs[1:]
    tok, gain, router, routes, cot, w_in, w_down = refs[:7]
    refs = refs[7:]
    parts, refs = refs[:shares], refs[shares:]
    if piece == 0:
        wo, refs = refs[0], refs[1:]
    normed, own, gates, ggate, act, slope, acc = refs
    rows_total = tok.shape[0] // pieces
    base = piece * rows_total
    share = rows_total // shares
    me = idx[0]
    expert = pl.program_id(0)

    @pl.when(expert == 0)
    def _():
        gain_row = gain[...].astype(F32).reshape(1, -1)
        router_wide = padded_rows(router[...].astype(F32), LANES).astype(BF16)
        if piece == 0:
            half = wo_own.shape[0] // 2
            mine = pl.ds(pl.multiple_of(idx[1] * half, half), half)
            other = pl.ds(pl.multiple_of((1 - idx[1]) * half, half), half)
            wo[0] = wo_own[...]
            for step in range(1, shares):
                wo[step, mine, :] = wo_fetched[step - 1][...]
                wo[step, other, :] = wo_swapped[step - 1]
        for block in range(rows_total // BLK):
            rows = pl.ds(block * BLK, BLK)
            outer = pl.ds(base + block * BLK, BLK)
            attn = dot(att[0][rows, :], wo[0])
            for step in range(1, shares):
                attn = attn + dot(att[step][rows, :], wo[step])
            hidden = tok[outer, :].astype(F32) + attn
            acc[rows, :] = hidden
            n = (hidden * row_scale(hidden) * gain_row).astype(BF16)
            normed[rows, :] = n
            logits = dot(n, router_wide, NT)
            lanes = lax.broadcasted_iota(jnp.int32, logits.shape, 1)
            first = lanes == routes[outer, 0:1]
            second = lanes == routes[outer, 1:2]
            one = jnp.sum(jnp.where(first, logits, 0.0), axis=1, keepdims=True)
            two = jnp.sum(jnp.where(second, logits, 0.0), axis=1, keepdims=True)
            peak = jnp.maximum(one, two)
            one = jnp.exp(one - peak)
            two = jnp.exp(two - peak)
            both = one + two
            gates[rows, :] = jnp.where(first, one / both, jnp.where(second, two / both, 0.0))
        own[...] = acc[pl.ds(pl.multiple_of(me * share, share), share), :]
        acc[...] = jnp.zeros_like(acc)
        ggate[...] = jnp.zeros_like(ggate)

    for block in range(rows_total // ROWS):
        rows = pl.ds(block * ROWS, ROWS)
        outer = pl.ds(base + block * ROWS, ROWS)
        lifted, bend = gelu_pair(dot(normed[rows, :], w_in[0]))
        lifted = lifted.astype(BF16)
        act[0, rows, :] = lifted
        slope[0, rows, :] = bend.astype(BF16)
        out = dot(lifted, w_down[0])
        gate = lane_pick(gates[rows, :], expert)
        acc[rows, :] += gate * out
        pulled = jnp.sum(cot[outer, :].astype(F32) * out, axis=1, keepdims=True)
        held = ggate[rows, :]
        lanes = lax.broadcasted_iota(jnp.int32, held.shape, 1)
        ggate[rows, :] = jnp.where(lanes == expert, pulled, held)

    @pl.when(expert == experts - 1)
    def _():
        for step in range(shares):
            start = pl.multiple_of((me ^ step) * share, share)
            parts[step][...] = acc[pl.ds(start, share), :].astype(BF16)


def moe_bwd_kernel(piece, shares, experts, idx, *refs):
    gates, ggate, cot, slope, router, w_in, w_down = refs[:7]
    refs = refs[7:]
    parts, refs = refs[:shares], refs[shares:]
    glog, gpre, acc = refs
    rows_total = gates.shape[0]
    base = piece * rows_total
    share = rows_total // shares
    me = idx[0]
    expert = pl.program_id(0)

    @pl.when(expert == 0)
    def _():
        router_wide = padded_rows(router[...].astype(F32), LANES)
        for block in range(rows_total // ROWS):
            rows = pl.ds(block * ROWS, ROWS)
            g, gg = gates[rows, :], ggate[rows, :]
            back = g * (gg - jnp.sum(g * gg, axis=1, keepdims=True))
            glog[rows, :] = back
            acc[rows, :] = dot(back, router_wide, NN, HIGHEST)

    for block in range(rows_total // ROWS):
        rows = pl.ds(block * ROWS, ROWS)
        gate = lane_pick(gates[rows, :], expert)
        weighted = cot[pl.ds(base + block * ROWS, ROWS), :].astype(F32)
        weighted = (gate * weighted).astype(BF16)
        gp = (dot(weighted, w_down[0], NT) * slope[0, rows, :].astype(F32)).astype(BF16)
        gpre[0, rows, :] = gp
        acc[rows, :] += dot(gp, w_in[0], NT)

    @pl.when(expert == experts - 1)
    def _():
        for step in range(shares):
            start = pl.multiple_of((me ^ step) * share, share)
            parts[step][...] = acc[pl.ds(start, share), :].astype(BF16)


def moe_weights_kernel(pieces, cot, *refs):
    gates, refs = refs[:pieces], refs[pieces:]
    glog, refs = refs[:pieces], refs[pieces:]
    normed, refs = refs[:pieces], refs[pieces:]
    act, refs = refs[:pieces], refs[pieces:]
    gpre, refs = refs[:pieces], refs[pieces:]
    out, router = refs
    rows_total = normed[0].shape[0]
    expert = pl.program_id(0)

    @pl.when(expert == 0)
    def _():
        total = jnp.zeros((LANES, cot.shape[1]), F32)
        for index in range(pieces):
            back = glog[index][...]
            high = back.astype(BF16)
            low = (back - high.astype(F32)).astype(BF16)
            total = total + dot(high, normed[index][...], TN)
            total = total + dot(low, normed[index][...], TN)
        router[...] = total[0:8, :]

    grad_in = jnp.zeros((normed[0].shape[1], gpre[0].shape[2]), F32)
    grad_down = jnp.zeros((act[0].shape[2], cot.shape[1]), F32)
    for index in range(pieces):
        gate = lane_pick(gates[index][...], expert)
        weighted = cot[pl.ds(index * rows_total, rows_total), :].astype(F32)
        weighted = (gate * weighted).astype(BF16)
        grad_in = grad_in + dot(normed[index][...], gpre[index][0], TN)
        grad_down = grad_down + dot(act[index][0], weighted, TN)
    out[0, 0] = grad_in.astype(BF16)
    out[0, 1] = grad_down.astype(BF16)


def hidden_back_kernel(piece, pieces, shares, got, idx, *refs):
    gx, refs = refs[:got], refs[got:]
    wo, own, cot, gain = refs[:4]
    refs = refs[4:]
    ga, refs = refs[:shares], refs[shares:]
    gh, gh_low, ggain = refs
    share = own.shape[0]
    grad = gx[0][...].astype(F32)
    for step in range(1, got):
        grad = grad + gx[step][...].astype(F32)
    hidden = own[...]
    scale = row_scale(hidden)
    unit = hidden * scale
    ggain[...] = jnp.sum(grad * unit, axis=0, keepdims=True)
    gained = grad * gain[...].astype(F32).reshape(1, -1)
    start = piece * (cot.shape[0] // pieces) + idx[0] * share
    mine = cot[pl.ds(pl.multiple_of(start, share), share), :].astype(F32)
    back = mine + scale * (gained - unit * jnp.mean(gained * unit, axis=-1, keepdims=True))
    gh[...] = back
    low = back.astype(BF16)
    gh_low[...] = low
    for step in range(shares):
        ga[step][...] = dot(low, wo[step], NT).astype(BF16)


def w_out_back_kernel(pieces, shares, idx, *refs):
    att, refs = refs[: pieces * shares], refs[pieces * shares :]
    gh_low, out = refs[:pieces], refs[pieces]
    share = gh_low[0].shape[0]
    rows = pl.ds(pl.multiple_of(idx[0] * share, share), share)
    for step in range(shares):
        total = dot(att[step][rows, :], gh_low[0][...], TN)
        for index in range(1, pieces):
            total = total + dot(att[index * shares + step][rows, :], gh_low[index][...], TN)
        out[step] = total.astype(BF16)


def join_kernel(pieces, count, *refs):
    own, refs = refs[:pieces], refs[pieces:]
    got, out = refs[: pieces * count], refs[pieces * count]
    share = own[0].shape[0]
    for index in range(pieces):
        total = own[index][...]
        for step in range(count):
            total = total + got[index * count + step][...].astype(F32)
        out[pl.ds(index * share, share), :] = total.astype(BF16)


def input_back_kernel(pieces, got, idx, *refs):
    gn, refs = refs[:got], refs[got:]
    ghs, refs = refs[:pieces], refs[pieces:]
    tok, gain, gt = refs
    share = ghs[0].shape[0]
    gain_row = gain[...].astype(F32).reshape(1, -1)
    for index in range(pieces):
        rows = pl.ds(index * share, share)
        grad = gn[0][rows, :].astype(F32)
        for step in range(1, got):
            grad = grad + gn[step][rows, :].astype(F32)
        start = index * (tok.shape[0] // pieces) + idx[0] * share
        x = tok[pl.ds(pl.multiple_of(start, share), share), :].astype(F32)
        scale = row_scale(x)
        unit = x * scale
        gained = grad * gain_row
        back = scale * (gained - unit * jnp.mean(gained * unit, axis=-1, keepdims=True))
        gt[rows, :] = (ghs[index][...] + back).astype(BF16)


def place_kernel(pieces, shares, idx, *refs):
    blocks, out = refs[:shares], refs[shares]
    rows_total = out.shape[0] // pieces
    share = rows_total // shares
    for step in range(shares):
        owner = idx[0] ^ step
        for index in range(pieces):
            start = pl.multiple_of(index * rows_total + owner * share, share)
            got = blocks[step][pl.ds(index * share, share), :]
            out[pl.ds(start, share), :] = got.astype(out.dtype)


ROWS = 512
PIECES = 1

SMEM = pl.BlockSpec(memory_space=pltpu.SMEM)
VMEM = pl.BlockSpec(memory_space=pltpu.VMEM)


def shaped(shape, dtype):
    return jax.ShapeDtypeStruct(shape, dtype)


def whole_call(kernel, outs, args, scratch=(), flops=0, moved=0, with_index=True):
    specs = ([SMEM] if with_index else []) + [VMEM] * (len(args) - (1 if with_index else 0))
    return pl.pallas_call(
        kernel,
        out_shape=outs,
        in_specs=specs,
        out_specs=[VMEM] * len(outs),
        scratch_shapes=list(scratch),
        compiler_params=pltpu.CompilerParams(vmem_limit_bytes=VMEM_LIMIT),
        cost_estimate=pl.CostEstimate(flops=flops, bytes_accessed=moved, transcendentals=0),
    )(*args)


def swap(value, axis, bit):
    count = lax.axis_size(axis)
    return lax.ppermute(value, axis, [(i, i ^ bit) for i in range(count)])


def sum_over(value, axis):
    bit = 1
    while bit < lax.axis_size(axis):
        value = value + swap(value, axis, bit)
        bit *= 2
    return value


def gather_parts(value, axis):
    count = lax.axis_size(axis)
    if count != 4:
        return [value] + [swap(value, axis, bit) for bit in range(1, count)]
    two = swap(value, axis, 2)
    one = swap(value, axis, 1)
    return [value, one, two, swap(after(two, one), axis, 1)]


def reduce_near(parts, axis):
    return swap(parts[3], axis, 1), swap(parts[1], axis, 1)


def reduce_far(parts, near, axis):
    pair = (parts[2].astype(F32) + near[0].astype(F32)).astype(parts[2].dtype)
    return [parts[0], near[1], swap(pair, axis, 2)], pair


def exchange(parts, axis):
    return [parts[0]] + [swap(parts[bit], axis, bit) for bit in range(1, len(parts))]


def halves_of(value, axis, chosen):
    half = value.shape[axis] // 2
    keep = lax.dynamic_slice_in_dim(value, chosen * half, half, axis)
    send = lax.dynamic_slice_in_dim(value, (1 - chosen) * half, half, axis)
    return keep, send


def bits_of(axis):
    count = lax.axis_size(axis)
    return [1 << level for level in range(count.bit_length() - 1)]


def gather_back(value, mesh_axis, axis):
    me = lax.axis_index(mesh_axis)
    for bit in reversed(bits_of(mesh_axis)):
        got = swap(value, mesh_axis, bit)
        low = (me // bit) % 2 == 0
        value = jnp.concatenate(
            [jnp.where(low, value, got), jnp.where(low, got, value)], axis=axis
        )
    return value


def together(*values):
    return lax.optimization_barrier(values)


def after(value, *others):
    return lax.optimization_barrier((value, *others))[0]


def body(
    tokens, segments, routes, grad_out, gain_attn, w_qkv, w_out, rel_bias,
    gain_moe, w_router, w_in, w_down,
):
    tok_rows, width = tokens.shape
    heads = rel_bias.shape[1]
    features = w_qkv.shape[2]
    head_size = features // heads
    experts, _, hidden_units = w_in.shape
    shares = lax.axis_size("tensor")
    rows = tok_rows // PIECES
    share = rows // shares
    me = lax.axis_index("tensor").astype(jnp.int32)
    side = (lax.axis_index("dp") % 2).astype(jnp.int32)
    idx = jnp.stack([me, side])
    mib = 1 << 20
    others = range(1, shares)
    four = shares == 4

    half_rows = features // 2
    my_half = lax.dynamic_slice_in_dim(w_out, side * half_rows, half_rows, 0)
    halves = [swap(my_half, "tensor", by) for by in others]

    build_hot, gather_hot = near_tables()
    build_hot = jnp.asarray(np.swapaxes(build_hot, 1, 2), BF16)
    gather_hot = jnp.asarray(gather_hot, F32)
    w_qkv_t = jnp.swapaxes(w_qkv, 1, 2)
    router_t = w_router.T

    normed_one, qh, k, v, _, att, ot, lse, bias, far = whole_call(
        functools.partial(attn_fwd_kernel, 0, PIECES, heads, head_size),
        [
            shaped((rows, width), BF16),
            shaped((heads, rows, features), BF16),
            shaped((rows, features), BF16),
            shaped((rows, features), BF16),
            shaped((features, rows), BF16),
            shaped((rows, features), BF16),
            shaped((features, rows), F32),
            shaped((8, rows), F32),
            shaped((2 * heads, BLK, BLK), F32),
            shaped((8, LANES), F32),
        ],
        [tokens, gain_attn, w_qkv_t, segments, rel_bias.T, build_hot],
        flops=6 * 10**9, moved=8 * mib, with_index=False,
    )
    att = after(att, *halves)
    atts = gather_parts(att, "tensor")
    swapped = swap(after(jnp.stack(halves), att), "dp", 1)

    full = lambda shape: pl.BlockSpec(shape, lambda e: (0,) * len(shape))
    per_expert = lambda shape: pl.BlockSpec((1,) + shape, lambda e: (e, 0, 0))
    params = pltpu.CompilerParams(
        vmem_limit_bytes=VMEM_LIMIT, dimension_semantics=("arbitrary",)
    )
    moe_flops = 4 * experts * rows * width * hidden_units

    fwd = pl.pallas_call(
        functools.partial(moe_fwd_kernel, 0, PIECES, shares, experts),
        grid=(experts,),
        in_specs=[SMEM]
        + [full((rows, features))] * shares
        + [full((features, width)), full((shares - 1, half_rows, width))]
        + [full((half_rows, width))] * (shares - 1)
        + [
            full((rows, width)), full((width,)), full((experts, width)),
            full((rows, 2)), full((rows, width)),
            per_expert((width, hidden_units)), per_expert((hidden_units, width)),
        ],
        out_specs=[full((share, width))] * shares
        + [
            full((shares, features, width)), full((rows, width)),
            full((share, width)), full((rows, LANES)), full((rows, LANES)),
            per_expert((rows, hidden_units)), per_expert((rows, hidden_units)),
        ],
        out_shape=[shaped((share, width), BF16)] * shares
        + [
            shaped((shares, features, width), BF16),
            shaped((rows, width), BF16),
            shaped((share, width), F32),
            shaped((rows, LANES), F32),
            shaped((rows, LANES), F32),
            shaped((experts, rows, hidden_units), BF16),
            shaped((experts, rows, hidden_units), BF16),
        ],
        scratch_shapes=[pltpu.VMEM((rows, width), F32)],
        compiler_params=params,
        cost_estimate=pl.CostEstimate(
            flops=moe_flops, bytes_accessed=32 * mib, transcendentals=0
        ),
    )(
        idx, *atts, w_out, swapped, *halves, tokens, gain_moe, router_t, routes, grad_out,
        w_in, w_down,
    )
    moe_parts = fwd[:shares]
    wo, normed_two, own_hidden, gates, ggate, act, slope = fwd[shares:]
    if four:
        moe_near = reduce_near(moe_parts, "tensor")
    else:
        moe_near = exchange(moe_parts, "tensor")[1:]

    bwd = pl.pallas_call(
        functools.partial(moe_bwd_kernel, 0, shares, experts),
        grid=(experts,),
        in_specs=[
            SMEM, full((rows, LANES)), full((rows, LANES)), full((rows, width)),
            per_expert((rows, hidden_units)), full((experts, width)),
            per_expert((width, hidden_units)), per_expert((hidden_units, width)),
        ],
        out_specs=[full((share, width))] * shares
        + [full((rows, LANES)), per_expert((rows, hidden_units))],
        out_shape=[shaped((share, width), BF16)] * shares
        + [
            shaped((rows, LANES), F32),
            shaped((experts, rows, hidden_units), BF16),
        ],
        scratch_shapes=[pltpu.VMEM((rows, width), F32)],
        compiler_params=params,
        cost_estimate=pl.CostEstimate(
            flops=moe_flops, bytes_accessed=26 * mib, transcendentals=0
        ),
    )(idx, gates, ggate, grad_out, slope, router_t, w_in, w_down)
    gx_parts = [after(part, *moe_near) for part in bwd[:shares]]
    glog, gpre = bwd[shares:]
    gx_near = reduce_near(gx_parts, "tensor") if four else exchange(gx_parts, "tensor")[1:]

    expert_grads, router_rows = pl.pallas_call(
        functools.partial(moe_weights_kernel, PIECES),
        grid=(experts,),
        in_specs=[
            full((rows, width)), full((rows, LANES)), full((rows, LANES)), full((rows, width)),
            per_expert((rows, hidden_units)), per_expert((rows, hidden_units)),
        ],
        out_specs=[
            pl.BlockSpec((1, 2, width, width), lambda e: (e, 0, 0, 0)), full((8, width))
        ],
        out_shape=[shaped((experts, 2, width, width), BF16), shaped((8, width), F32)],
        compiler_params=params,
        cost_estimate=pl.CostEstimate(
            flops=moe_flops, bytes_accessed=26 * mib, transcendentals=0
        ),
    )(grad_out, gates, glog, normed_two, act, gpre)
    expert_rows = after(expert_grads.reshape(experts * 2 * width, width), *gx_near)
    expert_rows = lax.psum_scatter(expert_rows, "dp", scatter_dimension=0, tiled=True)

    if four:
        gx_near = after(gx_near[0], router_rows), gx_near[1]
        gx_got, _ = reduce_far(gx_parts, gx_near, "tensor")
    else:
        gx_got = [gx_parts[0], *gx_near]
    back = whole_call(
        functools.partial(hidden_back_kernel, 0, PIECES, shares, len(gx_got)),
        [shaped((share, features), BF16)] * shares
        + [shaped((share, width), F32), shaped((share, width), BF16), shaped((1, width), F32)],
        [idx, *gx_got, wo, own_hidden, grad_out, gain_moe],
        flops=3 * 10**8, moved=5 * mib,
    )
    go = exchange(back[:shares], "tensor")
    grad_hidden, gh_low, ggain_two = back[shares:]
    w_out_rows = whole_call(
        functools.partial(w_out_back_kernel, PIECES, shares),
        [shaped((shares, features, width), BF16)],
        [idx, *atts, gh_low],
        flops=3 * 10**8, moved=4 * mib,
    )[0]
    go[1:] = after(go[1], w_out_rows), *go[2:]

    if four:
        moe_near = after(moe_near[0], *go[1:]), moe_near[1]
        moe_got, _ = reduce_far(moe_parts, moe_near, "tensor")
    else:
        moe_got = [moe_parts[0], *moe_near]
    result_share = whole_call(
        functools.partial(join_kernel, PIECES, len(moe_got)),
        [shaped((share, width), BF16)],
        [own_hidden, *moe_got],
        moved=3 * mib, with_index=False,
    )[0]
    attn_back = whole_call(
        functools.partial(attn_bwd_kernel, 0, PIECES, heads, head_size, shares),
        [shaped((share, width), BF16)] * shares
        + [shaped((3, rows, features), BF16), shaped((features, width), BF16)],
        [
            idx, *go, tokens, router_rows, ggain_two, qh, ot, lse, k, v, bias, far, segments,
            w_qkv_t, gather_hot,
        ],
        [pltpu.VMEM((rows, features), F32)] * 2
        + [
            pltpu.VMEM((features, rows), F32),
            pltpu.VMEM((2 * heads, BLK, BLK), F32),
            pltpu.VMEM((rows, features), BF16),
            pltpu.VMEM((features, width), F32),
            pltpu.VMEM((features, rows), BF16),
            pltpu.VMEM((8, rows), F32),
            pltpu.VMEM((2, 8, 2 * BLK), F32),
            pltpu.VMEM((8, BLK), F32),
        ],
        flops=14 * 10**9, moved=8 * mib,
    )
    gn_parts = [after(part, moe_got[-1]) for part in attn_back[:shares]]
    gproj, misc = attn_back[shares:]

    qkv_rows = whole_call(
        functools.partial(qkv_weights_kernel, PIECES),
        [shaped((3, features, width), BF16)],
        [normed_one, gproj],
        flops=10**9, moved=4 * mib, with_index=False,
    )[0]
    late = jnp.concatenate([qkv_rows, misc[None], w_out_rows], axis=0)
    if four:
        near = reduce_near(gn_parts, "tensor")
        near = after(near[0], late, near[1]), near[1]
        gn_got, mark = reduce_far(gn_parts, near, "tensor")
    else:
        gn_got = exchange(gn_parts, "tensor")
        mark = gn_got[-1]

    place = lax.axis_index("dp")

    def halve(value, bit, *ready):
        keep, send = halves_of(value, 1, (place // bit) % 2)
        got = swap(after(send, *ready), "dp", bit)
        return (keep.astype(F32) + got.astype(F32)).astype(BF16)

    bits = bits_of("dp")
    late = halve(late, 1)

    expert_rows = after(expert_rows, mark)
    grad_hidden = after(grad_hidden, late)
    gt_share = whole_call(
        functools.partial(input_back_kernel, PIECES, len(gn_got)),
        [shaped((share, width), BF16)],
        [idx, *gn_got, grad_hidden, tokens, gain_attn],
        moved=5 * mib,
    )[0]
    result_one = swap(after(result_share, mark), "tensor", 1)
    gt_now, result_one = together(gt_share, result_one)
    keep, send = halves_of(late, 1, (place // bits[1]) % 2)
    two, one, got = together(
        swap(gt_now, "tensor", 2), swap(gt_now, "tensor", 1),
        swap(after(send, gt_share), "dp", bits[1]),
    )
    late = (keep.astype(F32) + got.astype(F32)).astype(BF16)
    keep, send = halves_of(late, 1, (place // bits[2]) % 2)
    three, got = together(swap(two, "tensor", 1), swap(send, "dp", bits[2]))
    late = (keep.astype(F32) + got.astype(F32)).astype(BF16)
    for bit in bits[3:]:
        late = halve(late, bit)
    grad_tokens = whole_call(
        functools.partial(place_kernel, PIECES, shares),
        [shaped((rows, width), F32)], [idx, gt_share, one, two, three], moved=5 * mib,
    )[0]

    *sent, result_two, _ = together(
        *[swap(jnp.stack([late[4 + by], late[3]]), "tensor", by) for by in others],
        swap(after(result_share, two), "tensor", 2), grad_tokens,
    )
    out_sum, small = late[4].astype(F32), [late[3]]
    for got in sent:
        out_sum = out_sum + got[0].astype(F32)
        small.append(got[1])
    small = [part.astype(F32) for part in small]
    while len(small) > 1:
        small = [small[at] + small[at + 1] for at in range(0, len(small), 2)]
    late = jnp.concatenate(
        [late[:3], jnp.stack([small[0].astype(BF16), out_sum.astype(BF16)])], axis=0
    )

    expert_rows = lax.all_gather(expert_rows, "dp", axis=0, tiled=True)

    def joined(value, got, bit):
        low = (place // bit) % 2 == 0
        return jnp.concatenate([jnp.where(low, value, got), jnp.where(low, got, value)], axis=1)

    for bit in reversed(bits[3:]):
        late = joined(late, swap(late, "dp", bit), bit)
    late = joined(late, swap(late, "dp", bits[2]), bits[2])
    grad_w_in = expert_rows.reshape(experts, 2, width, width)[:, 0].astype(F32)
    got, _, result_three = together(
        swap(late, "dp", bits[1]), grad_w_in, swap(result_two, "tensor", 1)
    )
    late = joined(late, got, bits[1])
    expert_rows = after(expert_rows, got)
    grad_w_down = expert_rows.reshape(experts, 2, width, width)[:, 1].astype(F32)
    result = whole_call(
        functools.partial(place_kernel, PIECES, shares),
        [shaped((rows, width), BF16)],
        [idx, result_share, result_one, result_two, result_three],
        moved=3 * mib,
    )[0]
    got = after(swap(late, "dp", bits[0]), grad_w_down, result)
    late = joined(late, got, bits[0])
    grad_w_qkv = jnp.swapaxes(late[:3], 1, 2).astype(F32)
    grad_w_out = late[4].astype(F32)
    small = late[3].astype(F32)
    grad_rel = lax.dynamic_slice_in_dim(small, me * 8, 8, 0)
    first = 8 * shares
    return (
        result,
        grad_tokens,
        small[first + 8],
        grad_w_qkv,
        grad_w_out,
        grad_rel[:heads, :NB].T,
        small[first + 9],
        small[first : first + experts].T,
        grad_w_in,
        grad_w_down,
    )


def solution(mesh):
    placed = (
        P("dp", None),
        P("dp", None),
        P("dp", None),
        P("dp", None),
        P(),
        P(None, None, "tensor"),
        P("tensor", None),
        P(None, "tensor"),
        P(),
        P(),
        P(None, None, "tensor"),
        P(None, "tensor", None),
    )
    return jax.shard_map(
        body,
        mesh=mesh,
        in_specs=placed,
        out_specs=(
            P("dp", None),
            P("dp", None),
            P(),
            P(None, None, "tensor"),
            P("tensor", None),
            P(None, "tensor"),
            P(),
            P(),
            P(None, None, "tensor"),
            P(None, "tensor", None),
        ),
        check_vma=False,
    )
```

```python
import functools
import math

import jax
import jax.numpy as jnp
import numpy as np
from jax import lax
from jax.experimental import pallas as pl
from jax.experimental.pallas import tpu as pltpu
from jax.sharding import PartitionSpec as P

NB = 32
DIST = 128
EPSILON = 1e-06
NEGATIVE = -1e30
HIGHEST = lax.Precision.HIGHEST
F32 = jnp.float32
BF16 = jnp.bfloat16
BLK = 256
LANES = 128
VMEM_LIMIT = 56 * 1024 * 1024

NN = (((1,), (0,)), ((), ()))
NT = (((1,), (1,)), ((), ()))
TN = (((0,), (0,)), ((), ()))


def dot(a, b, dims=NN, precision=None):
    return lax.dot_general(a, b, dims, precision=precision, preferred_element_type=F32)


def bucket_of(distance):
    halfway = NB // 2
    thresholds = [
        int(math.ceil(halfway * (DIST / halfway) ** (step / halfway))) for step in range(halfway)
    ]
    beyond = sum((distance >= threshold).astype(np.int64) for threshold in thresholds)
    return np.where(distance < halfway, distance, halfway - 1 + beyond)


def near_tables():
    lanes = np.arange(2 * BLK)
    offset = np.where(lanes < BLK, lanes, lanes - 2 * BLK)
    build = np.stack([np.maximum(offset, 0), np.maximum(BLK + offset, 0)])
    gather = np.stack([lanes - (BLK - 1), lanes + 1])
    eye = np.eye(NB, dtype=np.float32)
    build_hot = eye[bucket_of(build)]
    gather_hot = eye[bucket_of(np.maximum(gather, 0))] * (gather >= 0)[..., None]
    return build_hot, gather_hot


def row_scale(values):
    return lax.rsqrt(jnp.mean(values * values, axis=-1, keepdims=True) + EPSILON)


def lane_pick(values, index):
    lanes = lax.broadcasted_iota(jnp.int32, values.shape, 1)
    return jnp.sum(jnp.where(lanes == index, values, 0.0), axis=1, keepdims=True)


def masked_scores(k_tile, qh_tile, bias, seg_k, seg_q, diagonal):
    scores = dot(k_tile, qh_tile, NT) + bias
    allowed = seg_k == seg_q
    if diagonal:
        key_at = lax.broadcasted_iota(jnp.int32, scores.shape, 0)
        query_at = lax.broadcasted_iota(jnp.int32, scores.shape, 1)
        allowed = allowed & (key_at <= query_at)
    return jnp.where(allowed, scores, NEGATIVE)


def tile_bias(bias_ref, far_ref, head, delta):
    if delta < 2:
        return bias_ref[2 * head + delta]
    return far_ref[pl.ds(head, 1), 0:1]


def column_of(row):
    spread = jnp.broadcast_to(row.astype(F32), (8, row.shape[1]))
    return spread.T[:, 0:1]


def attn_fwd_kernel(piece, pieces, heads, head_size, *refs):
    tok, gain, w, seg = refs[:4]
    refs = refs[4:]
    if piece == 0:
        rel, build = refs[:2]
        refs = refs[2:]
    else:
        bias, far = refs[:2]
        refs = refs[2:]
    old_k, refs = refs[:piece], refs[piece:]
    old_vt, refs = refs[:piece], refs[piece:]
    normed, qh, k, v, vt, att, ot, lse = refs[:8]
    if piece == 0:
        bias, far = refs[8:]
    keys_of, vt_of = [*old_k, k], [*old_vt, vt]
    rows_total = tok.shape[0] // pieces
    base = piece * rows_total
    features = w.shape[1]
    blocks = rows_total // BLK
    gain_row = gain[...].astype(F32).reshape(1, -1)
    lanes = lax.broadcasted_iota(jnp.int32, (BLK, features), 1)
    for block in range(blocks):
        rows = pl.ds(block * BLK, BLK)
        x = tok[pl.ds(base + block * BLK, BLK), :].astype(F32)
        n = (x * row_scale(x) * gain_row).astype(BF16)
        normed[rows, :] = n
        q_rows = dot(n, w[0], NT).astype(BF16).astype(F32) * (head_size**-0.5)
        for head in range(heads):
            inside = (lanes >= head * head_size) & (lanes < (head + 1) * head_size)
            qh[head, rows, :] = jnp.where(inside, q_rows, 0.0).astype(BF16)
        k[rows, :] = dot(n, w[1], NT).astype(BF16)
        v_rows = dot(n, w[2], NT).astype(BF16)
        v[rows, :] = v_rows
        vt[:, rows] = v_rows.astype(F32).T.astype(BF16)
    if piece == 0:
        far[...] = jnp.zeros_like(far)
        far[0:heads, :] = jnp.broadcast_to(rel[:, NB - 1 : NB].astype(F32), (heads, LANES))
        for delta in range(2):
            near = dot(rel[...], build[delta])
            for head in range(heads):
                spread = jnp.broadcast_to(near[head : head + 1, :], (BLK, 2 * BLK))
                turned = pltpu.roll(spread, 0, 1, stride=1, stride_axis=0)
                bias[2 * head + delta] = turned[:, :BLK]
    lse[...] = jnp.zeros_like(lse)
    seg_row = seg[...].astype(F32)
    seg_col = column_of(seg[...])

    def one_head(head, carry):
        part = pl.ds(pl.multiple_of(head * head_size, head_size), head_size)
        for block in range(blocks):
            qb = piece * blocks + block
            cols = pl.ds(block * BLK, BLK)
            q_tile = qh[head, cols, :]
            tiles = []
            for kb in range(qb + 1):
                keys = pl.ds(kb % blocks * BLK, BLK)
                tiles.append(
                    masked_scores(
                        keys_of[kb // blocks][keys, :], q_tile,
                        tile_bias(bias, far, head, qb - kb),
                        seg_col[kb * BLK : (kb + 1) * BLK, :],
                        seg_row[:, qb * BLK : (qb + 1) * BLK], kb == qb,
                    )
                )
            peak = functools.reduce(
                jnp.maximum, [jnp.max(t, axis=0, keepdims=True) for t in tiles]
            )
            total = jnp.zeros((1, BLK), F32)
            out = jnp.zeros((head_size, BLK), F32)
            for kb in range(qb + 1):
                raised = jnp.exp(tiles[kb] - peak)
                total = total + jnp.sum(raised, axis=0, keepdims=True)
                values = vt_of[kb // blocks][part, pl.ds(kb % blocks * BLK, BLK)]
                out = out + dot(values, raised.astype(BF16))
            ot[part, cols] = out / total
            lse[pl.ds(head, 1), cols] = peak + jnp.log(total)
        return carry

    lax.fori_loop(0, heads, one_head, 0)
    for block in range(blocks):
        cols = pl.ds(block * BLK, BLK)
        att[cols, :] = ot[:, cols].T.astype(BF16)


def attn_bwd_kernel(piece, pieces, heads, head_size, shares, idx, *refs):
    held = piece + 1
    last = held == pieces
    go_parts, refs = refs[:shares], refs[shares:]
    tok, router, gain_two, qh, ot, lse = refs[:6]
    refs = refs[6:]
    ks, refs = refs[:held], refs[held:]
    vs, refs = refs[:held], refs[held:]
    bias, far, seg = refs[:3]
    refs = refs[3:]
    if piece:
        gk_in, refs = refs[:piece], refs[piece:]
        gv_in, refs = refs[:piece], refs[piece:]
        gq_in, refs = refs[:piece], refs[piece:]
        acc_in, refs = refs[0], refs[1:]
    if last:
        w, hot = refs[:2]
        refs = refs[2:]
        gn_parts, refs = refs[:shares], refs[shares:]
        gproj, misc = refs[:2]
        refs = refs[2:]
        gk, refs = refs[:held], refs[held:]
        gv, refs = refs[:held], refs[held:]
        gq_t, acc = refs[:2]
        refs = refs[2:]
    else:
        gk, refs = refs[:held], refs[held:]
        gv, refs = refs[:held], refs[held:]
        gq_t, acc = refs[:2]
        refs = refs[2:]
    go, misc_sum, kt, d_row, near_sum, far_sum = refs
    rows_total, features = ks[0].shape
    blocks = rows_total // BLK
    share = rows_total // shares
    me = idx[0]
    for step in range(shares):
        start = pl.multiple_of((me ^ step) * share, share)
        go[pl.ds(start, share), :] = go_parts[step][...]
    for index in range(held):
        for block in range(blocks):
            cols = pl.ds(block * BLK, BLK)
            kt[:, pl.ds((index * blocks + block) * BLK, BLK)] = (
                ks[index][cols, :].astype(F32).T.astype(BF16)
            )
        if index < piece:
            gk[index][...] = gk_in[index][...]
            gv[index][...] = gv_in[index][...]
        else:
            gk[index][...] = jnp.zeros_like(gk[index])
            gv[index][...] = jnp.zeros_like(gv[index])
    if piece:
        acc[...] = acc_in[...]
    else:
        acc[...] = jnp.zeros_like(acc)
    for block in range(blocks):
        cols = pl.ds(block * BLK, BLK)
        product = go[cols, :].astype(F32).T * ot[:, cols]
        for head in range(heads):
            part = product[head * head_size : (head + 1) * head_size, :]
            d_row[head : head + 1, cols] = jnp.sum(part, axis=0, keepdims=True)
    near_sum[...] = jnp.zeros_like(near_sum)
    far_sum[...] = jnp.zeros_like(far_sum)
    key_at = lax.broadcasted_iota(jnp.int32, (BLK, BLK), 0)
    other_at = lax.broadcasted_iota(jnp.int32, (BLK, BLK), 1)
    flip = (key_at + other_at == BLK - 1).astype(F32)
    seg_row = seg[...].astype(F32)
    seg_col = column_of(seg[...])

    def one_head(head, carry):
        part = pl.ds(pl.multiple_of(head * head_size, head_size), head_size)
        lanes = lax.broadcasted_iota(jnp.int32, (BLK, features), 1)
        inside = (lanes >= head * head_size) & (lanes < (head + 1) * head_size)
        for block in range(blocks):
            qb = piece * blocks + block
            cols = pl.ds(block * BLK, BLK)
            q_tile = qh[head, cols, :]
            go_tile = jnp.where(inside, go[cols, :].astype(F32), 0.0).astype(BF16)
            log_total = lse[pl.ds(head, 1), cols]
            d_tile = d_row[pl.ds(head, 1), cols]
            gq = jnp.zeros((head_size, BLK), F32)
            for kb in range(qb + 1):
                index = kb // blocks
                keys = pl.ds(kb % blocks * BLK, BLK)
                delta = qb - kb
                scores = masked_scores(
                    ks[index][keys, :], q_tile, tile_bias(bias, far, head, delta),
                    seg_col[kb * BLK : (kb + 1) * BLK, :],
                    seg_row[:, qb * BLK : (qb + 1) * BLK], delta == 0,
                )
                probs = jnp.exp(scores - log_total)
                gs = probs * (dot(vs[index][keys, :], go_tile, NT) - d_tile)
                if delta < 2:
                    acc[2 * head + delta] += gs
                else:
                    far_sum[pl.ds(head, 1), :] += jnp.sum(gs, axis=0, keepdims=True)
                gs_low = gs.astype(BF16)
                gv[index][keys, :] += dot(probs.astype(BF16), go_tile)
                gk[index][keys, :] += dot(gs_low, q_tile)
                gq = gq + dot(kt[part, kb * BLK : (kb + 1) * BLK], gs_low)
            gq_t[part, cols] = gq * (head_size**-0.5)
        return carry

    lax.fori_loop(0, heads, one_head, 0)
    if not last:
        return
    gqs = [*(gq_in if piece else ()), gq_t]
    for index in range(held):
        for block in range(blocks):
            rows = pl.ds(block * BLK, BLK)
            out = pl.ds((index * blocks + block) * BLK, BLK)
            gproj[0, out, :] = gqs[index][:, rows].T.astype(BF16)
            gproj[1, out, :] = gk[index][rows, :].astype(BF16)
            gproj[2, out, :] = gv[index][rows, :].astype(BF16)
    gain_one = jnp.zeros_like(gain_two)
    for step in range(shares):
        for index in range(pieces):
            start = index * rows_total + (me ^ step) * share
            rows = pl.ds(pl.multiple_of(start, share), share)
            total = dot(gproj[0, rows, :], w[0])
            total = total + dot(gproj[1, rows, :], w[1])
            total = total + dot(gproj[2, rows, :], w[2])
            gn_parts[step][pl.ds(index * share, share), :] = total.astype(BF16)
            x = tok[rows, :].astype(F32)
            gain_one = gain_one + jnp.sum(total * (x * row_scale(x)), axis=0, keepdims=True)
    for head in range(heads):
        for delta in range(2):
            turned = dot(flip, acc[2 * head + delta], NN, HIGHEST)
            wide = jnp.concatenate([turned, jnp.zeros_like(turned)], axis=1)
            sheared = pltpu.roll(wide, 0, 1, stride=1, stride_axis=0)
            near_sum[delta, head : head + 1, :] = jnp.sum(sheared, axis=0, keepdims=True)
    summed = dot(near_sum[0], hot[0], NN, HIGHEST) + dot(near_sum[1], hot[1], NN, HIGHEST)
    buckets = lax.broadcasted_iota(jnp.int32, summed.shape, 1)
    beyond = jnp.sum(far_sum[...], axis=1, keepdims=True)
    summed = summed + jnp.where(buckets == NB - 1, beyond, 0.0)
    misc_sum[...] = jnp.zeros_like(misc_sum)
    misc_sum[pl.ds(pl.multiple_of(me * 8, 8), 8), 0:NB] = summed
    misc_sum[8 * shares : 8 * shares + 8, :] = router[...]
    misc_sum[8 * shares + 8 : 8 * shares + 9, :] = gain_one
    misc_sum[8 * shares + 9 : 8 * shares + 10, :] = gain_two[...]
    misc[...] = misc_sum[...].astype(BF16)


def qkv_weights_kernel(pieces, *refs):
    normed = refs[:pieces]
    gproj, out = refs[pieces:]
    rows_total = normed[0].shape[0]
    for c in range(3):
        total = dot(gproj[c, pl.ds(0, rows_total), :], normed[0][...], TN)
        for index in range(1, pieces):
            rows = pl.ds(index * rows_total, rows_total)
            total = total + dot(gproj[c, rows, :], normed[index][...], TN)
        out[c] = total.astype(BF16)


def gelu_pair(values):
    squared = values * values
    bent = jnp.tanh(values * (0.7978845608028654 + 0.7978845608028654 * 0.044715 * squared))
    half = 0.5 * (1.0 + bent)
    lifted = values * half
    slope = 0.7978845608028654 + 3.0 * 0.7978845608028654 * 0.044715 * squared
    return lifted, half + lifted * (1.0 - bent) * slope


def padded_rows(values, rows):
    missing = jnp.zeros((rows - values.shape[0], values.shape[1]), values.dtype)
    return jnp.concatenate([values, missing], axis=0)


def moe_fwd_kernel(piece, pieces, shares, experts, idx, *refs):
    att, refs = refs[:shares], refs[shares:]
    if piece == 0:
        wo_own, wo_swapped, refs = refs[0], refs[1], refs[2:]
        wo_fetched, refs = refs[: shares - 1], refs[shares - 1 :]
    else:
        wo, refs = refs[0], refs[1:]
    tok, gain, router, routes, cot, w_in, w_down = refs[:7]
    refs = refs[7:]
    parts, refs = refs[:shares], refs[shares:]
    if piece == 0:
        wo, refs = refs[0], refs[1:]
    normed, own, gates, ggate, act, slope, acc = refs
    rows_total = tok.shape[0] // pieces
    base = piece * rows_total
    share = rows_total // shares
    me = idx[0]
    expert = pl.program_id(0)

    @pl.when(expert == 0)
    def _():
        gain_row = gain[...].astype(F32).reshape(1, -1)
        router_wide = padded_rows(router[...].astype(F32), LANES).astype(BF16)
        if piece == 0:
            half = wo_own.shape[0] // 2
            mine = pl.ds(pl.multiple_of(idx[1] * half, half), half)
            other = pl.ds(pl.multiple_of((1 - idx[1]) * half, half), half)
            wo[0] = wo_own[...]
            for step in range(1, shares):
                wo[step, mine, :] = wo_fetched[step - 1][...]
                wo[step, other, :] = wo_swapped[step - 1]
        for block in range(rows_total // BLK):
            rows = pl.ds(block * BLK, BLK)
            outer = pl.ds(base + block * BLK, BLK)
            attn = dot(att[0][rows, :], wo[0])
            for step in range(1, shares):
                attn = attn + dot(att[step][rows, :], wo[step])
            hidden = tok[outer, :].astype(F32) + attn
            acc[rows, :] = hidden
            n = (hidden * row_scale(hidden) * gain_row).astype(BF16)
            normed[rows, :] = n
            logits = dot(n, router_wide, NT)
            lanes = lax.broadcasted_iota(jnp.int32, logits.shape, 1)
            first = lanes == routes[outer, 0:1]
            second = lanes == routes[outer, 1:2]
            one = jnp.sum(jnp.where(first, logits, 0.0), axis=1, keepdims=True)
            two = jnp.sum(jnp.where(second, logits, 0.0), axis=1, keepdims=True)
            peak = jnp.maximum(one, two)
            one = jnp.exp(one - peak)
            two = jnp.exp(two - peak)
            both = one + two
            gates[rows, :] = jnp.where(first, one / both, jnp.where(second, two / both, 0.0))
        own[...] = acc[pl.ds(pl.multiple_of(me * share, share), share), :]
        acc[...] = jnp.zeros_like(acc)
        ggate[...] = jnp.zeros_like(ggate)

    for block in range(rows_total // ROWS):
        rows = pl.ds(block * ROWS, ROWS)
        outer = pl.ds(base + block * ROWS, ROWS)
        lifted, bend = gelu_pair(dot(normed[rows, :], w_in[0]))
        lifted = lifted.astype(BF16)
        act[0, rows, :] = lifted
        slope[0, rows, :] = bend.astype(BF16)
        out = dot(lifted, w_down[0])
        gate = lane_pick(gates[rows, :], expert)
        acc[rows, :] += gate * out
        pulled = jnp.sum(cot[outer, :].astype(F32) * out, axis=1, keepdims=True)
        held = ggate[rows, :]
        lanes = lax.broadcasted_iota(jnp.int32, held.shape, 1)
        ggate[rows, :] = jnp.where(lanes == expert, pulled, held)

    @pl.when(expert == experts - 1)
    def _():
        for step in range(shares):
            start = pl.multiple_of((me ^ step) * share, share)
            parts[step][...] = acc[pl.ds(start, share), :].astype(BF16)


def moe_bwd_kernel(piece, shares, experts, idx, *refs):
    gates, ggate, cot, slope, router, w_in, w_down = refs[:7]
    refs = refs[7:]
    parts, refs = refs[:shares], refs[shares:]
    glog, gpre, acc = refs
    rows_total = gates.shape[0]
    base = piece * rows_total
    share = rows_total // shares
    me = idx[0]
    expert = pl.program_id(0)

    @pl.when(expert == 0)
    def _():
        router_wide = padded_rows(router[...].astype(F32), LANES)
        for block in range(rows_total // ROWS):
            rows = pl.ds(block * ROWS, ROWS)
            g, gg = gates[rows, :], ggate[rows, :]
            back = g * (gg - jnp.sum(g * gg, axis=1, keepdims=True))
            glog[rows, :] = back
            acc[rows, :] = dot(back, router_wide, NN, HIGHEST)

    for block in range(rows_total // ROWS):
        rows = pl.ds(block * ROWS, ROWS)
        gate = lane_pick(gates[rows, :], expert)
        weighted = cot[pl.ds(base + block * ROWS, ROWS), :].astype(F32)
        weighted = (gate * weighted).astype(BF16)
        gp = (dot(weighted, w_down[0], NT) * slope[0, rows, :].astype(F32)).astype(BF16)
        gpre[0, rows, :] = gp
        acc[rows, :] += dot(gp, w_in[0], NT)

    @pl.when(expert == experts - 1)
    def _():
        for step in range(shares):
            start = pl.multiple_of((me ^ step) * share, share)
            parts[step][...] = acc[pl.ds(start, share), :].astype(BF16)


def moe_weights_kernel(pieces, cot, *refs):
    gates, refs = refs[:pieces], refs[pieces:]
    glog, refs = refs[:pieces], refs[pieces:]
    normed, refs = refs[:pieces], refs[pieces:]
    act, refs = refs[:pieces], refs[pieces:]
    gpre, refs = refs[:pieces], refs[pieces:]
    out, router = refs
    rows_total = normed[0].shape[0]
    expert = pl.program_id(0)

    @pl.when(expert == 0)
    def _():
        total = jnp.zeros((LANES, cot.shape[1]), F32)
        for index in range(pieces):
            back = glog[index][...]
            high = back.astype(BF16)
            low = (back - high.astype(F32)).astype(BF16)
            total = total + dot(high, normed[index][...], TN)
            total = total + dot(low, normed[index][...], TN)
        router[...] = total[0:8, :]

    grad_in = jnp.zeros((normed[0].shape[1], gpre[0].shape[2]), F32)
    grad_down = jnp.zeros((act[0].shape[2], cot.shape[1]), F32)
    for index in range(pieces):
        gate = lane_pick(gates[index][...], expert)
        weighted = cot[pl.ds(index * rows_total, rows_total), :].astype(F32)
        weighted = (gate * weighted).astype(BF16)
        grad_in = grad_in + dot(normed[index][...], gpre[index][0], TN)
        grad_down = grad_down + dot(act[index][0], weighted, TN)
    out[0, 0] = grad_in.astype(BF16)
    out[0, 1] = grad_down.astype(BF16)


def hidden_back_kernel(piece, pieces, shares, got, idx, *refs):
    gx, refs = refs[:got], refs[got:]
    wo, own, cot, gain = refs[:4]
    refs = refs[4:]
    ga, refs = refs[:shares], refs[shares:]
    gh, gh_low, ggain = refs
    share = own.shape[0]
    grad = gx[0][...].astype(F32)
    for step in range(1, got):
        grad = grad + gx[step][...].astype(F32)
    hidden = own[...]
    scale = row_scale(hidden)
    unit = hidden * scale
    ggain[...] = jnp.sum(grad * unit, axis=0, keepdims=True)
    gained = grad * gain[...].astype(F32).reshape(1, -1)
    start = piece * (cot.shape[0] // pieces) + idx[0] * share
    mine = cot[pl.ds(pl.multiple_of(start, share), share), :].astype(F32)
    back = mine + scale * (gained - unit * jnp.mean(gained * unit, axis=-1, keepdims=True))
    gh[...] = back
    low = back.astype(BF16)
    gh_low[...] = low
    for step in range(shares):
        ga[step][...] = dot(low, wo[step], NT).astype(BF16)


def w_out_back_kernel(pieces, shares, idx, *refs):
    att, refs = refs[: pieces * shares], refs[pieces * shares :]
    gh_low, out = refs[:pieces], refs[pieces]
    share = gh_low[0].shape[0]
    rows = pl.ds(pl.multiple_of(idx[0] * share, share), share)
    for step in range(shares):
        total = dot(att[step][rows, :], gh_low[0][...], TN)
        for index in range(1, pieces):
            total = total + dot(att[index * shares + step][rows, :], gh_low[index][...], TN)
        out[step] = total.astype(BF16)


def join_kernel(pieces, count, *refs):
    own, refs = refs[:pieces], refs[pieces:]
    got, out = refs[: pieces * count], refs[pieces * count]
    share = own[0].shape[0]
    for index in range(pieces):
        total = own[index][...]
        for step in range(count):
            total = total + got[index * count + step][...].astype(F32)
        out[pl.ds(index * share, share), :] = total.astype(BF16)


def input_back_kernel(pieces, got, idx, *refs):
    gn, refs = refs[:got], refs[got:]
    ghs, refs = refs[:pieces], refs[pieces:]
    tok, gain, gt = refs
    share = ghs[0].shape[0]
    gain_row = gain[...].astype(F32).reshape(1, -1)
    for index in range(pieces):
        rows = pl.ds(index * share, share)
        grad = gn[0][rows, :].astype(F32)
        for step in range(1, got):
            grad = grad + gn[step][rows, :].astype(F32)
        start = index * (tok.shape[0] // pieces) + idx[0] * share
        x = tok[pl.ds(pl.multiple_of(start, share), share), :].astype(F32)
        scale = row_scale(x)
        unit = x * scale
        gained = grad * gain_row
        back = scale * (gained - unit * jnp.mean(gained * unit, axis=-1, keepdims=True))
        gt[rows, :] = (ghs[index][...] + back).astype(BF16)


def place_kernel(pieces, shares, idx, *refs):
    blocks, out = refs[:shares], refs[shares]
    rows_total = out.shape[0] // pieces
    share = rows_total // shares
    for step in range(shares):
        owner = idx[0] ^ step
        for index in range(pieces):
            start = pl.multiple_of(index * rows_total + owner * share, share)
            got = blocks[step][pl.ds(index * share, share), :]
            out[pl.ds(start, share), :] = got.astype(out.dtype)


ROWS = 512
PIECES = 1

SMEM = pl.BlockSpec(memory_space=pltpu.SMEM)
VMEM = pl.BlockSpec(memory_space=pltpu.VMEM)


def shaped(shape, dtype):
    return jax.ShapeDtypeStruct(shape, dtype)


def whole_call(kernel, outs, args, scratch=(), flops=0, moved=0, with_index=True):
    specs = ([SMEM] if with_index else []) + [VMEM] * (len(args) - (1 if with_index else 0))
    return pl.pallas_call(
        kernel,
        out_shape=outs,
        in_specs=specs,
        out_specs=[VMEM] * len(outs),
        scratch_shapes=list(scratch),
        compiler_params=pltpu.CompilerParams(vmem_limit_bytes=VMEM_LIMIT),
        cost_estimate=pl.CostEstimate(flops=flops, bytes_accessed=moved, transcendentals=0),
    )(*args)


def swap(value, axis, bit):
    count = lax.axis_size(axis)
    return lax.ppermute(value, axis, [(i, i ^ bit) for i in range(count)])


def sum_over(value, axis):
    bit = 1
    while bit < lax.axis_size(axis):
        value = value + swap(value, axis, bit)
        bit *= 2
    return value


def gather_parts(value, axis):
    count = lax.axis_size(axis)
    if count != 4:
        return [value] + [swap(value, axis, bit) for bit in range(1, count)]
    two = swap(value, axis, 2)
    one = swap(value, axis, 1)
    return [value, one, two, swap(after(two, one), axis, 1)]


def reduce_near(parts, axis):
    return swap(parts[3], axis, 1), swap(parts[1], axis, 1)


def reduce_far(parts, near, axis):
    pair = (parts[2].astype(F32) + near[0].astype(F32)).astype(parts[2].dtype)
    return [parts[0], near[1], swap(pair, axis, 2)], pair


def exchange(parts, axis):
    return [parts[0]] + [swap(parts[bit], axis, bit) for bit in range(1, len(parts))]


def halves_of(value, axis, chosen):
    half = value.shape[axis] // 2
    keep = lax.dynamic_slice_in_dim(value, chosen * half, half, axis)
    send = lax.dynamic_slice_in_dim(value, (1 - chosen) * half, half, axis)
    return keep, send


def bits_of(axis):
    count = lax.axis_size(axis)
    return [1 << level for level in range(count.bit_length() - 1)]


def gather_back(value, mesh_axis, axis):
    me = lax.axis_index(mesh_axis)
    for bit in reversed(bits_of(mesh_axis)):
        got = swap(value, mesh_axis, bit)
        low = (me // bit) % 2 == 0
        value = jnp.concatenate(
            [jnp.where(low, value, got), jnp.where(low, got, value)], axis=axis
        )
    return value


def together(*values):
    return lax.optimization_barrier(values)


def after(value, *others):
    return lax.optimization_barrier((value, *others))[0]


def body(
    tokens, segments, routes, grad_out, gain_attn, w_qkv, w_out, rel_bias,
    gain_moe, w_router, w_in, w_down,
):
    tok_rows, width = tokens.shape
    heads = rel_bias.shape[1]
    features = w_qkv.shape[2]
    head_size = features // heads
    experts, _, hidden_units = w_in.shape
    shares = lax.axis_size("tensor")
    rows = tok_rows // PIECES
    share = rows // shares
    me = lax.axis_index("tensor").astype(jnp.int32)
    side = (lax.axis_index("dp") % 2).astype(jnp.int32)
    idx = jnp.stack([me, side])
    mib = 1 << 20
    others = range(1, shares)
    four = shares == 4

    half_rows = features // 2
    my_half = lax.dynamic_slice_in_dim(w_out, side * half_rows, half_rows, 0)
    halves = [swap(my_half, "tensor", by) for by in others]

    build_hot, gather_hot = near_tables()
    build_hot = jnp.asarray(np.swapaxes(build_hot, 1, 2), BF16)
    gather_hot = jnp.asarray(gather_hot, F32)
    w_qkv_t = jnp.swapaxes(w_qkv, 1, 2)
    router_t = w_router.T

    normed_one, qh, k, v, _, att, ot, lse, bias, far = whole_call(
        functools.partial(attn_fwd_kernel, 0, PIECES, heads, head_size),
        [
            shaped((rows, width), BF16),
            shaped((heads, rows, features), BF16),
            shaped((rows, features), BF16),
            shaped((rows, features), BF16),
            shaped((features, rows), BF16),
            shaped((rows, features), BF16),
            shaped((features, rows), F32),
            shaped((8, rows), F32),
            shaped((2 * heads, BLK, BLK), F32),
            shaped((8, LANES), F32),
        ],
        [tokens, gain_attn, w_qkv_t, segments, rel_bias.T, build_hot],
        flops=6 * 10**9, moved=8 * mib, with_index=False,
    )
    att = after(att, *halves)
    atts = gather_parts(att, "tensor")
    swapped = swap(after(jnp.stack(halves), att), "dp", 1)

    full = lambda shape: pl.BlockSpec(shape, lambda e: (0,) * len(shape))
    per_expert = lambda shape: pl.BlockSpec((1,) + shape, lambda e: (e, 0, 0))
    params = pltpu.CompilerParams(
        vmem_limit_bytes=VMEM_LIMIT, dimension_semantics=("arbitrary",)
    )
    moe_flops = 4 * experts * rows * width * hidden_units

    fwd = pl.pallas_call(
        functools.partial(moe_fwd_kernel, 0, PIECES, shares, experts),
        grid=(experts,),
        in_specs=[SMEM]
        + [full((rows, features))] * shares
        + [full((features, width)), full((shares - 1, half_rows, width))]
        + [full((half_rows, width))] * (shares - 1)
        + [
            full((rows, width)), full((width,)), full((experts, width)),
            full((rows, 2)), full((rows, width)),
            per_expert((width, hidden_units)), per_expert((hidden_units, width)),
        ],
        out_specs=[full((share, width))] * shares
        + [
            full((shares, features, width)), full((rows, width)),
            full((share, width)), full((rows, LANES)), full((rows, LANES)),
            per_expert((rows, hidden_units)), per_expert((rows, hidden_units)),
        ],
        out_shape=[shaped((share, width), BF16)] * shares
        + [
            shaped((shares, features, width), BF16),
            shaped((rows, width), BF16),
            shaped((share, width), F32),
            shaped((rows, LANES), F32),
            shaped((rows, LANES), F32),
            shaped((experts, rows, hidden_units), BF16),
            shaped((experts, rows, hidden_units), BF16),
        ],
        scratch_shapes=[pltpu.VMEM((rows, width), F32)],
        compiler_params=params,
        cost_estimate=pl.CostEstimate(
            flops=moe_flops, bytes_accessed=32 * mib, transcendentals=0
        ),
    )(
        idx, *atts, w_out, swapped, *halves, tokens, gain_moe, router_t, routes, grad_out,
        w_in, w_down,
    )
    moe_parts = fwd[:shares]
    wo, normed_two, own_hidden, gates, ggate, act, slope = fwd[shares:]
    if four:
        moe_near = reduce_near(moe_parts, "tensor")
    else:
        moe_near = exchange(moe_parts, "tensor")[1:]

    bwd = pl.pallas_call(
        functools.partial(moe_bwd_kernel, 0, shares, experts),
        grid=(experts,),
        in_specs=[
            SMEM, full((rows, LANES)), full((rows, LANES)), full((rows, width)),
            per_expert((rows, hidden_units)), full((experts, width)),
            per_expert((width, hidden_units)), per_expert((hidden_units, width)),
        ],
        out_specs=[full((share, width))] * shares
        + [full((rows, LANES)), per_expert((rows, hidden_units))],
        out_shape=[shaped((share, width), BF16)] * shares
        + [
            shaped((rows, LANES), F32),
            shaped((experts, rows, hidden_units), BF16),
        ],
        scratch_shapes=[pltpu.VMEM((rows, width), F32)],
        compiler_params=params,
        cost_estimate=pl.CostEstimate(
            flops=moe_flops, bytes_accessed=26 * mib, transcendentals=0
        ),
    )(idx, gates, ggate, grad_out, slope, router_t, w_in, w_down)
    gx_parts = [after(part, *moe_near) for part in bwd[:shares]]
    glog, gpre = bwd[shares:]
    gx_near = reduce_near(gx_parts, "tensor") if four else exchange(gx_parts, "tensor")[1:]

    expert_grads, router_rows = pl.pallas_call(
        functools.partial(moe_weights_kernel, PIECES),
        grid=(experts,),
        in_specs=[
            full((rows, width)), full((rows, LANES)), full((rows, LANES)), full((rows, width)),
            per_expert((rows, hidden_units)), per_expert((rows, hidden_units)),
        ],
        out_specs=[
            pl.BlockSpec((1, 2, width, width), lambda e: (e, 0, 0, 0)), full((8, width))
        ],
        out_shape=[shaped((experts, 2, width, width), BF16), shaped((8, width), F32)],
        compiler_params=params,
        cost_estimate=pl.CostEstimate(
            flops=moe_flops, bytes_accessed=26 * mib, transcendentals=0
        ),
    )(grad_out, gates, glog, normed_two, act, gpre)
    expert_rows = after(expert_grads.reshape(experts * 2 * width, width), *gx_near)
    expert_rows = lax.psum_scatter(expert_rows, "dp", scatter_dimension=0, tiled=True)

    if four:
        gx_near = after(gx_near[0], router_rows), gx_near[1]
        gx_got, _ = reduce_far(gx_parts, gx_near, "tensor")
    else:
        gx_got = [gx_parts[0], *gx_near]
    back = whole_call(
        functools.partial(hidden_back_kernel, 0, PIECES, shares, len(gx_got)),
        [shaped((share, features), BF16)] * shares
        + [shaped((share, width), F32), shaped((share, width), BF16), shaped((1, width), F32)],
        [idx, *gx_got, wo, own_hidden, grad_out, gain_moe],
        flops=3 * 10**8, moved=5 * mib,
    )
    go = exchange(back[:shares], "tensor")
    grad_hidden, gh_low, ggain_two = back[shares:]
    w_out_rows = whole_call(
        functools.partial(w_out_back_kernel, PIECES, shares),
        [shaped((shares, features, width), BF16)],
        [idx, *atts, gh_low],
        flops=3 * 10**8, moved=4 * mib,
    )[0]
    go[1:] = after(go[1], w_out_rows), *go[2:]

    if four:
        moe_near = after(moe_near[0], *go[1:]), moe_near[1]
        moe_got, _ = reduce_far(moe_parts, moe_near, "tensor")
    else:
        moe_got = [moe_parts[0], *moe_near]
    result_share = whole_call(
        functools.partial(join_kernel, PIECES, len(moe_got)),
        [shaped((share, width), BF16)],
        [own_hidden, *moe_got],
        moved=3 * mib, with_index=False,
    )[0]
    attn_back = whole_call(
        functools.partial(attn_bwd_kernel, 0, PIECES, heads, head_size, shares),
        [shaped((share, width), BF16)] * shares
        + [shaped((3, rows, features), BF16), shaped((features, width), BF16)],
        [
            idx, *go, tokens, router_rows, ggain_two, qh, ot, lse, k, v, bias, far, segments,
            w_qkv_t, gather_hot,
        ],
        [pltpu.VMEM((rows, features), F32)] * 2
        + [
            pltpu.VMEM((features, rows), F32),
            pltpu.VMEM((2 * heads, BLK, BLK), F32),
            pltpu.VMEM((rows, features), BF16),
            pltpu.VMEM((features, width), F32),
            pltpu.VMEM((features, rows), BF16),
            pltpu.VMEM((8, rows), F32),
            pltpu.VMEM((2, 8, 2 * BLK), F32),
            pltpu.VMEM((8, BLK), F32),
        ],
        flops=14 * 10**9, moved=8 * mib,
    )
    gn_parts = [after(part, moe_got[-1]) for part in attn_back[:shares]]
    gproj, misc = attn_back[shares:]

    qkv_rows = whole_call(
        functools.partial(qkv_weights_kernel, PIECES),
        [shaped((3, features, width), BF16)],
        [normed_one, gproj],
        flops=10**9, moved=4 * mib, with_index=False,
    )[0]
    late = jnp.concatenate([qkv_rows, misc[None], w_out_rows], axis=0)
    if four:
        near = reduce_near(gn_parts, "tensor")
        near = after(near[0], late, near[1]), near[1]
        gn_got, mark = reduce_far(gn_parts, near, "tensor")
    else:
        gn_got = exchange(gn_parts, "tensor")
        mark = gn_got[-1]

    place = lax.axis_index("dp")

    def halve(value, bit, *ready):
        keep, send = halves_of(value, 1, (place // bit) % 2)
        got = swap(after(send, *ready), "dp", bit)
        return (keep.astype(F32) + got.astype(F32)).astype(BF16)

    bits = bits_of("dp")
    late = halve(late, 1)

    expert_rows = after(expert_rows, mark)
    grad_hidden = after(grad_hidden, late)
    gt_share = whole_call(
        functools.partial(input_back_kernel, PIECES, len(gn_got)),
        [shaped((share, width), BF16)],
        [idx, *gn_got, grad_hidden, tokens, gain_attn],
        moved=5 * mib,
    )[0]
    result_one = swap(after(result_share, mark), "tensor", 1)
    gt_now, result_one = together(gt_share, result_one)
    keep, send = halves_of(late, 1, (place // bits[1]) % 2)
    two, one, got = together(
        swap(gt_now, "tensor", 2), swap(gt_now, "tensor", 1),
        swap(after(send, gt_share), "dp", bits[1]),
    )
    late = (keep.astype(F32) + got.astype(F32)).astype(BF16)
    keep, send = halves_of(late, 1, (place // bits[2]) % 2)
    three, got = together(swap(two, "tensor", 1), swap(send, "dp", bits[2]))
    late = (keep.astype(F32) + got.astype(F32)).astype(BF16)
    for bit in bits[3:]:
        late = halve(late, bit)
    grad_tokens = whole_call(
        functools.partial(place_kernel, PIECES, shares),
        [shaped((rows, width), F32)], [idx, gt_share, one, two, three], moved=5 * mib,
    )[0]

    *sent, result_two, _ = together(
        *[swap(jnp.stack([late[4 + by], late[3]]), "tensor", by) for by in others],
        swap(after(result_share, two), "tensor", 2), grad_tokens,
    )
    out_sum, small = late[4].astype(F32), [late[3]]
    for got in sent:
        out_sum = out_sum + got[0].astype(F32)
        small.append(got[1])
    small = [part.astype(F32) for part in small]
    while len(small) > 1:
        small = [small[at] + small[at + 1] for at in range(0, len(small), 2)]
    late = jnp.concatenate(
        [late[:3], jnp.stack([small[0].astype(BF16), out_sum.astype(BF16)])], axis=0
    )

    expert_rows = lax.all_gather(expert_rows, "dp", axis=0, tiled=True)

    def joined(value, got, bit):
        low = (place // bit) % 2 == 0
        return jnp.concatenate([jnp.where(low, value, got), jnp.where(low, got, value)], axis=1)

    for bit in reversed(bits[3:]):
        late = joined(late, swap(late, "dp", bit), bit)
    grad_w_in = expert_rows.reshape(experts, 2, width, width)[:, 0].astype(F32)
    got = after(swap(late, "dp", bits[2]), grad_w_in)
    late = joined(late, got, bits[2])
    expert_rows = after(expert_rows, got)
    grad_w_down = expert_rows.reshape(experts, 2, width, width)[:, 1].astype(F32)
    got, _, result_three = together(
        swap(late, "dp", bits[1]), grad_w_down, swap(result_two, "tensor", 1)
    )
    late = joined(late, got, bits[1])
    result = whole_call(
        functools.partial(place_kernel, PIECES, shares),
        [shaped((rows, width), BF16)],
        [idx, result_share, result_one, result_two, result_three],
        moved=3 * mib,
    )[0]
    got = after(swap(late, "dp", bits[0]), result)
    late = joined(late, got, bits[0])
    grad_w_qkv = jnp.swapaxes(late[:3], 1, 2).astype(F32)
    grad_w_out = late[4].astype(F32)
    small = late[3].astype(F32)
    grad_rel = lax.dynamic_slice_in_dim(small, me * 8, 8, 0)
    first = 8 * shares
    return (
        result,
        grad_tokens,
        small[first + 8],
        grad_w_qkv,
        grad_w_out,
        grad_rel[:heads, :NB].T,
        small[first + 9],
        small[first : first + experts].T,
        grad_w_in,
        grad_w_down,
    )


def solution(mesh):
    placed = (
        P("dp", None),
        P("dp", None),
        P("dp", None),
        P("dp", None),
        P(),
        P(None, None, "tensor"),
        P("tensor", None),
        P(None, "tensor"),
        P(),
        P(),
        P(None, None, "tensor"),
        P(None, "tensor", None),
    )
    return jax.shard_map(
        body,
        mesh=mesh,
        in_specs=placed,
        out_specs=(
            P("dp", None),
            P("dp", None),
            P(),
            P(None, None, "tensor"),
            P("tensor", None),
            P(None, "tensor"),
            P(),
            P(),
            P(None, None, "tensor"),
            P(None, "tensor", None),
        ),
        check_vma=False,
    )
```
